32 devices in a mesh: dp: 8 (over z, x), tensor: 4 (over y, core).
Axes of the slice: x: 2, y: 2, z: 4, core: 2. Of those that a mesh axis runs over, the one named last changes fastest.
Arguments:
- inputs: float32 [16384, 1600], P(('dp', 'tensor')), may hold values from -6 to 6
- teacher: float32 [16384, 1600], P(('dp', 'tensor')), may hold values from -6 to 6
- segment_ids: int32 [16384], P('dp'), may hold values from 0 to 23, never falling along the last dimension, each value on 1 to 1536 neighbouring positions
- valid: int32 [16384], P(('dp', 'tensor')), may hold values from 0 to 1, as said below
- norm_in_gain: bfloat16 [1600], P('dp'), may hold values from 0.5 to 1.5
- w_query: bfloat16 [1600, 1600], P('dp'), may hold values from -0.15625 to 0.15625
- w_key: bfloat16 [1600, 320], P('dp'), may hold values from -0.15625 to 0.15625
- w_value: bfloat16 [1600, 320], P('dp'), may hold values from -0.15625 to 0.15625
- w_attn_out: bfloat16 [1600, 1600], P(None, 'dp'), may hold values from -0.15625 to 0.15625
- w_mamba_in: bfloat16 [1600, 2, 3200], P('dp', None, 'tensor'), may hold values from -0.15625 to 0.15625
- conv_weight: bfloat16 [4, 3200], P(None, 'dp'), may hold values from -3 to 3
- conv_bias: bfloat16 [3200], P('dp'), may hold values from -1 to 1
- x_proj: bfloat16 [3200, 132], P('dp'), may hold values from -0.21875 to 0.21875
- dt_proj: bfloat16 [100, 3200], P(None, 'dp'), may hold values from -0.625 to 0.625
- dt_bias: bfloat16 [3200], P('dp'), may hold values from -4 to -0.5
- a_log: bfloat16 [3200], P('dp'), may hold values from -5 to -0.5
- d_skip: bfloat16 [3200], P('dp'), may hold values from 0.5 to 1.5
- w_mamba_out: bfloat16 [3200, 1600], P('tensor', 'dp'), may hold values from -0.109375 to 0.109375
- attn_norm_gain: bfloat16 [1600], P('dp'), may hold values from 0.5 to 1.5
- ssm_norm_gain: bfloat16 [1600], P('dp'), may hold values from 0.5 to 1.5
- norm_mid_gain: bfloat16 [1600], P('dp'), may hold values from 0.5 to 1.5
- w_gate: bfloat16 [1600, 5504], P('dp', 'tensor'), may hold values from -0.15625 to 0.15625
- w_up: bfloat16 [1600, 5504], P('dp', 'tensor'), may hold values from -0.15625 to 0.15625
- w_down: bfloat16 [5504, 1600], P('tensor', 'dp'), may hold values from -0.078125 to 0.078125
Outputs:
- out: float32 [16384, 1600], P(('dp', 'tensor'))
- grad_inputs: float32 [16384, 1600], P(('dp', 'tensor'))
- grad_norm_in_gain: float32 [1600], P('dp')
- grad_w_query: float32 [1600, 1600], P('dp')
- grad_w_key: float32 [1600, 320], P('dp')
- grad_w_value: float32 [1600, 320], P('dp')
- grad_w_attn_out: float32 [1600, 1600], P(None, 'dp')
- grad_w_mamba_in: float32 [1600, 2, 3200], P('dp', None, 'tensor')
- grad_conv_weight: float32 [4, 3200], P(None, 'dp')
- grad_conv_bias: float32 [3200], P('dp')
- grad_x_proj: float32 [3200, 132], P('dp')
- grad_dt_proj: float32 [100, 3200], P(None, 'dp')
- grad_dt_bias: float32 [3200], P('dp')
- grad_a_log: float32 [3200], P('dp')
- grad_d_skip: float32 [3200], P('dp')
- grad_w_mamba_out: float32 [3200, 1600], P('tensor', 'dp')
- grad_attn_norm_gain: float32 [1600], P('dp')
- grad_ssm_norm_gain: float32 [1600], P('dp')
- grad_norm_mid_gain: float32 [1600], P('dp')
- grad_w_gate: float32 [1600, 5504], P('dp', 'tensor')
- grad_w_up: float32 [1600, 5504], P('dp', 'tensor')
- grad_w_down: float32 [5504, 1600], P('tensor', 'dp')
The draws below stay inside these ranges and needn't reach their ends.
Inputs may be any that keep to these rules, and one draw needn't show every extreme that they name: Every 16th token has valid = 1.
All inputs are finite; a program needn't handle non-finite values.
Results may differ from the reference program's by a relative error of at most 0.02.
The reference program's roundings to bfloat16 on the way count: a program that leaves them out, or rounds other values in their place, can miss the bound.
Values may be sent and summed in bfloat16 or wider, within the bound.
A program may use at most 448 MiB of HBM per device.

```python
import math
import jax
import jax.numpy as jnp
import numpy as np
from jax import lax

D = 1600
HEADS = 25
KV = 5
HEAD = 64
INNER = 3200
STATE = 16
RANK = 100
CONV = 4
FF = 5504
WINDOW = 1024
BLOCK = 512
STRETCH = 64
LEN = 2048
SEQ_GRP = 1
TOKENS = 16384


def draw_valid(key, part):
    positions = jnp.arange(TOKENS, dtype=jnp.int32)
    limit = 200 + 600 * positions // TOKENS
    rolls = jax.random.randint(key, (TOKENS,), 0, 1000, dtype=jnp.int32)
    return jnp.where((rolls < limit) | (positions % 16 == 0), 1, 0).astype(jnp.int32)


def shard_levels(key, dims, shards, low, top_value):
    level, own = 1.0, jax.random.fold_in(key, 6)
    for axis_at, blocks in shards:
        draws = jnp.exp(jax.random.uniform(jax.random.fold_in(own, axis_at), (blocks,), jnp.float32, low / len(shards), top_value / len(shards)))
        level = level * jnp.repeat(draws, dims[axis_at] // blocks).reshape([-1 if axis == axis_at else 1 for axis in range(len(dims))])
    return level


def split_up(number_of, total, bound, slope):
    weights = [(1 << 20) // math.isqrt(standing ** slope) + 1 for standing in range(2, number_of + 1)]
    surplus, given = total - bound - (number_of - 1), [1] * (number_of - 1)
    while surplus > 0:
        candidates = [i for i in range(number_of - 1) if given[i] < bound]
        mass, remaining = sum([weights[i] for i in candidates]), surplus
        for i in candidates:
            more = min(bound - given[i], max(1, remaining * weights[i] // mass), surplus)
            given[i] = given[i] + more
            surplus = surplus - more
    return np.array([bound] + given)


def uneven_parts(stream_key, amount, total, bound, skew):
    if amount == 2:
        one = jax.random.randint(stream_key, (), max(1, total - bound), min(bound, total - 1) + 1)
        return jnp.stack([one, total - one])
    lengths = jnp.asarray(split_up(amount, total, bound, skew), jnp.int32)
    couples = (amount - 1) // 2
    source_of, receiver = lengths[1:1 + 2 * couples:2], lengths[2:2 + 2 * couples:2]
    slack = jnp.minimum(source_of - 1, bound - receiver)
    shifted = jax.random.randint(jax.random.fold_in(stream_key, 1), (couples,), 0, 1 << 20) % (slack + 1)
    lengths = lengths.at[1:1 + 2 * couples:2].set(source_of - shifted).at[2:2 + 2 * couples:2].set(receiver + shifted)
    return lengths[jax.random.permutation(jax.random.fold_in(stream_key, 2), amount)]


def bell_draw(key, dims, scale, reach, shards=(), kind=jnp.bfloat16):
    level = shard_levels(key, dims, shards, -0.22, 0.18) if shards else 1.0
    drawn = jax.random.normal(key, dims, jnp.float32) * scale * level
    return jnp.minimum(jnp.maximum(drawn, -reach), reach).astype(kind)


def setup_inputs(seed: int = 0) -> dict:
    arg_keys = jax.random.split(jax.random.key(seed), 25)
    return {
        "inputs": bell_draw(arg_keys[0], (TOKENS, D), 1.0, 6.0, ((0, 32),), jnp.float32),
        "teacher": bell_draw(arg_keys[1], (TOKENS, D), 1.0, 6.0, ((0, 32),), jnp.float32),
        "segment_ids": jnp.searchsorted(jnp.cumsum(uneven_parts(arg_keys[2], TOKENS * 3 // LEN, TOKENS, LEN * 3 // 4, 2)), jnp.arange(TOKENS), side="right").astype(jnp.int32),
        "valid": draw_valid(jax.random.fold_in(arg_keys[24], 71), 0),
        "norm_in_gain": jnp.clip(1.0 + 0.1 * jax.random.normal(arg_keys[4], (D,), jnp.float32), 0.5, 1.5).astype(jnp.bfloat16),
        "w_query": bell_draw(arg_keys[5], (D, HEADS * HEAD), D ** -0.5, 0.15625, ((0, 8),)),
        "w_key": bell_draw(arg_keys[6], (D, KV * HEAD), D ** -0.5, 0.15625, ((0, 8),)),
        "w_value": bell_draw(arg_keys[7], (D, KV * HEAD), D ** -0.5, 0.15625, ((0, 8),)),
        "w_attn_out": bell_draw(arg_keys[8], (HEADS * HEAD, D), (HEADS * HEAD) ** -0.5, 0.15625, ((1, 8),)),
        "w_mamba_in": bell_draw(arg_keys[9], (D, 2, INNER), D ** -0.5, 0.15625, ((0, 8), (2, 4))),
        "conv_weight": bell_draw(arg_keys[10], (CONV, INNER), CONV ** -0.5, 3.0, ((1, 8),)),
        "conv_bias": jnp.clip(jax.random.uniform(arg_keys[11], (INNER,), jnp.float32, -1.0, 1.0) * shard_levels(arg_keys[11], (INNER,), ((0, 8),), -0.4, 0.0), -1.0, 1.0).astype(jnp.bfloat16),
        "x_proj": bell_draw(arg_keys[12], (INNER, RANK + 2 * STATE), (INNER // 4) ** -0.5, 0.21875, ((0, 8),)),
        "dt_proj": bell_draw(arg_keys[13], (RANK, INNER), RANK ** -0.5, 0.625, ((1, 8),)),
        "dt_bias": jnp.clip(-4.0 + 3.5 * jax.random.uniform(arg_keys[14], (INNER,), jnp.float32) ** shard_levels(arg_keys[14], (INNER,), ((0, 8),), -0.2, 0.2), -4.0, -0.5).astype(jnp.bfloat16),
        "a_log": jnp.clip(-5.0 + 4.5 * jax.random.uniform(arg_keys[15], (INNER,), jnp.float32) ** shard_levels(arg_keys[15], (INNER,), ((0, 8),), -0.2, 0.2), -5.0, -0.5).astype(jnp.bfloat16),
        "d_skip": jnp.clip(0.5 + 1.0 * jax.random.uniform(arg_keys[16], (INNER,), jnp.float32) ** shard_levels(arg_keys[16], (INNER,), ((0, 8),), -0.2, 0.2), 0.5, 1.5).astype(jnp.bfloat16),
        "w_mamba_out": bell_draw(arg_keys[17], (INNER, D), INNER ** -0.5, 0.109375, ((0, 4), (1, 8))),
        "attn_norm_gain": jnp.clip(1.0 + 0.1 * jax.random.normal(arg_keys[18], (D,), jnp.float32), 0.5, 1.5).astype(jnp.bfloat16),
        "ssm_norm_gain": jnp.clip(1.0 + 0.1 * jax.random.normal(arg_keys[19], (D,), jnp.float32), 0.5, 1.5).astype(jnp.bfloat16),
        "norm_mid_gain": jnp.clip(1.0 + 0.1 * jax.random.normal(arg_keys[20], (D,), jnp.float32), 0.5, 1.5).astype(jnp.bfloat16),
        "w_gate": bell_draw(arg_keys[21], (D, FF), D ** -0.5, 0.15625, ((0, 8), (1, 4))),
        "w_up": bell_draw(arg_keys[22], (D, FF), D ** -0.5, 0.15625, ((0, 8), (1, 4))),
        "w_down": bell_draw(arg_keys[23], (FF, D), FF ** -0.5, 0.078125, ((0, 4), (1, 8))),
    }


EPSILON = 1e-06
MASKED = -1e+30
HIGHEST = lax.Precision.HIGHEST

@jax.custom_vjp
def low(v):
    return lax.optimization_barrier(v.astype(jnp.bfloat16)).astype(jnp.float32)

@jax.custom_vjp
def low_back(v):
    return v

def low_keep(v):
    return (low(v), None)

def low_pass(kept, grad):
    return (grad,)

def back_keep(v):
    return (v, None)

def back_low(kept, grad):
    return (low(grad),)
low.defvjp(low_keep, low_pass)
low_back.defvjp(back_keep, back_low)

def round_both(values):
    return low(low_back(values))

def matmul(left, right):
    return jnp.dot(left, right, precision=HIGHEST)

def normalize(values, gain):
    return values * lax.rsqrt(lax.optimization_barrier(jnp.mean(values * values, axis=-1, keepdims=True)) + EPSILON) * gain

def join_rows(resid, attn_sum, ssm_sum, gain_attn, gain_ssm):
    return resid + 0.5 * (normalize(attn_sum, gain_attn) + normalize(ssm_sum, gain_ssm))

def front_pad(values, fill):
    new_shape = (WINDOW,) + values.shape[1:]
    return jnp.concatenate([jnp.full(new_shape, fill, values.dtype), values], axis=0)

def block_mask(block_start, query_seg, key_seg):
    query_pos = block_start + jnp.arange(BLOCK, dtype=jnp.int32)
    key_pos = block_start - WINDOW + jnp.arange(WINDOW + BLOCK, dtype=jnp.int32)
    offset = query_pos[:, None] - key_pos[None, :]
    return (offset >= 0) & (offset < WINDOW) & (query_seg[:, None] == key_seg[None, :])

def attend_sequence(pieces):
    queries, keys, values, segs = pieces
    key_pad = front_pad(keys, 0.0)
    value_pad = front_pad(values, 0.0)
    seg_pad = front_pad(segs, -1)

    def one_block(block_index):
        block_start = block_index * BLOCK
        query_blk = lax.dynamic_slice_in_dim(queries, block_start, BLOCK, 0)
        key_blk = lax.dynamic_slice_in_dim(key_pad, block_start, WINDOW + BLOCK, 0)
        value_blk = lax.dynamic_slice_in_dim(value_pad, block_start, WINDOW + BLOCK, 0)
        allowed = block_mask(block_start, lax.dynamic_slice_in_dim(segs, block_start, BLOCK, 0), lax.dynamic_slice_in_dim(seg_pad, block_start, WINDOW + BLOCK, 0))
        scores = low_back(jnp.einsum('qgjd,kgd->gjqk', query_blk, key_blk, precision=HIGHEST) * 0.125)
        masked = jnp.where(allowed, scores, MASKED)
        row_max = lax.optimization_barrier(jnp.max(masked, axis=-1, keepdims=True))
        expo = jnp.exp(masked - row_max)
        weights = low(expo / lax.optimization_barrier(jnp.sum(expo, axis=-1, keepdims=True)))
        return jnp.einsum('gjqk,kgd->qgjd', weights, value_blk, precision=HIGHEST)
    outputs = lax.map(jax.checkpoint(one_block), jnp.arange(LEN // BLOCK, dtype=jnp.int32))
    return outputs.reshape(LEN, HEADS * HEAD)

def conv_rows(x_in, conv_w, conv_b, segs_grid):
    seq_count, seq_len = segs_grid.shape
    width = x_in.shape[1]
    grid = x_in.reshape(seq_count, seq_len, width)
    pad_x = jnp.concatenate([jnp.zeros((seq_count, CONV - 1, width), jnp.float32), grid], axis=1)
    pad_seg = jnp.concatenate([jnp.full((seq_count, CONV - 1), -1, jnp.int32), segs_grid], axis=1)
    total = jnp.zeros((seq_count, seq_len, width), jnp.float32) + conv_b
    for tap in range(CONV):
        same = (pad_seg[:, tap:tap + seq_len] == segs_grid).astype(jnp.float32)
        total = total + conv_w[tap] * pad_x[:, tap:tap + seq_len] * same[:, :, None]
    return jax.nn.silu(total).reshape(seq_count * seq_len, width)

def stretch_step(carry_state, piece, decay_rate):
    carried, seg_before = carry_state
    inner_rows, step_rows, input_map, output_map, piece_segs = piece
    piece_len = piece_segs.shape[0]
    positions = jnp.arange(piece_len, dtype=jnp.int32)
    lower_tri = positions[:, None] >= positions[None, :]
    log_decay = -step_rows * decay_rate
    cumulated = jnp.dot(lower_tri.astype(jnp.float32), log_decay, precision=HIGHEST)
    allowed = lower_tri & (piece_segs[:, None] == piece_segs[None, :])
    gap_values = jnp.where(allowed[:, :, None], cumulated[:, None, :] - cumulated[None, :, :], 0.0)
    transfer = jnp.where(allowed[:, :, None], jnp.exp(gap_values), 0.0)
    gram_matrix = jnp.dot(output_map, input_map.T, precision=HIGHEST)
    drive_term = step_rows * inner_rows
    within = jnp.einsum('tsc,ts,sc->tc', transfer, gram_matrix, drive_term, precision=HIGHEST)
    linked = (piece_segs == seg_before).astype(jnp.float32)
    from_state = jnp.exp(cumulated) * jnp.dot(output_map, carried, precision=HIGHEST) * linked[:, None]
    last_seg = piece_segs[piece_len - 1]
    tail_mask = (piece_segs == last_seg).astype(jnp.float32)
    end_decay = cumulated[piece_len - 1]
    pushed = jnp.exp(end_decay[None, :] - cumulated) * tail_mask[:, None] * drive_term
    keep_state = jnp.where(last_seg == seg_before, 1.0, 0.0).astype(jnp.float32)
    fresh_state = jnp.exp(end_decay)[None, :] * carried * keep_state + jnp.dot(input_map.T, pushed, precision=HIGHEST)
    return ((fresh_state, last_seg), within + from_state)

def scan_sequence(pieces, decay_rate, skip):
    inner_part, gate_part, step_size, maps, segs = pieces
    count = segs.shape[0] // STRETCH
    width = inner_part.shape[1]
    parts = (inner_part.reshape(count, STRETCH, width), step_size.reshape(count, STRETCH, width), maps[:, :STATE].reshape(count, STRETCH, STATE), maps[:, STATE:].reshape(count, STRETCH, STATE), segs.reshape(count, STRETCH))
    initial = (jnp.zeros((STATE, width), jnp.float32), jnp.array(-1, jnp.int32))
    stepper = jax.checkpoint(stretch_step)
    _, outputs = lax.scan(lambda carry_state, piece: stepper(carry_state, piece, decay_rate), initial, parts)
    result = outputs.reshape(segs.shape[0], width) + skip * inner_part
    return result * jax.nn.silu(gate_part)

def mamba_rows(x_act, z_gate, x_dbl, dt_weight, vectors, segs_grid):
    seq_count, seq_len = segs_grid.shape
    width = x_act.shape[1]
    step_size = jax.nn.softplus(jnp.dot(x_dbl[:, :RANK], dt_weight, precision=HIGHEST) + vectors[0])
    decay_rate = jnp.exp(vectors[1])
    maps = x_dbl[:, RANK:]

    def one_sequence(pieces):
        return scan_sequence(pieces, decay_rate, vectors[2])
    outputs = lax.map(one_sequence, (x_act.reshape(seq_count, seq_len, width), z_gate.reshape(seq_count, seq_len, width), step_size.reshape(seq_count, seq_len, width), maps.reshape(seq_count, seq_len, 2 * STATE), segs_grid))
    return outputs.reshape(seq_count * seq_len, width)

def forward_rows(rows, segs, params):
    norm_in_gain, w_query, w_key, w_value, w_attn_out, w_mamba_in, conv_weight, conv_bias, x_proj, dt_proj, dt_bias, a_log, d_skip, w_mamba_out, attn_norm_gain, ssm_norm_gain, norm_mid_gain, w_gate, w_up, w_down = params
    rows_total = rows.shape[0]
    seq_count = rows_total // LEN
    segs_grid = segs.reshape(seq_count, LEN)
    normed_in = low(normalize(rows, norm_in_gain))
    queries = round_both(matmul(normed_in, w_query)).reshape(seq_count, LEN, KV, HEADS // KV, HEAD)
    keys = round_both(matmul(normed_in, w_key)).reshape(seq_count, LEN, KV, HEAD)
    values = round_both(matmul(normed_in, w_value)).reshape(seq_count, LEN, KV, HEAD)
    attended = lax.map(attend_sequence, (queries, keys, values, segs_grid))
    attended = round_both(attended.reshape(rows_total, HEADS * HEAD))
    attn_sum = low_back(matmul(attended, w_attn_out))
    mixing = low_back(matmul(normed_in, w_mamba_in.reshape(D, 2 * INNER))).reshape(rows_total, 2, INNER)
    x_act = low(conv_rows(mixing[:, 0], conv_weight, conv_bias, segs_grid))
    x_dbl = round_both(matmul(x_act, x_proj))
    vectors = jnp.stack([dt_bias, a_log, d_skip])
    ssm_rows = low(mamba_rows(x_act, mixing[:, 1], x_dbl, dt_proj, vectors, segs_grid))
    ssm_sum = low_back(matmul(ssm_rows, w_mamba_out))
    mixed = join_rows(rows, attn_sum, ssm_sum, attn_norm_gain, ssm_norm_gain)
    normed_mid = low(normalize(mixed, norm_mid_gain))
    gate = low_back(matmul(normed_mid, w_gate))
    upper = low_back(matmul(normed_mid, w_up))
    hidden = low(jax.nn.silu(gate) * upper)
    return mixed + low_back(matmul(hidden, w_down))

def reference(inputs, teacher, segment_ids, valid, norm_in_gain, w_query, w_key, w_value, w_attn_out, w_mamba_in, conv_weight, conv_bias, x_proj, dt_proj, dt_bias, a_log, d_skip, w_mamba_out, attn_norm_gain, ssm_norm_gain, norm_mid_gain, w_gate, w_up, w_down):
    weights = tuple((item.astype(jnp.float32) for item in (norm_in_gain, w_query, w_key, w_value, w_attn_out, w_mamba_in, conv_weight, conv_bias, x_proj, dt_proj, dt_bias, a_log, d_skip, w_mamba_out, attn_norm_gain, ssm_norm_gain, norm_mid_gain, w_gate, w_up, w_down)))
    valid_total = jnp.sum(valid).astype(jnp.float32)
    factor = TOKENS / valid_total
    group_rows = SEQ_GRP * LEN
    groups = TOKENS // group_rows

    def one_group(totals, pieces):
        rows, target, segs, marks = pieces

        def objective(rows_in, *params):
            result = forward_rows(rows_in, segs, params)
            error = result - target
            return (0.5 * factor * jnp.sum(marks[:, None] * error * error), result)
        _, pull, result = jax.vjp(objective, rows, *weights, has_aux=True)
        grads = pull(jnp.ones((), jnp.float32))
        return (tuple((left + right for left, right in zip(totals, grads[1:]))), (result, grads[0]))
    initial = tuple((jnp.zeros_like(item) for item in weights))
    totals, (results, grad_rows) = lax.scan(one_group, initial, (inputs.reshape(groups, group_rows, D), teacher.reshape(groups, group_rows, D), segment_ids.reshape(groups, group_rows), valid.astype(jnp.float32).reshape(groups, group_rows)))
    return (results.reshape(TOKENS, D), grad_rows.reshape(TOKENS, D), totals[0], totals[1], totals[2], totals[3], totals[4], totals[5], totals[6], totals[7], totals[8], totals[9], totals[10], totals[11], totals[12], totals[13], totals[14], totals[15], totals[16], totals[17], totals[18], totals[19])
```

```python
import functools

import jax
import jax.numpy as jnp
from jax import lax
from jax.experimental import pallas as pl
from jax.experimental.pallas import tpu as pltpu
from jax.sharding import PartitionSpec as P

HEADS = 25
KV = 5
HEAD = 64
STATE = 16
RANK = 100
CONV = 4
WINDOW = 1024
BLOCK = 512
STRETCH = 64
LEN = 2048


EPSILON = 1e-06
MASKED = -1e30
HIGHEST = lax.Precision.HIGHEST


def normalize_t(values, gain):
    return values * lax.rsqrt(jnp.mean(values * values, axis=0, keepdims=True) + EPSILON) * gain


def join_rows_t(resid, attn_sum, ssm_sum, gain_attn, gain_ssm):
    return resid + 0.5 * (normalize_t(attn_sum, gain_attn) + normalize_t(ssm_sum, gain_ssm))


def dot_plain(left, right):
    return jnp.dot(left, right, preferred_element_type=jnp.float32)


def dot_last(left, right):
    return lax.dot_general(
        left, right, (((1,), (1,)), ((), ())), preferred_element_type=jnp.float32
    )


def dot_first(left, right):
    return lax.dot_general(
        left, right, (((0,), (0,)), ((), ())), preferred_element_type=jnp.float32
    )


def pick_groups(weight, first_slot, second_slot, group_width, axis):
    return jnp.concatenate(
        [
            lax.dynamic_slice_in_dim(weight, first_slot * group_width, group_width, axis),
            lax.dynamic_slice_in_dim(weight, second_slot * group_width, group_width, axis),
        ],
        axis=axis,
    )


PIECES = 4
MESH = pl.DeviceIdType.MESH


def tensor_peers():
    me = lax.axis_index("tensor")
    side = me + 1 - 2 * lax.rem(me, 2)
    cross = lax.rem(me + 2, 4)
    return me, side, cross, lax.rem(side + 2, 4)


def greet(peers):
    barrier = pltpu.get_barrier_semaphore()
    for peer in peers:
        pl.semaphore_signal(barrier, inc=1, device_id={"tensor": peer}, device_id_type=MESH)
    pl.semaphore_wait(barrier, len(peers))


def push(src, dst, sems, index, peer):
    copy = pltpu.make_async_remote_copy(
        src_ref=src,
        dst_ref=dst,
        send_sem=sems[0].at[index],
        recv_sem=sems[1].at[index],
        device_id={"tensor": peer},
        device_id_type=MESH,
    )
    copy.start()
    return copy


def columns(block, size):
    return pl.ds(pl.multiple_of(block * size, size), size)


def gather_kernel(part_ref, whole_ref, own_sem, *sems):
    me, side, cross, diag = tensor_peers()
    depth, size = part_ref.shape
    step = depth // PIECES
    mine = columns(me, size)
    theirs = columns(cross, size)
    greet((side, cross))
    own = pltpu.make_async_copy(part_ref, whole_ref.at[:, mine], own_sem)
    own.start()
    over, near, relay = [], [], []
    for piece in range(PIECES):
        rows = pl.ds(piece * step, step)
        over.append(
            push(part_ref.at[rows], whole_ref.at[rows, mine], sems[0:2], piece, cross)
        )
    for piece in range(PIECES):
        rows = pl.ds(piece * step, step)
        near.append(push(part_ref.at[rows], whole_ref.at[rows, mine], sems[2:4], piece, side))
    for piece in range(PIECES):
        rows = pl.ds(piece * step, step)
        over[piece].wait_recv()
        relay.append(
            push(whole_ref.at[rows, theirs], whole_ref.at[rows, theirs], sems[4:6], piece, side)
        )
    own.wait()
    for piece in range(PIECES):
        over[piece].wait_send()
        near[piece].wait()
        relay[piece].wait()


def gather_rows(part, call_id):
    depth, size = part.shape
    return pl.pallas_call(
        gather_kernel,
        name="gather_rows",
        in_specs=[pl.BlockSpec(memory_space=pl.ANY)],
        out_specs=pl.BlockSpec(memory_space=pl.ANY),
        out_shape=jax.ShapeDtypeStruct((depth, 4 * size), part.dtype),
        scratch_shapes=[pltpu.SemaphoreType.DMA] + [pltpu.SemaphoreType.DMA((PIECES,))] * 6,
        compiler_params=pltpu.CompilerParams(
            collective_id=call_id, has_side_effects=True, vmem_limit_bytes=1 << 20
        ),
        cost_estimate=pl.CostEstimate(
            flops=0, bytes_accessed=depth * size * 2 * 90, transcendentals=0
        ),
    )(part)


def reduce_kernel(part_ref, out_ref, near_buf, own_buf, stage_buf, far_buf, *sems):
    me, side, cross, diag = tensor_peers()
    depth, size = out_ref.shape
    step = depth // PIECES
    greet((side, cross))
    first, second, third = [], [], []
    for piece in range(PIECES):
        rows = pl.ds(piece * step, step)
        first.append(
            push(part_ref.at[rows, columns(diag, size)], near_buf.at[rows], sems[0:2], piece, side)
        )
    for piece in range(PIECES):
        rows = pl.ds(piece * step, step)
        second.append(
            push(part_ref.at[rows, columns(side, size)], own_buf.at[rows], sems[2:4], piece, side)
        )
    for piece in range(PIECES):
        rows = pl.ds(piece * step, step)
        first[piece].wait_recv()
        stage_buf[rows] = (
            part_ref[rows, columns(cross, size)].astype(jnp.float32)
            + near_buf[rows].astype(jnp.float32)
        ).astype(jnp.bfloat16)
        third.append(push(stage_buf.at[rows], far_buf.at[rows], sems[4:6], piece, cross))
    for piece in range(PIECES):
        rows = pl.ds(piece * step, step)
        second[piece].wait_recv()
        out_ref[rows] = part_ref[rows, columns(me, size)].astype(jnp.float32) + own_buf[
            rows
        ].astype(jnp.float32)
    for piece in range(PIECES):
        rows = pl.ds(piece * step, step)
        third[piece].wait_recv()
        out_ref[rows] += far_buf[rows].astype(jnp.float32)
    for piece in range(PIECES):
        first[piece].wait_send()
        second[piece].wait_send()
        third[piece].wait_send()


def reduce_rows(part, call_id):
    depth, total = part.shape
    size = total // 4
    whole = pl.BlockSpec(memory_space=pltpu.VMEM)
    return pl.pallas_call(
        reduce_kernel,
        name="reduce_rows",
        in_specs=[whole],
        out_specs=whole,
        out_shape=jax.ShapeDtypeStruct((depth, size), jnp.float32),
        scratch_shapes=[pltpu.VMEM((depth, size), jnp.bfloat16)] * 4
        + [pltpu.SemaphoreType.DMA((PIECES,))] * 6,
        compiler_params=pltpu.CompilerParams(
            collective_id=call_id, has_side_effects=True, vmem_limit_bytes=32 << 20
        ),
        cost_estimate=pl.CostEstimate(
            flops=0, bytes_accessed=depth * size * 2 * 90, transcendentals=0
        ),
    )(part)


def total_kernel(part_ref, out_ref, near_buf, own_buf, stage_buf, far_buf, low_buf, own_sem, *sems):
    me, side, cross, diag = tensor_peers()
    size, wide = low_buf.shape
    half = size // 2
    greet((side, cross))
    rows_of = lambda block, at: pl.ds(pl.multiple_of(block * size + at, half), half)
    pieces = (0, half)
    first = [
        push(part_ref.at[rows_of(diag, at)], near_buf.at[pl.ds(at, half)], sems[0:2], i, side)
        for i, at in enumerate(pieces)
    ]
    second = [
        push(part_ref.at[rows_of(side, at)], own_buf.at[pl.ds(at, half)], sems[2:4], i, side)
        for i, at in enumerate(pieces)
    ]
    third, over, near, relay = [], [], [], []
    for i, at in enumerate(pieces):
        rows = pl.ds(at, half)
        first[i].wait_recv()
        stage_buf[rows] = (part_ref[rows_of(cross, at)] + near_buf[rows]).astype(jnp.bfloat16)
        third.append(push(stage_buf.at[rows], far_buf.at[rows], sems[4:6], i, cross))
    for i, at in enumerate(pieces):
        rows = pl.ds(at, half)
        second[i].wait_recv()
        third[i].wait_recv()
        low_buf[rows] = (
            part_ref[rows_of(me, at)] + own_buf[rows] + far_buf[rows].astype(jnp.float32)
        ).astype(jnp.bfloat16)
        over.append(push(low_buf.at[rows], out_ref.at[rows_of(me, at)], sems[6:8], i, cross))
        near.append(push(low_buf.at[rows], out_ref.at[rows_of(me, at)], sems[8:10], i, side))
    own = pltpu.make_async_copy(
        low_buf, out_ref.at[pl.ds(pl.multiple_of(me * size, size), size)], own_sem
    )
    own.start()
    for i, at in enumerate(pieces):
        over[i].wait_recv()
        relay.append(
            push(out_ref.at[rows_of(cross, at)], out_ref.at[rows_of(cross, at)], sems[10:12], i, side)
        )
    own.wait()
    for i in range(2):
        for group in (first, second, third, over):
            group[i].wait_send()
        near[i].wait()
        relay[i].wait()


def total_rows(part, call_id):
    tokens, wide = part.shape
    size = tokens // 4
    whole = pl.BlockSpec(memory_space=pltpu.VMEM)
    return pl.pallas_call(
        total_kernel,
        name="total_rows",
        in_specs=[whole],
        out_specs=whole,
        out_shape=jax.ShapeDtypeStruct((tokens, wide), jnp.bfloat16),
        scratch_shapes=[
            pltpu.VMEM((size, wide), jnp.float32),
            pltpu.VMEM((size, wide), jnp.float32),
            pltpu.VMEM((size, wide), jnp.bfloat16),
            pltpu.VMEM((size, wide), jnp.bfloat16),
            pltpu.VMEM((size, wide), jnp.bfloat16),
            pltpu.SemaphoreType.DMA,
        ]
        + [pltpu.SemaphoreType.DMA((2,))] * 12,
        compiler_params=pltpu.CompilerParams(
            collective_id=call_id, has_side_effects=True, vmem_limit_bytes=32 << 20
        ),
        cost_estimate=pl.CostEstimate(flops=0, bytes_accessed=60 << 20, transcendentals=0),
    )(part)


def hello_kernel(gain_ref, count_ref, gains_ref, counts_ref, sum_buf, local_buf, *sems):
    me = lax.axis_index("tensor")
    place = lax.axis_index("dp")
    ranks, groups = local_buf.shape[0], gains_ref.shape[0]
    barrier = pltpu.get_barrier_semaphore()
    others = [{"tensor": lax.rem(me + hop, ranks)} for hop in range(1, ranks)]
    far = [{"dp": lax.rem(place + hop, groups)} for hop in range(1, groups)]
    for peer in others + far:
        pl.semaphore_signal(barrier, inc=1, device_id=peer, device_id_type=MESH)
    pl.semaphore_wait(barrier, len(others) + len(far))

    def send(src, dst, index, peer):
        copy = pltpu.make_async_remote_copy(
            src_ref=src,
            dst_ref=dst,
            send_sem=sems[0].at[index],
            recv_sem=sems[1].at[index],
            device_id=peer,
            device_id_type=MESH,
        )
        copy.start()
        return copy

    first = [send(count_ref, local_buf.at[me], i, peer) for i, peer in enumerate(others)]
    local_buf[me] = count_ref[...]
    gains_ref[place] = gain_ref[...]
    base = len(first)
    second = [send(gain_ref, gains_ref.at[place], base + i, peer) for i, peer in enumerate(far)]
    base += len(second)
    for copy in first:
        copy.wait()
    sum_buf[...] = jnp.sum(local_buf[...], axis=0)
    counts_ref[place] = sum_buf[...]
    third = [send(sum_buf, counts_ref.at[place], base + i, peer) for i, peer in enumerate(far)]
    for copy in second + third:
        copy.wait()


def hello(gains, count):
    wide = -(-gains.shape[1] // 128) * 128
    block = jnp.zeros((8, wide), jnp.float32)
    block = lax.dynamic_update_slice(block, gains.astype(jnp.float32), (0, 0))
    counts = jnp.full((8, 128), count, jnp.float32)
    groups, ranks = lax.axis_size("dp"), lax.axis_size("tensor")
    copies = ranks - 1 + 2 * (groups - 1)
    whole = pl.BlockSpec(memory_space=pltpu.VMEM)
    gains_all, counts_all = pl.pallas_call(
        hello_kernel,
        name="hello",
        in_specs=[whole, whole],
        out_specs=[whole, whole],
        out_shape=[
            jax.ShapeDtypeStruct((groups, 8, wide), jnp.float32),
            jax.ShapeDtypeStruct((groups, 8, 128), jnp.float32),
        ],
        scratch_shapes=[
            pltpu.VMEM((8, 128), jnp.float32),
            pltpu.VMEM((ranks, 8, 128), jnp.float32),
        ]
        + [pltpu.SemaphoreType.DMA((copies,))] * 2,
        compiler_params=pltpu.CompilerParams(collective_id=0, has_side_effects=True),
        cost_estimate=pl.CostEstimate(flops=0, bytes_accessed=30 << 20, transcendentals=0),
    )(block, counts)
    gains_full = gains_all[:, :4, : gains.shape[1]].transpose(1, 0, 2).reshape(4, -1)
    return gains_full, jnp.sum(counts_all[:, 0, 0])


TILE = 400


def weights_kernel(plan, *refs):
    out_ref = refs[-1]
    index = 0
    for mode, offset, size, pad in plan:
        left = refs[index][...]
        if mode == "copy":
            product = left
            index += 1
        else:
            right = refs[index + 1][...]
            product = dot_last(left, right) if mode == "flip" else dot_plain(left, right)
            index += 2
        out_ref[:, offset : offset + size] = product.astype(jnp.bfloat16)
        if pad:
            out_ref[:, offset + size : offset + size + pad] = jnp.zeros(
                (out_ref.shape[0], pad), jnp.bfloat16
            )


def weight_grads(pairs, name, micros, widen=0):
    rows = pairs[0][0].shape[0]
    tile = TILE if rows % TILE == 0 else rows
    plan, specs, operands, offset = [], [], [], 0
    for left, right, flip in pairs:
        source = left if right is None else right
        size = source.shape[0] if flip else source.shape[1]
        pad = -size % 128 + (widen if len(plan) + 1 == len(pairs) else 0)
        mode = "copy" if right is None else "flip" if flip else "plain"
        plan.append((mode, offset, size, pad))
        offset += size + pad
        specs.append(pl.BlockSpec((tile, left.shape[1]), lambda i: (i, 0)))
        operands.append(left)
        if right is not None:
            specs.append(
                pl.BlockSpec(right.shape, lambda i: (0, 0), pipeline_mode=pl.Buffered(1))
            )
            operands.append(right)
    return pl.pallas_call(
        functools.partial(weights_kernel, plan),
        name=name,
        grid=(rows // tile,),
        in_specs=specs,
        out_specs=pl.BlockSpec((tile, offset), lambda i: (i, 0)),
        out_shape=jax.ShapeDtypeStruct((rows, offset), jnp.bfloat16),
        compiler_params=pltpu.CompilerParams(vmem_limit_bytes=52 << 20),
        cost_estimate=pl.CostEstimate(
            flops=0, bytes_accessed=int(micros * 3.6) << 20, transcendentals=0
        ),
    )(*operands)


def farewell_kernel(part_ref, out_ref, group_buf, sum_buf, rank_buf, *sems):
    me = lax.axis_index("tensor")
    place = lax.axis_index("dp")
    ranks, groups = rank_buf.shape[0], group_buf.shape[0]
    barrier = pltpu.get_barrier_semaphore()
    others = [lax.rem(me + hop, ranks) for hop in range(1, ranks)]
    far = [lax.rem(place + hop, groups) for hop in range(1, groups)]
    for peer in others:
        pl.semaphore_signal(barrier, inc=1, device_id={"tensor": peer}, device_id_type=MESH)
    for peer in far:
        pl.semaphore_signal(barrier, inc=1, device_id={"dp": peer}, device_id_type=MESH)
    pl.semaphore_wait(barrier, len(others) + len(far))

    def send(src, dst, index, peer):
        copy = pltpu.make_async_remote_copy(
            src_ref=src,
            dst_ref=dst,
            send_sem=sems[0].at[index],
            recv_sem=sems[1].at[index],
            device_id=peer,
            device_id_type=MESH,
        )
        copy.start()
        return copy

    first = [
        send(part_ref.at[peer], group_buf.at[place], i, {"dp": peer}) for i, peer in enumerate(far)
    ]
    group_buf[place] = part_ref[place]
    for copy in first:
        copy.wait()
    sum_buf[...] = jnp.sum(group_buf[...], axis=0)
    rank_buf[me] = sum_buf[...]
    second = [
        send(sum_buf, rank_buf.at[me], len(first) + i, {"tensor": peer})
        for i, peer in enumerate(others)
    ]
    for copy in second:
        copy.wait()
    out_ref[...] = jnp.sum(rank_buf[...], axis=0)


def farewell(grads):
    groups, ranks = lax.axis_size("dp"), lax.axis_size("tensor")
    kinds, total = grads.shape
    own = total // groups
    wide = -(-own // 128) * 128
    parts = jnp.pad(
        grads.reshape(kinds, groups, own).transpose(1, 0, 2),
        ((0, 0), (0, 8 - kinds), (0, wide - own)),
    )
    whole = pl.BlockSpec(memory_space=pltpu.VMEM)
    summed = pl.pallas_call(
        farewell_kernel,
        name="farewell",
        in_specs=[whole],
        out_specs=whole,
        out_shape=jax.ShapeDtypeStruct((8, wide), jnp.float32),
        scratch_shapes=[
            pltpu.VMEM((groups, 8, wide), jnp.float32),
            pltpu.VMEM((8, wide), jnp.float32),
            pltpu.VMEM((ranks, 8, wide), jnp.float32),
        ]
        + [pltpu.SemaphoreType.DMA((groups + ranks - 2,))] * 2,
        compiler_params=pltpu.CompilerParams(
            collective_id=4, has_side_effects=True, vmem_limit_bytes=4 << 20
        ),
        cost_estimate=pl.CostEstimate(flops=0, bytes_accessed=40 << 20, transcendentals=0),
    )(parts)
    return summed[:kinds, :own]


def stack_kernel(part_ref, whole_ref, own_sem, *sems):
    me, side, cross, diag = tensor_peers()
    step = part_ref.shape[1] // 2
    greet((side, cross))
    own = pltpu.make_async_copy(part_ref, whole_ref.at[me], own_sem)
    own.start()
    cols = [pl.ds(0, step), pl.ds(step, step)]
    over = [
        push(part_ref.at[:, at], whole_ref.at[me, :, at], sems[0:2], i, cross)
        for i, at in enumerate(cols)
    ]
    near = [
        push(part_ref.at[:, at], whole_ref.at[me, :, at], sems[2:4], i, side)
        for i, at in enumerate(cols)
    ]
    relay = []
    for i, at in enumerate(cols):
        over[i].wait_recv()
        relay.append(
            push(whole_ref.at[cross, :, at], whole_ref.at[cross, :, at], sems[4:6], i, side)
        )
    own.wait()
    for i in range(2):
        over[i].wait_send()
        near[i].wait()
        relay[i].wait()


def gather_stack(part):
    return pl.pallas_call(
        stack_kernel,
        name="gather_stack",
        in_specs=[pl.BlockSpec(memory_space=pl.ANY)],
        out_specs=pl.BlockSpec(memory_space=pl.ANY),
        out_shape=jax.ShapeDtypeStruct((4,) + part.shape, part.dtype),
        scratch_shapes=[pltpu.SemaphoreType.DMA] + [pltpu.SemaphoreType.DMA((2,))] * 6,
        compiler_params=pltpu.CompilerParams(
            collective_id=5, has_side_effects=True, vmem_limit_bytes=1 << 20
        ),
        cost_estimate=pl.CostEstimate(flops=0, bytes_accessed=60 << 20, transcendentals=0),
    )(part)


def place_block(piece, start, full_width, axis):
    new_shape = list(piece.shape)
    new_shape[axis] = full_width
    return lax.dynamic_update_slice_in_dim(
        jnp.zeros(tuple(new_shape), jnp.float32), piece, start, axis
    )


BQ = 256
BK = 256


def attn_mask(q_base, k_base, segq_row, segk_col):
    q_pos = q_base + lax.broadcasted_iota(jnp.int32, (BK, BQ), 1)
    k_pos = k_base + lax.broadcasted_iota(jnp.int32, (BK, BQ), 0)
    offset = q_pos - k_pos
    return (offset >= 0) & (offset < WINDOW) & (segk_col == segq_row)


def attn_fwd_kernel(first_ref, qt_ref, k_ref, vt_ref, segr_ref, segc_ref, ot_ref, lse_ref,
                    max_scr, sum_scr, acc_scr):
    heads = qt_ref.shape[0] // HEAD
    block = pl.program_id(1)
    q_base = block * BQ
    max_scr[...] = jnp.full_like(max_scr, MASKED)
    sum_scr[...] = jnp.zeros_like(sum_scr)
    acc_scr[...] = jnp.zeros_like(acc_scr)
    segq_row = segr_ref[0:1, :]

    def body(j, carry):
        k_base = pl.multiple_of(j * BK, BK)
        rows = pl.ds(k_base, BK)
        allowed = attn_mask(q_base, k_base, segq_row, segc_ref[rows, 0:1])
        bias = jnp.where(allowed, 0.0, MASKED)
        k_blk = k_ref[0, rows, :]
        v_blk = vt_ref[:, rows]
        for head in range(heads):
            cols = slice(head * HEAD, (head + 1) * HEAD)
            scores = dot_plain(k_blk, qt_ref[cols, :]) * 0.125 + bias
            old_max = max_scr[head : head + 1]
            new_max = jnp.maximum(old_max, jnp.max(scores, axis=0, keepdims=True))
            expo = jnp.exp(scores - new_max)
            ratio = jnp.exp(old_max - new_max)
            max_scr[head : head + 1] = new_max
            sum_scr[head : head + 1] = sum_scr[head : head + 1] * ratio + jnp.sum(
                expo, axis=0, keepdims=True
            )
            acc_scr[cols] = acc_scr[cols] * ratio + dot_plain(v_blk, expo.astype(jnp.bfloat16))
        return carry

    lax.fori_loop(first_ref[pl.program_id(0) * pl.num_programs(1) + block], block + 1, body, 0)
    for head in range(heads):
        cols = slice(head * HEAD, (head + 1) * HEAD)
        total = jnp.maximum(sum_scr[head : head + 1], 1e-30)
        ot_ref[cols] = (acc_scr[cols] / total).astype(jnp.bfloat16)
        lse_ref[0, head : head + 1] = max_scr[head : head + 1] + jnp.log(total)


def attn_forward(first, q_t, k_rows, v_t, seg_row, seg_col):
    width, tokens = q_t.shape
    slots = k_rows.shape[0]
    group = width // slots
    return pl.pallas_call(
        attn_fwd_kernel,
        name="attn_fwd",
        grid_spec=pltpu.PrefetchScalarGridSpec(
            num_scalar_prefetch=1,
            grid=(slots, tokens // BQ),
            in_specs=[
                pl.BlockSpec((group, BQ), lambda s, i, f: (s, i)),
                pl.BlockSpec((1, tokens, HEAD), lambda s, i, f: (s, 0, 0)),
                pl.BlockSpec((HEAD, tokens), lambda s, i, f: (s, 0)),
                pl.BlockSpec((1, BQ), lambda s, i, f: (0, i)),
                pl.BlockSpec((tokens, 8), lambda s, i, f: (0, 0)),
            ],
            out_specs=[
                pl.BlockSpec((group, BQ), lambda s, i, f: (s, i)),
                pl.BlockSpec((1, 8, BQ), lambda s, i, f: (s, 0, i)),
            ],
            scratch_shapes=[
                pltpu.VMEM((8, BQ), jnp.float32),
                pltpu.VMEM((8, BQ), jnp.float32),
                pltpu.VMEM((group, BQ), jnp.float32),
            ],
        ),
        out_shape=[
            jax.ShapeDtypeStruct((width, tokens), jnp.bfloat16),
            jax.ShapeDtypeStruct((slots, 8, tokens), jnp.float32),
        ],
        compiler_params=pltpu.CompilerParams(vmem_limit_bytes=40 << 20),
        cost_estimate=pl.CostEstimate(
            flops=0, bytes_accessed=198 << 20, transcendentals=0
        ),
    )(first, q_t, k_rows, v_t, seg_row, seg_col)


def attn_bwd_kernel(first_ref, qt_ref, dot_ref, ot_ref, lse_ref, k_ref, kt_ref, v_ref,
                    segr_ref, segc_ref, gqt_ref, gk_ref, gv_ref, delta_scr, acc_scr, q_ref, do_ref):
    heads = qt_ref.shape[0] // HEAD
    block = pl.program_id(1)
    q_base = block * BQ

    @pl.when(block == 0)
    def _():
        gk_ref[...] = jnp.zeros_like(gk_ref)
        gv_ref[...] = jnp.zeros_like(gv_ref)

    acc_scr[...] = jnp.zeros_like(acc_scr)
    for head in range(heads):
        cols = slice(head * HEAD, (head + 1) * HEAD)
        delta_scr[head : head + 1] = jnp.sum(
            dot_ref[cols].astype(jnp.float32) * ot_ref[cols].astype(jnp.float32),
            axis=0,
            keepdims=True,
        )
        q_ref[head] = jnp.transpose(qt_ref[cols].astype(jnp.float32)).astype(jnp.bfloat16)
        do_ref[head] = jnp.transpose(dot_ref[cols].astype(jnp.float32)).astype(jnp.bfloat16)
    segq_row = segr_ref[0:1, :]

    def body(j, carry):
        k_base = pl.multiple_of(j * BK, BK)
        rows = pl.ds(k_base, BK)
        allowed = attn_mask(q_base, k_base, segq_row, segc_ref[rows, 0:1])
        bias = jnp.where(allowed, 0.0, MASKED)
        k_blk = k_ref[0, rows, :]
        kt_blk = kt_ref[:, rows]
        v_blk = v_ref[0, rows, :]
        gk = jnp.zeros((BK, HEAD), jnp.float32)
        gv = jnp.zeros((BK, HEAD), jnp.float32)
        for head in range(heads):
            cols = slice(head * HEAD, (head + 1) * HEAD)
            scores = dot_plain(k_blk, qt_ref[cols, :]) * 0.125 + bias
            probs = jnp.exp(scores - lse_ref[0, head : head + 1])
            grad_p = dot_plain(v_blk, dot_ref[cols, :])
            grad_s = (probs * (grad_p - delta_scr[head : head + 1])).astype(jnp.bfloat16)
            gv += dot_plain(probs.astype(jnp.bfloat16), do_ref[head])
            gk += dot_plain(grad_s, q_ref[head])
            acc_scr[cols] += dot_plain(kt_blk, grad_s)
        gk_ref[0, rows, :] += gk * 0.125
        gv_ref[0, rows, :] += gv
        return carry

    lax.fori_loop(first_ref[pl.program_id(0) * pl.num_programs(1) + block], block + 1, body, 0)
    gqt_ref[...] = (acc_scr[...] * 0.125).astype(jnp.bfloat16)


def attn_backward(first, q_t, do_t, o_t, lse, k_rows, k_t, v_rows, seg_row, seg_col):
    width, tokens = q_t.shape
    slots = k_rows.shape[0]
    group = width // slots
    per = group // HEAD
    tall = pl.BlockSpec((group, BQ), lambda s, i, f: (s, i))
    keyed = pl.BlockSpec((1, tokens, HEAD), lambda s, i, f: (s, 0, 0))
    return pl.pallas_call(
        attn_bwd_kernel,
        name="attn_bwd",
        grid_spec=pltpu.PrefetchScalarGridSpec(
            num_scalar_prefetch=1,
            grid=(slots, tokens // BQ),
            in_specs=[
                tall,
                tall,
                tall,
                pl.BlockSpec((1, 8, BQ), lambda s, i, f: (s, 0, i)),
                keyed,
                pl.BlockSpec((HEAD, tokens), lambda s, i, f: (s, 0)),
                keyed,
                pl.BlockSpec((1, BQ), lambda s, i, f: (0, i)),
                pl.BlockSpec((tokens, 8), lambda s, i, f: (0, 0)),
            ],
            out_specs=[tall, keyed, keyed],
            scratch_shapes=[
                pltpu.VMEM((8, BQ), jnp.float32),
                pltpu.VMEM((group, BQ), jnp.float32),
                pltpu.VMEM((per, BQ, HEAD), jnp.bfloat16),
                pltpu.VMEM((per, BQ, HEAD), jnp.bfloat16),
            ],
        ),
        out_shape=[
            jax.ShapeDtypeStruct((width, tokens), jnp.bfloat16),
            jax.ShapeDtypeStruct((slots, tokens, HEAD), jnp.float32),
            jax.ShapeDtypeStruct((slots, tokens, HEAD), jnp.float32),
        ],
        compiler_params=pltpu.CompilerParams(vmem_limit_bytes=40 << 20),
        cost_estimate=pl.CostEstimate(
            flops=0, bytes_accessed=190 << 20, transcendentals=0
        ),
    )(first, q_t, do_t, o_t, lse, k_rows, k_t, v_rows, seg_row, seg_col)


def first_blocks(segs_flat):
    tokens = segs_flat.shape[0]
    starts = segs_flat[::BQ]
    positions = jnp.arange(tokens // BQ, dtype=jnp.int32) * BQ
    seg_start = jnp.sum((segs_flat[None, :] < starts[:, None]).astype(jnp.int32), axis=1)
    return jnp.maximum(jnp.maximum(seg_start, positions - WINDOW + 1), 0) // BK


def conv_rows(x_in, conv_w, conv_b, segs_grid):
    seq_count, seq_len = segs_grid.shape
    width = x_in.shape[1]
    grid = x_in.reshape(seq_count, seq_len, width)
    pad_x = jnp.concatenate([jnp.zeros((seq_count, CONV - 1, width), jnp.float32), grid], axis=1)
    pad_seg = jnp.concatenate([jnp.full((seq_count, CONV - 1), -1, jnp.int32), segs_grid], axis=1)
    total = jnp.zeros((seq_count, seq_len, width), jnp.float32) + conv_b
    for tap in range(CONV):
        same = (pad_seg[:, tap : tap + seq_len] == segs_grid).astype(jnp.float32)
        total = total + conv_w[tap] * pad_x[:, tap : tap + seq_len] * same[:, :, None]
    return jax.nn.silu(total).reshape(seq_count * seq_len, width)


CHUNK = 64
ROWS = 256
RANGE = 100.0
LANES = 256


def spans(width, size):
    return [(at, min(at + size, width)) for at in range(0, width, size)]


def softplus_parts(pre):
    small = jnp.exp(-jnp.abs(pre))
    step = jnp.maximum(pre, 0.0) + jnp.log1p(small)
    slope = jnp.where(pre >= 0.0, 1.0, small) / (1.0 + small)
    return step, slope


def split_sum(tri, values):
    high = values.astype(jnp.bfloat16)
    low = (values - high.astype(jnp.float32)).astype(jnp.bfloat16)
    return dot_plain(tri, high) + dot_plain(tri, low)


def tri_matrix(upper):
    row = lax.broadcasted_iota(jnp.int32, (CHUNK, CHUNK), 0)
    col = lax.broadcasted_iota(jnp.int32, (CHUNK, CHUNK), 1)
    return (col >= row) if upper else (row >= col)


def scan_setup(dbl_ref, dtw_ref, vec_ref, xa_ref, step_scr, cum_scr, slope_scr):
    width = xa_ref.shape[1]
    tri = tri_matrix(False).astype(jnp.bfloat16)
    lowest = jnp.zeros((), jnp.float32)
    for lo, hi in spans(width, LANES):
        bias = vec_ref[0:1, lo:hi]
        rate = jnp.exp(vec_ref[1:2, lo:hi])
        least = jnp.zeros((1, hi - lo), jnp.float32)
        for at in range(0, ROWS, CHUNK):
            pre = dot_plain(dbl_ref[at : at + CHUNK, :RANK], dtw_ref[:, lo:hi]) + bias
            step, slope = softplus_parts(pre)
            cum = split_sum(tri, -step * rate)
            step_scr[at : at + CHUNK, lo:hi] = step
            cum_scr[at : at + CHUNK, lo:hi] = cum
            if slope_scr is not None:
                slope_scr[at : at + CHUNK, lo:hi] = slope
            least = jnp.minimum(least, cum[CHUNK - 1 : CHUNK])
        lowest = jnp.minimum(lowest, jnp.min(least))
    return lowest


def chunk_maps(dbl_ref, mask_ref, segr_ref, at):
    rows = slice(at, at + CHUNK)
    b_map = dbl_ref[rows, 128 : 128 + STATE]
    c_map = dbl_ref[rows, 128 + STATE : 128 + 2 * STATE]
    linked = mask_ref[rows, 0:1]
    tail = mask_ref[rows, 1:2]
    keep = mask_ref[at + CHUNK - 1 : at + CHUNK, 2:3]
    allowed = tri_matrix(False) & (mask_ref[rows, 4:5] == segr_ref[0:1, rows])
    gram = jnp.where(allowed, dot_last(c_map, b_map), 0.0).astype(jnp.bfloat16)
    c_link = (c_map.astype(jnp.float32) * linked).astype(jnp.bfloat16)
    b_tail = (b_map.astype(jnp.float32) * tail).astype(jnp.bfloat16)
    return b_map, c_map, linked, tail, keep, allowed, gram, c_link, b_tail


def token_column(block, lane_index):
    lanes = lax.broadcasted_iota(jnp.int32, block.shape, 1)
    return jnp.sum(jnp.where(lanes == lane_index, block, 0.0), axis=1, keepdims=True)


def scan_fwd_kernel(
    xa_ref, z_ref, dbl_ref, mask_ref, segr_ref, dtw_ref, vec_ref,
    out_ref, hsave_ref, h_scr, step_scr, cum_scr, y_scr,
):
    width = xa_ref.shape[1]

    @pl.when(pl.program_id(0) == 0)
    def _():
        h_scr[...] = jnp.zeros_like(h_scr)

    lowest = scan_setup(dbl_ref, dtw_ref, vec_ref, xa_ref, step_scr, cum_scr, None)

    @pl.when(lowest >= -RANGE)
    def _():
        for index, at in enumerate(range(0, ROWS, CHUNK)):
            rows = slice(at, at + CHUNK)
            _, _, _, _, keep, _, gram, c_link, b_tail = chunk_maps(dbl_ref, mask_ref, segr_ref, at)
            for lo, hi in spans(width, LANES):
                cum = cum_scr[rows, lo:hi]
                half = 0.5 * cum[CHUNK - 1 : CHUNK]
                gap = cum - half
                rise = jnp.exp(half)
                h_old = h_scr[:, lo:hi]
                hsave_ref[index, :, lo:hi] = h_old
                x_f = xa_ref[rows, lo:hi].astype(jnp.float32)
                drive = (jnp.exp(-gap) * (step_scr[rows, lo:hi] * x_f)).astype(jnp.bfloat16)
                inner = dot_plain(gram, drive) + dot_plain(
                    c_link, (rise * h_old).astype(jnp.bfloat16)
                )
                total = jnp.exp(gap) * inner + vec_ref[2:3, lo:hi] * x_f
                out_ref[rows, lo:hi] = (total * jax.nn.silu(z_ref[rows, lo:hi])).astype(
                    jnp.bfloat16
                )
                h_scr[:, lo:hi] = rise * dot_first(b_tail, drive) + (rise * rise * keep) * h_old

    @pl.when(lowest < -RANGE)
    def _():
        for index, at in enumerate(range(0, ROWS, CHUNK)):
            rows = slice(at, at + CHUNK)
            hsave_ref[index] = h_scr[...]
            b_cols = jnp.transpose(dbl_ref[rows, 128 : 128 + STATE].astype(jnp.float32))
            c_cols = jnp.transpose(dbl_ref[rows, 128 + STATE : 128 + 2 * STATE].astype(jnp.float32))
            y_scr[...] = xa_ref[rows].astype(jnp.float32)
            rate = jnp.exp(vec_ref[1:2])

            def token(t, carry):
                step = step_scr[pl.ds(at + t, 1)]
                keep = mask_ref[pl.ds(at + t, 1)][:, 3:4]
                state = (jnp.exp(-step * rate) * keep) * h_scr[...] + token_column(b_cols, t) * (
                    step * y_scr[pl.ds(t, 1)]
                )
                h_scr[...] = state
                y_scr[pl.ds(t, 1)] = (
                    jnp.sum(state * token_column(c_cols, t), axis=0, keepdims=True)
                    + vec_ref[2:3] * y_scr[pl.ds(t, 1)]
                )
                return carry

            lax.fori_loop(0, CHUNK, token, 0)
            out_ref[rows] = (y_scr[...] * jax.nn.silu(z_ref[rows])).astype(jnp.bfloat16)


def scan_bwd_kernel(
    xa_ref, z_ref, dbl_ref, mask_ref, segr_ref, dtw_ref, vec_ref, hsave_ref, gs_ref,
    gz_ref, gx_ref, gdbl_ref, gdtw_ref, gvec_ref,
    g_scr, step_scr, cum_scr, slope_scr, gl_scr, gu_scr, hall_scr, y_scr,
):
    width = xa_ref.shape[1]

    @pl.when(pl.program_id(0) == 0)
    def _():
        g_scr[...] = jnp.zeros_like(g_scr)
        gdtw_ref[...] = jnp.zeros_like(gdtw_ref)
        gvec_ref[...] = jnp.zeros_like(gvec_ref)

    lowest = scan_setup(dbl_ref, dtw_ref, vec_ref, xa_ref, step_scr, cum_scr, slope_scr)
    triu = tri_matrix(True).astype(jnp.bfloat16)
    count = ROWS // CHUNK

    def finish(at, lo, hi, gu, gl, gy, first):
        rows = slice(at, at + CHUNK)
        step = step_scr[rows, lo:hi]
        x_f = xa_ref[rows, lo:hi].astype(jnp.float32)
        rate = jnp.exp(vec_ref[1:2, lo:hi])
        gx_ref[rows, lo:hi] = step * gu + vec_ref[2:3, lo:hi] * gy
        gpre = (x_f * gu - rate * gl) * slope_scr[rows, lo:hi]
        gvec_ref[0:1, lo:hi] += jnp.sum(gpre, axis=0, keepdims=True)
        gvec_ref[1:2, lo:hi] += jnp.sum(-step * rate * gl, axis=0, keepdims=True)
        gvec_ref[2:3, lo:hi] += jnp.sum(gy * x_f, axis=0, keepdims=True)
        gpre_low = gpre.astype(jnp.bfloat16)
        gdtw_ref[:, lo:hi] += dot_first(dbl_ref[rows, :RANK], gpre_low)
        part = dot_last(gpre_low, dtw_ref[:, lo:hi])
        if first:
            gdbl_ref[rows, :RANK] = part
        else:
            gdbl_ref[rows, :RANK] += part

    def gate_grads(rows, lo, hi, total):
        z_f = z_ref[rows, lo:hi]
        grad = gs_ref[rows, lo:hi]
        sig = jax.nn.sigmoid(z_f)
        gz_ref[rows, lo:hi] = (grad * total * (sig * (1.0 + z_f * (1.0 - sig)))).astype(
            jnp.bfloat16
        )

    def gate_pull(rows, lo, hi):
        return gs_ref[rows, lo:hi] * jax.nn.silu(z_ref[rows, lo:hi])

    @pl.when(lowest >= -RANGE)
    def _():
        for index in range(count - 1, -1, -1):
            at = index * CHUNK
            rows = slice(at, at + CHUNK)
            b_map, c_map, linked, tail, keep, allowed, gram, c_link, b_tail = chunk_maps(
                dbl_ref, mask_ref, segr_ref, at
            )
            g_gram = jnp.zeros((CHUNK, CHUNK), jnp.float32)
            g_c = jnp.zeros((CHUNK, STATE), jnp.float32)
            g_b = jnp.zeros((CHUNK, STATE), jnp.float32)
            for lo, hi in spans(width, LANES):
                cum = cum_scr[rows, lo:hi]
                half = 0.5 * cum[CHUNK - 1 : CHUNK]
                gap = cum - half
                fall = jnp.exp(gap)
                grow = jnp.exp(-gap)
                rise = jnp.exp(half)
                h_old = hsave_ref[index, :, lo:hi]
                g_new = g_scr[:, lo:hi]
                x_f = xa_ref[rows, lo:hi].astype(jnp.float32)
                drive = (grow * (step_scr[rows, lo:hi] * x_f)).astype(jnp.bfloat16)
                h_low = (rise * h_old).astype(jnp.bfloat16)
                g_low = (rise * g_new).astype(jnp.bfloat16)
                inner = dot_plain(gram, drive) + dot_plain(c_link, h_low)
                gate_grads(rows, lo, hi, fall * inner + vec_ref[2:3, lo:hi] * x_f)
                gy = gate_pull(rows, lo, hi)
                pulled = (fall * gy).astype(jnp.bfloat16)
                back = dot_first(gram, pulled) + dot_plain(b_tail, g_low)
                g_gram += dot_last(pulled, drive)
                g_c += dot_last(pulled, h_low)
                g_b += dot_last(drive, g_low)
                pushed = dot_first(b_tail, drive)
                ends = jnp.sum(g_low.astype(jnp.float32) * pushed, axis=0, keepdims=True) + (
                    rise * rise * keep
                ) * jnp.sum(g_new * h_old, axis=0, keepdims=True)
                diff = (
                    pulled.astype(jnp.float32) * inner - drive.astype(jnp.float32) * back
                )
                gl = split_sum(triu, diff) + ends
                g_scr[:, lo:hi] = rise * dot_first(c_link, pulled) + (rise * rise * keep) * g_new
                finish(at, lo, hi, grow * back, gl, gy, lo == 0)
            g_gram = jnp.where(allowed, g_gram, 0.0).astype(jnp.bfloat16)
            gdbl_ref[rows, 128 : 128 + STATE] = dot_first(g_gram, c_map) + tail * g_b
            gdbl_ref[rows, 128 + STATE : 128 + 2 * STATE] = dot_plain(g_gram, b_map) + linked * g_c

    @pl.when(lowest < -RANGE)
    def _():
        rate = jnp.exp(vec_ref[1:2])

        def chunk_step(reverse, carry):
            index = count - 1 - reverse
            at = pl.multiple_of(index * CHUNK, CHUNK)
            rows = pl.ds(at, CHUNK)
            b_cols = jnp.transpose(dbl_ref[rows, 128 : 128 + STATE].astype(jnp.float32))
            c_cols = jnp.transpose(dbl_ref[rows, 128 + STATE : 128 + 2 * STATE].astype(jnp.float32))
            hall_scr[0] = hsave_ref[index]
            y_scr[...] = xa_ref[rows].astype(jnp.float32)
            gu_scr[...] = gate_pull(rows, 0, width)

            def forward(t, inner_carry):
                step = step_scr[pl.ds(at + t, 1)]
                keep = mask_ref[pl.ds(at + t, 1)][:, 3:4]
                state = (jnp.exp(-step * rate) * keep) * hall_scr[t] + token_column(b_cols, t) * (
                    step * y_scr[pl.ds(t, 1)]
                )
                hall_scr[t + 1] = state
                return inner_carry

            lax.fori_loop(0, CHUNK, forward, 0)

            def backward(back, inner_carry):
                g_b, g_c = inner_carry
                t = CHUNK - 1 - back
                step = step_scr[pl.ds(at + t, 1)]
                keep = mask_ref[pl.ds(at + t, 1)][:, 3:4]
                decay = jnp.exp(-step * rate) * keep
                gy = gu_scr[pl.ds(t, 1)]
                x_f = y_scr[pl.ds(t, 1)]
                c_col = token_column(c_cols, t)
                b_col = token_column(b_cols, t)
                here = hall_scr[t + 1]
                grad = g_scr[...] + c_col * gy
                lanes = lax.broadcasted_iota(jnp.int32, (STATE, CHUNK), 1)
                g_b = jnp.where(
                    lanes == t, jnp.sum(grad * (step * x_f), axis=1, keepdims=True), g_b
                )
                g_c = jnp.where(lanes == t, jnp.sum(here * gy, axis=1, keepdims=True), g_c)
                gl_scr[pl.ds(t, 1)] = decay * jnp.sum(grad * hall_scr[t], axis=0, keepdims=True)
                gu_scr[pl.ds(t, 1)] = jnp.sum(grad * b_col, axis=0, keepdims=True)
                y_scr[pl.ds(t, 1)] = (
                    jnp.sum(here * c_col, axis=0, keepdims=True) + vec_ref[2:3] * x_f
                )
                g_scr[...] = decay * grad
                return g_b, g_c

            blank = jnp.zeros((STATE, CHUNK), jnp.float32)
            g_b, g_c = lax.fori_loop(0, CHUNK, backward, (blank, blank))
            gdbl_ref[rows, 128 : 128 + STATE] = jnp.transpose(g_b)
            gdbl_ref[rows, 128 + STATE : 128 + 2 * STATE] = jnp.transpose(g_c)
            z_f = z_ref[rows]
            grad = gs_ref[rows]
            sig = jax.nn.sigmoid(z_f)
            gz_ref[rows] = (grad * y_scr[...] * (sig * (1.0 + z_f * (1.0 - sig)))).astype(
                jnp.bfloat16
            )
            gy = grad * (z_f * sig)
            step = step_scr[rows]
            x_f = xa_ref[rows].astype(jnp.float32)
            gu, gl = gu_scr[...], gl_scr[...]
            gx_ref[rows] = step * gu + vec_ref[2:3] * gy
            gpre = (x_f * gu - rate * gl) * slope_scr[rows]
            gvec_ref[0:1] += jnp.sum(gpre, axis=0, keepdims=True)
            gvec_ref[1:2] += jnp.sum(-step * rate * gl, axis=0, keepdims=True)
            gvec_ref[2:3] += jnp.sum(gy * x_f, axis=0, keepdims=True)
            gpre_low = gpre.astype(jnp.bfloat16)
            gdtw_ref[...] += dot_first(dbl_ref[rows, :RANK], gpre_low)
            gdbl_ref[rows, :RANK] = dot_last(gpre_low, dtw_ref[...])
            return carry

        lax.fori_loop(0, count, chunk_step, 0)


def scan_specs(width, backward, blocks):
    def at(i):
        return (blocks - 1 - i) if backward else i

    rows = lambda cols: pl.BlockSpec((ROWS, cols), lambda i: (at(i), 0))
    whole = lambda *shape: pl.BlockSpec(shape, lambda i: (0, 0))
    return [
        rows(width),
        rows(width),
        rows(256),
        rows(8),
        pl.BlockSpec((1, ROWS), lambda i: (0, at(i))),
        whole(RANK, width),
        whole(8, width),
    ], pl.BlockSpec((ROWS // CHUNK, STATE, width), lambda i: (at(i), 0, 0)), rows, whole


def scan_forward(x_act, z_gate, dbl, masks, seg_row, dt_weight, vectors):
    tokens, width = x_act.shape
    blocks = tokens // ROWS
    in_specs, state_spec, rows, whole = scan_specs(width, False, blocks)
    return pl.pallas_call(
        scan_fwd_kernel,
        name="scan_fwd",
        grid=(blocks,),
        in_specs=in_specs,
        out_specs=[rows(width), state_spec],
        out_shape=[
            jax.ShapeDtypeStruct((tokens, width), jnp.bfloat16),
            jax.ShapeDtypeStruct((tokens // CHUNK, STATE, width), jnp.float32),
        ],
        scratch_shapes=[
            pltpu.VMEM((STATE, width), jnp.float32),
            pltpu.VMEM((ROWS, width), jnp.float32),
            pltpu.VMEM((ROWS, width), jnp.float32),
            pltpu.VMEM((CHUNK, width), jnp.float32),
        ],
        compiler_params=pltpu.CompilerParams(vmem_limit_bytes=40 << 20),
        cost_estimate=pl.CostEstimate(
            flops=0, bytes_accessed=93 << 20, transcendentals=0
        ),
    )(x_act, z_gate, dbl, masks, seg_row, dt_weight, vectors)


def scan_backward(x_act, z_gate, dbl, masks, seg_row, dt_weight, vectors, states, grad_rows):
    tokens, width = x_act.shape
    blocks = tokens // ROWS
    in_specs, state_spec, rows, whole = scan_specs(width, True, blocks)
    return pl.pallas_call(
        scan_bwd_kernel,
        name="scan_bwd",
        grid=(blocks,),
        in_specs=in_specs + [state_spec, rows(width)],
        out_specs=[rows(width), rows(width), rows(256), whole(RANK, width), whole(8, width)],
        out_shape=[
            jax.ShapeDtypeStruct((tokens, width), jnp.bfloat16),
            jax.ShapeDtypeStruct((tokens, width), jnp.float32),
            jax.ShapeDtypeStruct((tokens, 256), jnp.float32),
            jax.ShapeDtypeStruct((RANK, width), jnp.float32),
            jax.ShapeDtypeStruct((8, width), jnp.float32),
        ],
        scratch_shapes=[
            pltpu.VMEM((STATE, width), jnp.float32),
            pltpu.VMEM((ROWS, width), jnp.float32),
            pltpu.VMEM((ROWS, width), jnp.float32),
            pltpu.VMEM((ROWS, width), jnp.float32),
            pltpu.VMEM((CHUNK, width), jnp.float32),
            pltpu.VMEM((CHUNK, width), jnp.float32),
            pltpu.VMEM((CHUNK + 1, STATE, width), jnp.float32),
            pltpu.VMEM((CHUNK, width), jnp.float32),
        ],
        compiler_params=pltpu.CompilerParams(vmem_limit_bytes=48 << 20),
        cost_estimate=pl.CostEstimate(
            flops=0, bytes_accessed=244 << 20, transcendentals=0
        ),
    )(x_act, z_gate, dbl, masks, seg_row, dt_weight, vectors, states, grad_rows)


def scan_masks(segs_flat):
    tokens = segs_flat.shape[0]
    before = jnp.concatenate([jnp.full((1,), -1, jnp.int32), segs_flat[:-1]])
    chunked = segs_flat.reshape(tokens // CHUNK, CHUNK)
    prior = before.reshape(tokens // CHUNK, CHUNK)[:, :1]
    last = chunked[:, CHUNK - 1 :]
    linked = chunked == prior
    tail = chunked == last
    keep = jnp.broadcast_to(last == prior, chunked.shape)
    same = (segs_flat == before).reshape(chunked.shape)
    blank = jnp.zeros_like(linked)
    stacked = jnp.stack([linked, tail, keep, same], axis=-1).reshape(tokens, 4).astype(jnp.float32)
    number = segs_flat.astype(jnp.float32)
    masks = jnp.concatenate(
        [stacked, number[:, None], jnp.zeros((tokens, 3), jnp.float32)], axis=1
    )
    return masks, number[None, :]


def per_device(
    inputs,
    teacher,
    segment_ids,
    valid,
    norm_in_gain,
    w_query,
    w_key,
    w_value,
    w_attn_out,
    w_mamba_in,
    conv_weight,
    conv_bias,
    x_proj,
    dt_proj,
    dt_bias,
    a_log,
    d_skip,
    w_mamba_out,
    attn_norm_gain,
    ssm_norm_gain,
    norm_mid_gain,
    w_gate,
    w_up,
    w_down,
):
    rank_index = lax.axis_index("tensor")
    first_slot = jnp.where(rank_index == 0, 0, rank_index + 1)
    second_slot = jnp.where(rank_index == 0, 1, rank_index + 1)
    per_slot = HEADS // KV
    group_width = per_slot * HEAD
    query_width = 2 * group_width
    qkv_width = query_width + 4 * HEAD
    width = inputs.shape[1]
    inner_width = w_mamba_out.shape[0]
    inner_start = rank_index * inner_width
    inner_all = inner_width * lax.axis_size("tensor")
    low = lambda values: values.astype(jnp.bfloat16)
    gather_dp = lambda part: lax.all_gather(part, "dp", axis=0, tiled=True)
    scatter_dp = lambda part: lax.psum_scatter(part, "dp", scatter_dimension=0, tiled=True)
    gather_t = lambda part: gather_rows(part, 1)
    reduce_t = lambda part: reduce_rows(part, 2)
    tie = lax.optimization_barrier

    own_width = w_query.shape[0]
    qkv_local = jnp.concatenate(
        [
            pick_groups(w_query, first_slot, second_slot, group_width, 1),
            pick_groups(w_key, first_slot, second_slot, HEAD, 1),
            pick_groups(w_value, first_slot, second_slot, HEAD, 1),
        ],
        axis=1,
    )
    qkv_w = gather_dp(qkv_local)
    gain_rows = jnp.stack([norm_in_gain, attn_norm_gain, ssm_norm_gain, norm_mid_gain])
    gain_rows, _ = tie((gain_rows, qkv_local))
    gains, valid_total = hello(gain_rows, jnp.sum(valid).astype(jnp.float32))
    gain_in, gain_attn, gain_ssm, gain_mid = [gains[index][:, None] for index in range(4)]
    inputs_t = inputs.T
    normed_in, pull_in = jax.vjp(normalize_t, inputs_t, gain_in)
    normed_low, x_proj, dt_proj, conv_weight, w_mamba_in = tie(
        (low(normed_in), x_proj, dt_proj, conv_weight, w_mamba_in)
    )
    inner_local = jnp.concatenate(
        [
            dt_bias[:, None],
            a_log[:, None],
            d_skip[:, None],
            conv_bias[:, None],
            conv_weight.T,
            x_proj,
            dt_proj.T,
        ],
        axis=1,
    ).reshape(own_width, -1)
    mamba_local = jnp.concatenate(
        [
            w_mamba_in.reshape(own_width, 2 * inner_width),
            jnp.zeros((own_width, -2 * inner_width % 128), jnp.bfloat16),
            inner_local,
        ],
        axis=1,
    )
    mamba_all = gather_dp(mamba_local)
    normed_low, _ = tie((normed_low, mamba_local))
    whole_in = gather_t(normed_low)
    whole_in, w_attn_out, w_mamba_out, w_gate, w_up, w_down = tie(
        (whole_in, w_attn_out, w_mamba_out, w_gate, w_up, w_down)
    )
    out_local = jnp.concatenate(
        [pick_groups(w_attn_out, first_slot, second_slot, group_width, 0).T, w_mamba_out.T], axis=1
    )
    outs_all = gather_dp(out_local)
    ff_width = w_gate.shape[1]
    ff_step = -(-ff_width // 128) * 128
    blank = jnp.zeros((own_width, ff_step - ff_width), jnp.bfloat16)
    qkv_cols = low(dot_first(qkv_w, whole_in))
    qkv_cols, w_gate, w_up, w_down = tie((qkv_cols, w_gate, w_up, w_down))
    gate_up_all = gather_dp(jnp.concatenate([w_gate, blank, w_up, blank], axis=1))
    queries_t = qkv_cols[:query_width]
    keys_t = qkv_cols[query_width : query_width + 2 * HEAD]
    values_t = qkv_cols[query_width + 2 * HEAD :]
    group_rows = whole_in.shape[1]
    seq_count = group_rows // LEN
    segs_grid = segment_ids.reshape(seq_count, LEN)
    segs_flat = (segs_grid + 128 * jnp.arange(seq_count, dtype=jnp.int32)[:, None]).reshape(-1)
    scan_mask, seg_row = scan_masks(segs_flat)
    seg_col = jnp.broadcast_to(segs_flat.astype(jnp.float32)[:, None], (group_rows, 8))
    starts = first_blocks(segs_flat)
    blocks = jnp.arange(group_rows // BQ, dtype=jnp.int32)
    firsts = jnp.concatenate([starts, jnp.where(rank_index == 0, starts, blocks + 1)])
    keys_r = keys_t.reshape(2, HEAD, group_rows).transpose(0, 2, 1)
    values_r = values_t.reshape(2, HEAD, group_rows).transpose(0, 2, 1)
    attended_t, log_totals = attn_forward(firsts, queries_t, keys_r, values_t, seg_row, seg_col)
    attended_t, mamba_all, w_down = tie((attended_t, mamba_all, w_down))
    down_all = gather_dp(w_down.T)
    inner_rows = lax.dynamic_slice_in_dim(
        mamba_all[:, -inner_local.shape[1] :].reshape(inner_all, -1), inner_start, inner_width, 0
    )

    vector_rows = inner_rows[:, :8].astype(jnp.float32).T
    xproj_rows = inner_rows[:, 8 : 8 + RANK + 2 * STATE]
    dt_weight = inner_rows[:, 8 + RANK + 2 * STATE :].T
    xproj_pad = jnp.concatenate(
        [
            xproj_rows[:, :RANK],
            jnp.zeros((inner_width, 128 - RANK), jnp.bfloat16),
            xproj_rows[:, RANK:],
            jnp.zeros((inner_width, 128 - 2 * STATE), jnp.bfloat16),
        ],
        axis=1,
    )
    weight_x = mamba_all[:, :inner_width]
    weight_z = mamba_all[:, inner_width : 2 * inner_width]
    x_in = dot_first(whole_in, weight_x)
    x_pre, pull_conv = jax.vjp(
        lambda x_part, taps, shift: conv_rows(x_part, taps, shift, segs_grid),
        x_in,
        vector_rows[4:],
        vector_rows[3],
    )
    x_act = low(x_pre)
    dbl_pad = total_rows(dot_plain(x_act, xproj_pad), 3)
    z_gate = dot_first(whole_in, weight_z)
    ssm_rows, states = scan_forward(
        x_act, z_gate, dbl_pad, scan_mask, seg_row, dt_weight, vector_rows
    )
    attended_t, ssm_rows, outs_all = tie((attended_t, ssm_rows, outs_all))
    out_w = outs_all[:, :query_width]
    mamba_out_w = outs_all[:, query_width:]
    attn_sum = reduce_t(low(dot_plain(out_w, attended_t)))
    ssm_part = low(dot_last(mamba_out_w, ssm_rows))
    ssm_part, attn_sum = tie((ssm_part, attn_sum))
    ssm_sum = reduce_t(ssm_part)
    mixed, pull_join = jax.vjp(join_rows_t, inputs_t, attn_sum, ssm_sum, gain_attn, gain_ssm)
    normed_mid, pull_mid = jax.vjp(normalize_t, mixed, gain_mid)
    whole_mid = gather_t(low(normed_mid))
    whole_mid, gate_up_all = tie((whole_mid, gate_up_all))
    gate_all = gate_up_all[:, :ff_width]
    up_all = gate_up_all[:, ff_step : ff_step + ff_width]
    gate_rows = dot_first(whole_mid, gate_all)
    up_rows = dot_first(whole_mid, up_all)
    sigmoid_gate = jax.nn.sigmoid(gate_rows)
    hidden = low(gate_rows * sigmoid_gate * up_rows)
    ffn_rows = reduce_t(low(dot_last(down_all, hidden)))
    result = mixed + ffn_rows
    all_rows = inputs.shape[0] * lax.axis_size("dp") * lax.axis_size("tensor")
    grad_out = all_rows / valid_total * valid.astype(jnp.float32)[None, :] * (result - teacher.T)
    grad_ffn = gather_t(low(grad_out))
    grad_hidden = dot_first(grad_ffn, down_all)
    grad_gate = low(grad_hidden * up_rows * sigmoid_gate * (1.0 + gate_rows * (1.0 - sigmoid_gate)))
    grad_up = low(grad_hidden * gate_rows * sigmoid_gate)
    ffn_grads = weight_grads(
        [
            (whole_mid, grad_gate, False),
            (whole_mid, grad_up, False),
            (grad_ffn, hidden, False),
        ],
        "ffn_weight_grads",
        44,
    )
    grad_gate, grad_up, ffn_grads = tie((grad_gate, grad_up, ffn_grads))
    ffn_shard = scatter_dp(ffn_grads)
    mid_part = low(dot_last(gate_all, grad_gate) + dot_last(up_all, grad_up))
    grad_mid_rows = reduce_t(mid_part)
    grad_mixed_norm, grad_gain_mid = pull_mid(grad_mid_rows)
    grad_mixed = grad_out + grad_mixed_norm
    grad_resid, grad_attn_sum, grad_ssm_sum, grad_gain_attn, grad_gain_ssm = pull_join(grad_mixed)
    grad_ssm_whole = gather_t(low(grad_ssm_sum))
    grad_attn_low, grad_ssm_whole = tie((low(grad_attn_sum), grad_ssm_whole))
    grad_attn_whole = gather_t(grad_attn_low)
    grad_ssm_whole, grad_attn_whole = tie((grad_ssm_whole, grad_attn_whole))
    grad_ssm_rows = dot_first(grad_ssm_whole, mamba_out_w)
    grad_gate_part, grad_act_scan, grad_dbl_part, grad_dtproj, grad_vectors = scan_backward(
        x_act, z_gate, dbl_pad, scan_mask, seg_row, dt_weight, vector_rows, states, grad_ssm_rows
    )
    mid_grads = weight_grads(
        [
            (grad_attn_whole, attended_t, True),
            (grad_ssm_whole, ssm_rows, False),
            (whole_in, grad_gate_part, False),
        ],
        "mid_weight_grads",
        26,
        128,
    )
    grad_att_t = low(
        lax.dot_general(
            out_w, grad_attn_whole, (((0,), (0,)), ((), ())), preferred_element_type=jnp.float32
        )
    )
    grad_dbl_part, mid_grads, ffn_shard = tie((grad_dbl_part, mid_grads, ffn_shard))
    mid_shard = scatter_dp(mid_grads)
    grad_queries_t, grad_keys, grad_values = attn_backward(
        firsts,
        queries_t,
        grad_att_t,
        attended_t,
        log_totals,
        keys_r,
        keys_t,
        values_r,
        seg_row,
        seg_col,
    )
    columns_of = lambda rows: low(rows.transpose(0, 2, 1).reshape(2 * HEAD, group_rows))
    grad_qkv = jnp.concatenate(
        [grad_queries_t, columns_of(grad_keys), columns_of(grad_values)], axis=0
    )
    grad_dbl = total_rows(grad_dbl_part, 3)
    grad_act = grad_act_scan + dot_last(grad_dbl, xproj_pad)
    grad_xproj_w = dot_first(x_act, grad_dbl)
    grad_x_part, grad_taps, grad_shift = pull_conv(grad_act)
    grad_x_low = low(grad_x_part)
    inner_grads = jnp.concatenate(
        [
            grad_vectors[:3].T,
            grad_shift[:, None],
            grad_taps.T,
            grad_xproj_w[:, :RANK],
            grad_xproj_w[:, 128 : 128 + 2 * STATE],
            grad_dtproj.T,
        ],
        axis=1,
    )
    inner_full = low(place_block(inner_grads, inner_start, inner_all, 0)).reshape(width, -1)
    last_grads = weight_grads(
        [(whole_in, grad_x_low, False), (whole_in, grad_qkv, True), (inner_full, None, False)],
        "last_weight_grads",
        20,
    )
    grad_x_low, grad_qkv, last_grads, mid_shard = tie(
        (grad_x_low, grad_qkv, last_grads, mid_shard)
    )
    last_shard = scatter_dp(last_grads)
    in_part = low(
        dot_plain(qkv_w, grad_qkv)
        + dot_last(weight_x, grad_x_low)
        + dot_last(weight_z, grad_gate_part)
    )
    grad_in_rows = reduce_t(in_part)
    grad_in_norm, grad_gain_in = pull_in(grad_in_rows)
    grad_inputs = grad_resid + grad_in_norm
    gain_grads = jnp.concatenate(
        [grad_gain_in, grad_gain_attn, grad_gain_ssm, grad_gain_mid], axis=1
    )
    gains_own = farewell(gain_grads.T)
    gains_own, last_shard, grad_inputs = tie((gains_own, last_shard, grad_inputs))
    inner_step = -(-inner_width // 128) * 128
    shared = jnp.concatenate(
        [
            last_shard[:, inner_step : inner_step + qkv_width],
            mid_shard[:, :query_width],
            last_shard[:, inner_step + qkv_width : inner_step + qkv_width + inner_full.shape[1]],
        ],
        axis=1,
    )
    shared = jnp.pad(shared, ((0, 0), (0, -shared.shape[1] % 256)))
    shared_all = gather_stack(shared)
    inner_sum = jnp.sum(
        shared_all[:, :, qkv_width + query_width : qkv_width + query_width + inner_full.shape[1]].astype(jnp.float32), axis=0
    ).reshape(inner_all // lax.axis_size("dp"), -1)
    mamba_at = query_width
    gate_at = query_width + inner_step
    ranks = [0] + list(range(lax.axis_size("tensor")))
    slots = [0, 1] + [0] * (lax.axis_size("tensor") - 1)

    def merge(start, size):
        parts = [
            shared_all[rank, :, start + slot * size : start + (slot + 1) * size]
            for rank, slot in zip(ranks, slots)
        ]
        return jnp.concatenate(parts, axis=1).astype(jnp.float32)

    return (
        result.T,
        grad_inputs.T,
        gains_own[0],
        merge(0, group_width),
        merge(query_width, HEAD),
        merge(query_width + 2 * HEAD, HEAD),
        merge(qkv_width, group_width).T,
        jnp.stack(
            [last_shard[:, :inner_width], mid_shard[:, gate_at : gate_at + inner_width]], axis=1
        ).astype(jnp.float32),
        inner_sum[:, 4:8].T,
        inner_sum[:, 3],
        inner_sum[:, 8 : 8 + RANK + 2 * STATE],
        inner_sum[:, 8 + RANK + 2 * STATE :].T,
        inner_sum[:, 0],
        inner_sum[:, 1],
        inner_sum[:, 2],
        mid_shard[:, mamba_at : mamba_at + inner_width].T.astype(jnp.float32),
        gains_own[1],
        gains_own[2],
        gains_own[3],
        ffn_shard[:, :ff_width].astype(jnp.float32),
        ffn_shard[:, ff_step : ff_step + ff_width].astype(jnp.float32),
        ffn_shard[:, 2 * ff_step : 2 * ff_step + ff_width].astype(jnp.float32).T,
    )


def solution(mesh):
    placed = (
        P(("dp", "tensor"), None),
        P(("dp", "tensor"), None),
        P("dp"),
        P(("dp", "tensor")),
        P("dp"),
        P("dp", None),
        P("dp", None),
        P("dp", None),
        P(None, "dp"),
        P("dp", None, "tensor"),
        P(None, "dp"),
        P("dp"),
        P("dp", None),
        P(None, "dp"),
        P("dp"),
        P("dp"),
        P("dp"),
        P("tensor", "dp"),
        P("dp"),
        P("dp"),
        P("dp"),
        P("dp", "tensor"),
        P("dp", "tensor"),
        P("tensor", "dp"),
    )
    return jax.shard_map(
        per_device,
        mesh=mesh,
        in_specs=placed,
        out_specs=(
            P(("dp", "tensor"), None),
            P(("dp", "tensor"), None),
            P("dp"),
            P("dp", None),
            P("dp", None),
            P("dp", None),
            P(None, "dp"),
            P("dp", None, "tensor"),
            P(None, "dp"),
            P("dp"),
            P("dp", None),
            P(None, "dp"),
            P("dp"),
            P("dp"),
            P("dp"),
            P("tensor", "dp"),
            P("dp"),
            P("dp"),
            P("dp"),
            P("dp", "tensor"),
            P("dp", "tensor"),
            P("tensor", "dp"),
        ),
        check_vma=False,
    )
```

```python
import functools

import jax
import jax.numpy as jnp
from jax import lax
from jax.experimental import pallas as pl
from jax.experimental.pallas import tpu as pltpu
from jax.sharding import PartitionSpec as P

HEADS = 25
KV = 5
HEAD = 64
STATE = 16
RANK = 100
CONV = 4
WINDOW = 1024
BLOCK = 512
STRETCH = 64
LEN = 2048


EPSILON = 1e-06
MASKED = -1e30
HIGHEST = lax.Precision.HIGHEST


def normalize_t(values, gain):
    return values * lax.rsqrt(jnp.mean(values * values, axis=0, keepdims=True) + EPSILON) * gain


def join_rows_t(resid, attn_sum, ssm_sum, gain_attn, gain_ssm):
    return resid + 0.5 * (normalize_t(attn_sum, gain_attn) + normalize_t(ssm_sum, gain_ssm))


def dot_plain(left, right):
    return jnp.dot(left, right, preferred_element_type=jnp.float32)


def dot_last(left, right):
    return lax.dot_general(
        left, right, (((1,), (1,)), ((), ())), preferred_element_type=jnp.float32
    )


def dot_first(left, right):
    return lax.dot_general(
        left, right, (((0,), (0,)), ((), ())), preferred_element_type=jnp.float32
    )


def pick_groups(weight, first_slot, second_slot, group_width, axis):
    return jnp.concatenate(
        [
            lax.dynamic_slice_in_dim(weight, first_slot * group_width, group_width, axis),
            lax.dynamic_slice_in_dim(weight, second_slot * group_width, group_width, axis),
        ],
        axis=axis,
    )


PIECES = 4
MESH = pl.DeviceIdType.MESH


def tensor_peers():
    me = lax.axis_index("tensor")
    side = me + 1 - 2 * lax.rem(me, 2)
    cross = lax.rem(me + 2, 4)
    return me, side, cross, lax.rem(side + 2, 4)


def greet(peers):
    barrier = pltpu.get_barrier_semaphore()
    for peer in peers:
        pl.semaphore_signal(barrier, inc=1, device_id={"tensor": peer}, device_id_type=MESH)
    pl.semaphore_wait(barrier, len(peers))


def push(src, dst, sems, index, peer):
    copy = pltpu.make_async_remote_copy(
        src_ref=src,
        dst_ref=dst,
        send_sem=sems[0].at[index],
        recv_sem=sems[1].at[index],
        device_id={"tensor": peer},
        device_id_type=MESH,
    )
    copy.start()
    return copy


def columns(block, size):
    return pl.ds(pl.multiple_of(block * size, size), size)


def gather_kernel(part_ref, whole_ref, own_sem, *sems):
    me, side, cross, diag = tensor_peers()
    depth, size = part_ref.shape
    step = depth // PIECES
    mine = columns(me, size)
    theirs = columns(cross, size)
    greet((side, cross))
    own = pltpu.make_async_copy(part_ref, whole_ref.at[:, mine], own_sem)
    own.start()
    over, near, relay = [], [], []
    for piece in range(PIECES):
        rows = pl.ds(piece * step, step)
        over.append(
            push(part_ref.at[rows], whole_ref.at[rows, mine], sems[0:2], piece, cross)
        )
    for piece in range(PIECES):
        rows = pl.ds(piece * step, step)
        near.append(push(part_ref.at[rows], whole_ref.at[rows, mine], sems[2:4], piece, side))
    for piece in range(PIECES):
        rows = pl.ds(piece * step, step)
        over[piece].wait_recv()
        relay.append(
            push(whole_ref.at[rows, theirs], whole_ref.at[rows, theirs], sems[4:6], piece, side)
        )
    own.wait()
    for piece in range(PIECES):
        over[piece].wait_send()
        near[piece].wait()
        relay[piece].wait()


def gather_rows(part, call_id):
    depth, size = part.shape
    return pl.pallas_call(
        gather_kernel,
        name="gather_rows",
        in_specs=[pl.BlockSpec(memory_space=pl.ANY)],
        out_specs=pl.BlockSpec(memory_space=pl.ANY),
        out_shape=jax.ShapeDtypeStruct((depth, 4 * size), part.dtype),
        scratch_shapes=[pltpu.SemaphoreType.DMA] + [pltpu.SemaphoreType.DMA((PIECES,))] * 6,
        compiler_params=pltpu.CompilerParams(
            collective_id=call_id, has_side_effects=True, vmem_limit_bytes=1 << 20
        ),
        cost_estimate=pl.CostEstimate(
            flops=0, bytes_accessed=depth * size * 2 * 90, transcendentals=0
        ),
    )(part)


def total_kernel(part_ref, out_ref, near_buf, own_buf, stage_buf, far_buf, low_buf, own_sem, *sems):
    me, side, cross, diag = tensor_peers()
    size, wide = low_buf.shape
    half = size // 2
    greet((side, cross))
    rows_of = lambda block, at: pl.ds(pl.multiple_of(block * size + at, half), half)
    pieces = (0, half)
    first = [
        push(part_ref.at[rows_of(diag, at)], near_buf.at[pl.ds(at, half)], sems[0:2], i, side)
        for i, at in enumerate(pieces)
    ]
    second = [
        push(part_ref.at[rows_of(side, at)], own_buf.at[pl.ds(at, half)], sems[2:4], i, side)
        for i, at in enumerate(pieces)
    ]
    third, over, near, relay = [], [], [], []
    for i, at in enumerate(pieces):
        rows = pl.ds(at, half)
        first[i].wait_recv()
        stage_buf[rows] = (part_ref[rows_of(cross, at)] + near_buf[rows]).astype(jnp.bfloat16)
        third.append(push(stage_buf.at[rows], far_buf.at[rows], sems[4:6], i, cross))
    for i, at in enumerate(pieces):
        rows = pl.ds(at, half)
        second[i].wait_recv()
        third[i].wait_recv()
        low_buf[rows] = (
            part_ref[rows_of(me, at)] + own_buf[rows] + far_buf[rows].astype(jnp.float32)
        ).astype(jnp.bfloat16)
        over.append(push(low_buf.at[rows], out_ref.at[rows_of(me, at)], sems[6:8], i, cross))
        near.append(push(low_buf.at[rows], out_ref.at[rows_of(me, at)], sems[8:10], i, side))
    own = pltpu.make_async_copy(
        low_buf, out_ref.at[pl.ds(pl.multiple_of(me * size, size), size)], own_sem
    )
    own.start()
    for i, at in enumerate(pieces):
        over[i].wait_recv()
        relay.append(
            push(out_ref.at[rows_of(cross, at)], out_ref.at[rows_of(cross, at)], sems[10:12], i, side)
        )
    own.wait()
    for i in range(2):
        for group in (first, second, third, over):
            group[i].wait_send()
        near[i].wait()
        relay[i].wait()


def total_rows(part, call_id):
    tokens, wide = part.shape
    size = tokens // 4
    whole = pl.BlockSpec(memory_space=pltpu.VMEM)
    return pl.pallas_call(
        total_kernel,
        name="total_rows",
        in_specs=[whole],
        out_specs=whole,
        out_shape=jax.ShapeDtypeStruct((tokens, wide), jnp.bfloat16),
        scratch_shapes=[
            pltpu.VMEM((size, wide), jnp.float32),
            pltpu.VMEM((size, wide), jnp.float32),
            pltpu.VMEM((size, wide), jnp.bfloat16),
            pltpu.VMEM((size, wide), jnp.bfloat16),
            pltpu.VMEM((size, wide), jnp.bfloat16),
            pltpu.SemaphoreType.DMA,
        ]
        + [pltpu.SemaphoreType.DMA((2,))] * 12,
        compiler_params=pltpu.CompilerParams(
            collective_id=call_id, has_side_effects=True, vmem_limit_bytes=32 << 20
        ),
        cost_estimate=pl.CostEstimate(flops=0, bytes_accessed=60 << 20, transcendentals=0),
    )(part)


def hello_kernel(gain_ref, count_ref, gains_ref, counts_ref, sum_buf, local_buf, *sems):
    me = lax.axis_index("tensor")
    place = lax.axis_index("dp")
    ranks, groups = local_buf.shape[0], gains_ref.shape[0]
    barrier = pltpu.get_barrier_semaphore()
    others = [{"tensor": lax.rem(me + hop, ranks)} for hop in range(1, ranks)]
    far = [{"dp": lax.rem(place + hop, groups)} for hop in range(1, groups)]
    for peer in others + far:
        pl.semaphore_signal(barrier, inc=1, device_id=peer, device_id_type=MESH)
    pl.semaphore_wait(barrier, len(others) + len(far))

    def send(src, dst, index, peer):
        copy = pltpu.make_async_remote_copy(
            src_ref=src,
            dst_ref=dst,
            send_sem=sems[0].at[index],
            recv_sem=sems[1].at[index],
            device_id=peer,
            device_id_type=MESH,
        )
        copy.start()
        return copy

    first = [send(count_ref, local_buf.at[me], i, peer) for i, peer in enumerate(others)]
    local_buf[me] = count_ref[...]
    gains_ref[place] = gain_ref[...]
    base = len(first)
    second = [send(gain_ref, gains_ref.at[place], base + i, peer) for i, peer in enumerate(far)]
    base += len(second)
    for copy in first:
        copy.wait()
    sum_buf[...] = jnp.sum(local_buf[...], axis=0)
    counts_ref[place] = sum_buf[...]
    third = [send(sum_buf, counts_ref.at[place], base + i, peer) for i, peer in enumerate(far)]
    for copy in second + third:
        copy.wait()


def hello(gains, count):
    wide = -(-gains.shape[1] // 128) * 128
    block = jnp.zeros((8, wide), jnp.float32)
    block = lax.dynamic_update_slice(block, gains.astype(jnp.float32), (0, 0))
    counts = jnp.full((8, 128), count, jnp.float32)
    groups, ranks = lax.axis_size("dp"), lax.axis_size("tensor")
    copies = ranks - 1 + 2 * (groups - 1)
    whole = pl.BlockSpec(memory_space=pltpu.VMEM)
    gains_all, counts_all = pl.pallas_call(
        hello_kernel,
        name="hello",
        in_specs=[whole, whole],
        out_specs=[whole, whole],
        out_shape=[
            jax.ShapeDtypeStruct((groups, 8, wide), jnp.float32),
            jax.ShapeDtypeStruct((groups, 8, 128), jnp.float32),
        ],
        scratch_shapes=[
            pltpu.VMEM((8, 128), jnp.float32),
            pltpu.VMEM((ranks, 8, 128), jnp.float32),
        ]
        + [pltpu.SemaphoreType.DMA((copies,))] * 2,
        compiler_params=pltpu.CompilerParams(collective_id=0, has_side_effects=True),
        cost_estimate=pl.CostEstimate(flops=0, bytes_accessed=30 << 20, transcendentals=0),
    )(block, counts)
    gains_full = gains_all[:, :4, : gains.shape[1]].transpose(1, 0, 2).reshape(4, -1)
    return gains_full, jnp.sum(counts_all[:, 0, 0])


TILE = 400


def weights_kernel(plan, *refs):
    out_ref = refs[-1]
    index = 0
    for mode, offset, size, pad in plan:
        left = refs[index][...]
        if mode == "copy":
            product = left
            index += 1
        else:
            right = refs[index + 1][...]
            product = dot_last(left, right) if mode == "flip" else dot_plain(left, right)
            index += 2
        out_ref[:, offset : offset + size] = product.astype(jnp.bfloat16)
        if pad:
            out_ref[:, offset + size : offset + size + pad] = jnp.zeros(
                (out_ref.shape[0], pad), jnp.bfloat16
            )


def weight_grads(pairs, name, micros, widen=0):
    rows = pairs[0][0].shape[0]
    tile = TILE if rows % TILE == 0 else rows
    plan, specs, operands, offset = [], [], [], 0
    for left, right, flip in pairs:
        source = left if right is None else right
        size = source.shape[0] if flip else source.shape[1]
        pad = -size % 128 + (widen if len(plan) + 1 == len(pairs) else 0)
        mode = "copy" if right is None else "flip" if flip else "plain"
        plan.append((mode, offset, size, pad))
        offset += size + pad
        specs.append(pl.BlockSpec((tile, left.shape[1]), lambda i: (i, 0)))
        operands.append(left)
        if right is not None:
            specs.append(
                pl.BlockSpec(right.shape, lambda i: (0, 0), pipeline_mode=pl.Buffered(1))
            )
            operands.append(right)
    return pl.pallas_call(
        functools.partial(weights_kernel, plan),
        name=name,
        grid=(rows // tile,),
        in_specs=specs,
        out_specs=pl.BlockSpec((tile, offset), lambda i: (i, 0)),
        out_shape=jax.ShapeDtypeStruct((rows, offset), jnp.bfloat16),
        compiler_params=pltpu.CompilerParams(vmem_limit_bytes=52 << 20),
        cost_estimate=pl.CostEstimate(
            flops=0, bytes_accessed=int(micros * 3.6) << 20, transcendentals=0
        ),
    )(*operands)


def farewell_kernel(part_ref, out_ref, group_buf, sum_buf, rank_buf, *sems):
    me = lax.axis_index("tensor")
    place = lax.axis_index("dp")
    ranks, groups = rank_buf.shape[0], group_buf.shape[0]
    barrier = pltpu.get_barrier_semaphore()
    others = [lax.rem(me + hop, ranks) for hop in range(1, ranks)]
    far = [lax.rem(place + hop, groups) for hop in range(1, groups)]
    for peer in others:
        pl.semaphore_signal(barrier, inc=1, device_id={"tensor": peer}, device_id_type=MESH)
    for peer in far:
        pl.semaphore_signal(barrier, inc=1, device_id={"dp": peer}, device_id_type=MESH)
    pl.semaphore_wait(barrier, len(others) + len(far))

    def send(src, dst, index, peer):
        copy = pltpu.make_async_remote_copy(
            src_ref=src,
            dst_ref=dst,
            send_sem=sems[0].at[index],
            recv_sem=sems[1].at[index],
            device_id=peer,
            device_id_type=MESH,
        )
        copy.start()
        return copy

    first = [
        send(part_ref.at[peer], group_buf.at[place], i, {"dp": peer}) for i, peer in enumerate(far)
    ]
    group_buf[place] = part_ref[place]
    for copy in first:
        copy.wait()
    sum_buf[...] = jnp.sum(group_buf[...], axis=0)
    rank_buf[me] = sum_buf[...]
    second = [
        send(sum_buf, rank_buf.at[me], len(first) + i, {"tensor": peer})
        for i, peer in enumerate(others)
    ]
    for copy in second:
        copy.wait()
    out_ref[...] = jnp.sum(rank_buf[...], axis=0)


def farewell(grads):
    groups, ranks = lax.axis_size("dp"), lax.axis_size("tensor")
    kinds, total = grads.shape
    own = total // groups
    wide = -(-own // 128) * 128
    parts = jnp.pad(
        grads.reshape(kinds, groups, own).transpose(1, 0, 2),
        ((0, 0), (0, 8 - kinds), (0, wide - own)),
    )
    whole = pl.BlockSpec(memory_space=pltpu.VMEM)
    summed = pl.pallas_call(
        farewell_kernel,
        name="farewell",
        in_specs=[whole],
        out_specs=whole,
        out_shape=jax.ShapeDtypeStruct((8, wide), jnp.float32),
        scratch_shapes=[
            pltpu.VMEM((groups, 8, wide), jnp.float32),
            pltpu.VMEM((8, wide), jnp.float32),
            pltpu.VMEM((ranks, 8, wide), jnp.float32),
        ]
        + [pltpu.SemaphoreType.DMA((groups + ranks - 2,))] * 2,
        compiler_params=pltpu.CompilerParams(
            collective_id=4, has_side_effects=True, vmem_limit_bytes=4 << 20
        ),
        cost_estimate=pl.CostEstimate(flops=0, bytes_accessed=40 << 20, transcendentals=0),
    )(parts)
    return summed[:kinds, :own]


def stack_kernel(part_ref, whole_ref, own_sem, *sems):
    me, side, cross, diag = tensor_peers()
    step = part_ref.shape[1] // 2
    greet((side, cross))
    own = pltpu.make_async_copy(part_ref, whole_ref.at[me], own_sem)
    own.start()
    cols = [pl.ds(0, step), pl.ds(step, step)]
    over = [
        push(part_ref.at[:, at], whole_ref.at[me, :, at], sems[0:2], i, cross)
        for i, at in enumerate(cols)
    ]
    near = [
        push(part_ref.at[:, at], whole_ref.at[me, :, at], sems[2:4], i, side)
        for i, at in enumerate(cols)
    ]
    relay = []
    for i, at in enumerate(cols):
        over[i].wait_recv()
        relay.append(
            push(whole_ref.at[cross, :, at], whole_ref.at[cross, :, at], sems[4:6], i, side)
        )
    own.wait()
    for i in range(2):
        over[i].wait_send()
        near[i].wait()
        relay[i].wait()


def gather_stack(part, call_id):
    return pl.pallas_call(
        stack_kernel,
        name="gather_stack",
        in_specs=[pl.BlockSpec(memory_space=pl.ANY)],
        out_specs=pl.BlockSpec(memory_space=pl.ANY),
        out_shape=jax.ShapeDtypeStruct((4,) + part.shape, part.dtype),
        scratch_shapes=[pltpu.SemaphoreType.DMA] + [pltpu.SemaphoreType.DMA((2,))] * 6,
        compiler_params=pltpu.CompilerParams(
            collective_id=call_id, has_side_effects=True, vmem_limit_bytes=1 << 20
        ),
        cost_estimate=pl.CostEstimate(flops=0, bytes_accessed=60 << 20, transcendentals=0),
    )(part)


def product_kernel(plan, left_count, right_flips, *refs):
    lefts = refs[:left_count]
    right_count = len(right_flips)
    rights = refs[left_count : left_count + right_count]
    out_ref = refs[left_count + right_count]
    scratch = refs[left_count + right_count + 1 :]
    left_bufs = scratch[:left_count]
    right_bufs = scratch[left_count : left_count + right_count]
    diag_buf, side_buf, near_buf, own_buf, stage_buf, far_buf, left_sem, right_sem = scratch[
        left_count + right_count : left_count + right_count + 8
    ]
    sems = scratch[left_count + right_count + 8 :]
    me, side, cross, diag = tensor_peers()
    depth, size = out_ref.shape
    step = depth // PIECES
    rows_of = lambda piece: pl.ds(pl.multiple_of(piece * step, 16), step)

    def left_load(index, piece):
        rows = rows_of(piece)
        return pltpu.make_async_copy(
            lefts[index].at[rows], left_bufs[index].at[rows], left_sem.at[index, piece]
        )

    def right_load(index, order, block):
        at = columns(block, size)
        view = (slice(None), at) if right_flips[index] else (at,)
        return pltpu.make_async_copy(
            rights[index].at[view], right_bufs[index].at[view], right_sem.at[index, order]
        )

    turns = (diag, cross, side, me)
    for order, block in enumerate(turns):
        for index in range(right_count):
            right_load(index, order, block).start()
        for index in range(left_count):
            left_load(index, order).start()
    greet((side, cross))

    def product(piece, block):
        rows, at = rows_of(piece), columns(block, size)
        total = jnp.zeros((step, size), jnp.float32)
        for left, low_col, high_col, right in plan:
            weight = left_bufs[left][rows, low_col:high_col]
            if right_flips[right]:
                total += dot_plain(weight, right_bufs[right][:, at])
            else:
                total += dot_last(weight, right_bufs[right][at, :])
        return total

    def transfer(src, dst, group, piece, peer):
        rows = rows_of(piece)
        return pltpu.make_async_remote_copy(
            src_ref=src.at[rows],
            dst_ref=dst.at[rows],
            send_sem=sems[2 * group].at[piece],
            recv_sem=sems[2 * group + 1].at[piece],
            device_id={"tensor": peer},
            device_id_type=MESH,
        )

    first = lambda piece: transfer(diag_buf, near_buf, 0, piece, side)
    second = lambda piece: transfer(side_buf, own_buf, 1, piece, side)
    third = lambda piece: transfer(stage_buf, far_buf, 2, piece, cross)

    for order in (0, 1):
        for index in range(right_count):
            right_load(index, order, turns[order]).wait()

    def outward(piece, carry):
        rows = rows_of(piece)
        for index in range(left_count):
            left_load(index, piece).wait()
        diag_buf[rows] = product(piece, diag).astype(jnp.bfloat16)
        first(piece).start()
        kept = product(piece, cross)
        first(piece).wait_recv()
        stage_buf[rows] = (kept + near_buf[rows].astype(jnp.float32)).astype(jnp.bfloat16)
        third(piece).start()
        return carry

    lax.fori_loop(0, PIECES, outward, 0)
    for order in (2, 3):
        for index in range(right_count):
            right_load(index, order, turns[order]).wait()

    def inward(piece, carry):
        rows = rows_of(piece)
        side_buf[rows] = product(piece, side).astype(jnp.bfloat16)
        second(piece).start()
        out_ref[rows] = product(piece, me)
        return carry

    lax.fori_loop(0, PIECES, inward, 0)

    def finish(piece, carry):
        rows = rows_of(piece)
        second(piece).wait_recv()
        third(piece).wait_recv()
        out_ref[rows] += own_buf[rows].astype(jnp.float32) + far_buf[rows].astype(jnp.float32)
        first(piece).wait_send()
        second(piece).wait_send()
        third(piece).wait_send()
        return carry

    lax.fori_loop(0, PIECES, finish, 0)


def product_reduce(lefts, rights, plan, call_id, name, micros):
    depth = lefts[0].shape[0]
    right_flips = tuple(flip for _, flip in rights)
    tokens = rights[0][0].shape[1] if right_flips[0] else rights[0][0].shape[0]
    size = tokens // 4
    anywhere = pl.BlockSpec(memory_space=pl.ANY)
    return pl.pallas_call(
        functools.partial(product_kernel, plan, len(lefts), right_flips),
        name=name,
        in_specs=[anywhere] * (len(lefts) + len(rights)),
        out_specs=pl.BlockSpec(memory_space=pltpu.VMEM),
        out_shape=jax.ShapeDtypeStruct((depth, size), jnp.float32),
        scratch_shapes=[pltpu.VMEM(left.shape, left.dtype) for left in lefts]
        + [pltpu.VMEM(right.shape, right.dtype) for right, _ in rights]
        + [pltpu.VMEM((depth, size), jnp.bfloat16)] * 6
        + [
            pltpu.SemaphoreType.DMA((len(lefts), PIECES)),
            pltpu.SemaphoreType.DMA((len(rights), 4)),
        ]
        + [pltpu.SemaphoreType.DMA((PIECES,))] * 6,
        compiler_params=pltpu.CompilerParams(
            collective_id=call_id, has_side_effects=True, vmem_limit_bytes=48 << 20
        ),
        cost_estimate=pl.CostEstimate(
            flops=0, bytes_accessed=int(micros * 3.6) << 20, transcendentals=0
        ),
    )(*lefts, *[right for right, _ in rights])


def place_block(piece, start, full_width, axis):
    new_shape = list(piece.shape)
    new_shape[axis] = full_width
    return lax.dynamic_update_slice_in_dim(
        jnp.zeros(tuple(new_shape), jnp.float32), piece, start, axis
    )


BQ = 256
BK = 256


def attn_bias(q_base, k_base, segq_row, segk_col):
    q_pos = q_base + lax.broadcasted_iota(jnp.int32, (BK, BQ), 1)
    k_pos = k_base + lax.broadcasted_iota(jnp.int32, (BK, BQ), 0)
    offset = q_pos - k_pos
    allowed = (offset >= 0) & (offset < WINDOW) & (segk_col == segq_row)
    return jnp.where(allowed, 0.0, MASKED)


def flip_rows(cols_ref, rows_scr):
    for at in range(0, rows_scr.shape[0], BK):
        block = cols_ref[:, at : at + BK].astype(jnp.float32)
        rows_scr[at : at + BK] = jnp.transpose(block).astype(jnp.bfloat16)


def attn_fwd_kernel(first_ref, qt_ref, kt_ref, vt_ref, segr_ref, mask_ref, ot_ref, lse_ref,
                    max_scr, sum_scr, acc_scr, k_scr):
    heads = qt_ref.shape[0] // HEAD
    block = pl.program_id(1)
    q_base = block * BQ

    @pl.when(block == 0)
    def _():
        flip_rows(kt_ref, k_scr)

    max_scr[...] = jnp.full_like(max_scr, MASKED)
    sum_scr[...] = jnp.zeros_like(sum_scr)
    acc_scr[...] = jnp.zeros_like(acc_scr)
    segq_row = segr_ref[0:1, :]

    def body(j, carry):
        k_base = pl.multiple_of(j * BK, BK)
        rows = pl.ds(k_base, BK)
        bias = attn_bias(q_base, k_base, segq_row, mask_ref[rows, 4:5])
        k_blk = k_scr[rows, :]
        v_blk = vt_ref[:, rows]
        for head in range(heads):
            cols = slice(head * HEAD, (head + 1) * HEAD)
            scores = dot_plain(k_blk, qt_ref[cols, :]) * 0.125 + bias
            old_max = max_scr[head : head + 1]
            new_max = jnp.maximum(old_max, jnp.max(scores, axis=0, keepdims=True))
            expo = jnp.exp(scores - new_max)
            ratio = jnp.exp(old_max - new_max)
            max_scr[head : head + 1] = new_max
            sum_scr[head : head + 1] = sum_scr[head : head + 1] * ratio + jnp.sum(
                expo, axis=0, keepdims=True
            )
            acc_scr[cols] = acc_scr[cols] * ratio + dot_plain(v_blk, expo.astype(jnp.bfloat16))
        return carry

    start = first_ref[pl.program_id(0) * pl.num_programs(1) + block]
    lax.fori_loop(start, block + 1, body, 0)
    for head in range(heads):
        cols = slice(head * HEAD, (head + 1) * HEAD)
        total = jnp.maximum(sum_scr[head : head + 1], 1e-30)
        ot_ref[cols] = (acc_scr[cols] / total).astype(jnp.bfloat16)
        lse_ref[0, head : head + 1] = max_scr[head : head + 1] + jnp.log(total)


def attn_specs(slots, group, tokens):
    queries = pl.BlockSpec((group, BQ), lambda s, i, f: (s, i))
    base = slots * group // HEAD
    keys = pl.BlockSpec((HEAD, tokens), lambda s, i, f: (base + s, 0))
    values = pl.BlockSpec((HEAD, tokens), lambda s, i, f: (base + slots + s, 0))
    stats = pl.BlockSpec((1, 8, BQ), lambda s, i, f: (s, 0, i))
    seg_row = pl.BlockSpec((1, BQ), lambda s, i, f: (0, i))
    seg_col = pl.BlockSpec((tokens, 8), lambda s, i, f: (0, 0))
    return queries, keys, values, stats, seg_row, seg_col


def attn_forward(first, qkv_t, seg_row, masks, slots):
    tokens = qkv_t.shape[1]
    group = qkv_t.shape[0] // slots - 2 * HEAD
    queries, keys, values, stats, segr, segc = attn_specs(slots, group, tokens)
    return pl.pallas_call(
        attn_fwd_kernel,
        name="attn_fwd",
        grid_spec=pltpu.PrefetchScalarGridSpec(
            num_scalar_prefetch=1,
            grid=(slots, tokens // BQ),
            in_specs=[queries, keys, values, segr, segc],
            out_specs=[queries, stats],
            scratch_shapes=[
                pltpu.VMEM((8, BQ), jnp.float32),
                pltpu.VMEM((8, BQ), jnp.float32),
                pltpu.VMEM((group, BQ), jnp.float32),
                pltpu.VMEM((tokens, HEAD), jnp.bfloat16),
            ],
        ),
        out_shape=[
            jax.ShapeDtypeStruct((slots * group, tokens), jnp.bfloat16),
            jax.ShapeDtypeStruct((slots, 8, tokens), jnp.float32),
        ],
        compiler_params=pltpu.CompilerParams(vmem_limit_bytes=32 << 20),
        cost_estimate=pl.CostEstimate(flops=0, bytes_accessed=150 << 20, transcendentals=0),
    )(first, qkv_t, qkv_t, qkv_t, seg_row, masks)


def attn_bwd_kernel(first_ref, qt_ref, dot_ref, ot_ref, lse_ref, kt_ref, vt_ref, segr_ref, mask_ref,
                    grad_ref, delta_scr, acc_scr, q_scr, do_scr, k_scr, v_scr, gk_scr, gv_scr):
    group = qt_ref.shape[0]
    heads = group // HEAD
    slot = pl.program_id(0)
    slots = pl.num_programs(0)
    block = pl.program_id(1)
    q_base = pl.multiple_of(block * BQ, BQ)

    @pl.when(block == 0)
    def _():
        flip_rows(kt_ref, k_scr)
        flip_rows(vt_ref, v_scr)
        gk_scr[...] = jnp.zeros_like(gk_scr)
        gv_scr[...] = jnp.zeros_like(gv_scr)

    acc_scr[...] = jnp.zeros_like(acc_scr)
    start = first_ref[slot * pl.num_programs(1) + block]

    @pl.when(start <= block)
    def _():
        for head in range(heads):
            cols = slice(head * HEAD, (head + 1) * HEAD)
            grad_out = dot_ref[cols].astype(jnp.float32)
            delta_scr[head : head + 1] = jnp.sum(
                grad_out * ot_ref[cols].astype(jnp.float32), axis=0, keepdims=True
            )
            q_scr[head] = jnp.transpose(qt_ref[cols].astype(jnp.float32)).astype(jnp.bfloat16)
            do_scr[head] = jnp.transpose(grad_out).astype(jnp.bfloat16)

    segq_row = segr_ref[0:1, :]

    def body(j, carry):
        k_base = pl.multiple_of(j * BK, BK)
        rows = pl.ds(k_base, BK)
        bias = attn_bias(q_base, k_base, segq_row, mask_ref[rows, 4:5])
        k_blk = k_scr[rows, :]
        kt_blk = kt_ref[:, rows]
        v_blk = v_scr[rows, :]
        gk = jnp.zeros((BK, HEAD), jnp.float32)
        gv = jnp.zeros((BK, HEAD), jnp.float32)
        for head in range(heads):
            cols = slice(head * HEAD, (head + 1) * HEAD)
            scores = dot_plain(k_blk, qt_ref[cols, :]) * 0.125 + bias
            probs = jnp.exp(scores - lse_ref[0, head : head + 1])
            grad_p = dot_plain(v_blk, dot_ref[cols, :])
            grad_s = (probs * (grad_p - delta_scr[head : head + 1])).astype(jnp.bfloat16)
            gv += dot_plain(probs.astype(jnp.bfloat16), do_scr[head])
            gk += dot_plain(grad_s, q_scr[head])
            acc_scr[cols] += dot_plain(kt_blk, grad_s)
        gk_scr[rows, :] += gk * 0.125
        gv_scr[rows, :] += gv
        return carry

    lax.fori_loop(start, block + 1, body, 0)
    grad_ref[pl.ds(pl.multiple_of(slot * group, HEAD), group), pl.ds(q_base, BQ)] = (
        acc_scr[...] * 0.125
    ).astype(jnp.bfloat16)

    @pl.when(block == pl.num_programs(1) - 1)
    def _():
        key_rows = pl.ds(pl.multiple_of(slots * group + slot * HEAD, HEAD), HEAD)
        value_rows = pl.ds(pl.multiple_of(slots * group + (slots + slot) * HEAD, HEAD), HEAD)
        for at in range(0, gk_scr.shape[0], BK):
            cols = pl.ds(at, BK)
            grad_ref[key_rows, cols] = jnp.transpose(gk_scr[at : at + BK]).astype(jnp.bfloat16)
            grad_ref[value_rows, cols] = jnp.transpose(gv_scr[at : at + BK]).astype(jnp.bfloat16)


def attn_backward(first, qkv_t, do_t, o_t, lse, seg_row, masks, slots):
    width, tokens = qkv_t.shape
    group = width // slots - 2 * HEAD
    queries, keys, values, stats, segr, segc = attn_specs(slots, group, tokens)
    return pl.pallas_call(
        attn_bwd_kernel,
        name="attn_bwd",
        grid_spec=pltpu.PrefetchScalarGridSpec(
            num_scalar_prefetch=1,
            grid=(slots, tokens // BQ),
            in_specs=[queries, queries, queries, stats, keys, values, segr, segc],
            out_specs=pl.BlockSpec((width, tokens), lambda s, i, f: (0, 0)),
            scratch_shapes=[
                pltpu.VMEM((8, BQ), jnp.float32),
                pltpu.VMEM((group, BQ), jnp.float32),
                pltpu.VMEM((group // HEAD, BQ, HEAD), jnp.bfloat16),
                pltpu.VMEM((group // HEAD, BQ, HEAD), jnp.bfloat16),
                pltpu.VMEM((tokens, HEAD), jnp.bfloat16),
                pltpu.VMEM((tokens, HEAD), jnp.bfloat16),
                pltpu.VMEM((tokens, HEAD), jnp.float32),
                pltpu.VMEM((tokens, HEAD), jnp.float32),
            ],
        ),
        out_shape=jax.ShapeDtypeStruct((width, tokens), jnp.bfloat16),
        compiler_params=pltpu.CompilerParams(vmem_limit_bytes=40 << 20),
        cost_estimate=pl.CostEstimate(flops=0, bytes_accessed=160 << 20, transcendentals=0),
    )(first, qkv_t, do_t, o_t, lse, qkv_t, qkv_t, seg_row, masks)


def first_blocks(segs_flat):
    tokens = segs_flat.shape[0]
    starts = segs_flat[::BQ]
    positions = jnp.arange(tokens // BQ, dtype=jnp.int32) * BQ
    seg_start = jnp.sum((segs_flat[None, :] < starts[:, None]).astype(jnp.int32), axis=1)
    return jnp.maximum(jnp.maximum(seg_start, positions - WINDOW + 1), 0) // BK


def conv_rows(x_in, conv_w, conv_b, segs_grid):
    seq_count, seq_len = segs_grid.shape
    width = x_in.shape[1]
    grid = x_in.reshape(seq_count, seq_len, width)
    pad_x = jnp.concatenate([jnp.zeros((seq_count, CONV - 1, width), jnp.float32), grid], axis=1)
    pad_seg = jnp.concatenate([jnp.full((seq_count, CONV - 1), -1, jnp.int32), segs_grid], axis=1)
    total = jnp.zeros((seq_count, seq_len, width), jnp.float32) + conv_b
    for tap in range(CONV):
        same = (pad_seg[:, tap : tap + seq_len] == segs_grid).astype(jnp.float32)
        total = total + conv_w[tap] * pad_x[:, tap : tap + seq_len] * same[:, :, None]
    return jax.nn.silu(total).reshape(seq_count * seq_len, width)


CHUNK = 64
ROWS = 256
RANGE = 120.0
LANES = 256


def spans(width, size):
    return [(at, min(at + size, width)) for at in range(0, width, size)]


def softplus_parts(pre):
    small = jnp.exp(-jnp.abs(pre))
    step = jnp.maximum(pre, 0.0) + jnp.log1p(small)
    slope = jnp.where(pre >= 0.0, 1.0, small) / (1.0 + small)
    return step, slope


def split_sum(tri, values):
    high = values.astype(jnp.bfloat16)
    low = (values - high.astype(jnp.float32)).astype(jnp.bfloat16)
    return dot_plain(tri, high) + dot_plain(tri, low)


def tri_matrix(size, upper):
    row = lax.broadcasted_iota(jnp.int32, (size, size), 0)
    col = lax.broadcasted_iota(jnp.int32, (size, size), 1)
    order = (col >= row) if upper else (row >= col)
    return order & (lax.div(row, CHUNK) == lax.div(col, CHUNK))


def scan_setup(dbl_ref, dtw_ref, vec_ref, step_scr, cum_scr, slope_scr):
    width = dtw_ref.shape[1]
    tri = tri_matrix(ROWS, False).astype(jnp.bfloat16)
    dt_low = dbl_ref[:, :RANK]
    lowest = jnp.zeros((), jnp.float32)
    for lo, hi in spans(width, LANES):
        pre = dot_plain(dt_low, dtw_ref[:, lo:hi]) + vec_ref[0:1, lo:hi]
        step, slope = softplus_parts(pre)
        cum = split_sum(tri, -step * jnp.exp(vec_ref[1:2, lo:hi]))
        step_scr[:, lo:hi] = step
        cum_scr[:, lo:hi] = cum
        if slope_scr is not None:
            slope_scr[:, lo:hi] = slope
        least = jnp.zeros((1, hi - lo), jnp.float32)
        for at in range(0, ROWS, CHUNK):
            least = jnp.minimum(least, cum[at + CHUNK - 1 : at + CHUNK])
        lowest = jnp.minimum(lowest, jnp.min(least))
    return lowest


def chunk_maps(dbl_ref, mask_ref, segr_ref, at):
    rows = slice(at, at + CHUNK)
    b_map = dbl_ref[rows, 128 : 128 + STATE]
    c_map = dbl_ref[rows, 128 + STATE : 128 + 2 * STATE]
    linked = mask_ref[rows, 0:1]
    tail = mask_ref[rows, 1:2]
    keep = mask_ref[at + CHUNK - 1 : at + CHUNK, 2:3]
    allowed = tri_matrix(CHUNK, False) & (mask_ref[rows, 4:5] == segr_ref[0:1, rows])
    gram = jnp.where(allowed, dot_last(c_map, b_map), 0.0)
    c_link = c_map.astype(jnp.float32) * linked
    b_tail = b_map.astype(jnp.float32) * tail
    return b_map, c_map, linked, tail, keep, allowed, gram, c_link, b_tail


def mixer(square, side, bottom):
    corner = jnp.zeros((STATE, STATE), jnp.float32)
    top = jnp.concatenate([square, side], axis=1)
    low = jnp.concatenate([jnp.transpose(bottom), corner], axis=1)
    return jnp.concatenate([top, low], axis=0).astype(jnp.bfloat16)


def token_column(block, lane_index):
    lanes = lax.broadcasted_iota(jnp.int32, block.shape, 1)
    return jnp.sum(jnp.where(lanes == lane_index, block, 0.0), axis=1, keepdims=True)


def scan_fwd_kernel(
    xa_ref, z_ref, dbl_ref, mask_ref, segr_ref, dtw_ref, vec_ref,
    out_ref, hsave_ref, h_scr, step_scr, cum_scr, y_scr,
):
    width = xa_ref.shape[1]

    @pl.when(pl.program_id(0) == 0)
    def _():
        h_scr[...] = jnp.zeros_like(h_scr)

    lowest = scan_setup(dbl_ref, dtw_ref, vec_ref, step_scr, cum_scr, None)

    @pl.when(lowest >= -RANGE)
    def _():
        for index, at in enumerate(range(0, ROWS, CHUNK)):
            rows = slice(at, at + CHUNK)
            _, _, _, _, keep, _, gram, c_link, b_tail = chunk_maps(dbl_ref, mask_ref, segr_ref, at)
            forward = mixer(gram, c_link, b_tail)
            for lo, hi in spans(width, LANES):
                cum = cum_scr[rows, lo:hi]
                half = 0.5 * cum[CHUNK - 1 : CHUNK]
                gap = cum - half
                rise = jnp.exp(half)
                h_old = h_scr[:, lo:hi]
                hsave_ref[index, :, lo:hi] = h_old
                x_f = xa_ref[rows, lo:hi].astype(jnp.float32)
                sources = jnp.concatenate(
                    [jnp.exp(-gap) * (step_scr[rows, lo:hi] * x_f), rise * h_old], axis=0
                ).astype(jnp.bfloat16)
                mixed = dot_plain(forward, sources)
                total = jnp.exp(gap) * mixed[:CHUNK] + vec_ref[2:3, lo:hi] * x_f
                out_ref[rows, lo:hi] = (total * jax.nn.silu(z_ref[rows, lo:hi])).astype(
                    jnp.bfloat16
                )
                h_scr[:, lo:hi] = rise * mixed[CHUNK:] + (rise * rise * keep) * h_old

    @pl.when(lowest < -RANGE)
    def _():
        for index, at in enumerate(range(0, ROWS, CHUNK)):
            rows = slice(at, at + CHUNK)
            hsave_ref[index] = h_scr[...]
            b_cols = jnp.transpose(dbl_ref[rows, 128 : 128 + STATE].astype(jnp.float32))
            c_cols = jnp.transpose(dbl_ref[rows, 128 + STATE : 128 + 2 * STATE].astype(jnp.float32))
            y_scr[...] = xa_ref[rows].astype(jnp.float32)
            rate = jnp.exp(vec_ref[1:2])

            def token(t, carry):
                step = step_scr[pl.ds(at + t, 1)]
                keep = mask_ref[pl.ds(at + t, 1)][:, 3:4]
                state = (jnp.exp(-step * rate) * keep) * h_scr[...] + token_column(b_cols, t) * (
                    step * y_scr[pl.ds(t, 1)]
                )
                h_scr[...] = state
                y_scr[pl.ds(t, 1)] = (
                    jnp.sum(state * token_column(c_cols, t), axis=0, keepdims=True)
                    + vec_ref[2:3] * y_scr[pl.ds(t, 1)]
                )
                return carry

            lax.fori_loop(0, CHUNK, token, 0)
            out_ref[rows] = (y_scr[...] * jax.nn.silu(z_ref[rows])).astype(jnp.bfloat16)


def scan_bwd_kernel(
    xa_ref, z_ref, dbl_ref, mask_ref, segr_ref, dtw_ref, vec_ref, hsave_ref, gs_ref,
    gz_ref, gx_ref, gdbl_ref, gdtw_ref, gvec_ref,
    g_scr, step_scr, cum_scr, slope_scr, gl_scr, gu_scr, gpre_scr, hall_scr, y_scr,
):
    width = xa_ref.shape[1]

    @pl.when(pl.program_id(0) == 0)
    def _():
        g_scr[...] = jnp.zeros_like(g_scr)
        gdtw_ref[...] = jnp.zeros_like(gdtw_ref)
        gvec_ref[...] = jnp.zeros_like(gvec_ref)

    lowest = scan_setup(dbl_ref, dtw_ref, vec_ref, step_scr, cum_scr, slope_scr)
    count = ROWS // CHUNK

    @pl.when(lowest >= -RANGE)
    def _():
        for index in range(count - 1, -1, -1):
            at = index * CHUNK
            rows = slice(at, at + CHUNK)
            b_map, c_map, linked, tail, keep, allowed, gram, c_link, b_tail = chunk_maps(
                dbl_ref, mask_ref, segr_ref, at
            )
            forward = mixer(gram, c_link, b_tail)
            reverse = mixer(jnp.transpose(gram), b_tail, c_link)
            cross = jnp.zeros((CHUNK + STATE, CHUNK + STATE), jnp.float32)
            for lo, hi in spans(width, LANES):
                cum = cum_scr[rows, lo:hi]
                half = 0.5 * cum[CHUNK - 1 : CHUNK]
                gap = cum - half
                fall = jnp.exp(gap)
                grow = jnp.exp(-gap)
                rise = jnp.exp(half)
                h_old = hsave_ref[index, :, lo:hi]
                g_new = g_scr[:, lo:hi]
                step = step_scr[rows, lo:hi]
                x_f = xa_ref[rows, lo:hi].astype(jnp.float32)
                skip = vec_ref[2:3, lo:hi]
                sources = jnp.concatenate([grow * (step * x_f), rise * h_old], axis=0).astype(
                    jnp.bfloat16
                )
                mixed = dot_plain(forward, sources)
                inner = mixed[:CHUNK]
                z_f = z_ref[rows, lo:hi]
                grad = gs_ref[rows, lo:hi]
                sig = jax.nn.sigmoid(z_f)
                gated = z_f * sig
                gy = grad * gated
                gz_ref[rows, lo:hi] = (
                    grad * (fall * inner + skip * x_f) * (sig + gated * (1.0 - sig))
                ).astype(jnp.bfloat16)
                sinks = jnp.concatenate([fall * gy, rise * g_new], axis=0).astype(jnp.bfloat16)
                pulled = dot_plain(reverse, sinks)
                back = pulled[:CHUNK]
                cross += dot_last(sinks, sources)
                sinks_f = sinks.astype(jnp.float32)
                sources_f = sources.astype(jnp.float32)
                ends = jnp.sum(sinks_f[CHUNK:] * mixed[CHUNK:], axis=0, keepdims=True) + (
                    rise * rise * keep
                ) * jnp.sum(g_new * h_old, axis=0, keepdims=True)
                diff = sinks_f[:CHUNK] * inner - sources_f[:CHUNK] * back
                gl_scr[rows, lo:hi] = diff
                gl_scr[at + CHUNK - 1 : at + CHUNK, lo:hi] = diff[CHUNK - 1 : CHUNK] + ends
                g_scr[:, lo:hi] = rise * pulled[CHUNK:] + (rise * rise * keep) * g_new
                gu = grow * back
                gu_scr[rows, lo:hi] = gu
                gx_ref[rows, lo:hi] = step * gu + skip * gy
                gvec_ref[2:3, lo:hi] += jnp.sum(gy * x_f, axis=0, keepdims=True)
            g_gram = jnp.where(allowed, cross[:CHUNK, :CHUNK], 0.0).astype(jnp.bfloat16)
            gdbl_ref[rows, 128 : 128 + STATE] = dot_first(g_gram, c_map) + tail * jnp.transpose(
                cross[CHUNK:, :CHUNK]
            )
            gdbl_ref[rows, 128 + STATE : 128 + 2 * STATE] = (
                dot_plain(g_gram, b_map) + linked * cross[:CHUNK, CHUNK:]
            )
        triu = tri_matrix(ROWS, True).astype(jnp.bfloat16)
        for lo, hi in spans(width, LANES):
            gl_scr[:, lo:hi] = split_sum(triu, gl_scr[:, lo:hi])

    @pl.when(lowest < -RANGE)
    def _():
        rate = jnp.exp(vec_ref[1:2])

        def chunk_step(reverse, carry):
            index = count - 1 - reverse
            at = pl.multiple_of(index * CHUNK, CHUNK)
            rows = pl.ds(at, CHUNK)
            b_cols = jnp.transpose(dbl_ref[rows, 128 : 128 + STATE].astype(jnp.float32))
            c_cols = jnp.transpose(dbl_ref[rows, 128 + STATE : 128 + 2 * STATE].astype(jnp.float32))
            hall_scr[0] = hsave_ref[index]
            y_scr[...] = xa_ref[rows].astype(jnp.float32)
            gu_scr[rows] = gs_ref[rows] * jax.nn.silu(z_ref[rows])

            def forward(t, inner_carry):
                step = step_scr[pl.ds(at + t, 1)]
                keep = mask_ref[pl.ds(at + t, 1)][:, 3:4]
                state = (jnp.exp(-step * rate) * keep) * hall_scr[t] + token_column(b_cols, t) * (
                    step * y_scr[pl.ds(t, 1)]
                )
                hall_scr[t + 1] = state
                return inner_carry

            lax.fori_loop(0, CHUNK, forward, 0)

            def backward(back, inner_carry):
                g_b, g_c = inner_carry
                t = CHUNK - 1 - back
                step = step_scr[pl.ds(at + t, 1)]
                keep = mask_ref[pl.ds(at + t, 1)][:, 3:4]
                decay = jnp.exp(-step * rate) * keep
                gy = gu_scr[pl.ds(at + t, 1)]
                x_f = y_scr[pl.ds(t, 1)]
                c_col = token_column(c_cols, t)
                b_col = token_column(b_cols, t)
                here = hall_scr[t + 1]
                grad = g_scr[...] + c_col * gy
                lanes = lax.broadcasted_iota(jnp.int32, (STATE, CHUNK), 1)
                g_b = jnp.where(
                    lanes == t, jnp.sum(grad * (step * x_f), axis=1, keepdims=True), g_b
                )
                g_c = jnp.where(lanes == t, jnp.sum(here * gy, axis=1, keepdims=True), g_c)
                gl_scr[pl.ds(at + t, 1)] = decay * jnp.sum(
                    grad * hall_scr[t], axis=0, keepdims=True
                )
                gu_scr[pl.ds(at + t, 1)] = jnp.sum(grad * b_col, axis=0, keepdims=True)
                y_scr[pl.ds(t, 1)] = (
                    jnp.sum(here * c_col, axis=0, keepdims=True) + vec_ref[2:3] * x_f
                )
                g_scr[...] = decay * grad
                return g_b, g_c

            blank = jnp.zeros((STATE, CHUNK), jnp.float32)
            g_b, g_c = lax.fori_loop(0, CHUNK, backward, (blank, blank))
            gdbl_ref[rows, 128 : 128 + STATE] = jnp.transpose(g_b)
            gdbl_ref[rows, 128 + STATE : 128 + 2 * STATE] = jnp.transpose(g_c)
            z_f = z_ref[rows]
            grad = gs_ref[rows]
            sig = jax.nn.sigmoid(z_f)
            gz_ref[rows] = (grad * y_scr[...] * (sig * (1.0 + z_f * (1.0 - sig)))).astype(
                jnp.bfloat16
            )
            gy = grad * (z_f * sig)
            x_f = xa_ref[rows].astype(jnp.float32)
            gx_ref[rows] = step_scr[rows] * gu_scr[rows] + vec_ref[2:3] * gy
            gvec_ref[2:3] += jnp.sum(gy * x_f, axis=0, keepdims=True)
            return carry

        lax.fori_loop(0, count, chunk_step, 0)

    for lo, hi in spans(width, LANES):
        rate = jnp.exp(vec_ref[1:2, lo:hi])
        x_f = xa_ref[:, lo:hi].astype(jnp.float32)
        gl = rate * gl_scr[:, lo:hi]
        gpre = (x_f * gu_scr[:, lo:hi] - gl) * slope_scr[:, lo:hi]
        gvec_ref[0:1, lo:hi] += jnp.sum(gpre, axis=0, keepdims=True)
        gvec_ref[1:2, lo:hi] -= jnp.sum(step_scr[:, lo:hi] * gl, axis=0, keepdims=True)
        gpre_scr[:, lo:hi] = gpre.astype(jnp.bfloat16)
    gdtw_ref[...] += dot_first(dbl_ref[:, :RANK], gpre_scr[...])
    gdbl_ref[:, :RANK] = dot_last(gpre_scr[...], dtw_ref[...])


def scan_specs(width, backward, blocks):
    def at(i):
        return (blocks - 1 - i) if backward else i

    rows = lambda cols: pl.BlockSpec((ROWS, cols), lambda i: (at(i), 0))
    whole = lambda *shape: pl.BlockSpec(shape, lambda i: (0, 0))
    return [
        rows(width),
        rows(width),
        rows(256),
        rows(8),
        pl.BlockSpec((1, ROWS), lambda i: (0, at(i))),
        whole(RANK, width),
        whole(8, width),
    ], pl.BlockSpec((ROWS // CHUNK, STATE, width), lambda i: (at(i), 0, 0)), rows, whole


def scan_forward(x_act, z_gate, dbl, masks, seg_row, dt_weight, vectors):
    tokens, width = x_act.shape
    blocks = tokens // ROWS
    in_specs, state_spec, rows, whole = scan_specs(width, False, blocks)
    return pl.pallas_call(
        scan_fwd_kernel,
        name="scan_fwd",
        grid=(blocks,),
        in_specs=in_specs,
        out_specs=[rows(width), state_spec],
        out_shape=[
            jax.ShapeDtypeStruct((tokens, width), jnp.bfloat16),
            jax.ShapeDtypeStruct((tokens // CHUNK, STATE, width), jnp.float32),
        ],
        scratch_shapes=[
            pltpu.VMEM((STATE, width), jnp.float32),
            pltpu.VMEM((ROWS, width), jnp.float32),
            pltpu.VMEM((ROWS, width), jnp.float32),
            pltpu.VMEM((CHUNK, width), jnp.float32),
        ],
        compiler_params=pltpu.CompilerParams(vmem_limit_bytes=40 << 20),
        cost_estimate=pl.CostEstimate(
            flops=0, bytes_accessed=93 << 20, transcendentals=0
        ),
    )(x_act, z_gate, dbl, masks, seg_row, dt_weight, vectors)


def scan_backward(x_act, z_gate, dbl, masks, seg_row, dt_weight, vectors, states, grad_rows):
    tokens, width = x_act.shape
    blocks = tokens // ROWS
    in_specs, state_spec, rows, whole = scan_specs(width, True, blocks)
    return pl.pallas_call(
        scan_bwd_kernel,
        name="scan_bwd",
        grid=(blocks,),
        in_specs=in_specs + [state_spec, rows(width)],
        out_specs=[rows(width), rows(width), rows(256), whole(RANK, width), whole(8, width)],
        out_shape=[
            jax.ShapeDtypeStruct((tokens, width), jnp.bfloat16),
            jax.ShapeDtypeStruct((tokens, width), jnp.float32),
            jax.ShapeDtypeStruct((tokens, 256), jnp.float32),
            jax.ShapeDtypeStruct((RANK, width), jnp.float32),
            jax.ShapeDtypeStruct((8, width), jnp.float32),
        ],
        scratch_shapes=[
            pltpu.VMEM((STATE, width), jnp.float32),
            pltpu.VMEM((ROWS, width), jnp.float32),
            pltpu.VMEM((ROWS, width), jnp.float32),
            pltpu.VMEM((ROWS, width), jnp.float32),
            pltpu.VMEM((ROWS, width), jnp.float32),
            pltpu.VMEM((ROWS, width), jnp.float32),
            pltpu.VMEM((ROWS, width), jnp.bfloat16),
            pltpu.VMEM((CHUNK + 1, STATE, width), jnp.float32),
            pltpu.VMEM((CHUNK, width), jnp.float32),
        ],
        compiler_params=pltpu.CompilerParams(vmem_limit_bytes=48 << 20),
        cost_estimate=pl.CostEstimate(
            flops=0, bytes_accessed=244 << 20, transcendentals=0
        ),
    )(x_act, z_gate, dbl, masks, seg_row, dt_weight, vectors, states, grad_rows)


def scan_masks(segs_flat):
    tokens = segs_flat.shape[0]
    before = jnp.concatenate([jnp.full((1,), -1, jnp.int32), segs_flat[:-1]])
    chunked = segs_flat.reshape(tokens // CHUNK, CHUNK)
    prior = before.reshape(tokens // CHUNK, CHUNK)[:, :1]
    last = chunked[:, CHUNK - 1 :]
    linked = chunked == prior
    tail = chunked == last
    keep = jnp.broadcast_to(last == prior, chunked.shape)
    same = (segs_flat == before).reshape(chunked.shape)
    blank = jnp.zeros_like(linked)
    stacked = jnp.stack([linked, tail, keep, same], axis=-1).reshape(tokens, 4).astype(jnp.float32)
    number = segs_flat.astype(jnp.float32)
    masks = jnp.concatenate(
        [stacked, number[:, None], jnp.zeros((tokens, 3), jnp.float32)], axis=1
    )
    return masks, number[None, :]


def per_device(
    inputs,
    teacher,
    segment_ids,
    valid,
    norm_in_gain,
    w_query,
    w_key,
    w_value,
    w_attn_out,
    w_mamba_in,
    conv_weight,
    conv_bias,
    x_proj,
    dt_proj,
    dt_bias,
    a_log,
    d_skip,
    w_mamba_out,
    attn_norm_gain,
    ssm_norm_gain,
    norm_mid_gain,
    w_gate,
    w_up,
    w_down,
):
    rank_index = lax.axis_index("tensor")
    first_slot, second_slot = rank_index, KV - 1
    per_slot = HEADS // KV
    group_width = per_slot * HEAD
    query_width = 2 * group_width
    qkv_width = query_width + 4 * HEAD
    width = inputs.shape[1]
    inner_width = w_mamba_out.shape[0]
    inner_start = rank_index * inner_width
    inner_all = inner_width * lax.axis_size("tensor")
    low = lambda values: values.astype(jnp.bfloat16)
    gather_dp = lambda part: lax.all_gather(part, "dp", axis=0, tiled=True)
    scatter_dp = lambda part: lax.psum_scatter(part, "dp", scatter_dimension=0, tiled=True)
    gather_t = lambda part: gather_rows(part, 1)
    tie = lax.optimization_barrier

    own_width = w_query.shape[0]
    inner_local = jnp.concatenate(
        [
            dt_bias[:, None],
            a_log[:, None],
            d_skip[:, None],
            conv_bias[:, None],
            conv_weight.T,
            x_proj,
            dt_proj.T,
        ],
        axis=1,
    ).reshape(own_width, -1)
    mamba_local = jnp.concatenate(
        [
            w_mamba_in.reshape(own_width, 2 * inner_width),
            jnp.zeros((own_width, -2 * inner_width % 128), jnp.bfloat16),
            inner_local,
        ],
        axis=1,
    )
    mamba_all = gather_dp(mamba_local)
    gain_rows = jnp.stack([norm_in_gain, attn_norm_gain, ssm_norm_gain, norm_mid_gain])
    gain_rows, w_query, w_key, w_value, _ = tie((gain_rows, w_query, w_key, w_value, mamba_local))
    gains, valid_total = hello(gain_rows, jnp.sum(valid).astype(jnp.float32))
    gain_in, gain_attn, gain_ssm, gain_mid = [gains[index][:, None] for index in range(4)]
    inputs_t = inputs.T
    normed_in, pull_in = jax.vjp(normalize_t, inputs_t, gain_in)
    qkv_local = jnp.concatenate(
        [
            pick_groups(w_query, first_slot, second_slot, group_width, 1),
            pick_groups(w_key, first_slot, second_slot, HEAD, 1),
            pick_groups(w_value, first_slot, second_slot, HEAD, 1),
        ],
        axis=1,
    )
    normed_low, qkv_local = tie((low(normed_in), qkv_local))
    qkv_w = gather_dp(qkv_local)
    whole_in = gather_t(normed_low)
    whole_in, w_attn_out, w_mamba_out, w_gate, w_up, w_down = tie(
        (whole_in, w_attn_out, w_mamba_out, w_gate, w_up, w_down)
    )
    out_local = jnp.concatenate(
        [pick_groups(w_attn_out, first_slot, second_slot, group_width, 0).T, w_mamba_out.T], axis=1
    )
    out_local, w_gate, w_up, w_down = tie((out_local, w_gate, w_up, w_down))
    outs_all = gather_dp(out_local)
    out_w = outs_all[:, :query_width]
    mamba_out_w = outs_all[:, query_width:]
    weight_x = mamba_all[:, :inner_width]
    weight_z = mamba_all[:, inner_width : 2 * inner_width]
    inner_rows = lax.dynamic_slice_in_dim(
        mamba_all[:, -inner_local.shape[1] :].reshape(inner_all, -1), inner_start, inner_width, 0
    )
    x_in = dot_first(whole_in, weight_x)
    ff_width = w_gate.shape[1]
    ff_step = -(-ff_width // 128) * 128
    blank = jnp.zeros((own_width, ff_step - ff_width), jnp.bfloat16)
    gate_up_all = gather_dp(jnp.concatenate([w_gate, blank, w_up, blank], axis=1))
    group_rows = whole_in.shape[1]
    seq_count = group_rows // LEN
    segs_grid = segment_ids.reshape(seq_count, LEN)
    segs_flat = (segs_grid + 128 * jnp.arange(seq_count, dtype=jnp.int32)[:, None]).reshape(-1)
    scan_mask, seg_row = scan_masks(segs_flat)
    vector_rows = inner_rows[:, :8].astype(jnp.float32).T
    xproj_rows = inner_rows[:, 8 : 8 + RANK + 2 * STATE]
    dt_weight = inner_rows[:, 8 + RANK + 2 * STATE :].T
    xproj_pad = jnp.concatenate(
        [
            xproj_rows[:, :RANK],
            jnp.zeros((inner_width, 128 - RANK), jnp.bfloat16),
            xproj_rows[:, RANK:],
            jnp.zeros((inner_width, 128 - 2 * STATE), jnp.bfloat16),
        ],
        axis=1,
    )
    x_pre, pull_conv = jax.vjp(
        lambda x_part, taps, shift: conv_rows(x_part, taps, shift, segs_grid),
        x_in,
        vector_rows[4:],
        vector_rows[3],
    )
    x_act, w_down = tie((low(x_pre), w_down))
    down_all = gather_dp(w_down.T)
    dbl_pad = total_rows(dot_plain(x_act, xproj_pad), 3)
    z_gate = dot_first(whole_in, weight_z)
    ssm_rows, states = scan_forward(
        x_act, z_gate, dbl_pad, scan_mask, seg_row, dt_weight, vector_rows
    )
    starts = first_blocks(segs_flat)
    blocks = jnp.arange(group_rows // BQ, dtype=jnp.int32)
    shared_here = blocks // (group_rows // BQ // 4) == rank_index
    firsts = jnp.concatenate([starts, jnp.where(shared_here, starts, blocks + 1)])
    qkv_w, ssm_rows = tie((qkv_w, ssm_rows))
    qkv_cols = low(dot_first(qkv_w, whole_in))
    attended_t, log_totals = attn_forward(firsts, qkv_cols, seg_row, scan_mask, 2)
    attn_sum = product_reduce(
        [outs_all], [(attended_t, True)], [(0, 0, query_width, 0)], 10, "attn_reduce", 43
    )
    ssm_rows, attn_sum = tie((ssm_rows, attn_sum))
    ssm_sum = product_reduce(
        [outs_all],
        [(ssm_rows, False)],
        [(0, query_width, query_width + inner_width, 0)],
        11,
        "ssm_reduce",
        43,
    )
    mixed, pull_join = jax.vjp(join_rows_t, inputs_t, attn_sum, ssm_sum, gain_attn, gain_ssm)
    normed_mid, pull_mid = jax.vjp(normalize_t, mixed, gain_mid)
    whole_mid = gather_t(low(normed_mid))
    whole_mid, gate_up_all = tie((whole_mid, gate_up_all))
    gate_all = gate_up_all[:, :ff_width]
    up_all = gate_up_all[:, ff_step : ff_step + ff_width]
    gate_rows = dot_first(whole_mid, gate_all)
    up_rows = dot_first(whole_mid, up_all)
    sigmoid_gate = jax.nn.sigmoid(gate_rows)
    hidden = low(gate_rows * sigmoid_gate * up_rows)
    ffn_rows = product_reduce(
        [down_all], [(hidden, False)], [(0, 0, ff_width, 0)], 6, "down_reduce", 45
    )
    result = mixed + ffn_rows
    all_rows = inputs.shape[0] * lax.axis_size("dp") * lax.axis_size("tensor")
    grad_out = all_rows / valid_total * valid.astype(jnp.float32)[None, :] * (result - teacher.T)
    grad_ffn = gather_t(low(grad_out))
    grad_hidden = dot_first(grad_ffn, down_all)
    grad_gate = low(grad_hidden * up_rows * sigmoid_gate * (1.0 + gate_rows * (1.0 - sigmoid_gate)))
    grad_up = low(grad_hidden * gate_rows * sigmoid_gate)
    ffn_grads = weight_grads(
        [
            (whole_mid, grad_gate, False),
            (whole_mid, grad_up, False),
            (grad_ffn, hidden, False),
        ],
        "ffn_weight_grads",
        44,
    )
    grad_gate, grad_up, ffn_grads = tie((grad_gate, grad_up, ffn_grads))
    ffn_shard = scatter_dp(ffn_grads)
    grad_mid_rows = product_reduce(
        [gate_up_all],
        [(grad_gate, False), (grad_up, False)],
        [(0, 0, ff_width, 0), (0, ff_step, ff_step + ff_width, 1)],
        7,
        "mid_reduce",
        50,
    )
    grad_mixed_norm, grad_gain_mid = pull_mid(grad_mid_rows)
    grad_mixed = grad_out + grad_mixed_norm
    grad_resid, grad_attn_sum, grad_ssm_sum, grad_gain_attn, grad_gain_ssm = pull_join(grad_mixed)
    grad_ssm_whole = gather_t(low(grad_ssm_sum))
    grad_attn_low, grad_ssm_whole = tie((low(grad_attn_sum), grad_ssm_whole))
    grad_attn_whole = gather_t(grad_attn_low)
    grad_ssm_whole, grad_attn_whole = tie((grad_ssm_whole, grad_attn_whole))
    grad_ssm_rows = dot_first(grad_ssm_whole, mamba_out_w)
    grad_gate_part, grad_act_scan, grad_dbl_part, grad_dtproj, grad_vectors = scan_backward(
        x_act, z_gate, dbl_pad, scan_mask, seg_row, dt_weight, vector_rows, states, grad_ssm_rows
    )
    mid_grads = weight_grads(
        [
            (grad_attn_whole, attended_t, True),
            (grad_ssm_whole, ssm_rows, False),
            (whole_in, grad_gate_part, False),
        ],
        "mid_weight_grads",
        26,
        128,
    )
    grad_att_t = low(
        lax.dot_general(
            out_w, grad_attn_whole, (((0,), (0,)), ((), ())), preferred_element_type=jnp.float32
        )
    )
    grad_dbl_part, mid_grads, ffn_shard = tie((grad_dbl_part, mid_grads, ffn_shard))
    mid_shard = scatter_dp(mid_grads)
    grad_qkv = attn_backward(
        firsts, qkv_cols, grad_att_t, attended_t, log_totals, seg_row, scan_mask, 2
    )
    grad_dbl = total_rows(grad_dbl_part, 3)
    grad_act = grad_act_scan + dot_last(grad_dbl, xproj_pad)
    grad_xproj_w = dot_first(x_act, grad_dbl)
    grad_x_part, grad_taps, grad_shift = pull_conv(grad_act)
    grad_x_low = low(grad_x_part)
    inner_grads = jnp.concatenate(
        [
            grad_vectors[:3].T,
            grad_shift[:, None],
            grad_taps.T,
            grad_xproj_w[:, :RANK],
            grad_xproj_w[:, 128 : 128 + 2 * STATE],
            grad_dtproj.T,
        ],
        axis=1,
    )
    inner_full = low(place_block(inner_grads, inner_start, inner_all, 0)).reshape(width, -1)
    last_grads = weight_grads(
        [(whole_in, grad_x_low, False), (whole_in, grad_qkv, True), (inner_full, None, False)],
        "last_weight_grads",
        20,
    )
    grad_x_low, grad_qkv, last_grads, mid_shard = tie(
        (grad_x_low, grad_qkv, last_grads, mid_shard)
    )
    last_shard = scatter_dp(last_grads)
    grad_in_rows = product_reduce(
        [qkv_w, mamba_all],
        [(grad_qkv, True), (grad_x_low, False), (grad_gate_part, False)],
        [
            (0, 0, qkv_width, 0),
            (1, 0, inner_width, 1),
            (1, inner_width, 2 * inner_width, 2),
        ],
        8,
        "in_reduce",
        52,
    )
    grad_in_norm, grad_gain_in = pull_in(grad_in_rows)
    grad_inputs = grad_resid + grad_in_norm
    gain_grads = jnp.concatenate(
        [grad_gain_in, grad_gain_attn, grad_gain_ssm, grad_gain_mid], axis=1
    )
    gains_own = farewell(gain_grads.T)
    wide = lambda part: jnp.pad(part, ((0, 0), (0, -part.shape[1] % 256)))
    out_stack = gather_stack(wide(mid_shard[:, :query_width]), 5)
    gains_own, last_shard, grad_inputs, out_stack = tie(
        (gains_own, last_shard, grad_inputs, out_stack)
    )
    inner_step = -(-inner_width // 128) * 128
    inner_cols = inner_full.shape[1]
    shared_all = gather_stack(
        wide(last_shard[:, inner_step : inner_step + qkv_width + inner_cols]), 9
    )
    inner_sum = jnp.sum(
        shared_all[:, :, qkv_width : qkv_width + inner_cols].astype(jnp.float32), axis=0
    ).reshape(inner_all // lax.axis_size("dp"), -1)
    mamba_at = query_width
    gate_at = query_width + inner_step
    def merge(stack, start, size):
        own = [stack[rank, :, start : start + size].astype(jnp.float32) for rank in range(4)]
        both = jnp.sum(
            stack[:, :, start + size : start + 2 * size].astype(jnp.float32), axis=0
        )
        return jnp.concatenate(own + [both], axis=1)

    return (
        result.T,
        grad_inputs.T,
        gains_own[0],
        merge(shared_all, 0, group_width),
        merge(shared_all, query_width, HEAD),
        merge(shared_all, query_width + 2 * HEAD, HEAD),
        merge(out_stack, 0, group_width).T,
        jnp.stack(
            [last_shard[:, :inner_width], mid_shard[:, gate_at : gate_at + inner_width]], axis=1
        ).astype(jnp.float32),
        inner_sum[:, 4:8].T,
        inner_sum[:, 3],
        inner_sum[:, 8 : 8 + RANK + 2 * STATE],
        inner_sum[:, 8 + RANK + 2 * STATE :].T,
        inner_sum[:, 0],
        inner_sum[:, 1],
        inner_sum[:, 2],
        mid_shard[:, mamba_at : mamba_at + inner_width].T.astype(jnp.float32),
        gains_own[1],
        gains_own[2],
        gains_own[3],
        ffn_shard[:, :ff_width].astype(jnp.float32),
        ffn_shard[:, ff_step : ff_step + ff_width].astype(jnp.float32),
        ffn_shard[:, 2 * ff_step : 2 * ff_step + ff_width].astype(jnp.float32).T,
    )


def solution(mesh):
    placed = (
        P(("dp", "tensor"), None),
        P(("dp", "tensor"), None),
        P("dp"),
        P(("dp", "tensor")),
        P("dp"),
        P("dp", None),
        P("dp", None),
        P("dp", None),
        P(None, "dp"),
        P("dp", None, "tensor"),
        P(None, "dp"),
        P("dp"),
        P("dp", None),
        P(None, "dp"),
        P("dp"),
        P("dp"),
        P("dp"),
        P("tensor", "dp"),
        P("dp"),
        P("dp"),
        P("dp"),
        P("dp", "tensor"),
        P("dp", "tensor"),
        P("tensor", "dp"),
    )
    return jax.shard_map(
        per_device,
        mesh=mesh,
        in_specs=placed,
        out_specs=(
            P(("dp", "tensor"), None),
            P(("dp", "tensor"), None),
            P("dp"),
            P("dp", None),
            P("dp", None),
            P("dp", None),
            P(None, "dp"),
            P("dp", None, "tensor"),
            P(None, "dp"),
            P("dp"),
            P("dp", None),
            P(None, "dp"),
            P("dp"),
            P("dp"),
            P("dp"),
            P("tensor", "dp"),
            P("dp"),
            P("dp"),
            P("dp"),
            P("dp", "tensor"),
            P("dp", "tensor"),
            P("tensor", "dp"),
        ),
        check_vma=False,
    )
```

```python
import functools

import jax
import jax.numpy as jnp
from jax import lax
from jax.experimental import pallas as pl
from jax.experimental.pallas import tpu as pltpu
from jax.sharding import PartitionSpec as P

HEADS = 25
KV = 5
HEAD = 64
STATE = 16
RANK = 100
CONV = 4
WINDOW = 1024
BLOCK = 512
STRETCH = 64
LEN = 2048


EPSILON = 1e-06
MASKED = -1e30
HIGHEST = lax.Precision.HIGHEST


def normalize_t(values, gain):
    return values * lax.rsqrt(jnp.mean(values * values, axis=0, keepdims=True) + EPSILON) * gain


def join_rows_t(resid, attn_sum, ssm_sum, gain_attn, gain_ssm):
    return resid + 0.5 * (normalize_t(attn_sum, gain_attn) + normalize_t(ssm_sum, gain_ssm))


def dot_plain(left, right):
    return jnp.dot(left, right, preferred_element_type=jnp.float32)


def dot_last(left, right):
    return lax.dot_general(
        left, right, (((1,), (1,)), ((), ())), preferred_element_type=jnp.float32
    )


def dot_first(left, right):
    return lax.dot_general(
        left, right, (((0,), (0,)), ((), ())), preferred_element_type=jnp.float32
    )


def pick_groups(weight, first_slot, second_slot, group_width, axis):
    return jnp.concatenate(
        [
            lax.dynamic_slice_in_dim(weight, first_slot * group_width, group_width, axis),
            lax.dynamic_slice_in_dim(weight, second_slot * group_width, group_width, axis),
        ],
        axis=axis,
    )


PIECES = 4
MESH = pl.DeviceIdType.MESH


def tensor_peers():
    me = lax.axis_index("tensor")
    side = me + 1 - 2 * lax.rem(me, 2)
    cross = lax.rem(me + 2, 4)
    return me, side, cross, lax.rem(side + 2, 4)


def greet(peers):
    barrier = pltpu.get_barrier_semaphore()
    for peer in peers:
        pl.semaphore_signal(barrier, inc=1, device_id={"tensor": peer}, device_id_type=MESH)
    pl.semaphore_wait(barrier, len(peers))


def push(src, dst, sems, index, peer):
    copy = pltpu.make_async_remote_copy(
        src_ref=src,
        dst_ref=dst,
        send_sem=sems[0].at[index],
        recv_sem=sems[1].at[index],
        device_id={"tensor": peer},
        device_id_type=MESH,
    )
    copy.start()
    return copy


def columns(block, size):
    return pl.ds(pl.multiple_of(block * size, size), size)


def gather_kernel(part_ref, whole_ref, own_sem, *sems):
    me, side, cross, diag = tensor_peers()
    depth, size = part_ref.shape
    step = depth // PIECES
    mine = columns(me, size)
    theirs = columns(cross, size)
    greet((side, cross))
    own = pltpu.make_async_copy(part_ref, whole_ref.at[:, mine], own_sem)
    own.start()
    over, near, relay = [], [], []
    for piece in range(PIECES):
        rows = pl.ds(piece * step, step)
        over.append(
            push(part_ref.at[rows], whole_ref.at[rows, mine], sems[0:2], piece, cross)
        )
    for piece in range(PIECES):
        rows = pl.ds(piece * step, step)
        near.append(push(part_ref.at[rows], whole_ref.at[rows, mine], sems[2:4], piece, side))
    for piece in range(PIECES):
        rows = pl.ds(piece * step, step)
        over[piece].wait_recv()
        relay.append(
            push(whole_ref.at[rows, theirs], whole_ref.at[rows, theirs], sems[4:6], piece, side)
        )
    own.wait()
    for piece in range(PIECES):
        over[piece].wait_send()
        near[piece].wait()
        relay[piece].wait()


def gather_rows(part, call_id):
    depth, size = part.shape
    return pl.pallas_call(
        gather_kernel,
        name="gather_rows",
        in_specs=[pl.BlockSpec(memory_space=pl.ANY)],
        out_specs=pl.BlockSpec(memory_space=pl.ANY),
        out_shape=jax.ShapeDtypeStruct((depth, 4 * size), part.dtype),
        scratch_shapes=[pltpu.SemaphoreType.DMA] + [pltpu.SemaphoreType.DMA((PIECES,))] * 6,
        compiler_params=pltpu.CompilerParams(
            collective_id=call_id, has_side_effects=True, vmem_limit_bytes=1 << 20
        ),
        cost_estimate=pl.CostEstimate(
            flops=0, bytes_accessed=depth * size * 2 * 90, transcendentals=0
        ),
    )(part)


def first_kernel(part_ref, shard_ref, whole_ref, all_ref, own_sem, *sems):
    me, side, cross, diag = tensor_peers()
    depth, size = part_ref.shape
    step = depth // PIECES
    mine, theirs = columns(me, size), columns(cross, size)
    place = lax.axis_index("dp")
    spot, lane = lax.div(place, 2), lax.rem(place, 2)
    length = all_ref.shape[0] // 2
    partner = 2 * spot + 1 - lane
    barrier = pltpu.get_barrier_semaphore()
    for peer in (side, cross):
        pl.semaphore_signal(barrier, inc=1, device_id={"tensor": peer}, device_id_type=MESH)
    pl.semaphore_signal(barrier, inc=1, device_id={"dp": partner}, device_id_type=MESH)
    has_left, has_right = spot > 0, spot < length - 1

    @pl.when(has_left)
    def _():
        pl.semaphore_signal(barrier, inc=1, device_id={"dp": place - 2}, device_id_type=MESH)

    @pl.when(has_right)
    def _():
        pl.semaphore_signal(barrier, inc=1, device_id={"dp": place + 2}, device_id_type=MESH)

    pl.semaphore_wait(barrier, 3 + has_left.astype(jnp.int32) + has_right.astype(jnp.int32))

    def line(origin, group, peer, source):
        slot = all_ref.at[2 * origin + lane]
        return pltpu.make_async_remote_copy(
            src_ref=slot if source is None else source,
            dst_ref=slot,
            send_sem=sems[6 + 2 * group].at[origin],
            recv_sem=sems[7 + 2 * group].at[origin],
            device_id={"dp": peer},
            device_id_type=MESH,
        )

    to_right = lambda origin, source=None: line(origin, 0, place + 2, source)
    to_left = lambda origin, source=None: line(origin, 1, place - 2, source)
    to_partner = lambda origin, source=None: line(origin, 2, partner, source)

    own = pltpu.make_async_copy(part_ref, whole_ref.at[:, mine], own_sem.at[0])
    own.start()
    kept = pltpu.make_async_copy(shard_ref, all_ref.at[place], own_sem.at[1])
    kept.start()
    pl.when(has_right)(to_right(spot, shard_ref).start)
    pl.when(has_left)(to_left(spot, shard_ref).start)
    to_partner(spot, shard_ref).start()
    over, near, relay = [], [], []
    for piece in range(PIECES):
        rows = pl.ds(piece * step, step)
        over.append(push(part_ref.at[rows], whole_ref.at[rows, mine], sems[0:2], piece, cross))
    for piece in range(PIECES):
        rows = pl.ds(piece * step, step)
        near.append(push(part_ref.at[rows], whole_ref.at[rows, mine], sems[2:4], piece, side))

    def pass_on(hop):
        left, right = spot - hop, spot + hop

        @pl.when(left >= 0)
        def _():
            to_right(left).wait_recv()
            pl.when(has_right)(to_right(left).start)
            to_partner(left).start()

        @pl.when(right < length)
        def _():
            to_left(right).wait_recv()
            pl.when(has_left)(to_left(right).start)
            to_partner(right).start()

    hops = list(range(1, length))
    for piece in range(PIECES):
        rows = pl.ds(piece * step, step)
        over[piece].wait_recv()
        relay.append(
            push(whole_ref.at[rows, theirs], whole_ref.at[rows, theirs], sems[4:6], piece, side)
        )
        if piece and hops:
            pass_on(hops.pop(0))
    for hop in hops:
        pass_on(hop)
    own.wait()
    kept.wait()
    for piece in range(PIECES):
        over[piece].wait_send()
        near[piece].wait()
        relay[piece].wait()
    for origin in range(length):
        pl.when(has_right & (origin <= spot))(to_right(origin).wait_send)
        pl.when(has_left & (origin >= spot))(to_left(origin).wait_send)
        to_partner(origin).wait_send()
        arrival = pltpu.make_async_remote_copy(
            src_ref=shard_ref,
            dst_ref=all_ref.at[2 * origin + 1 - lane],
            send_sem=sems[10].at[origin],
            recv_sem=sems[11].at[origin],
            device_id={"dp": partner},
            device_id_type=MESH,
        )
        arrival.wait_recv()


def gather_first(part, shard):
    depth, size = part.shape
    groups = lax.axis_size("dp")
    anywhere = pl.BlockSpec(memory_space=pl.ANY)
    whole, stacked = pl.pallas_call(
        first_kernel,
        name="gather_first",
        in_specs=[anywhere] * 2,
        out_specs=[anywhere] * 2,
        out_shape=[
            jax.ShapeDtypeStruct((depth, 4 * size), part.dtype),
            jax.ShapeDtypeStruct((groups,) + shard.shape, shard.dtype),
        ],
        scratch_shapes=[pltpu.SemaphoreType.DMA((2,))]
        + [pltpu.SemaphoreType.DMA((PIECES,))] * 6
        + [pltpu.SemaphoreType.DMA((groups // 2,))] * 6,
        compiler_params=pltpu.CompilerParams(
            collective_id=14, has_side_effects=True, vmem_limit_bytes=1 << 20
        ),
        cost_estimate=pl.CostEstimate(flops=0, bytes_accessed=270 << 20, transcendentals=0),
    )(part, shard)
    return whole, stacked.reshape(-1, shard.shape[1])


def turn_kernel(combine, plan, n_in, n_out, *refs):
    part_ref, weight_ref = refs[:2]
    ins = refs[2 : 2 + n_in]
    whole_ref = refs[2 + n_in]
    outs = refs[3 + n_in : 3 + n_in + n_out]
    scratch = refs[3 + n_in + n_out :]
    weight_bufs, scratch = scratch[: len(plan)], scratch[len(plan) :]
    in_bufs, out_bufs = scratch[:n_in], scratch[n_in : n_in + n_out]
    weight_sem, in_sem, out_sem, own_sem = scratch[n_in + n_out : n_in + n_out + 4]
    sems = scratch[n_in + n_out + 4 :]
    me, side, cross, diag = tensor_peers()
    depth, size = part_ref.shape
    half = size // 2
    tiles = [(block, at) for block in (me, side) for at in (0, 1)]
    tiles += [(block, at) for at in (0, 1) for block in (cross, diag)]
    place = lambda block, at: pl.ds(pl.multiple_of(block * size + at * half, half), half)
    local = lambda at: pl.ds(at * half, half)

    weight_loads = [
        pltpu.make_async_copy(
            weight_ref.at[:, pl.ds(low, buf.shape[1])], buf, weight_sem.at[index]
        )
        for index, ((low, _), buf) in enumerate(zip(plan, weight_bufs))
    ]
    own = pltpu.make_async_copy(part_ref, whole_ref.at[:, columns(me, size)], own_sem)
    own.start()
    for load in weight_loads:
        load.start()

    def in_load(index, tile):
        return pltpu.make_async_copy(
            ins[index].at[place(*tiles[tile])],
            in_bufs[index].at[tile % 2],
            in_sem.at[index, tile % 2],
        )

    def out_store(index, tile):
        return pltpu.make_async_copy(
            out_bufs[index].at[tile % 2],
            outs[index].at[place(*tiles[tile])],
            out_sem.at[index, tile % 2],
        )

    for index in range(n_in):
        in_load(index, 0).start()
    greet((side, cross))
    over = [
        push(part_ref.at[:, local(at)], whole_ref.at[:, place(me, at)], sems[0:2], at, cross)
        for at in (0, 1)
    ]
    near = [
        push(part_ref.at[:, local(at)], whole_ref.at[:, place(me, at)], sems[2:4], at, side)
        for at in (0, 1)
    ]
    relay = [None, None]
    own.wait()
    for tile, (block, at) in enumerate(tiles):
        if tile + 1 < len(tiles):
            for index in range(n_in):
                in_load(index, tile + 1).start()
        if tile in (2, 3):
            near[at].wait_recv()
        if tile in (4, 6):
            over[at].wait_recv()
            relay[at] = push(
                whole_ref.at[:, place(cross, at)],
                whole_ref.at[:, place(cross, at)],
                sems[4:6],
                at,
                side,
            )
        if tile in (5, 7):
            relay[at].wait_recv()
        left = whole_ref[:, place(block, at)]
        products = []
        for index, (low, high) in enumerate(plan):
            if tile == 0:
                weight_loads[index].wait()
            products.append(dot_first(left, weight_bufs[index][:, : high - low]))
        for index in range(n_in):
            in_load(index, tile).wait()
        results = combine(products, [buf[tile % 2] for buf in in_bufs])
        for index, result in enumerate(results):
            if tile >= 2:
                out_store(index, tile - 2).wait()
            out_bufs[index][tile % 2] = result
            out_store(index, tile).start()
    for tile in (len(tiles) - 2, len(tiles) - 1):
        for index in range(n_out):
            out_store(index, tile).wait()
    for at in (0, 1):
        over[at].wait_send()
        near[at].wait_send()
        relay[at].wait_send()


def turn_rows(part, weight, ins, outs, plan, combine, call_id, name, micros):
    depth, size = part.shape
    half = size // 2
    anywhere = pl.BlockSpec(memory_space=pl.ANY)
    return pl.pallas_call(
        functools.partial(turn_kernel, combine, plan, len(ins), len(outs)),
        name=name,
        in_specs=[pl.BlockSpec(memory_space=pltpu.VMEM)] + [anywhere] * (1 + len(ins)),
        out_specs=[pl.BlockSpec(memory_space=pltpu.VMEM)] + [anywhere] * len(outs),
        out_shape=[jax.ShapeDtypeStruct((depth, 4 * size), part.dtype)]
        + [jax.ShapeDtypeStruct((4 * size, cols), dtype) for cols, dtype in outs],
        scratch_shapes=[
            pltpu.VMEM((depth, -(-(high - low) // 128) * 128), weight.dtype) for low, high in plan
        ]
        + [pltpu.VMEM((2, half, value.shape[1]), value.dtype) for value in ins]
        + [pltpu.VMEM((2, half, cols), dtype) for cols, dtype in outs]
        + [
            pltpu.SemaphoreType.DMA((len(plan),)),
            pltpu.SemaphoreType.DMA((max(len(ins), 1), 2)),
            pltpu.SemaphoreType.DMA((len(outs), 2)),
            pltpu.SemaphoreType.DMA,
        ]
        + [pltpu.SemaphoreType.DMA((2,))] * 6,
        compiler_params=pltpu.CompilerParams(
            collective_id=call_id, has_side_effects=True, vmem_limit_bytes=52 << 20
        ),
        cost_estimate=pl.CostEstimate(
            flops=0, bytes_accessed=int(micros * 3.6) << 20, transcendentals=0
        ),
    )(part, weight, *ins)


def forward_gate(products, _):
    gate, up = products
    return gate, up, (gate * jax.nn.sigmoid(gate) * up).astype(jnp.bfloat16)


def backward_gate(products, saved):
    (grad,), (gate, up) = products, saved
    sig = jax.nn.sigmoid(gate)
    grad_gate = grad * up * sig * (1.0 + gate * (1.0 - sig))
    return grad_gate.astype(jnp.bfloat16), (grad * gate * sig).astype(jnp.bfloat16)


def total_kernel(part_ref, out_ref, near_buf, own_buf, stage_buf, far_buf, low_buf, own_sem, *sems):
    me, side, cross, diag = tensor_peers()
    size, wide = low_buf.shape
    half = size // 2
    greet((side, cross))
    rows_of = lambda block, at: pl.ds(pl.multiple_of(block * size + at, half), half)
    pieces = (0, half)
    first = [
        push(part_ref.at[rows_of(diag, at)], near_buf.at[pl.ds(at, half)], sems[0:2], i, side)
        for i, at in enumerate(pieces)
    ]
    second = [
        push(part_ref.at[rows_of(side, at)], own_buf.at[pl.ds(at, half)], sems[2:4], i, side)
        for i, at in enumerate(pieces)
    ]
    third, over, near, relay = [], [], [], []
    for i, at in enumerate(pieces):
        rows = pl.ds(at, half)
        first[i].wait_recv()
        stage_buf[rows] = (part_ref[rows_of(cross, at)] + near_buf[rows]).astype(jnp.bfloat16)
        third.append(push(stage_buf.at[rows], far_buf.at[rows], sems[4:6], i, cross))
    for i, at in enumerate(pieces):
        rows = pl.ds(at, half)
        second[i].wait_recv()
        third[i].wait_recv()
        low_buf[rows] = (
            part_ref[rows_of(me, at)] + own_buf[rows] + far_buf[rows].astype(jnp.float32)
        ).astype(jnp.bfloat16)
        over.append(push(low_buf.at[rows], out_ref.at[rows_of(me, at)], sems[6:8], i, cross))
        near.append(push(low_buf.at[rows], out_ref.at[rows_of(me, at)], sems[8:10], i, side))
    own = pltpu.make_async_copy(
        low_buf, out_ref.at[pl.ds(pl.multiple_of(me * size, size), size)], own_sem
    )
    own.start()
    for i, at in enumerate(pieces):
        over[i].wait_recv()
        relay.append(
            push(out_ref.at[rows_of(cross, at)], out_ref.at[rows_of(cross, at)], sems[10:12], i, side)
        )
    own.wait()
    for i in range(2):
        for group in (first, second, third, over):
            group[i].wait_send()
        near[i].wait()
        relay[i].wait()


def total_rows(part, call_id):
    tokens, wide = part.shape
    size = tokens // 4
    whole = pl.BlockSpec(memory_space=pltpu.VMEM)
    return pl.pallas_call(
        total_kernel,
        name="total_rows",
        in_specs=[whole],
        out_specs=whole,
        out_shape=jax.ShapeDtypeStruct((tokens, wide), jnp.bfloat16),
        scratch_shapes=[
            pltpu.VMEM((size, wide), jnp.float32),
            pltpu.VMEM((size, wide), jnp.float32),
            pltpu.VMEM((size, wide), jnp.bfloat16),
            pltpu.VMEM((size, wide), jnp.bfloat16),
            pltpu.VMEM((size, wide), jnp.bfloat16),
            pltpu.SemaphoreType.DMA,
        ]
        + [pltpu.SemaphoreType.DMA((2,))] * 12,
        compiler_params=pltpu.CompilerParams(
            collective_id=call_id, has_side_effects=True, vmem_limit_bytes=32 << 20
        ),
        cost_estimate=pl.CostEstimate(flops=0, bytes_accessed=60 << 20, transcendentals=0),
    )(part)


def hello_kernel(gain_ref, count_ref, gains_ref, counts_ref, sum_buf, local_buf, *sems):
    me = lax.axis_index("tensor")
    place = lax.axis_index("dp")
    ranks, groups = local_buf.shape[0], gains_ref.shape[0]
    barrier = pltpu.get_barrier_semaphore()
    others = [{"tensor": lax.rem(me + hop, ranks)} for hop in range(1, ranks)]
    far = [{"dp": lax.rem(place + hop, groups)} for hop in range(1, groups)]
    for peer in others + far:
        pl.semaphore_signal(barrier, inc=1, device_id=peer, device_id_type=MESH)
    pl.semaphore_wait(barrier, len(others) + len(far))

    def send(src, dst, index, peer):
        copy = pltpu.make_async_remote_copy(
            src_ref=src,
            dst_ref=dst,
            send_sem=sems[0].at[index],
            recv_sem=sems[1].at[index],
            device_id=peer,
            device_id_type=MESH,
        )
        copy.start()
        return copy

    first = [send(count_ref, local_buf.at[me], i, peer) for i, peer in enumerate(others)]
    local_buf[me] = count_ref[...]
    gains_ref[place] = gain_ref[...]
    base = len(first)
    second = [send(gain_ref, gains_ref.at[place], base + i, peer) for i, peer in enumerate(far)]
    base += len(second)
    for copy in first:
        copy.wait()
    sum_buf[...] = jnp.sum(local_buf[...], axis=0)
    counts_ref[place] = sum_buf[...]
    third = [send(sum_buf, counts_ref.at[place], base + i, peer) for i, peer in enumerate(far)]
    for copy in second + third:
        copy.wait()


def hello(gains, count):
    wide = -(-gains.shape[1] // 128) * 128
    block = jnp.zeros((8, wide), jnp.float32)
    block = lax.dynamic_update_slice(block, gains.astype(jnp.float32), (0, 0))
    counts = jnp.full((8, 128), count, jnp.float32)
    groups, ranks = lax.axis_size("dp"), lax.axis_size("tensor")
    copies = ranks - 1 + 2 * (groups - 1)
    whole = pl.BlockSpec(memory_space=pltpu.VMEM)
    gains_all, counts_all = pl.pallas_call(
        hello_kernel,
        name="hello",
        in_specs=[whole, whole],
        out_specs=[whole, whole],
        out_shape=[
            jax.ShapeDtypeStruct((groups, 8, wide), jnp.float32),
            jax.ShapeDtypeStruct((groups, 8, 128), jnp.float32),
        ],
        scratch_shapes=[
            pltpu.VMEM((8, 128), jnp.float32),
            pltpu.VMEM((ranks, 8, 128), jnp.float32),
        ]
        + [pltpu.SemaphoreType.DMA((copies,))] * 2,
        compiler_params=pltpu.CompilerParams(collective_id=0, has_side_effects=True),
        cost_estimate=pl.CostEstimate(flops=0, bytes_accessed=30 << 20, transcendentals=0),
    )(block, counts)
    gains_full = gains_all[:, :4, : gains.shape[1]].transpose(1, 0, 2).reshape(4, -1)
    return gains_full, jnp.sum(counts_all[:, 0, 0])


TILE = 400


def weights_kernel(plan, *refs):
    out_ref = refs[-1]
    index = 0
    for mode, offset, size, pad in plan:
        left = refs[index][...]
        if mode == "copy":
            product = left
            index += 1
        else:
            right = refs[index + 1][...]
            product = dot_last(left, right) if mode == "flip" else dot_plain(left, right)
            index += 2
        out_ref[:, offset : offset + size] = product.astype(jnp.bfloat16)
        if pad:
            out_ref[:, offset + size : offset + size + pad] = jnp.zeros(
                (out_ref.shape[0], pad), jnp.bfloat16
            )


def weight_grads(pairs, name, micros, tight=False):
    rows = pairs[0][0].shape[0]
    tile = TILE if rows % TILE == 0 else rows
    plan, specs, operands, offset = [], [], [], 0
    for left, right, flip in pairs:
        source = left if right is None else right
        size = source.shape[0] if flip else source.shape[1]
        pad = 0 if tight else -size % 128
        mode = "copy" if right is None else "flip" if flip else "plain"
        plan.append((mode, offset, size, pad))
        offset += size + pad
        specs.append(pl.BlockSpec((tile, left.shape[1]), lambda i: (i, 0)))
        operands.append(left)
        if right is not None:
            specs.append(
                pl.BlockSpec(right.shape, lambda i: (0, 0), pipeline_mode=pl.Buffered(1))
            )
            operands.append(right)
    return pl.pallas_call(
        functools.partial(weights_kernel, plan),
        name=name,
        grid=(rows // tile,),
        in_specs=specs,
        out_specs=pl.BlockSpec((tile, offset), lambda i: (i, 0)),
        out_shape=jax.ShapeDtypeStruct((rows, offset), jnp.bfloat16),
        compiler_params=pltpu.CompilerParams(vmem_limit_bytes=52 << 20),
        cost_estimate=pl.CostEstimate(
            flops=0, bytes_accessed=int(micros * 3.6) << 20, transcendentals=0
        ),
    )(*operands)


def farewell_kernel(part_ref, out_ref, group_buf, sum_buf, rank_buf, *sems):
    me = lax.axis_index("tensor")
    place = lax.axis_index("dp")
    ranks, groups = rank_buf.shape[0], group_buf.shape[0]
    barrier = pltpu.get_barrier_semaphore()
    others = [lax.rem(me + hop, ranks) for hop in range(1, ranks)]
    far = [lax.rem(place + hop, groups) for hop in range(1, groups)]
    for peer in others:
        pl.semaphore_signal(barrier, inc=1, device_id={"tensor": peer}, device_id_type=MESH)
    for peer in far:
        pl.semaphore_signal(barrier, inc=1, device_id={"dp": peer}, device_id_type=MESH)
    pl.semaphore_wait(barrier, len(others) + len(far))

    def send(src, dst, index, peer):
        copy = pltpu.make_async_remote_copy(
            src_ref=src,
            dst_ref=dst,
            send_sem=sems[0].at[index],
            recv_sem=sems[1].at[index],
            device_id=peer,
            device_id_type=MESH,
        )
        copy.start()
        return copy

    first = [
        send(part_ref.at[peer], group_buf.at[place], i, {"dp": peer}) for i, peer in enumerate(far)
    ]
    group_buf[place] = part_ref[place]
    for copy in first:
        copy.wait()
    sum_buf[...] = jnp.sum(group_buf[...], axis=0)
    rank_buf[me] = sum_buf[...]
    second = [
        send(sum_buf, rank_buf.at[me], len(first) + i, {"tensor": peer})
        for i, peer in enumerate(others)
    ]
    for copy in second:
        copy.wait()
    out_ref[...] = jnp.sum(rank_buf[...], axis=0)


def farewell(grads):
    groups, ranks = lax.axis_size("dp"), lax.axis_size("tensor")
    kinds, total = grads.shape
    own = total // groups
    wide = -(-own // 128) * 128
    parts = jnp.pad(
        grads.reshape(kinds, groups, own).transpose(1, 0, 2),
        ((0, 0), (0, 8 - kinds), (0, wide - own)),
    )
    whole = pl.BlockSpec(memory_space=pltpu.VMEM)
    summed = pl.pallas_call(
        farewell_kernel,
        name="farewell",
        in_specs=[whole],
        out_specs=whole,
        out_shape=jax.ShapeDtypeStruct((8, wide), jnp.float32),
        scratch_shapes=[
            pltpu.VMEM((groups, 8, wide), jnp.float32),
            pltpu.VMEM((8, wide), jnp.float32),
            pltpu.VMEM((ranks, 8, wide), jnp.float32),
        ]
        + [pltpu.SemaphoreType.DMA((groups + ranks - 2,))] * 2,
        compiler_params=pltpu.CompilerParams(
            collective_id=4, has_side_effects=True, vmem_limit_bytes=4 << 20
        ),
        cost_estimate=pl.CostEstimate(flops=0, bytes_accessed=40 << 20, transcendentals=0),
    )(parts)
    return summed[:kinds, :own]


def stack_kernel(part_ref, whole_ref, own_sem, *sems):
    me, side, cross, diag = tensor_peers()
    step = part_ref.shape[1] // 2
    greet((side, cross))
    own = pltpu.make_async_copy(part_ref, whole_ref.at[me], own_sem)
    own.start()
    cols = [pl.ds(0, step), pl.ds(step, step)]
    over = [
        push(part_ref.at[:, at], whole_ref.at[me, :, at], sems[0:2], i, cross)
        for i, at in enumerate(cols)
    ]
    near = [
        push(part_ref.at[:, at], whole_ref.at[me, :, at], sems[2:4], i, side)
        for i, at in enumerate(cols)
    ]
    relay = []
    for i, at in enumerate(cols):
        over[i].wait_recv()
        relay.append(
            push(whole_ref.at[cross, :, at], whole_ref.at[cross, :, at], sems[4:6], i, side)
        )
    own.wait()
    for i in range(2):
        over[i].wait_send()
        near[i].wait()
        relay[i].wait()


def gather_stack(part, call_id):
    return pl.pallas_call(
        stack_kernel,
        name="gather_stack",
        in_specs=[pl.BlockSpec(memory_space=pl.ANY)],
        out_specs=pl.BlockSpec(memory_space=pl.ANY),
        out_shape=jax.ShapeDtypeStruct((4,) + part.shape, part.dtype),
        scratch_shapes=[pltpu.SemaphoreType.DMA] + [pltpu.SemaphoreType.DMA((2,))] * 6,
        compiler_params=pltpu.CompilerParams(
            collective_id=call_id, has_side_effects=True, vmem_limit_bytes=1 << 20
        ),
        cost_estimate=pl.CostEstimate(flops=0, bytes_accessed=60 << 20, transcendentals=0),
    )(part)


def product_kernel(plan, leads, right_flips, *refs):
    left_count = len(leads)
    lefts = [ref if lead is None else ref.at[lead] for ref, (lead, _) in zip(refs, leads)]
    right_count = len(right_flips)
    rights = refs[left_count : left_count + right_count]
    out_ref = refs[left_count + right_count]
    scratch = refs[left_count + right_count + 1 :]
    left_bufs = scratch[:left_count]
    right_bufs = scratch[left_count : left_count + right_count]
    diag_buf, side_buf, near_buf, own_buf, stage_buf, far_buf, left_sem, right_sem = scratch[
        left_count + right_count : left_count + right_count + 8
    ]
    sems = scratch[left_count + right_count + 8 :]
    me, side, cross, diag = tensor_peers()
    depth, size = out_ref.shape
    step = depth // PIECES
    rows_of = lambda piece: pl.ds(pl.multiple_of(piece * step, 16), step)

    def left_load(index, piece):
        rows = rows_of(piece)
        start = leads[index][1]
        source = lefts[index].at[rows]
        if start is not None:
            source = lefts[index].at[rows, pl.ds(start, left_bufs[index].shape[1])]
        return pltpu.make_async_copy(source, left_bufs[index].at[rows], left_sem.at[index, piece])

    def right_load(index, order, block):
        at = columns(block, size)
        view = (slice(None), at) if right_flips[index] else (at,)
        return pltpu.make_async_copy(
            rights[index].at[view], right_bufs[index].at[view], right_sem.at[index, order]
        )

    turns = (diag, cross, side, me)
    for order, block in enumerate(turns):
        for index in range(right_count):
            right_load(index, order, block).start()
        for index in range(left_count):
            left_load(index, order).start()
    greet((side, cross))

    def product(piece, block):
        rows, at = rows_of(piece), columns(block, size)
        total = jnp.zeros((step, size), jnp.float32)
        for left, low_col, high_col, right in plan:
            weight = left_bufs[left][rows, low_col:high_col]
            if right_flips[right]:
                total += dot_plain(weight, right_bufs[right][:, at])
            else:
                total += dot_last(weight, right_bufs[right][at, :])
        return total

    def transfer(src, dst, group, piece, peer):
        rows = rows_of(piece)
        return pltpu.make_async_remote_copy(
            src_ref=src.at[rows],
            dst_ref=dst.at[rows],
            send_sem=sems[2 * group].at[piece],
            recv_sem=sems[2 * group + 1].at[piece],
            device_id={"tensor": peer},
            device_id_type=MESH,
        )

    first = lambda piece: transfer(diag_buf, near_buf, 0, piece, side)
    second = lambda piece: transfer(side_buf, own_buf, 1, piece, side)
    third = lambda piece: transfer(stage_buf, far_buf, 2, piece, cross)

    for order in (0, 1):
        for index in range(right_count):
            right_load(index, order, turns[order]).wait()

    def outward(piece, carry):
        rows = rows_of(piece)
        for index in range(left_count):
            left_load(index, piece).wait()
        diag_buf[rows] = product(piece, diag).astype(jnp.bfloat16)
        first(piece).start()
        kept = product(piece, cross)
        first(piece).wait_recv()
        stage_buf[rows] = (kept + near_buf[rows].astype(jnp.float32)).astype(jnp.bfloat16)
        third(piece).start()
        return carry

    lax.fori_loop(0, PIECES, outward, 0)
    for order in (2, 3):
        for index in range(right_count):
            right_load(index, order, turns[order]).wait()

    def inward(piece, carry):
        rows = rows_of(piece)
        side_buf[rows] = product(piece, side).astype(jnp.bfloat16)
        second(piece).start()
        out_ref[rows] = product(piece, me)
        return carry

    lax.fori_loop(0, PIECES, inward, 0)

    def finish(piece, carry):
        rows = rows_of(piece)
        second(piece).wait_recv()
        third(piece).wait_recv()
        out_ref[rows] += own_buf[rows].astype(jnp.float32) + far_buf[rows].astype(jnp.float32)
        first(piece).wait_send()
        second(piece).wait_send()
        third(piece).wait_send()
        return carry

    lax.fori_loop(0, PIECES, finish, 0)


def product_reduce(lefts, rights, plan, call_id, name, micros):
    leads = tuple((lead, start) for _, lead, start, _ in lefts)
    widths = [size for _, _, _, size in lefts]
    lefts = [left for left, _, _, _ in lefts]
    depth = lefts[0].shape[-2]
    right_flips = tuple(flip for _, flip in rights)
    tokens = rights[0][0].shape[1] if right_flips[0] else rights[0][0].shape[0]
    size = tokens // 4
    anywhere = pl.BlockSpec(memory_space=pl.ANY)
    return pl.pallas_call(
        functools.partial(product_kernel, plan, leads, right_flips),
        name=name,
        in_specs=[anywhere] * (len(lefts) + len(rights)),
        out_specs=pl.BlockSpec(memory_space=pltpu.VMEM),
        out_shape=jax.ShapeDtypeStruct((depth, size), jnp.float32),
        scratch_shapes=[pltpu.VMEM((depth, size), jnp.bfloat16) for size in widths]
        + [pltpu.VMEM(right.shape, right.dtype) for right, _ in rights]
        + [pltpu.VMEM((depth, size), jnp.bfloat16)] * 6
        + [
            pltpu.SemaphoreType.DMA((len(lefts), PIECES)),
            pltpu.SemaphoreType.DMA((len(rights), 4)),
        ]
        + [pltpu.SemaphoreType.DMA((PIECES,))] * 6,
        compiler_params=pltpu.CompilerParams(
            collective_id=call_id, has_side_effects=True, vmem_limit_bytes=48 << 20
        ),
        cost_estimate=pl.CostEstimate(
            flops=0, bytes_accessed=int(micros * 3.6) << 20, transcendentals=0
        ),
    )(*lefts, *[right for right, _ in rights])


def spread_kernel(part_ref, out_ref, own_sem, *sems):
    rank, place = lax.axis_index("tensor"), lax.axis_index("dp")
    share = out_ref.shape[0]
    target, slot = lax.div(place, share), lax.rem(place, share)
    replica = lax.rem(place, 4)
    barrier = pltpu.get_barrier_semaphore()
    for index in range(share):
        source = rank * share + index

        @pl.when((source != place) | (replica != rank))
        def _():
            pl.semaphore_signal(
                barrier,
                inc=1,
                device_id={"dp": source, "tensor": replica},
                device_id_type=MESH,
            )

    goals = [(rank + 4 * index != place) | (target != rank) for index in range(share)]
    pl.semaphore_wait(barrier, sum(goal.astype(jnp.int32) for goal in goals))

    def outgoing(index):
        goal = rank + 4 * index
        copy = pltpu.make_async_remote_copy(
            src_ref=part_ref,
            dst_ref=out_ref.at[slot],
            send_sem=sems[0].at[index],
            recv_sem=sems[1].at[slot],
            device_id={"dp": goal, "tensor": target},
            device_id_type=MESH,
        )
        return copy, (goal != place) | (target != rank)

    own = pltpu.make_async_copy(part_ref, out_ref.at[slot], own_sem)
    for index in range(share):
        copy, away = outgoing(index)
        pl.when(away)(copy.start)
        pl.when(jnp.logical_not(away))(own.start)
    for index in range(share):
        copy, away = outgoing(index)
        pl.when(away)(copy.wait_send)
        pl.when(jnp.logical_not(away))(own.wait)
        source = rank * share + index
        arrival = pltpu.make_async_remote_copy(
            src_ref=part_ref,
            dst_ref=out_ref.at[index],
            send_sem=sems[0].at[index],
            recv_sem=sems[1].at[index],
            device_id={"dp": source, "tensor": replica},
            device_id_type=MESH,
        )
        pl.when((source != place) | (replica != rank))(arrival.wait_recv)


def inner_spread(part):
    groups, ranks = lax.axis_size("dp"), lax.axis_size("tensor")
    share = groups // ranks
    rows, cols = part.shape
    padded = jnp.pad(part, ((0, -rows % 16), (0, -cols % 128)))
    whole = pl.BlockSpec(memory_space=pltpu.VMEM)
    spread = pl.pallas_call(
        spread_kernel,
        name="inner_spread",
        in_specs=[whole],
        out_specs=whole,
        out_shape=jax.ShapeDtypeStruct((share,) + padded.shape, part.dtype),
        scratch_shapes=[pltpu.SemaphoreType.DMA] + [pltpu.SemaphoreType.DMA((share,))] * 2,
        compiler_params=pltpu.CompilerParams(
            collective_id=12, has_side_effects=True, vmem_limit_bytes=8 << 20
        ),
        cost_estimate=pl.CostEstimate(flops=0, bytes_accessed=40 << 20, transcendentals=0),
    )(padded)
    return spread[:, :rows, :cols].reshape(share * rows, cols)


def final_kernel(part_ref, inner_ref, whole_ref, owned_ref, own_sem, *sems):
    me, side, cross, diag = tensor_peers()
    place = lax.axis_index("dp")
    ranks = owned_ref.shape[0]
    share = lax.axis_size("dp") // ranks
    owner, slot = me * share + lax.div(place, ranks), lax.rem(place, ranks)
    source_rank, source_base = lax.div(place, share), ranks * lax.rem(place, share)
    barrier = pltpu.get_barrier_semaphore()
    for peer in (side, cross):
        pl.semaphore_signal(barrier, inc=1, device_id={"tensor": peer}, device_id_type=MESH)
    for index in range(ranks):
        source = source_base + index

        @pl.when((source != place) | (source_rank != me))
        def _():
            pl.semaphore_signal(
                barrier,
                inc=1,
                device_id={"dp": source, "tensor": source_rank},
                device_id_type=MESH,
            )

    goals = [(owner != place) | (me != index) for index in range(ranks)]
    pl.semaphore_wait(barrier, 2 + sum(goal.astype(jnp.int32) for goal in goals))

    step = part_ref.shape[1] // 2
    own = pltpu.make_async_copy(part_ref, whole_ref.at[me], own_sem.at[0])
    own.start()
    cols = [pl.ds(0, step), pl.ds(step, step)]
    over = [
        push(part_ref.at[:, at], whole_ref.at[me, :, at], sems[0:2], i, cross)
        for i, at in enumerate(cols)
    ]
    near = [
        push(part_ref.at[:, at], whole_ref.at[me, :, at], sems[2:4], i, side)
        for i, at in enumerate(cols)
    ]
    kept = pltpu.make_async_copy(inner_ref, owned_ref.at[slot], own_sem.at[1])

    def outgoing(index):
        copy = pltpu.make_async_remote_copy(
            src_ref=inner_ref,
            dst_ref=owned_ref.at[slot],
            send_sem=sems[6].at[index],
            recv_sem=sems[7].at[slot],
            device_id={"dp": owner, "tensor": index},
            device_id_type=MESH,
        )
        return copy, (owner != place) | (me != index)

    for index in range(ranks):
        copy, away = outgoing(index)
        pl.when(away)(copy.start)
        pl.when(jnp.logical_not(away))(kept.start)
    relay = []
    for i, at in enumerate(cols):
        over[i].wait_recv()
        relay.append(
            push(whole_ref.at[cross, :, at], whole_ref.at[cross, :, at], sems[4:6], i, side)
        )
    own.wait()
    for i in range(2):
        over[i].wait_send()
        near[i].wait()
        relay[i].wait()
    for index in range(ranks):
        copy, away = outgoing(index)
        pl.when(away)(copy.wait_send)
        pl.when(jnp.logical_not(away))(kept.wait)
        source = source_base + index
        arrival = pltpu.make_async_remote_copy(
            src_ref=inner_ref,
            dst_ref=owned_ref.at[index],
            send_sem=sems[6].at[index],
            recv_sem=sems[7].at[index],
            device_id={"dp": source, "tensor": source_rank},
            device_id_type=MESH,
        )
        pl.when((source != place) | (source_rank != me))(arrival.wait_recv)


def gather_final(part, inner):
    anywhere = pl.BlockSpec(memory_space=pl.ANY)
    return pl.pallas_call(
        final_kernel,
        name="gather_final",
        in_specs=[anywhere] * 2,
        out_specs=[anywhere] * 2,
        out_shape=[
            jax.ShapeDtypeStruct((4,) + part.shape, part.dtype),
            jax.ShapeDtypeStruct((4,) + inner.shape, inner.dtype),
        ],
        scratch_shapes=[pltpu.SemaphoreType.DMA((2,))]
        + [pltpu.SemaphoreType.DMA((2,))] * 6
        + [pltpu.SemaphoreType.DMA((4,))] * 2,
        compiler_params=pltpu.CompilerParams(
            collective_id=9, has_side_effects=True, vmem_limit_bytes=1 << 20
        ),
        cost_estimate=pl.CostEstimate(flops=0, bytes_accessed=60 << 20, transcendentals=0),
    )(part, inner)


BQ = 256
BK = 256


def attn_bias(q_base, k_base, segq_row, segk_col):
    q_pos = q_base + lax.broadcasted_iota(jnp.int32, (BK, BQ), 1)
    k_pos = k_base + lax.broadcasted_iota(jnp.int32, (BK, BQ), 0)
    offset = q_pos - k_pos
    allowed = (offset >= 0) & (offset < WINDOW) & (segk_col == segq_row)
    return jnp.where(allowed, 0.0, MASKED)


def flip_rows(cols_ref, rows_scr):
    for at in range(0, rows_scr.shape[0], BK):
        block = cols_ref[:, at : at + BK].astype(jnp.float32)
        rows_scr[at : at + BK] = jnp.transpose(block).astype(jnp.bfloat16)


def attn_fwd_kernel(first_ref, qt_ref, kt_ref, vt_ref, segr_ref, mask_ref, ot_ref, lse_ref,
                    max_scr, sum_scr, acc_scr, k_scr):
    heads = qt_ref.shape[0] // HEAD
    block = pl.program_id(1)
    q_base = block * BQ

    @pl.when(block == 0)
    def _():
        flip_rows(kt_ref, k_scr)

    max_scr[...] = jnp.full_like(max_scr, MASKED)
    sum_scr[...] = jnp.zeros_like(sum_scr)
    acc_scr[...] = jnp.zeros_like(acc_scr)
    segq_row = segr_ref[0:1, :]

    def body(j, carry):
        k_base = pl.multiple_of(j * BK, BK)
        rows = pl.ds(k_base, BK)
        bias = attn_bias(q_base, k_base, segq_row, mask_ref[rows, 4:5])
        k_blk = k_scr[rows, :]
        v_blk = vt_ref[:, rows]
        for head in range(heads):
            cols = slice(head * HEAD, (head + 1) * HEAD)
            scores = dot_plain(k_blk, qt_ref[cols, :]) * 0.125 + bias
            old_max = max_scr[head : head + 1]
            new_max = jnp.maximum(old_max, jnp.max(scores, axis=0, keepdims=True))
            expo = jnp.exp(scores - new_max)
            ratio = jnp.exp(old_max - new_max)
            max_scr[head : head + 1] = new_max
            sum_scr[head : head + 1] = sum_scr[head : head + 1] * ratio + jnp.sum(
                expo, axis=0, keepdims=True
            )
            acc_scr[cols] = acc_scr[cols] * ratio + dot_plain(v_blk, expo.astype(jnp.bfloat16))
        return carry

    start = first_ref[pl.program_id(0) * pl.num_programs(1) + block]
    lax.fori_loop(start, block + 1, body, 0)
    for head in range(heads):
        cols = slice(head * HEAD, (head + 1) * HEAD)
        total = jnp.maximum(sum_scr[head : head + 1], 1e-30)
        ot_ref[cols] = (acc_scr[cols] / total).astype(jnp.bfloat16)
        lse_ref[0, head : head + 1] = max_scr[head : head + 1] + jnp.log(total)


def attn_specs(slots, group, tokens):
    queries = pl.BlockSpec((group, BQ), lambda s, i, f: (s, i))
    base = slots * group // HEAD
    keys = pl.BlockSpec((HEAD, tokens), lambda s, i, f: (base + s, 0))
    values = pl.BlockSpec((HEAD, tokens), lambda s, i, f: (base + slots + s, 0))
    stats = pl.BlockSpec((1, 8, BQ), lambda s, i, f: (s, 0, i))
    seg_row = pl.BlockSpec((1, BQ), lambda s, i, f: (0, i))
    seg_col = pl.BlockSpec((tokens, 8), lambda s, i, f: (0, 0))
    return queries, keys, values, stats, seg_row, seg_col


def attn_forward(first, qkv_t, seg_row, masks, slots):
    tokens = qkv_t.shape[1]
    group = qkv_t.shape[0] // slots - 2 * HEAD
    queries, keys, values, stats, segr, segc = attn_specs(slots, group, tokens)
    return pl.pallas_call(
        attn_fwd_kernel,
        name="attn_fwd",
        grid_spec=pltpu.PrefetchScalarGridSpec(
            num_scalar_prefetch=1,
            grid=(slots, tokens // BQ),
            in_specs=[queries, keys, values, segr, segc],
            out_specs=[queries, stats],
            scratch_shapes=[
                pltpu.VMEM((8, BQ), jnp.float32),
                pltpu.VMEM((8, BQ), jnp.float32),
                pltpu.VMEM((group, BQ), jnp.float32),
                pltpu.VMEM((tokens, HEAD), jnp.bfloat16),
            ],
        ),
        out_shape=[
            jax.ShapeDtypeStruct((slots * group, tokens), jnp.bfloat16),
            jax.ShapeDtypeStruct((slots, 8, tokens), jnp.float32),
        ],
        compiler_params=pltpu.CompilerParams(vmem_limit_bytes=32 << 20),
        cost_estimate=pl.CostEstimate(flops=0, bytes_accessed=150 << 20, transcendentals=0),
    )(first, qkv_t, qkv_t, qkv_t, seg_row, masks)


def attn_bwd_kernel(first_ref, qt_ref, dot_ref, ot_ref, lse_ref, kt_ref, vt_ref, segr_ref, mask_ref,
                    grad_ref, delta_scr, acc_scr, q_scr, do_scr, k_scr, v_scr, gk_scr, gv_scr):
    group = qt_ref.shape[0]
    heads = group // HEAD
    slot = pl.program_id(0)
    slots = pl.num_programs(0)
    block = pl.program_id(1)
    q_base = pl.multiple_of(block * BQ, BQ)

    @pl.when(block == 0)
    def _():
        flip_rows(kt_ref, k_scr)
        flip_rows(vt_ref, v_scr)
        gk_scr[...] = jnp.zeros_like(gk_scr)
        gv_scr[...] = jnp.zeros_like(gv_scr)

    acc_scr[...] = jnp.zeros_like(acc_scr)
    start = first_ref[slot * pl.num_programs(1) + block]

    @pl.when(start <= block)
    def _():
        for head in range(heads):
            cols = slice(head * HEAD, (head + 1) * HEAD)
            grad_out = dot_ref[cols].astype(jnp.float32)
            delta_scr[head : head + 1] = jnp.sum(
                grad_out * ot_ref[cols].astype(jnp.float32), axis=0, keepdims=True
            )
            q_scr[head] = jnp.transpose(qt_ref[cols].astype(jnp.float32)).astype(jnp.bfloat16)
            do_scr[head] = jnp.transpose(grad_out).astype(jnp.bfloat16)

    segq_row = segr_ref[0:1, :]

    def body(j, carry):
        k_base = pl.multiple_of(j * BK, BK)
        rows = pl.ds(k_base, BK)
        bias = attn_bias(q_base, k_base, segq_row, mask_ref[rows, 4:5])
        k_blk = k_scr[rows, :]
        kt_blk = kt_ref[:, rows]
        v_blk = v_scr[rows, :]
        gk = jnp.zeros((BK, HEAD), jnp.float32)
        gv = jnp.zeros((BK, HEAD), jnp.float32)
        for head in range(heads):
            cols = slice(head * HEAD, (head + 1) * HEAD)
            scores = dot_plain(k_blk, qt_ref[cols, :]) * 0.125 + bias
            probs = jnp.exp(scores - lse_ref[0, head : head + 1])
            grad_p = dot_plain(v_blk, dot_ref[cols, :])
            grad_s = (probs * (grad_p - delta_scr[head : head + 1])).astype(jnp.bfloat16)
            gv += dot_plain(probs.astype(jnp.bfloat16), do_scr[head])
            gk += dot_plain(grad_s, q_scr[head])
            acc_scr[cols] += dot_plain(kt_blk, grad_s)
        gk_scr[rows, :] += gk * 0.125
        gv_scr[rows, :] += gv
        return carry

    lax.fori_loop(start, block + 1, body, 0)
    grad_ref[pl.ds(pl.multiple_of(slot * group, HEAD), group), pl.ds(q_base, BQ)] = (
        acc_scr[...] * 0.125
    ).astype(jnp.bfloat16)

    @pl.when(block == pl.num_programs(1) - 1)
    def _():
        key_rows = pl.ds(pl.multiple_of(slots * group + slot * HEAD, HEAD), HEAD)
        value_rows = pl.ds(pl.multiple_of(slots * group + (slots + slot) * HEAD, HEAD), HEAD)
        for at in range(0, gk_scr.shape[0], BK):
            cols = pl.ds(at, BK)
            grad_ref[key_rows, cols] = jnp.transpose(gk_scr[at : at + BK]).astype(jnp.bfloat16)
            grad_ref[value_rows, cols] = jnp.transpose(gv_scr[at : at + BK]).astype(jnp.bfloat16)


def attn_backward(first, qkv_t, do_t, o_t, lse, seg_row, masks, slots):
    width, tokens = qkv_t.shape
    group = width // slots - 2 * HEAD
    queries, keys, values, stats, segr, segc = attn_specs(slots, group, tokens)
    return pl.pallas_call(
        attn_bwd_kernel,
        name="attn_bwd",
        grid_spec=pltpu.PrefetchScalarGridSpec(
            num_scalar_prefetch=1,
            grid=(slots, tokens // BQ),
            in_specs=[queries, queries, queries, stats, keys, values, segr, segc],
            out_specs=pl.BlockSpec((width, tokens), lambda s, i, f: (0, 0)),
            scratch_shapes=[
                pltpu.VMEM((8, BQ), jnp.float32),
                pltpu.VMEM((group, BQ), jnp.float32),
                pltpu.VMEM((group // HEAD, BQ, HEAD), jnp.bfloat16),
                pltpu.VMEM((group // HEAD, BQ, HEAD), jnp.bfloat16),
                pltpu.VMEM((tokens, HEAD), jnp.bfloat16),
                pltpu.VMEM((tokens, HEAD), jnp.bfloat16),
                pltpu.VMEM((tokens, HEAD), jnp.float32),
                pltpu.VMEM((tokens, HEAD), jnp.float32),
            ],
        ),
        out_shape=jax.ShapeDtypeStruct((width, tokens), jnp.bfloat16),
        compiler_params=pltpu.CompilerParams(vmem_limit_bytes=40 << 20),
        cost_estimate=pl.CostEstimate(flops=0, bytes_accessed=160 << 20, transcendentals=0),
    )(first, qkv_t, do_t, o_t, lse, qkv_t, qkv_t, seg_row, masks)


def first_blocks(segs_flat):
    tokens = segs_flat.shape[0]
    starts = segs_flat[::BQ]
    positions = jnp.arange(tokens // BQ, dtype=jnp.int32) * BQ
    seg_start = jnp.sum((segs_flat[None, :] < starts[:, None]).astype(jnp.int32), axis=1)
    return jnp.maximum(jnp.maximum(seg_start, positions - WINDOW + 1), 0) // BK


def conv_rows(x_in, conv_w, conv_b, segs_grid):
    seq_count, seq_len = segs_grid.shape
    width = x_in.shape[1]
    grid = x_in.reshape(seq_count, seq_len, width)
    pad_x = jnp.concatenate([jnp.zeros((seq_count, CONV - 1, width), jnp.float32), grid], axis=1)
    pad_seg = jnp.concatenate([jnp.full((seq_count, CONV - 1), -1, jnp.int32), segs_grid], axis=1)
    total = jnp.zeros((seq_count, seq_len, width), jnp.float32) + conv_b
    for tap in range(CONV):
        same = (pad_seg[:, tap : tap + seq_len] == segs_grid).astype(jnp.float32)
        total = total + conv_w[tap] * pad_x[:, tap : tap + seq_len] * same[:, :, None]
    return jax.nn.silu(total).reshape(seq_count * seq_len, width)


CHUNK = 64
ROWS = 256
RANGE = 120.0
LANES = 256


def spans(width, size):
    return [(at, min(at + size, width)) for at in range(0, width, size)]


def softplus_parts(pre):
    small = jnp.exp(-jnp.abs(pre))
    step = jnp.maximum(pre, 0.0) + jnp.log1p(small)
    slope = jnp.where(pre >= 0.0, 1.0, small) / (1.0 + small)
    return step, slope


def split_sum(tri, values):
    high = values.astype(jnp.bfloat16)
    low = (values - high.astype(jnp.float32)).astype(jnp.bfloat16)
    return dot_plain(tri, high) + dot_plain(tri, low)


def tri_matrix(size, upper):
    row = lax.broadcasted_iota(jnp.int32, (size, size), 0)
    col = lax.broadcasted_iota(jnp.int32, (size, size), 1)
    order = (col >= row) if upper else (row >= col)
    return order & (lax.div(row, CHUNK) == lax.div(col, CHUNK))


def scan_setup(dbl_ref, dtw_ref, vec_ref, step_scr, cum_scr, slope_scr):
    width = dtw_ref.shape[1]
    tri = tri_matrix(ROWS, False).astype(jnp.bfloat16)
    dt_low = dbl_ref[:, :RANK]
    lowest = jnp.zeros((), jnp.float32)
    for lo, hi in spans(width, LANES):
        pre = dot_plain(dt_low, dtw_ref[:, lo:hi]) + vec_ref[0:1, lo:hi]
        step, slope = softplus_parts(pre)
        cum = split_sum(tri, -step * jnp.exp(vec_ref[1:2, lo:hi]))
        step_scr[:, lo:hi] = step
        cum_scr[:, lo:hi] = cum
        if slope_scr is not None:
            slope_scr[:, lo:hi] = slope
        least = jnp.zeros((1, hi - lo), jnp.float32)
        for at in range(0, ROWS, CHUNK):
            least = jnp.minimum(least, cum[at + CHUNK - 1 : at + CHUNK])
        lowest = jnp.minimum(lowest, jnp.min(least))
    return lowest


def chunk_maps(dbl_ref, mask_ref, segr_ref, at):
    rows = slice(at, at + CHUNK)
    b_map = dbl_ref[rows, 128 : 128 + STATE]
    c_map = dbl_ref[rows, 128 + STATE : 128 + 2 * STATE]
    linked = mask_ref[rows, 0:1]
    tail = mask_ref[rows, 1:2]
    keep = mask_ref[at + CHUNK - 1 : at + CHUNK, 2:3]
    allowed = tri_matrix(CHUNK, False) & (mask_ref[rows, 4:5] == segr_ref[0:1, rows])
    gram = jnp.where(allowed, dot_last(c_map, b_map), 0.0)
    c_link = c_map.astype(jnp.float32) * linked
    b_tail = b_map.astype(jnp.float32) * tail
    return b_map, c_map, linked, tail, keep, allowed, gram, c_link, b_tail


def mixer(square, side, bottom):
    corner = jnp.zeros((STATE, STATE), jnp.float32)
    top = jnp.concatenate([square, side], axis=1)
    low = jnp.concatenate([jnp.transpose(bottom), corner], axis=1)
    return jnp.concatenate([top, low], axis=0).astype(jnp.bfloat16)


def token_column(block, lane_index):
    lanes = lax.broadcasted_iota(jnp.int32, block.shape, 1)
    return jnp.sum(jnp.where(lanes == lane_index, block, 0.0), axis=1, keepdims=True)


def scan_fwd_kernel(
    xa_ref, z_ref, dbl_ref, mask_ref, segr_ref, dtw_ref, vec_ref,
    out_ref, hsave_ref, h_scr, step_scr, cum_scr, y_scr,
):
    width = xa_ref.shape[1]

    @pl.when(pl.program_id(0) == 0)
    def _():
        h_scr[...] = jnp.zeros_like(h_scr)

    lowest = scan_setup(dbl_ref, dtw_ref, vec_ref, step_scr, cum_scr, None)

    @pl.when(lowest >= -RANGE)
    def _():
        for index, at in enumerate(range(0, ROWS, CHUNK)):
            rows = slice(at, at + CHUNK)
            _, _, _, _, keep, _, gram, c_link, b_tail = chunk_maps(dbl_ref, mask_ref, segr_ref, at)
            forward = mixer(gram, c_link, b_tail)
            for lo, hi in spans(width, LANES):
                cum = cum_scr[rows, lo:hi]
                half = 0.5 * cum[CHUNK - 1 : CHUNK]
                gap = cum - half
                rise = jnp.exp(half)
                h_old = h_scr[:, lo:hi]
                hsave_ref[index, :, lo:hi] = h_old
                x_f = xa_ref[rows, lo:hi].astype(jnp.float32)
                sources = jnp.concatenate(
                    [jnp.exp(-gap) * (step_scr[rows, lo:hi] * x_f), rise * h_old], axis=0
                ).astype(jnp.bfloat16)
                mixed = dot_plain(forward, sources)
                total = jnp.exp(gap) * mixed[:CHUNK] + vec_ref[2:3, lo:hi] * x_f
                out_ref[rows, lo:hi] = (total * jax.nn.silu(z_ref[rows, lo:hi])).astype(
                    jnp.bfloat16
                )
                h_scr[:, lo:hi] = rise * mixed[CHUNK:] + (rise * rise * keep) * h_old

    @pl.when(lowest < -RANGE)
    def _():
        for index, at in enumerate(range(0, ROWS, CHUNK)):
            rows = slice(at, at + CHUNK)
            hsave_ref[index] = h_scr[...]
            b_cols = jnp.transpose(dbl_ref[rows, 128 : 128 + STATE].astype(jnp.float32))
            c_cols = jnp.transpose(dbl_ref[rows, 128 + STATE : 128 + 2 * STATE].astype(jnp.float32))
            y_scr[...] = xa_ref[rows].astype(jnp.float32)
            rate = jnp.exp(vec_ref[1:2])

            def token(t, carry):
                step = step_scr[pl.ds(at + t, 1)]
                keep = mask_ref[pl.ds(at + t, 1)][:, 3:4]
                state = (jnp.exp(-step * rate) * keep) * h_scr[...] + token_column(b_cols, t) * (
                    step * y_scr[pl.ds(t, 1)]
                )
                h_scr[...] = state
                y_scr[pl.ds(t, 1)] = (
                    jnp.sum(state * token_column(c_cols, t), axis=0, keepdims=True)
                    + vec_ref[2:3] * y_scr[pl.ds(t, 1)]
                )
                return carry

            lax.fori_loop(0, CHUNK, token, 0)
            out_ref[rows] = (y_scr[...] * jax.nn.silu(z_ref[rows])).astype(jnp.bfloat16)


def scan_bwd_kernel(
    xa_ref, z_ref, dbl_ref, mask_ref, segr_ref, dtw_ref, vec_ref, hsave_ref, gs_ref,
    gz_ref, gx_ref, gdbl_ref, gdtw_ref, gvec_ref,
    g_scr, step_scr, cum_scr, slope_scr, gl_scr, gu_scr, gpre_scr, hall_scr, y_scr,
):
    width = xa_ref.shape[1]

    @pl.when(pl.program_id(0) == 0)
    def _():
        g_scr[...] = jnp.zeros_like(g_scr)
        gdtw_ref[...] = jnp.zeros_like(gdtw_ref)
        gvec_ref[...] = jnp.zeros_like(gvec_ref)

    lowest = scan_setup(dbl_ref, dtw_ref, vec_ref, step_scr, cum_scr, slope_scr)
    count = ROWS // CHUNK

    @pl.when(lowest >= -RANGE)
    def _():
        for index in range(count - 1, -1, -1):
            at = index * CHUNK
            rows = slice(at, at + CHUNK)
            b_map, c_map, linked, tail, keep, allowed, gram, c_link, b_tail = chunk_maps(
                dbl_ref, mask_ref, segr_ref, at
            )
            forward = mixer(gram, c_link, b_tail)
            reverse = mixer(jnp.transpose(gram), b_tail, c_link)
            cross = jnp.zeros((CHUNK + STATE, CHUNK + STATE), jnp.float32)
            for lo, hi in spans(width, LANES):
                cum = cum_scr[rows, lo:hi]
                half = 0.5 * cum[CHUNK - 1 : CHUNK]
                gap = cum - half
                fall = jnp.exp(gap)
                grow = jnp.exp(-gap)
                rise = jnp.exp(half)
                h_old = hsave_ref[index, :, lo:hi]
                g_new = g_scr[:, lo:hi]
                step = step_scr[rows, lo:hi]
                x_f = xa_ref[rows, lo:hi].astype(jnp.float32)
                skip = vec_ref[2:3, lo:hi]
                sources = jnp.concatenate([grow * (step * x_f), rise * h_old], axis=0).astype(
                    jnp.bfloat16
                )
                mixed = dot_plain(forward, sources)
                inner = mixed[:CHUNK]
                z_f = z_ref[rows, lo:hi]
                grad = gs_ref[rows, lo:hi]
                sig = jax.nn.sigmoid(z_f)
                gated = z_f * sig
                gy = grad * gated
                gz_ref[rows, lo:hi] = (
                    grad * (fall * inner + skip * x_f) * (sig + gated * (1.0 - sig))
                ).astype(jnp.bfloat16)
                sinks = jnp.concatenate([fall * gy, rise * g_new], axis=0).astype(jnp.bfloat16)
                pulled = dot_plain(reverse, sinks)
                back = pulled[:CHUNK]
                cross += dot_last(sinks, sources)
                sinks_f = sinks.astype(jnp.float32)
                sources_f = sources.astype(jnp.float32)
                ends = jnp.sum(sinks_f[CHUNK:] * mixed[CHUNK:], axis=0, keepdims=True) + (
                    rise * rise * keep
                ) * jnp.sum(g_new * h_old, axis=0, keepdims=True)
                diff = sinks_f[:CHUNK] * inner - sources_f[:CHUNK] * back
                gl_scr[rows, lo:hi] = diff
                gl_scr[at + CHUNK - 1 : at + CHUNK, lo:hi] = diff[CHUNK - 1 : CHUNK] + ends
                g_scr[:, lo:hi] = rise * pulled[CHUNK:] + (rise * rise * keep) * g_new
                gu = grow * back
                gu_scr[rows, lo:hi] = gu
                gx_ref[rows, lo:hi] = step * gu + skip * gy
                gvec_ref[2:3, lo:hi] += jnp.sum(gy * x_f, axis=0, keepdims=True)
            g_gram = jnp.where(allowed, cross[:CHUNK, :CHUNK], 0.0).astype(jnp.bfloat16)
            gdbl_ref[rows, 128 : 128 + STATE] = dot_first(g_gram, c_map) + tail * jnp.transpose(
                cross[CHUNK:, :CHUNK]
            )
            gdbl_ref[rows, 128 + STATE : 128 + 2 * STATE] = (
                dot_plain(g_gram, b_map) + linked * cross[:CHUNK, CHUNK:]
            )
        triu = tri_matrix(ROWS, True).astype(jnp.bfloat16)
        for lo, hi in spans(width, LANES):
            gl_scr[:, lo:hi] = split_sum(triu, gl_scr[:, lo:hi])

    @pl.when(lowest < -RANGE)
    def _():
        rate = jnp.exp(vec_ref[1:2])

        def chunk_step(reverse, carry):
            index = count - 1 - reverse
            at = pl.multiple_of(index * CHUNK, CHUNK)
            rows = pl.ds(at, CHUNK)
            b_cols = jnp.transpose(dbl_ref[rows, 128 : 128 + STATE].astype(jnp.float32))
            c_cols = jnp.transpose(dbl_ref[rows, 128 + STATE : 128 + 2 * STATE].astype(jnp.float32))
            hall_scr[0] = hsave_ref[index]
            y_scr[...] = xa_ref[rows].astype(jnp.float32)
            gu_scr[rows] = gs_ref[rows] * jax.nn.silu(z_ref[rows])

            def forward(t, inner_carry):
                step = step_scr[pl.ds(at + t, 1)]
                keep = mask_ref[pl.ds(at + t, 1)][:, 3:4]
                state = (jnp.exp(-step * rate) * keep) * hall_scr[t] + token_column(b_cols, t) * (
                    step * y_scr[pl.ds(t, 1)]
                )
                hall_scr[t + 1] = state
                return inner_carry

            lax.fori_loop(0, CHUNK, forward, 0)

            def backward(back, inner_carry):
                g_b, g_c = inner_carry
                t = CHUNK - 1 - back
                step = step_scr[pl.ds(at + t, 1)]
                keep = mask_ref[pl.ds(at + t, 1)][:, 3:4]
                decay = jnp.exp(-step * rate) * keep
                gy = gu_scr[pl.ds(at + t, 1)]
                x_f = y_scr[pl.ds(t, 1)]
                c_col = token_column(c_cols, t)
                b_col = token_column(b_cols, t)
                here = hall_scr[t + 1]
                grad = g_scr[...] + c_col * gy
                lanes = lax.broadcasted_iota(jnp.int32, (STATE, CHUNK), 1)
                g_b = jnp.where(
                    lanes == t, jnp.sum(grad * (step * x_f), axis=1, keepdims=True), g_b
                )
                g_c = jnp.where(lanes == t, jnp.sum(here * gy, axis=1, keepdims=True), g_c)
                gl_scr[pl.ds(at + t, 1)] = decay * jnp.sum(
                    grad * hall_scr[t], axis=0, keepdims=True
                )
                gu_scr[pl.ds(at + t, 1)] = jnp.sum(grad * b_col, axis=0, keepdims=True)
                y_scr[pl.ds(t, 1)] = (
                    jnp.sum(here * c_col, axis=0, keepdims=True) + vec_ref[2:3] * x_f
                )
                g_scr[...] = decay * grad
                return g_b, g_c

            blank = jnp.zeros((STATE, CHUNK), jnp.float32)
            g_b, g_c = lax.fori_loop(0, CHUNK, backward, (blank, blank))
            gdbl_ref[rows, 128 : 128 + STATE] = jnp.transpose(g_b)
            gdbl_ref[rows, 128 + STATE : 128 + 2 * STATE] = jnp.transpose(g_c)
            z_f = z_ref[rows]
            grad = gs_ref[rows]
            sig = jax.nn.sigmoid(z_f)
            gz_ref[rows] = (grad * y_scr[...] * (sig * (1.0 + z_f * (1.0 - sig)))).astype(
                jnp.bfloat16
            )
            gy = grad * (z_f * sig)
            x_f = xa_ref[rows].astype(jnp.float32)
            gx_ref[rows] = step_scr[rows] * gu_scr[rows] + vec_ref[2:3] * gy
            gvec_ref[2:3] += jnp.sum(gy * x_f, axis=0, keepdims=True)
            return carry

        lax.fori_loop(0, count, chunk_step, 0)

    for lo, hi in spans(width, LANES):
        rate = jnp.exp(vec_ref[1:2, lo:hi])
        x_f = xa_ref[:, lo:hi].astype(jnp.float32)
        gl = rate * gl_scr[:, lo:hi]
        gpre = (x_f * gu_scr[:, lo:hi] - gl) * slope_scr[:, lo:hi]
        gvec_ref[0:1, lo:hi] += jnp.sum(gpre, axis=0, keepdims=True)
        gvec_ref[1:2, lo:hi] -= jnp.sum(step_scr[:, lo:hi] * gl, axis=0, keepdims=True)
        gpre_scr[:, lo:hi] = gpre.astype(jnp.bfloat16)
    gdtw_ref[...] += dot_first(dbl_ref[:, :RANK], gpre_scr[...])
    gdbl_ref[:, :RANK] = dot_last(gpre_scr[...], dtw_ref[...])


def scan_specs(width, backward, blocks):
    def at(i):
        return (blocks - 1 - i) if backward else i

    rows = lambda cols: pl.BlockSpec((ROWS, cols), lambda i: (at(i), 0))
    whole = lambda *shape: pl.BlockSpec(shape, lambda i: (0, 0))
    return [
        rows(width),
        rows(width),
        rows(256),
        rows(8),
        pl.BlockSpec((1, ROWS), lambda i: (0, at(i))),
        whole(RANK, width),
        whole(8, width),
    ], pl.BlockSpec((ROWS // CHUNK, STATE, width), lambda i: (at(i), 0, 0)), rows, whole


def scan_forward(x_act, z_gate, dbl, masks, seg_row, dt_weight, vectors):
    tokens, width = x_act.shape
    blocks = tokens // ROWS
    in_specs, state_spec, rows, whole = scan_specs(width, False, blocks)
    return pl.pallas_call(
        scan_fwd_kernel,
        name="scan_fwd",
        grid=(blocks,),
        in_specs=in_specs,
        out_specs=[rows(width), state_spec],
        out_shape=[
            jax.ShapeDtypeStruct((tokens, width), jnp.bfloat16),
            jax.ShapeDtypeStruct((tokens // CHUNK, STATE, width), jnp.float32),
        ],
        scratch_shapes=[
            pltpu.VMEM((STATE, width), jnp.float32),
            pltpu.VMEM((ROWS, width), jnp.float32),
            pltpu.VMEM((ROWS, width), jnp.float32),
            pltpu.VMEM((CHUNK, width), jnp.float32),
        ],
        compiler_params=pltpu.CompilerParams(vmem_limit_bytes=40 << 20),
        cost_estimate=pl.CostEstimate(
            flops=0, bytes_accessed=93 << 20, transcendentals=0
        ),
    )(x_act, z_gate, dbl, masks, seg_row, dt_weight, vectors)


def scan_backward(x_act, z_gate, dbl, masks, seg_row, dt_weight, vectors, states, grad_rows):
    tokens, width = x_act.shape
    blocks = tokens // ROWS
    in_specs, state_spec, rows, whole = scan_specs(width, True, blocks)
    return pl.pallas_call(
        scan_bwd_kernel,
        name="scan_bwd",
        grid=(blocks,),
        in_specs=in_specs + [state_spec, rows(width)],
        out_specs=[rows(width), rows(width), rows(256), whole(RANK, width), whole(8, width)],
        out_shape=[
            jax.ShapeDtypeStruct((tokens, width), jnp.bfloat16),
            jax.ShapeDtypeStruct((tokens, width), jnp.float32),
            jax.ShapeDtypeStruct((tokens, 256), jnp.float32),
            jax.ShapeDtypeStruct((RANK, width), jnp.float32),
            jax.ShapeDtypeStruct((8, width), jnp.float32),
        ],
        scratch_shapes=[
            pltpu.VMEM((STATE, width), jnp.float32),
            pltpu.VMEM((ROWS, width), jnp.float32),
            pltpu.VMEM((ROWS, width), jnp.float32),
            pltpu.VMEM((ROWS, width), jnp.float32),
            pltpu.VMEM((ROWS, width), jnp.float32),
            pltpu.VMEM((ROWS, width), jnp.float32),
            pltpu.VMEM((ROWS, width), jnp.bfloat16),
            pltpu.VMEM((CHUNK + 1, STATE, width), jnp.float32),
            pltpu.VMEM((CHUNK, width), jnp.float32),
        ],
        compiler_params=pltpu.CompilerParams(vmem_limit_bytes=48 << 20),
        cost_estimate=pl.CostEstimate(
            flops=0, bytes_accessed=244 << 20, transcendentals=0
        ),
    )(x_act, z_gate, dbl, masks, seg_row, dt_weight, vectors, states, grad_rows)


def scan_masks(segs_flat):
    tokens = segs_flat.shape[0]
    before = jnp.concatenate([jnp.full((1,), -1, jnp.int32), segs_flat[:-1]])
    chunked = segs_flat.reshape(tokens // CHUNK, CHUNK)
    prior = before.reshape(tokens // CHUNK, CHUNK)[:, :1]
    last = chunked[:, CHUNK - 1 :]
    linked = chunked == prior
    tail = chunked == last
    keep = jnp.broadcast_to(last == prior, chunked.shape)
    same = (segs_flat == before).reshape(chunked.shape)
    blank = jnp.zeros_like(linked)
    stacked = jnp.stack([linked, tail, keep, same], axis=-1).reshape(tokens, 4).astype(jnp.float32)
    number = segs_flat.astype(jnp.float32)
    masks = jnp.concatenate(
        [stacked, number[:, None], jnp.zeros((tokens, 3), jnp.float32)], axis=1
    )
    return masks, number[None, :]


def per_device(
    inputs,
    teacher,
    segment_ids,
    valid,
    norm_in_gain,
    w_query,
    w_key,
    w_value,
    w_attn_out,
    w_mamba_in,
    conv_weight,
    conv_bias,
    x_proj,
    dt_proj,
    dt_bias,
    a_log,
    d_skip,
    w_mamba_out,
    attn_norm_gain,
    ssm_norm_gain,
    norm_mid_gain,
    w_gate,
    w_up,
    w_down,
):
    rank_index = lax.axis_index("tensor")
    first_slot, second_slot = rank_index, KV - 1
    per_slot = HEADS // KV
    group_width = per_slot * HEAD
    query_width = 2 * group_width
    qkv_width = query_width + 4 * HEAD
    width = inputs.shape[1]
    inner_width = w_mamba_out.shape[0]
    low = lambda values: values.astype(jnp.bfloat16)
    gather_dp = lambda part: lax.all_gather(part, "dp", axis=0, tiled=True)
    scatter_dp = lambda part: lax.psum_scatter(part, "dp", scatter_dimension=0, tiled=True)
    gather_t = lambda part: gather_rows(part, 1)
    tie = lax.optimization_barrier

    own_width = w_query.shape[0]
    out_local = pick_groups(w_attn_out, first_slot, second_slot, group_width, 0).T
    mamba_local = jnp.concatenate(
        [out_local, w_mamba_in.reshape(own_width, 2 * inner_width), w_mamba_out.T], axis=1
    )
    x_at, z_at = query_width, query_width + inner_width
    back_at = z_at + inner_width
    mamba_local = jnp.pad(mamba_local, ((0, 0), (0, -mamba_local.shape[1] % 128)))
    mamba_all = gather_dp(mamba_local)
    part_of = lambda at: (mamba_all, None, at // 128 * 128, -(-(at % 128 + inner_width) // 128) * 128)
    w_query, w_key, w_value, norm_in_gain, _ = tie(
        (w_query, w_key, w_value, norm_in_gain, mamba_local)
    )
    group_rows = 4 * inputs.shape[0]
    seq_count = group_rows // LEN
    segs_grid = segment_ids.reshape(seq_count, LEN)
    segs_flat = (segs_grid + 128 * jnp.arange(seq_count, dtype=jnp.int32)[:, None]).reshape(-1)
    scan_mask, seg_row = scan_masks(segs_flat)
    starts = first_blocks(segs_flat)
    blocks = jnp.arange(group_rows // BQ, dtype=jnp.int32)
    shared_here = blocks // (group_rows // BQ // 4) == rank_index
    firsts = jnp.concatenate([starts, jnp.where(shared_here, starts, blocks + 1)])
    first_local = jnp.concatenate(
        [
            pick_groups(w_query, first_slot, second_slot, group_width, 1),
            pick_groups(w_key, first_slot, second_slot, HEAD, 1),
            pick_groups(w_value, first_slot, second_slot, HEAD, 1),
        ],
        axis=1,
    )
    gain_rows = jnp.stack([norm_in_gain, attn_norm_gain, ssm_norm_gain, norm_mid_gain])
    gains, valid_total = hello(gain_rows, jnp.sum(valid).astype(jnp.float32))
    gain_in, gain_attn, gain_ssm, gain_mid = [gains[index][:, None] for index in range(4)]
    inputs_t = inputs.T
    normed_in, pull_in = jax.vjp(normalize_t, inputs_t, gain_in)
    normed_low, first_local, w_gate, w_up, w_down = tie(
        (low(normed_in), first_local, w_gate, w_up, w_down)
    )
    whole_in, qkv_w = gather_first(normed_low, first_local)
    whole_in, w_gate, w_up, w_down = tie((whole_in, w_gate, w_up, w_down))
    qkv_cols = low(dot_first(qkv_w, whole_in))
    attended_t, log_totals = attn_forward(firsts, qkv_cols, seg_row, scan_mask, 2)
    attended_t, x_proj, dt_proj, conv_weight = tie((attended_t, x_proj, dt_proj, conv_weight))
    inner_local = jnp.concatenate(
        [
            dt_bias[:, None],
            a_log[:, None],
            d_skip[:, None],
            conv_bias[:, None],
            conv_weight.T,
            x_proj,
            dt_proj.T,
        ],
        axis=1,
    )
    inner_rows = inner_spread(inner_local)
    attended_t, inner_rows = tie((attended_t, inner_rows))
    attn_sum = product_reduce(
        [(mamba_all, None, 0, query_width)],
        [(attended_t, True)],
        [(0, 0, query_width, 0)],
        10,
        "attn_reduce",
        43,
    )
    out_w = mamba_all[:, :query_width]
    weight_x = mamba_all[:, x_at:z_at]
    weight_z = mamba_all[:, z_at:back_at]
    mamba_out_w = mamba_all[:, back_at : back_at + inner_width]
    x_in = dot_first(whole_in, weight_x)
    ff_width = w_gate.shape[1]
    ff_step = -(-ff_width // 128) * 128
    blank = jnp.zeros((own_width, ff_step - ff_width), jnp.bfloat16)
    ffn_all = gather_dp(jnp.concatenate([w_gate, blank, w_up, blank, w_down.T, blank], axis=1))
    vector_rows = inner_rows[:, :8].astype(jnp.float32).T
    xproj_rows = inner_rows[:, 8 : 8 + RANK + 2 * STATE]
    dt_weight = inner_rows[:, 8 + RANK + 2 * STATE :].T
    xproj_pad = jnp.concatenate(
        [
            xproj_rows[:, :RANK],
            jnp.zeros((inner_width, 128 - RANK), jnp.bfloat16),
            xproj_rows[:, RANK:],
            jnp.zeros((inner_width, 128 - 2 * STATE), jnp.bfloat16),
        ],
        axis=1,
    )
    x_pre, pull_conv = jax.vjp(
        lambda x_part, taps, shift: conv_rows(x_part, taps, shift, segs_grid),
        x_in,
        vector_rows[4:],
        vector_rows[3],
    )
    x_act = low(x_pre)
    dbl_pad = total_rows(dot_plain(x_act, xproj_pad), 3)
    z_gate = dot_first(whole_in, weight_z)
    ssm_rows, states = scan_forward(
        x_act, z_gate, dbl_pad, scan_mask, seg_row, dt_weight, vector_rows
    )
    ssm_sum = product_reduce(
        [part_of(back_at)],
        [(ssm_rows, False)],
        [(0, back_at % 128, back_at % 128 + inner_width, 0)],
        11,
        "ssm_reduce",
        43,
    )
    mixed, pull_join = jax.vjp(join_rows_t, inputs_t, attn_sum, ssm_sum, gain_attn, gain_ssm)
    normed_mid, pull_mid = jax.vjp(normalize_t, mixed, gain_mid)
    normed_low, ffn_all = tie((low(normed_mid), ffn_all))
    whole_mid, gate_rows, up_rows, hidden = turn_rows(
        normed_low,
        ffn_all,
        [],
        [(ff_width, jnp.float32), (ff_width, jnp.float32), (ff_width, jnp.bfloat16)],
        [(0, ff_width), (ff_step, ff_step + ff_width)],
        forward_gate,
        15,
        "gate_turn",
        52,
    )
    ffn_rows = product_reduce(
        [(ffn_all, None, 2 * ff_step, ff_step)], [(hidden, False)], [(0, 0, ff_width, 0)], 6, "down_reduce", 45
    )
    result = mixed + ffn_rows
    all_rows = inputs.shape[0] * lax.axis_size("dp") * lax.axis_size("tensor")
    grad_out = all_rows / valid_total * valid.astype(jnp.float32)[None, :] * (result - teacher.T)
    grad_ffn, grad_gate, grad_up = turn_rows(
        low(grad_out),
        ffn_all,
        [gate_rows, up_rows],
        [(ff_width, jnp.bfloat16), (ff_width, jnp.bfloat16)],
        [(2 * ff_step, 2 * ff_step + ff_width)],
        backward_gate,
        16,
        "grad_turn",
        52,
    )
    ffn_grads = weight_grads(
        [
            (whole_mid, grad_gate, False),
            (whole_mid, grad_up, False),
            (grad_ffn, hidden, False),
        ],
        "ffn_weight_grads",
        44,
    )
    grad_gate, grad_up, ffn_grads = tie((grad_gate, grad_up, ffn_grads))
    ffn_shard = scatter_dp(ffn_grads)
    grad_mid_rows = product_reduce(
        [(ffn_all, None, 0, 2 * ff_step)],
        [(grad_gate, False), (grad_up, False)],
        [(0, 0, ff_width, 0), (0, ff_step, ff_step + ff_width, 1)],
        7,
        "mid_reduce",
        50,
    )
    grad_mixed_norm, grad_gain_mid = pull_mid(grad_mid_rows)
    grad_mixed = grad_out + grad_mixed_norm
    grad_resid, grad_attn_sum, grad_ssm_sum, grad_gain_attn, grad_gain_ssm = pull_join(grad_mixed)
    grad_ssm_whole = gather_t(low(grad_ssm_sum))
    grad_attn_low, grad_ssm_whole = tie((low(grad_attn_sum), grad_ssm_whole))
    grad_attn_whole = gather_t(grad_attn_low)
    grad_ssm_whole, grad_attn_whole = tie((grad_ssm_whole, grad_attn_whole))
    grad_ssm_rows = dot_first(grad_ssm_whole, mamba_out_w)
    grad_gate_part, grad_act_scan, grad_dbl_part, grad_dtproj, grad_vectors = scan_backward(
        x_act, z_gate, dbl_pad, scan_mask, seg_row, dt_weight, vector_rows, states, grad_ssm_rows
    )
    mid_grads = weight_grads(
        [
            (grad_attn_whole, attended_t, True),
            (grad_ssm_whole, ssm_rows, False),
            (whole_in, grad_gate_part, False),
        ],
        "mid_weight_grads",
        26,
        tight=True,
    )
    grad_att_t = low(
        lax.dot_general(
            out_w, grad_attn_whole, (((0,), (0,)), ((), ())), preferred_element_type=jnp.float32
        )
    )
    grad_dbl_part, mid_grads, ffn_shard = tie((grad_dbl_part, mid_grads, ffn_shard))
    mid_shard = scatter_dp(mid_grads)
    grad_qkv = attn_backward(
        firsts, qkv_cols, grad_att_t, attended_t, log_totals, seg_row, scan_mask, 2
    )
    grad_dbl = total_rows(grad_dbl_part, 3)
    grad_act = grad_act_scan + dot_last(grad_dbl, xproj_pad)
    grad_xproj_w = dot_first(x_act, grad_dbl)
    grad_x_part, grad_taps, grad_shift = pull_conv(grad_act)
    grad_x_low = low(grad_x_part)
    inner_grads = jnp.concatenate(
        [
            grad_vectors[:3].T,
            grad_shift[:, None],
            grad_taps.T,
            grad_xproj_w[:, :RANK],
            grad_xproj_w[:, 128 : 128 + 2 * STATE],
            grad_dtproj.T,
        ],
        axis=1,
    )
    last_grads = weight_grads(
        [
            (whole_in, grad_x_low, False),
            (whole_in, grad_qkv, True),
            (low(inner_grads).reshape(width, -1), None, False),
        ],
        "last_weight_grads",
        20,
    )
    grad_x_low, grad_qkv, last_grads, mid_shard = tie(
        (grad_x_low, grad_qkv, last_grads, mid_shard)
    )
    last_shard = scatter_dp(last_grads)
    grad_in_rows = product_reduce(
        [
            (qkv_w, None, None, qkv_width),
            part_of(x_at),
            part_of(z_at),
        ],
        [(grad_qkv, True), (grad_x_low, False), (grad_gate_part, False)],
        [
            (0, 0, qkv_width, 0),
            (1, x_at % 128, x_at % 128 + inner_width, 1),
            (2, z_at % 128, z_at % 128 + inner_width, 2),
        ],
        8,
        "in_reduce",
        52,
    )
    grad_in_norm, grad_gain_in = pull_in(grad_in_rows)
    grad_inputs = grad_resid + grad_in_norm
    gain_grads = jnp.concatenate(
        [grad_gain_in, grad_gain_attn, grad_gain_ssm, grad_gain_mid], axis=1
    )
    gains_own = farewell(gain_grads.T)
    wide = lambda part: jnp.pad(part, ((0, 0), (0, -part.shape[1] % 256)))
    out_stack = gather_stack(wide(mid_shard[:, :query_width]), 5)
    gains_own, last_shard, grad_inputs, out_stack = tie(
        (gains_own, last_shard, grad_inputs, out_stack)
    )
    inner_step = -(-inner_width // 128) * 128
    inner_at = inner_step + qkv_width
    shared_all, owned = gather_final(wide(last_shard[:, inner_step:inner_at]), last_shard[:, inner_at:])
    inner_cols = inner_grads.size // width
    inner_sum = owned[:, :, :inner_cols].astype(jnp.float32).reshape(-1, inner_grads.shape[1])
    mamba_at = query_width
    gate_at = query_width + inner_width
    def merge(stack, start, size):
        own = [stack[rank, :, start : start + size].astype(jnp.float32) for rank in range(4)]
        both = jnp.sum(
            stack[:, :, start + size : start + 2 * size].astype(jnp.float32), axis=0
        )
        return jnp.concatenate(own + [both], axis=1)

    return (
        result.T,
        grad_inputs.T,
        gains_own[0],
        merge(shared_all, 0, group_width),
        merge(shared_all, query_width, HEAD),
        merge(shared_all, query_width + 2 * HEAD, HEAD),
        merge(out_stack, 0, group_width).T,
        jnp.stack(
            [last_shard[:, :inner_width], mid_shard[:, gate_at : gate_at + inner_width]], axis=1
        ).astype(jnp.float32),
        inner_sum[:, 4:8].T,
        inner_sum[:, 3],
        inner_sum[:, 8 : 8 + RANK + 2 * STATE],
        inner_sum[:, 8 + RANK + 2 * STATE :].T,
        inner_sum[:, 0],
        inner_sum[:, 1],
        inner_sum[:, 2],
        mid_shard[:, mamba_at : mamba_at + inner_width].T.astype(jnp.float32),
        gains_own[1],
        gains_own[2],
        gains_own[3],
        ffn_shard[:, :ff_width].astype(jnp.float32),
        ffn_shard[:, ff_step : ff_step + ff_width].astype(jnp.float32),
        ffn_shard[:, 2 * ff_step : 2 * ff_step + ff_width].astype(jnp.float32).T,
    )


def solution(mesh):
    placed = (
        P(("dp", "tensor"), None),
        P(("dp", "tensor"), None),
        P("dp"),
        P(("dp", "tensor")),
        P("dp"),
        P("dp", None),
        P("dp", None),
        P("dp", None),
        P(None, "dp"),
        P("dp", None, "tensor"),
        P(None, "dp"),
        P("dp"),
        P("dp", None),
        P(None, "dp"),
        P("dp"),
        P("dp"),
        P("dp"),
        P("tensor", "dp"),
        P("dp"),
        P("dp"),
        P("dp"),
        P("dp", "tensor"),
        P("dp", "tensor"),
        P("tensor", "dp"),
    )
    return jax.shard_map(
        per_device,
        mesh=mesh,
        in_specs=placed,
        out_specs=(
            P(("dp", "tensor"), None),
            P(("dp", "tensor"), None),
            P("dp"),
            P("dp", None),
            P("dp", None),
            P("dp", None),
            P(None, "dp"),
            P("dp", None, "tensor"),
            P(None, "dp"),
            P("dp"),
            P("dp", None),
            P(None, "dp"),
            P("dp"),
            P("dp"),
            P("dp"),
            P("tensor", "dp"),
            P("dp"),
            P("dp"),
            P("dp"),
            P("dp", "tensor"),
            P("dp", "tensor"),
            P("tensor", "dp"),
        ),
        check_vma=False,
    )
```

```python
import functools

import jax
import jax.numpy as jnp
from jax import lax
from jax.experimental import pallas as pl
from jax.experimental.pallas import tpu as pltpu
from jax.sharding import PartitionSpec as P

HEADS = 25
KV = 5
HEAD = 64
STATE = 16
RANK = 100
CONV = 4
WINDOW = 1024
BLOCK = 512
STRETCH = 64
LEN = 2048


EPSILON = 1e-06
MASKED = -1e30
HIGHEST = lax.Precision.HIGHEST


def normalize_t(values, gain):
    return values * lax.rsqrt(jnp.mean(values * values, axis=0, keepdims=True) + EPSILON) * gain


def join_rows_t(resid, attn_sum, ssm_sum, gain_attn, gain_ssm):
    return resid + 0.5 * (normalize_t(attn_sum, gain_attn) + normalize_t(ssm_sum, gain_ssm))


def dot_plain(left, right):
    return jnp.dot(left, right, preferred_element_type=jnp.float32)


def dot_last(left, right):
    return lax.dot_general(
        left, right, (((1,), (1,)), ((), ())), preferred_element_type=jnp.float32
    )


def dot_first(left, right):
    return lax.dot_general(
        left, right, (((0,), (0,)), ((), ())), preferred_element_type=jnp.float32
    )


def pick_groups(weight, first_slot, second_slot, group_width, axis):
    return jnp.concatenate(
        [
            lax.dynamic_slice_in_dim(weight, first_slot * group_width, group_width, axis),
            lax.dynamic_slice_in_dim(weight, second_slot * group_width, group_width, axis),
        ],
        axis=axis,
    )


PIECES = 4
MESH = pl.DeviceIdType.MESH


def tensor_peers():
    me = lax.axis_index("tensor")
    side = me + 1 - 2 * lax.rem(me, 2)
    cross = lax.rem(me + 2, 4)
    return me, side, cross, lax.rem(side + 2, 4)


def greet(peers):
    barrier = pltpu.get_barrier_semaphore()
    for peer in peers:
        pl.semaphore_signal(barrier, inc=1, device_id={"tensor": peer}, device_id_type=MESH)
    pl.semaphore_wait(barrier, len(peers))


def push(src, dst, sems, index, peer):
    copy = pltpu.make_async_remote_copy(
        src_ref=src,
        dst_ref=dst,
        send_sem=sems[0].at[index],
        recv_sem=sems[1].at[index],
        device_id={"tensor": peer},
        device_id_type=MESH,
    )
    copy.start()
    return copy


def columns(block, size):
    return pl.ds(pl.multiple_of(block * size, size), size)


def gather_kernel(part_ref, whole_ref, own_sem, *sems):
    me, side, cross, diag = tensor_peers()
    depth, size = part_ref.shape
    step = depth // PIECES
    mine = columns(me, size)
    theirs = columns(cross, size)
    greet((side, cross))
    own = pltpu.make_async_copy(part_ref, whole_ref.at[:, mine], own_sem)
    own.start()
    over, near, relay = [], [], []
    for piece in range(PIECES):
        rows = pl.ds(piece * step, step)
        over.append(
            push(part_ref.at[rows], whole_ref.at[rows, mine], sems[0:2], piece, cross)
        )
    for piece in range(PIECES):
        rows = pl.ds(piece * step, step)
        near.append(push(part_ref.at[rows], whole_ref.at[rows, mine], sems[2:4], piece, side))
    for piece in range(PIECES):
        rows = pl.ds(piece * step, step)
        over[piece].wait_recv()
        relay.append(
            push(whole_ref.at[rows, theirs], whole_ref.at[rows, theirs], sems[4:6], piece, side)
        )
    own.wait()
    for piece in range(PIECES):
        over[piece].wait_send()
        near[piece].wait()
        relay[piece].wait()


def gather_rows(part, call_id):
    depth, size = part.shape
    return pl.pallas_call(
        gather_kernel,
        name="gather_rows",
        in_specs=[pl.BlockSpec(memory_space=pl.ANY)],
        out_specs=pl.BlockSpec(memory_space=pl.ANY),
        out_shape=jax.ShapeDtypeStruct((depth, 4 * size), part.dtype),
        scratch_shapes=[pltpu.SemaphoreType.DMA] + [pltpu.SemaphoreType.DMA((PIECES,))] * 6,
        compiler_params=pltpu.CompilerParams(
            collective_id=call_id, has_side_effects=True, vmem_limit_bytes=1 << 20
        ),
        cost_estimate=pl.CostEstimate(
            flops=0, bytes_accessed=depth * size * 2 * 90, transcendentals=0
        ),
    )(part)


def first_kernel(part_ref, shard_ref, whole_ref, all_ref, own_sem, *sems):
    me, side, cross, diag = tensor_peers()
    depth, size = part_ref.shape
    step = depth // PIECES
    mine, theirs = columns(me, size), columns(cross, size)
    place = lax.axis_index("dp")
    spot, lane = lax.div(place, 2), lax.rem(place, 2)
    length = all_ref.shape[0] // 2
    partner = 2 * spot + 1 - lane
    barrier = pltpu.get_barrier_semaphore()
    for peer in (side, cross):
        pl.semaphore_signal(barrier, inc=1, device_id={"tensor": peer}, device_id_type=MESH)
    pl.semaphore_signal(barrier, inc=1, device_id={"dp": partner}, device_id_type=MESH)
    has_left, has_right = spot > 0, spot < length - 1

    @pl.when(has_left)
    def _():
        pl.semaphore_signal(barrier, inc=1, device_id={"dp": place - 2}, device_id_type=MESH)

    @pl.when(has_right)
    def _():
        pl.semaphore_signal(barrier, inc=1, device_id={"dp": place + 2}, device_id_type=MESH)

    pl.semaphore_wait(barrier, 3 + has_left.astype(jnp.int32) + has_right.astype(jnp.int32))

    def line(origin, group, peer, source):
        slot = all_ref.at[2 * origin + lane]
        return pltpu.make_async_remote_copy(
            src_ref=slot if source is None else source,
            dst_ref=slot,
            send_sem=sems[6 + 2 * group].at[origin],
            recv_sem=sems[7 + 2 * group].at[origin],
            device_id={"dp": peer},
            device_id_type=MESH,
        )

    to_right = lambda origin, source=None: line(origin, 0, place + 2, source)
    to_left = lambda origin, source=None: line(origin, 1, place - 2, source)
    to_partner = lambda origin, source=None: line(origin, 2, partner, source)

    own = pltpu.make_async_copy(part_ref, whole_ref.at[:, mine], own_sem.at[0])
    own.start()
    kept = pltpu.make_async_copy(shard_ref, all_ref.at[place], own_sem.at[1])
    kept.start()
    pl.when(has_right)(to_right(spot, shard_ref).start)
    pl.when(has_left)(to_left(spot, shard_ref).start)
    to_partner(spot, shard_ref).start()
    over, near, relay = [], [], []
    for piece in range(PIECES):
        rows = pl.ds(piece * step, step)
        over.append(push(part_ref.at[rows], whole_ref.at[rows, mine], sems[0:2], piece, cross))
    for piece in range(PIECES):
        rows = pl.ds(piece * step, step)
        near.append(push(part_ref.at[rows], whole_ref.at[rows, mine], sems[2:4], piece, side))

    def pass_on(hop):
        left, right = spot - hop, spot + hop

        @pl.when(left >= 0)
        def _():
            to_right(left).wait_recv()
            pl.when(has_right)(to_right(left).start)
            to_partner(left).start()

        @pl.when(right < length)
        def _():
            to_left(right).wait_recv()
            pl.when(has_left)(to_left(right).start)
            to_partner(right).start()

    hops = list(range(1, length))
    for piece in range(PIECES):
        rows = pl.ds(piece * step, step)
        over[piece].wait_recv()
        relay.append(
            push(whole_ref.at[rows, theirs], whole_ref.at[rows, theirs], sems[4:6], piece, side)
        )
        if piece and hops:
            pass_on(hops.pop(0))
    for hop in hops:
        pass_on(hop)
    own.wait()
    kept.wait()
    for piece in range(PIECES):
        over[piece].wait_send()
        near[piece].wait()
        relay[piece].wait()
    for origin in range(length):
        pl.when(has_right & (origin <= spot))(to_right(origin).wait_send)
        pl.when(has_left & (origin >= spot))(to_left(origin).wait_send)
        to_partner(origin).wait_send()
        arrival = pltpu.make_async_remote_copy(
            src_ref=shard_ref,
            dst_ref=all_ref.at[2 * origin + 1 - lane],
            send_sem=sems[10].at[origin],
            recv_sem=sems[11].at[origin],
            device_id={"dp": partner},
            device_id_type=MESH,
        )
        arrival.wait_recv()


def gather_first(part, shard):
    depth, size = part.shape
    groups = lax.axis_size("dp")
    anywhere = pl.BlockSpec(memory_space=pl.ANY)
    whole, stacked = pl.pallas_call(
        first_kernel,
        name="gather_first",
        in_specs=[anywhere] * 2,
        out_specs=[anywhere] * 2,
        out_shape=[
            jax.ShapeDtypeStruct((depth, 4 * size), part.dtype),
            jax.ShapeDtypeStruct((groups,) + shard.shape, shard.dtype),
        ],
        scratch_shapes=[pltpu.SemaphoreType.DMA((2,))]
        + [pltpu.SemaphoreType.DMA((PIECES,))] * 6
        + [pltpu.SemaphoreType.DMA((groups // 2,))] * 6,
        compiler_params=pltpu.CompilerParams(
            collective_id=14, has_side_effects=True, vmem_limit_bytes=1 << 20
        ),
        cost_estimate=pl.CostEstimate(flops=0, bytes_accessed=270 << 20, transcendentals=0),
    )(part, shard)
    return whole, stacked.reshape(-1, shard.shape[1])


def turn_kernel(combine, plan, n_in, n_out, *refs):
    part_ref, weight_ref = refs[:2]
    ins = refs[2 : 2 + n_in]
    whole_ref = refs[2 + n_in]
    outs = refs[3 + n_in : 3 + n_in + n_out]
    scratch = refs[3 + n_in + n_out :]
    weight_bufs, scratch = scratch[: len(plan)], scratch[len(plan) :]
    in_bufs, out_bufs = scratch[:n_in], scratch[n_in : n_in + n_out]
    weight_sem, in_sem, out_sem, own_sem = scratch[n_in + n_out : n_in + n_out + 4]
    sems = scratch[n_in + n_out + 4 :]
    me, side, cross, diag = tensor_peers()
    depth, size = part_ref.shape
    half = size // PIECES
    tiles = [(block, at) for block in (me, side) for at in range(PIECES)]
    tiles += [(block, at) for at in range(PIECES) for block in (cross, diag)]
    place = lambda block, at: pl.ds(pl.multiple_of(block * size + at * half, half), half)
    local = lambda at: pl.ds(at * half, half)

    weight_loads = [
        pltpu.make_async_copy(
            weight_ref.at[:, pl.ds(low, buf.shape[1])], buf, weight_sem.at[index]
        )
        for index, ((low, _), buf) in enumerate(zip(plan, weight_bufs))
    ]
    own = pltpu.make_async_copy(part_ref, whole_ref.at[:, columns(me, size)], own_sem)
    own.start()
    for load in weight_loads:
        load.start()

    def in_load(index, tile):
        return pltpu.make_async_copy(
            ins[index].at[place(*tiles[tile])],
            in_bufs[index].at[tile % 2],
            in_sem.at[index, tile % 2],
        )

    def out_store(index, tile):
        return pltpu.make_async_copy(
            out_bufs[index].at[tile % 2],
            outs[index].at[place(*tiles[tile])],
            out_sem.at[index, tile % 2],
        )

    for index in range(n_in):
        in_load(index, 0).start()
    greet((side, cross))
    over = [
        push(part_ref.at[:, local(at)], whole_ref.at[:, place(me, at)], sems[0:2], at, cross)
        for at in range(PIECES)
    ]
    near = [
        push(part_ref.at[:, local(at)], whole_ref.at[:, place(me, at)], sems[2:4], at, side)
        for at in range(PIECES)
    ]
    relay = [None] * PIECES
    own.wait()
    for tile, (block, at) in enumerate(tiles):
        if tile + 1 < len(tiles):
            for index in range(n_in):
                in_load(index, tile + 1).start()
        if PIECES <= tile < 2 * PIECES:
            near[at].wait_recv()
        if tile >= 2 * PIECES and tile % 2 == 0:
            over[at].wait_recv()
            relay[at] = push(
                whole_ref.at[:, place(cross, at)],
                whole_ref.at[:, place(cross, at)],
                sems[4:6],
                at,
                side,
            )
        if tile >= 2 * PIECES and tile % 2 == 1:
            relay[at].wait_recv()
        left = whole_ref[:, place(block, at)]
        products = []
        for index, (low, high) in enumerate(plan):
            if tile == 0:
                weight_loads[index].wait()
            products.append(dot_first(left, weight_bufs[index][:, : high - low]))
        for index in range(n_in):
            in_load(index, tile).wait()
        results = combine(products, [buf[tile % 2] for buf in in_bufs])
        for index, result in enumerate(results):
            if tile >= 2:
                out_store(index, tile - 2).wait()
            out_bufs[index][tile % 2] = result
            out_store(index, tile).start()
    for tile in (len(tiles) - 2, len(tiles) - 1):
        for index in range(n_out):
            out_store(index, tile).wait()
    for at in range(PIECES):
        over[at].wait_send()
        near[at].wait_send()
        relay[at].wait_send()


def turn_rows(part, weight, ins, outs, plan, combine, call_id, name, micros):
    depth, size = part.shape
    half = size // PIECES
    anywhere = pl.BlockSpec(memory_space=pl.ANY)
    return pl.pallas_call(
        functools.partial(turn_kernel, combine, plan, len(ins), len(outs)),
        name=name,
        in_specs=[pl.BlockSpec(memory_space=pltpu.VMEM)] + [anywhere] * (1 + len(ins)),
        out_specs=[pl.BlockSpec(memory_space=pltpu.VMEM)] + [anywhere] * len(outs),
        out_shape=[jax.ShapeDtypeStruct((depth, 4 * size), part.dtype)]
        + [jax.ShapeDtypeStruct((4 * size, cols), dtype) for cols, dtype in outs],
        scratch_shapes=[
            pltpu.VMEM((depth, -(-(high - low) // 128) * 128), weight.dtype) for low, high in plan
        ]
        + [pltpu.VMEM((2, half, value.shape[1]), value.dtype) for value in ins]
        + [pltpu.VMEM((2, half, cols), dtype) for cols, dtype in outs]
        + [
            pltpu.SemaphoreType.DMA((len(plan),)),
            pltpu.SemaphoreType.DMA((max(len(ins), 1), 2)),
            pltpu.SemaphoreType.DMA((len(outs), 2)),
            pltpu.SemaphoreType.DMA,
        ]
        + [pltpu.SemaphoreType.DMA((PIECES,))] * 6,
        compiler_params=pltpu.CompilerParams(
            collective_id=call_id, has_side_effects=True, vmem_limit_bytes=52 << 20
        ),
        cost_estimate=pl.CostEstimate(
            flops=0, bytes_accessed=int(micros * 3.6) << 20, transcendentals=0
        ),
    )(part, weight, *ins)


def forward_gate(products, _):
    gate, up = products
    return gate, up, (gate * jax.nn.sigmoid(gate) * up).astype(jnp.bfloat16)


def backward_gate(products, saved):
    (grad,), (gate, up) = products, saved
    sig = jax.nn.sigmoid(gate)
    grad_gate = grad * up * sig * (1.0 + gate * (1.0 - sig))
    return grad_gate.astype(jnp.bfloat16), (grad * gate * sig).astype(jnp.bfloat16)


def total_kernel(part_ref, out_ref, near_buf, own_buf, stage_buf, far_buf, low_buf, own_sem, *sems):
    me, side, cross, diag = tensor_peers()
    size, wide = low_buf.shape
    half = size // 2
    greet((side, cross))
    rows_of = lambda block, at: pl.ds(pl.multiple_of(block * size + at, half), half)
    pieces = (0, half)
    first = [
        push(part_ref.at[rows_of(diag, at)], near_buf.at[pl.ds(at, half)], sems[0:2], i, side)
        for i, at in enumerate(pieces)
    ]
    second = [
        push(part_ref.at[rows_of(side, at)], own_buf.at[pl.ds(at, half)], sems[2:4], i, side)
        for i, at in enumerate(pieces)
    ]
    third, over, near, relay = [], [], [], []
    for i, at in enumerate(pieces):
        rows = pl.ds(at, half)
        first[i].wait_recv()
        stage_buf[rows] = (part_ref[rows_of(cross, at)] + near_buf[rows]).astype(jnp.bfloat16)
        third.append(push(stage_buf.at[rows], far_buf.at[rows], sems[4:6], i, cross))
    for i, at in enumerate(pieces):
        rows = pl.ds(at, half)
        second[i].wait_recv()
        third[i].wait_recv()
        low_buf[rows] = (
            part_ref[rows_of(me, at)] + own_buf[rows] + far_buf[rows].astype(jnp.float32)
        ).astype(jnp.bfloat16)
        over.append(push(low_buf.at[rows], out_ref.at[rows_of(me, at)], sems[6:8], i, cross))
        near.append(push(low_buf.at[rows], out_ref.at[rows_of(me, at)], sems[8:10], i, side))
    own = pltpu.make_async_copy(
        low_buf, out_ref.at[pl.ds(pl.multiple_of(me * size, size), size)], own_sem
    )
    own.start()
    for i, at in enumerate(pieces):
        over[i].wait_recv()
        relay.append(
            push(out_ref.at[rows_of(cross, at)], out_ref.at[rows_of(cross, at)], sems[10:12], i, side)
        )
    own.wait()
    for i in range(2):
        for group in (first, second, third, over):
            group[i].wait_send()
        near[i].wait()
        relay[i].wait()


def total_rows(part, call_id):
    tokens, wide = part.shape
    size = tokens // 4
    whole = pl.BlockSpec(memory_space=pltpu.VMEM)
    return pl.pallas_call(
        total_kernel,
        name="total_rows",
        in_specs=[whole],
        out_specs=whole,
        out_shape=jax.ShapeDtypeStruct((tokens, wide), jnp.bfloat16),
        scratch_shapes=[
            pltpu.VMEM((size, wide), jnp.float32),
            pltpu.VMEM((size, wide), jnp.float32),
            pltpu.VMEM((size, wide), jnp.bfloat16),
            pltpu.VMEM((size, wide), jnp.bfloat16),
            pltpu.VMEM((size, wide), jnp.bfloat16),
            pltpu.SemaphoreType.DMA,
        ]
        + [pltpu.SemaphoreType.DMA((2,))] * 12,
        compiler_params=pltpu.CompilerParams(
            collective_id=call_id, has_side_effects=True, vmem_limit_bytes=32 << 20
        ),
        cost_estimate=pl.CostEstimate(flops=0, bytes_accessed=60 << 20, transcendentals=0),
    )(part)


def hello_kernel(gain_ref, count_ref, gains_ref, counts_ref, sum_buf, local_buf, *sems):
    me = lax.axis_index("tensor")
    place = lax.axis_index("dp")
    ranks, groups = local_buf.shape[0], gains_ref.shape[0]
    barrier = pltpu.get_barrier_semaphore()
    others = [{"tensor": lax.rem(me + hop, ranks)} for hop in range(1, ranks)]
    far = [{"dp": lax.rem(place + hop, groups)} for hop in range(1, groups)]
    for peer in others + far:
        pl.semaphore_signal(barrier, inc=1, device_id=peer, device_id_type=MESH)
    pl.semaphore_wait(barrier, len(others) + len(far))

    def send(src, dst, index, peer):
        copy = pltpu.make_async_remote_copy(
            src_ref=src,
            dst_ref=dst,
            send_sem=sems[0].at[index],
            recv_sem=sems[1].at[index],
            device_id=peer,
            device_id_type=MESH,
        )
        copy.start()
        return copy

    first = [send(count_ref, local_buf.at[me], i, peer) for i, peer in enumerate(others)]
    local_buf[me] = count_ref[...]
    gains_ref[place] = gain_ref[...]
    base = len(first)
    second = [send(gain_ref, gains_ref.at[place], base + i, peer) for i, peer in enumerate(far)]
    base += len(second)
    for copy in first:
        copy.wait()
    sum_buf[...] = jnp.sum(local_buf[...], axis=0)
    counts_ref[place] = sum_buf[...]
    third = [send(sum_buf, counts_ref.at[place], base + i, peer) for i, peer in enumerate(far)]
    for copy in second + third:
        copy.wait()


def hello(gains, count):
    wide = -(-gains.shape[1] // 128) * 128
    block = jnp.zeros((8, wide), jnp.float32)
    block = lax.dynamic_update_slice(block, gains.astype(jnp.float32), (0, 0))
    counts = jnp.full((8, 128), count, jnp.float32)
    groups, ranks = lax.axis_size("dp"), lax.axis_size("tensor")
    copies = ranks - 1 + 2 * (groups - 1)
    whole = pl.BlockSpec(memory_space=pltpu.VMEM)
    gains_all, counts_all = pl.pallas_call(
        hello_kernel,
        name="hello",
        in_specs=[whole, whole],
        out_specs=[whole, whole],
        out_shape=[
            jax.ShapeDtypeStruct((groups, 8, wide), jnp.float32),
            jax.ShapeDtypeStruct((groups, 8, 128), jnp.float32),
        ],
        scratch_shapes=[
            pltpu.VMEM((8, 128), jnp.float32),
            pltpu.VMEM((ranks, 8, 128), jnp.float32),
        ]
        + [pltpu.SemaphoreType.DMA((copies,))] * 2,
        compiler_params=pltpu.CompilerParams(collective_id=0, has_side_effects=True),
        cost_estimate=pl.CostEstimate(flops=0, bytes_accessed=30 << 20, transcendentals=0),
    )(block, counts)
    gains_full = gains_all[:, :4, : gains.shape[1]].transpose(1, 0, 2).reshape(4, -1)
    return gains_full, jnp.sum(counts_all[:, 0, 0])


TILE = 320


def weights_kernel(plan, *refs):
    out_ref = refs[-1]
    index = 0
    for mode, offset, size, pad in plan:
        left = refs[index][...]
        if mode == "copy":
            product = left
            index += 1
        else:
            right = refs[index + 1][...]
            product = dot_last(left, right) if mode == "flip" else dot_plain(left, right)
            index += 2
        out_ref[:, offset : offset + size] = product.astype(jnp.bfloat16)
        if pad:
            out_ref[:, offset + size : offset + size + pad] = jnp.zeros(
                (out_ref.shape[0], pad), jnp.bfloat16
            )


def weight_grads(pairs, name, micros, tight=False):
    rows = pairs[0][0].shape[0]
    tile = TILE if rows % TILE == 0 else rows
    plan, specs, operands, offset = [], [], [], 0
    for left, right, flip in pairs:
        source = left if right is None else right
        size = source.shape[0] if flip else source.shape[1]
        pad = 0 if tight else -size % 128
        mode = "copy" if right is None else "flip" if flip else "plain"
        plan.append((mode, offset, size, pad))
        offset += size + pad
        specs.append(pl.BlockSpec((tile, left.shape[1]), lambda i: (i, 0)))
        operands.append(left)
        if right is not None:
            specs.append(
                pl.BlockSpec(right.shape, lambda i: (0, 0), pipeline_mode=pl.Buffered(1))
            )
            operands.append(right)
    return pl.pallas_call(
        functools.partial(weights_kernel, plan),
        name=name,
        grid=(rows // tile,),
        in_specs=specs,
        out_specs=pl.BlockSpec((tile, offset), lambda i: (i, 0)),
        out_shape=jax.ShapeDtypeStruct((rows, offset), jnp.bfloat16),
        compiler_params=pltpu.CompilerParams(vmem_limit_bytes=52 << 20),
        cost_estimate=pl.CostEstimate(
            flops=0, bytes_accessed=int(micros * 3.6) << 20, transcendentals=0
        ),
    )(*operands)


def farewell_kernel(part_ref, out_ref, group_buf, sum_buf, rank_buf, *sems):
    me = lax.axis_index("tensor")
    place = lax.axis_index("dp")
    ranks, groups = rank_buf.shape[0], group_buf.shape[0]
    barrier = pltpu.get_barrier_semaphore()
    others = [lax.rem(me + hop, ranks) for hop in range(1, ranks)]
    far = [lax.rem(place + hop, groups) for hop in range(1, groups)]
    for peer in others:
        pl.semaphore_signal(barrier, inc=1, device_id={"tensor": peer}, device_id_type=MESH)
    for peer in far:
        pl.semaphore_signal(barrier, inc=1, device_id={"dp": peer}, device_id_type=MESH)
    pl.semaphore_wait(barrier, len(others) + len(far))

    def send(src, dst, index, peer):
        copy = pltpu.make_async_remote_copy(
            src_ref=src,
            dst_ref=dst,
            send_sem=sems[0].at[index],
            recv_sem=sems[1].at[index],
            device_id=peer,
            device_id_type=MESH,
        )
        copy.start()
        return copy

    first = [
        send(part_ref.at[peer], group_buf.at[place], i, {"dp": peer}) for i, peer in enumerate(far)
    ]
    group_buf[place] = part_ref[place]
    for copy in first:
        copy.wait()
    sum_buf[...] = jnp.sum(group_buf[...], axis=0)
    rank_buf[me] = sum_buf[...]
    second = [
        send(sum_buf, rank_buf.at[me], len(first) + i, {"tensor": peer})
        for i, peer in enumerate(others)
    ]
    for copy in second:
        copy.wait()
    out_ref[...] = jnp.sum(rank_buf[...], axis=0)


def farewell(grads):
    groups, ranks = lax.axis_size("dp"), lax.axis_size("tensor")
    kinds, total = grads.shape
    own = total // groups
    wide = -(-own // 128) * 128
    parts = jnp.pad(
        grads.reshape(kinds, groups, own).transpose(1, 0, 2),
        ((0, 0), (0, 8 - kinds), (0, wide - own)),
    )
    whole = pl.BlockSpec(memory_space=pltpu.VMEM)
    summed = pl.pallas_call(
        farewell_kernel,
        name="farewell",
        in_specs=[whole],
        out_specs=whole,
        out_shape=jax.ShapeDtypeStruct((8, wide), jnp.float32),
        scratch_shapes=[
            pltpu.VMEM((groups, 8, wide), jnp.float32),
            pltpu.VMEM((8, wide), jnp.float32),
            pltpu.VMEM((ranks, 8, wide), jnp.float32),
        ]
        + [pltpu.SemaphoreType.DMA((groups + ranks - 2,))] * 2,
        compiler_params=pltpu.CompilerParams(
            collective_id=4, has_side_effects=True, vmem_limit_bytes=4 << 20
        ),
        cost_estimate=pl.CostEstimate(flops=0, bytes_accessed=40 << 20, transcendentals=0),
    )(parts)
    return summed[:kinds, :own]


def stack_kernel(part_ref, whole_ref, own_sem, *sems):
    me, side, cross, diag = tensor_peers()
    step = part_ref.shape[1] // 2
    greet((side, cross))
    own = pltpu.make_async_copy(part_ref, whole_ref.at[me], own_sem)
    own.start()
    cols = [pl.ds(0, step), pl.ds(step, step)]
    over = [
        push(part_ref.at[:, at], whole_ref.at[me, :, at], sems[0:2], i, cross)
        for i, at in enumerate(cols)
    ]
    near = [
        push(part_ref.at[:, at], whole_ref.at[me, :, at], sems[2:4], i, side)
        for i, at in enumerate(cols)
    ]
    relay = []
    for i, at in enumerate(cols):
        over[i].wait_recv()
        relay.append(
            push(whole_ref.at[cross, :, at], whole_ref.at[cross, :, at], sems[4:6], i, side)
        )
    own.wait()
    for i in range(2):
        over[i].wait_send()
        near[i].wait()
        relay[i].wait()


def gather_stack(part, call_id):
    return pl.pallas_call(
        stack_kernel,
        name="gather_stack",
        in_specs=[pl.BlockSpec(memory_space=pl.ANY)],
        out_specs=pl.BlockSpec(memory_space=pl.ANY),
        out_shape=jax.ShapeDtypeStruct((4,) + part.shape, part.dtype),
        scratch_shapes=[pltpu.SemaphoreType.DMA] + [pltpu.SemaphoreType.DMA((2,))] * 6,
        compiler_params=pltpu.CompilerParams(
            collective_id=call_id, has_side_effects=True, vmem_limit_bytes=1 << 20
        ),
        cost_estimate=pl.CostEstimate(flops=0, bytes_accessed=60 << 20, transcendentals=0),
    )(part)


def product_kernel(plan, leads, right_flips, *refs):
    left_count = len(leads)
    lefts = [ref if lead is None else ref.at[lead] for ref, (lead, _) in zip(refs, leads)]
    right_count = len(right_flips)
    rights = refs[left_count : left_count + right_count]
    out_ref = refs[left_count + right_count]
    scratch = refs[left_count + right_count + 1 :]
    left_bufs = scratch[:left_count]
    right_bufs = scratch[left_count : left_count + right_count]
    diag_buf, side_buf, near_buf, own_buf, stage_buf, far_buf, left_sem, right_sem = scratch[
        left_count + right_count : left_count + right_count + 8
    ]
    sems = scratch[left_count + right_count + 8 :]
    me, side, cross, diag = tensor_peers()
    depth, size = out_ref.shape
    step = depth // PIECES
    rows_of = lambda piece: pl.ds(pl.multiple_of(piece * step, 16), step)

    def left_load(index, piece):
        rows = rows_of(piece)
        start = leads[index][1]
        source = lefts[index].at[rows]
        if start is not None:
            source = lefts[index].at[rows, pl.ds(start, left_bufs[index].shape[1])]
        return pltpu.make_async_copy(source, left_bufs[index].at[rows], left_sem.at[index, piece])

    def right_load(index, order, block):
        at = columns(block, size)
        view = (slice(None), at) if right_flips[index] else (at,)
        return pltpu.make_async_copy(
            rights[index].at[view], right_bufs[index].at[view], right_sem.at[index, order]
        )

    turns = (diag, cross, side, me)
    for order, block in enumerate(turns):
        for index in range(right_count):
            right_load(index, order, block).start()
        for index in range(left_count):
            left_load(index, order).start()
    greet((side, cross))

    def product(piece, block):
        rows, at = rows_of(piece), columns(block, size)
        total = jnp.zeros((step, size), jnp.float32)
        for left, low_col, high_col, right in plan:
            weight = left_bufs[left][rows, low_col:high_col]
            if right_flips[right]:
                total += dot_plain(weight, right_bufs[right][:, at])
            else:
                total += dot_last(weight, right_bufs[right][at, :])
        return total

    def transfer(src, dst, group, piece, peer):
        rows = rows_of(piece)
        return pltpu.make_async_remote_copy(
            src_ref=src.at[rows],
            dst_ref=dst.at[rows],
            send_sem=sems[2 * group].at[piece],
            recv_sem=sems[2 * group + 1].at[piece],
            device_id={"tensor": peer},
            device_id_type=MESH,
        )

    first = lambda piece: transfer(diag_buf, near_buf, 0, piece, side)
    second = lambda piece: transfer(side_buf, own_buf, 1, piece, side)
    third = lambda piece: transfer(stage_buf, far_buf, 2, piece, cross)

    for order in (0, 1):
        for index in range(right_count):
            right_load(index, order, turns[order]).wait()

    def outward(piece, carry):
        rows = rows_of(piece)
        for index in range(left_count):
            left_load(index, piece).wait()
        diag_buf[rows] = product(piece, diag).astype(jnp.bfloat16)
        first(piece).start()
        kept = product(piece, cross)
        first(piece).wait_recv()
        stage_buf[rows] = (kept + near_buf[rows].astype(jnp.float32)).astype(jnp.bfloat16)
        third(piece).start()
        return carry

    lax.fori_loop(0, PIECES, outward, 0)
    for order in (2, 3):
        for index in range(right_count):
            right_load(index, order, turns[order]).wait()

    def inward(piece, carry):
        rows = rows_of(piece)
        side_buf[rows] = product(piece, side).astype(jnp.bfloat16)
        second(piece).start()
        out_ref[rows] = product(piece, me)
        return carry

    lax.fori_loop(0, PIECES, inward, 0)

    def finish(piece, carry):
        rows = rows_of(piece)
        second(piece).wait_recv()
        third(piece).wait_recv()
        out_ref[rows] += own_buf[rows].astype(jnp.float32) + far_buf[rows].astype(jnp.float32)
        first(piece).wait_send()
        second(piece).wait_send()
        third(piece).wait_send()
        return carry

    lax.fori_loop(0, PIECES, finish, 0)


def product_reduce(lefts, rights, plan, call_id, name, micros):
    leads = tuple((lead, start) for _, lead, start, _ in lefts)
    widths = [size for _, _, _, size in lefts]
    lefts = [left for left, _, _, _ in lefts]
    depth = lefts[0].shape[-2]
    right_flips = tuple(flip for _, flip in rights)
    tokens = rights[0][0].shape[1] if right_flips[0] else rights[0][0].shape[0]
    size = tokens // 4
    anywhere = pl.BlockSpec(memory_space=pl.ANY)
    return pl.pallas_call(
        functools.partial(product_kernel, plan, leads, right_flips),
        name=name,
        in_specs=[anywhere] * (len(lefts) + len(rights)),
        out_specs=pl.BlockSpec(memory_space=pltpu.VMEM),
        out_shape=jax.ShapeDtypeStruct((depth, size), jnp.float32),
        scratch_shapes=[pltpu.VMEM((depth, size), jnp.bfloat16) for size in widths]
        + [pltpu.VMEM(right.shape, right.dtype) for right, _ in rights]
        + [pltpu.VMEM((depth, size), jnp.bfloat16)] * 6
        + [
            pltpu.SemaphoreType.DMA((len(lefts), PIECES)),
            pltpu.SemaphoreType.DMA((len(rights), 4)),
        ]
        + [pltpu.SemaphoreType.DMA((PIECES,))] * 6,
        compiler_params=pltpu.CompilerParams(
            collective_id=call_id, has_side_effects=True, vmem_limit_bytes=48 << 20
        ),
        cost_estimate=pl.CostEstimate(
            flops=0, bytes_accessed=int(micros * 3.6) << 20, transcendentals=0
        ),
    )(*lefts, *[right for right, _ in rights])


def spread_kernel(part_ref, out_ref, own_sem, *sems):
    rank, place = lax.axis_index("tensor"), lax.axis_index("dp")
    share = out_ref.shape[0]
    target, slot = lax.div(place, share), lax.rem(place, share)
    replica = lax.rem(place, 4)
    barrier = pltpu.get_barrier_semaphore()
    for index in range(share):
        source = rank * share + index

        @pl.when((source != place) | (replica != rank))
        def _():
            pl.semaphore_signal(
                barrier,
                inc=1,
                device_id={"dp": source, "tensor": replica},
                device_id_type=MESH,
            )

    goals = [(rank + 4 * index != place) | (target != rank) for index in range(share)]
    pl.semaphore_wait(barrier, sum(goal.astype(jnp.int32) for goal in goals))

    def outgoing(index):
        goal = rank + 4 * index
        copy = pltpu.make_async_remote_copy(
            src_ref=part_ref,
            dst_ref=out_ref.at[slot],
            send_sem=sems[0].at[index],
            recv_sem=sems[1].at[slot],
            device_id={"dp": goal, "tensor": target},
            device_id_type=MESH,
        )
        return copy, (goal != place) | (target != rank)

    own = pltpu.make_async_copy(part_ref, out_ref.at[slot], own_sem)
    for index in range(share):
        copy, away = outgoing(index)
        pl.when(away)(copy.start)
        pl.when(jnp.logical_not(away))(own.start)
    for index in range(share):
        copy, away = outgoing(index)
        pl.when(away)(copy.wait_send)
        pl.when(jnp.logical_not(away))(own.wait)
        source = rank * share + index
        arrival = pltpu.make_async_remote_copy(
            src_ref=part_ref,
            dst_ref=out_ref.at[index],
            send_sem=sems[0].at[index],
            recv_sem=sems[1].at[index],
            device_id={"dp": source, "tensor": replica},
            device_id_type=MESH,
        )
        pl.when((source != place) | (replica != rank))(arrival.wait_recv)


def inner_spread(part):
    groups, ranks = lax.axis_size("dp"), lax.axis_size("tensor")
    share = groups // ranks
    rows, cols = part.shape
    padded = jnp.pad(part, ((0, -rows % 16), (0, -cols % 128)))
    whole = pl.BlockSpec(memory_space=pltpu.VMEM)
    spread = pl.pallas_call(
        spread_kernel,
        name="inner_spread",
        in_specs=[whole],
        out_specs=whole,
        out_shape=jax.ShapeDtypeStruct((share,) + padded.shape, part.dtype),
        scratch_shapes=[pltpu.SemaphoreType.DMA] + [pltpu.SemaphoreType.DMA((share,))] * 2,
        compiler_params=pltpu.CompilerParams(
            collective_id=12, has_side_effects=True, vmem_limit_bytes=8 << 20
        ),
        cost_estimate=pl.CostEstimate(flops=0, bytes_accessed=40 << 20, transcendentals=0),
    )(padded)
    return spread[:, :rows, :cols].reshape(share * rows, cols)


def final_kernel(starts, last_ref, whole_ref, owned_ref, own_sem, *sems):
    part_ref = last_ref.at[:, pl.ds(starts[0], whole_ref.shape[2])]
    inner_ref = last_ref.at[:, pl.ds(starts[1], owned_ref.shape[2])]
    me, side, cross, diag = tensor_peers()
    place = lax.axis_index("dp")
    ranks = owned_ref.shape[0]
    share = lax.axis_size("dp") // ranks
    owner, slot = me * share + lax.div(place, ranks), lax.rem(place, ranks)
    source_rank, source_base = lax.div(place, share), ranks * lax.rem(place, share)
    barrier = pltpu.get_barrier_semaphore()
    for peer in (side, cross):
        pl.semaphore_signal(barrier, inc=1, device_id={"tensor": peer}, device_id_type=MESH)
    for index in range(ranks):
        source = source_base + index

        @pl.when((source != place) | (source_rank != me))
        def _():
            pl.semaphore_signal(
                barrier,
                inc=1,
                device_id={"dp": source, "tensor": source_rank},
                device_id_type=MESH,
            )

    goals = [(owner != place) | (me != index) for index in range(ranks)]
    pl.semaphore_wait(barrier, 2 + sum(goal.astype(jnp.int32) for goal in goals))

    span = whole_ref.shape[2]
    step = -(-span // 256) * 128
    own = pltpu.make_async_copy(part_ref, whole_ref.at[me], own_sem.at[0])
    own.start()
    cols = [pl.ds(0, step), pl.ds(step, span - step)]
    shift = lambda at: pl.ds(starts[0] + at.start, at.size)
    over = [
        push(last_ref.at[:, shift(at)], whole_ref.at[me, :, at], sems[0:2], i, cross)
        for i, at in enumerate(cols)
    ]
    near = [
        push(last_ref.at[:, shift(at)], whole_ref.at[me, :, at], sems[2:4], i, side)
        for i, at in enumerate(cols)
    ]
    kept = pltpu.make_async_copy(inner_ref, owned_ref.at[slot], own_sem.at[1])

    def outgoing(index):
        copy = pltpu.make_async_remote_copy(
            src_ref=inner_ref,
            dst_ref=owned_ref.at[slot],
            send_sem=sems[6].at[index],
            recv_sem=sems[7].at[slot],
            device_id={"dp": owner, "tensor": index},
            device_id_type=MESH,
        )
        return copy, (owner != place) | (me != index)

    for index in range(ranks):
        copy, away = outgoing(index)
        pl.when(away)(copy.start)
        pl.when(jnp.logical_not(away))(kept.start)
    relay = []
    for i, at in enumerate(cols):
        over[i].wait_recv()
        relay.append(
            push(whole_ref.at[cross, :, at], whole_ref.at[cross, :, at], sems[4:6], i, side)
        )
    own.wait()
    for i in range(2):
        over[i].wait_send()
        near[i].wait()
        relay[i].wait()
    for index in range(ranks):
        copy, away = outgoing(index)
        pl.when(away)(copy.wait_send)
        pl.when(jnp.logical_not(away))(kept.wait)
        source = source_base + index
        arrival = pltpu.make_async_remote_copy(
            src_ref=inner_ref,
            dst_ref=owned_ref.at[index],
            send_sem=sems[6].at[index],
            recv_sem=sems[7].at[index],
            device_id={"dp": source, "tensor": source_rank},
            device_id_type=MESH,
        )
        pl.when((source != place) | (source_rank != me))(arrival.wait_recv)


def gather_final(last, start, middle):
    anywhere = pl.BlockSpec(memory_space=pl.ANY)
    rows, total = last.shape
    return pl.pallas_call(
        functools.partial(final_kernel, (start, middle)),
        name="gather_final",
        in_specs=[anywhere],
        out_specs=[anywhere] * 2,
        out_shape=[
            jax.ShapeDtypeStruct((4, rows, middle - start), last.dtype),
            jax.ShapeDtypeStruct((4, rows, total - middle), last.dtype),
        ],
        scratch_shapes=[pltpu.SemaphoreType.DMA((2,))]
        + [pltpu.SemaphoreType.DMA((2,))] * 6
        + [pltpu.SemaphoreType.DMA((4,))] * 2,
        compiler_params=pltpu.CompilerParams(
            collective_id=9, has_side_effects=True, vmem_limit_bytes=1 << 20
        ),
        cost_estimate=pl.CostEstimate(flops=0, bytes_accessed=60 << 20, transcendentals=0),
    )(last)


BQ = 256
BK = 256


def attn_bias(q_base, k_base, segq_row, segk_col):
    q_pos = q_base + lax.broadcasted_iota(jnp.int32, (BK, BQ), 1)
    k_pos = k_base + lax.broadcasted_iota(jnp.int32, (BK, BQ), 0)
    offset = q_pos - k_pos
    allowed = (offset >= 0) & (offset < WINDOW) & (segk_col == segq_row)
    return jnp.where(allowed, 0.0, MASKED)


def flip_rows(cols_ref, rows_scr):
    for at in range(0, rows_scr.shape[0], BK):
        block = cols_ref[:, at : at + BK].astype(jnp.float32)
        rows_scr[at : at + BK] = jnp.transpose(block).astype(jnp.bfloat16)


def attn_fwd_kernel(first_ref, qt_ref, kt_ref, vt_ref, segr_ref, mask_ref, ot_ref, lse_ref,
                    max_scr, sum_scr, acc_scr, k_scr):
    heads = qt_ref.shape[0] // HEAD
    block = pl.program_id(1)
    q_base = block * BQ

    @pl.when(block == 0)
    def _():
        flip_rows(kt_ref, k_scr)

    max_scr[...] = jnp.full_like(max_scr, MASKED)
    sum_scr[...] = jnp.zeros_like(sum_scr)
    acc_scr[...] = jnp.zeros_like(acc_scr)
    segq_row = segr_ref[0:1, :]

    def body(j, carry):
        k_base = pl.multiple_of(j * BK, BK)
        rows = pl.ds(k_base, BK)
        bias = attn_bias(q_base, k_base, segq_row, mask_ref[rows, 4:5])
        k_blk = k_scr[rows, :]
        v_blk = vt_ref[:, rows]
        for head in range(heads):
            cols = slice(head * HEAD, (head + 1) * HEAD)
            scores = dot_plain(k_blk, qt_ref[cols, :]) * 0.125 + bias
            old_max = max_scr[head : head + 1]
            new_max = jnp.maximum(old_max, jnp.max(scores, axis=0, keepdims=True))
            expo = jnp.exp(scores - new_max)
            ratio = jnp.exp(old_max - new_max)
            max_scr[head : head + 1] = new_max
            sum_scr[head : head + 1] = sum_scr[head : head + 1] * ratio + jnp.sum(
                expo, axis=0, keepdims=True
            )
            acc_scr[cols] = acc_scr[cols] * ratio + dot_plain(v_blk, expo.astype(jnp.bfloat16))
        return carry

    start = first_ref[pl.program_id(0) * pl.num_programs(1) + block]
    lax.fori_loop(start, block + 1, body, 0)
    for head in range(heads):
        cols = slice(head * HEAD, (head + 1) * HEAD)
        total = jnp.maximum(sum_scr[head : head + 1], 1e-30)
        ot_ref[cols] = (acc_scr[cols] / total).astype(jnp.bfloat16)
        lse_ref[0, head : head + 1] = max_scr[head : head + 1] + jnp.log(total)


def attn_specs(slots, group, tokens):
    queries = pl.BlockSpec((group, BQ), lambda s, i, f: (s, i))
    base = slots * group // HEAD
    keys = pl.BlockSpec((HEAD, tokens), lambda s, i, f: (base + s, 0))
    values = pl.BlockSpec((HEAD, tokens), lambda s, i, f: (base + slots + s, 0))
    stats = pl.BlockSpec((1, 8, BQ), lambda s, i, f: (s, 0, i))
    seg_row = pl.BlockSpec((1, BQ), lambda s, i, f: (0, i))
    seg_col = pl.BlockSpec((tokens, 8), lambda s, i, f: (0, 0))
    return queries, keys, values, stats, seg_row, seg_col


def attn_forward(first, qkv_t, seg_row, masks, slots):
    tokens = qkv_t.shape[1]
    group = qkv_t.shape[0] // slots - 2 * HEAD
    queries, keys, values, stats, segr, segc = attn_specs(slots, group, tokens)
    return pl.pallas_call(
        attn_fwd_kernel,
        name="attn_fwd",
        grid_spec=pltpu.PrefetchScalarGridSpec(
            num_scalar_prefetch=1,
            grid=(slots, tokens // BQ),
            in_specs=[queries, keys, values, segr, segc],
            out_specs=[queries, stats],
            scratch_shapes=[
                pltpu.VMEM((8, BQ), jnp.float32),
                pltpu.VMEM((8, BQ), jnp.float32),
                pltpu.VMEM((group, BQ), jnp.float32),
                pltpu.VMEM((tokens, HEAD), jnp.bfloat16),
            ],
        ),
        out_shape=[
            jax.ShapeDtypeStruct((slots * group, tokens), jnp.bfloat16),
            jax.ShapeDtypeStruct((slots, 8, tokens), jnp.float32),
        ],
        compiler_params=pltpu.CompilerParams(vmem_limit_bytes=32 << 20),
        cost_estimate=pl.CostEstimate(flops=0, bytes_accessed=150 << 20, transcendentals=0),
    )(first, qkv_t, qkv_t, qkv_t, seg_row, masks)


def attn_bwd_kernel(first_ref, qt_ref, dot_ref, ot_ref, lse_ref, kt_ref, vt_ref, segr_ref, mask_ref,
                    grad_ref, delta_scr, acc_scr, q_scr, do_scr, k_scr, v_scr, gk_scr, gv_scr):
    group = qt_ref.shape[0]
    heads = group // HEAD
    slot = pl.program_id(0)
    slots = pl.num_programs(0)
    block = pl.program_id(1)
    q_base = pl.multiple_of(block * BQ, BQ)

    @pl.when(block == 0)
    def _():
        flip_rows(kt_ref, k_scr)
        flip_rows(vt_ref, v_scr)
        gk_scr[...] = jnp.zeros_like(gk_scr)
        gv_scr[...] = jnp.zeros_like(gv_scr)

    acc_scr[...] = jnp.zeros_like(acc_scr)
    start = first_ref[slot * pl.num_programs(1) + block]

    @pl.when(start <= block)
    def _():
        for head in range(heads):
            cols = slice(head * HEAD, (head + 1) * HEAD)
            grad_out = dot_ref[cols].astype(jnp.float32)
            delta_scr[head : head + 1] = jnp.sum(
                grad_out * ot_ref[cols].astype(jnp.float32), axis=0, keepdims=True
            )
            q_scr[head] = jnp.transpose(qt_ref[cols].astype(jnp.float32)).astype(jnp.bfloat16)
            do_scr[head] = jnp.transpose(grad_out).astype(jnp.bfloat16)

    segq_row = segr_ref[0:1, :]

    def body(j, carry):
        k_base = pl.multiple_of(j * BK, BK)
        rows = pl.ds(k_base, BK)
        bias = attn_bias(q_base, k_base, segq_row, mask_ref[rows, 4:5])
        k_blk = k_scr[rows, :]
        kt_blk = kt_ref[:, rows]
        v_blk = v_scr[rows, :]
        gk = jnp.zeros((BK, HEAD), jnp.float32)
        gv = jnp.zeros((BK, HEAD), jnp.float32)
        for head in range(heads):
            cols = slice(head * HEAD, (head + 1) * HEAD)
            scores = dot_plain(k_blk, qt_ref[cols, :]) * 0.125 + bias
            probs = jnp.exp(scores - lse_ref[0, head : head + 1])
            grad_p = dot_plain(v_blk, dot_ref[cols, :])
            grad_s = (probs * (grad_p - delta_scr[head : head + 1])).astype(jnp.bfloat16)
            gv += dot_plain(probs.astype(jnp.bfloat16), do_scr[head])
            gk += dot_plain(grad_s, q_scr[head])
            acc_scr[cols] += dot_plain(kt_blk, grad_s)
        gk_scr[rows, :] += gk * 0.125
        gv_scr[rows, :] += gv
        return carry

    lax.fori_loop(start, block + 1, body, 0)
    grad_ref[pl.ds(pl.multiple_of(slot * group, HEAD), group), pl.ds(q_base, BQ)] = (
        acc_scr[...] * 0.125
    ).astype(jnp.bfloat16)

    @pl.when(block == pl.num_programs(1) - 1)
    def _():
        key_rows = pl.ds(pl.multiple_of(slots * group + slot * HEAD, HEAD), HEAD)
        value_rows = pl.ds(pl.multiple_of(slots * group + (slots + slot) * HEAD, HEAD), HEAD)
        for at in range(0, gk_scr.shape[0], BK):
            cols = pl.ds(at, BK)
            grad_ref[key_rows, cols] = jnp.transpose(gk_scr[at : at + BK]).astype(jnp.bfloat16)
            grad_ref[value_rows, cols] = jnp.transpose(gv_scr[at : at + BK]).astype(jnp.bfloat16)


def attn_backward(first, qkv_t, do_t, o_t, lse, seg_row, masks, slots):
    width, tokens = qkv_t.shape
    group = width // slots - 2 * HEAD
    queries, keys, values, stats, segr, segc = attn_specs(slots, group, tokens)
    return pl.pallas_call(
        attn_bwd_kernel,
        name="attn_bwd",
        grid_spec=pltpu.PrefetchScalarGridSpec(
            num_scalar_prefetch=1,
            grid=(slots, tokens // BQ),
            in_specs=[queries, queries, queries, stats, keys, values, segr, segc],
            out_specs=pl.BlockSpec((width, tokens), lambda s, i, f: (0, 0)),
            scratch_shapes=[
                pltpu.VMEM((8, BQ), jnp.float32),
                pltpu.VMEM((group, BQ), jnp.float32),
                pltpu.VMEM((group // HEAD, BQ, HEAD), jnp.bfloat16),
                pltpu.VMEM((group // HEAD, BQ, HEAD), jnp.bfloat16),
                pltpu.VMEM((tokens, HEAD), jnp.bfloat16),
                pltpu.VMEM((tokens, HEAD), jnp.bfloat16),
                pltpu.VMEM((tokens, HEAD), jnp.float32),
                pltpu.VMEM((tokens, HEAD), jnp.float32),
            ],
        ),
        out_shape=jax.ShapeDtypeStruct((width, tokens), jnp.bfloat16),
        compiler_params=pltpu.CompilerParams(vmem_limit_bytes=40 << 20),
        cost_estimate=pl.CostEstimate(flops=0, bytes_accessed=160 << 20, transcendentals=0),
    )(first, qkv_t, do_t, o_t, lse, qkv_t, qkv_t, seg_row, masks)


def first_blocks(segs_flat):
    tokens = segs_flat.shape[0]
    starts = segs_flat[::BQ]
    positions = jnp.arange(tokens // BQ, dtype=jnp.int32) * BQ
    seg_start = jnp.sum((segs_flat[None, :] < starts[:, None]).astype(jnp.int32), axis=1)
    return jnp.maximum(jnp.maximum(seg_start, positions - WINDOW + 1), 0) // BK


def conv_rows(x_in, conv_w, conv_b, segs_grid):
    seq_count, seq_len = segs_grid.shape
    width = x_in.shape[1]
    grid = x_in.reshape(seq_count, seq_len, width)
    pad_x = jnp.concatenate([jnp.zeros((seq_count, CONV - 1, width), jnp.float32), grid], axis=1)
    pad_seg = jnp.concatenate([jnp.full((seq_count, CONV - 1), -1, jnp.int32), segs_grid], axis=1)
    total = jnp.zeros((seq_count, seq_len, width), jnp.float32) + conv_b
    for tap in range(CONV):
        same = (pad_seg[:, tap : tap + seq_len] == segs_grid).astype(jnp.float32)
        total = total + conv_w[tap] * pad_x[:, tap : tap + seq_len] * same[:, :, None]
    return jax.nn.silu(total).reshape(seq_count * seq_len, width)


CHUNK = 64
ROWS = 256
RANGE = 120.0
LANES = 256


def spans(width, size):
    return [(at, min(at + size, width)) for at in range(0, width, size)]


def softplus_parts(pre):
    small = jnp.exp(-jnp.abs(pre))
    step = jnp.maximum(pre, 0.0) + jnp.log1p(small)
    slope = jnp.where(pre >= 0.0, 1.0, small) / (1.0 + small)
    return step, slope


def split_sum(tri, values):
    high = values.astype(jnp.bfloat16)
    low = (values - high.astype(jnp.float32)).astype(jnp.bfloat16)
    return dot_plain(tri, high) + dot_plain(tri, low)


def tri_matrix(size, upper):
    row = lax.broadcasted_iota(jnp.int32, (size, size), 0)
    col = lax.broadcasted_iota(jnp.int32, (size, size), 1)
    order = (col >= row) if upper else (row >= col)
    return order & (lax.div(row, CHUNK) == lax.div(col, CHUNK))


def scan_setup(dbl_ref, dtw_ref, vec_ref, step_scr, cum_scr, slope_scr):
    width = dtw_ref.shape[1]
    tri = tri_matrix(ROWS, False).astype(jnp.bfloat16)
    dt_low = dbl_ref[:, :RANK]
    lowest = jnp.zeros((), jnp.float32)
    for lo, hi in spans(width, LANES):
        pre = dot_plain(dt_low, dtw_ref[:, lo:hi]) + vec_ref[0:1, lo:hi]
        step, slope = softplus_parts(pre)
        cum = split_sum(tri, -step * jnp.exp(vec_ref[1:2, lo:hi]))
        step_scr[:, lo:hi] = step
        cum_scr[:, lo:hi] = cum
        if slope_scr is not None:
            slope_scr[:, lo:hi] = slope
        least = jnp.zeros((1, hi - lo), jnp.float32)
        for at in range(0, ROWS, CHUNK):
            least = jnp.minimum(least, cum[at + CHUNK - 1 : at + CHUNK])
        lowest = jnp.minimum(lowest, jnp.min(least))
    return lowest


def chunk_maps(dbl_ref, mask_ref, segr_ref, at):
    rows = slice(at, at + CHUNK)
    b_map = dbl_ref[rows, 128 : 128 + STATE]
    c_map = dbl_ref[rows, 128 + STATE : 128 + 2 * STATE]
    linked = mask_ref[rows, 0:1]
    tail = mask_ref[rows, 1:2]
    keep = mask_ref[at + CHUNK - 1 : at + CHUNK, 2:3]
    allowed = tri_matrix(CHUNK, False) & (mask_ref[rows, 4:5] == segr_ref[0:1, rows])
    gram = jnp.where(allowed, dot_last(c_map, b_map), 0.0)
    c_link = c_map.astype(jnp.float32) * linked
    b_tail = b_map.astype(jnp.float32) * tail
    return b_map, c_map, linked, tail, keep, allowed, gram, c_link, b_tail


def mixer(square, side, bottom):
    corner = jnp.zeros((STATE, STATE), jnp.float32)
    top = jnp.concatenate([square, side], axis=1)
    low = jnp.concatenate([jnp.transpose(bottom), corner], axis=1)
    return jnp.concatenate([top, low], axis=0).astype(jnp.bfloat16)


def token_column(block, lane_index):
    lanes = lax.broadcasted_iota(jnp.int32, block.shape, 1)
    return jnp.sum(jnp.where(lanes == lane_index, block, 0.0), axis=1, keepdims=True)


def scan_fwd_kernel(
    xa_ref, z_ref, dbl_ref, mask_ref, segr_ref, dtw_ref, vec_ref,
    out_ref, hsave_ref, h_scr, step_scr, cum_scr, y_scr,
):
    width = xa_ref.shape[1]

    @pl.when(pl.program_id(0) == 0)
    def _():
        h_scr[...] = jnp.zeros_like(h_scr)

    lowest = scan_setup(dbl_ref, dtw_ref, vec_ref, step_scr, cum_scr, None)

    @pl.when(lowest >= -RANGE)
    def _():
        for index, at in enumerate(range(0, ROWS, CHUNK)):
            rows = slice(at, at + CHUNK)
            _, _, _, _, keep, _, gram, c_link, b_tail = chunk_maps(dbl_ref, mask_ref, segr_ref, at)
            forward = mixer(gram, c_link, b_tail)
            for lo, hi in spans(width, LANES):
                cum = cum_scr[rows, lo:hi]
                half = 0.5 * cum[CHUNK - 1 : CHUNK]
                gap = cum - half
                rise = jnp.exp(half)
                h_old = h_scr[:, lo:hi]
                hsave_ref[index, :, lo:hi] = h_old
                x_f = xa_ref[rows, lo:hi].astype(jnp.float32)
                sources = jnp.concatenate(
                    [jnp.exp(-gap) * (step_scr[rows, lo:hi] * x_f), rise * h_old], axis=0
                ).astype(jnp.bfloat16)
                mixed = dot_plain(forward, sources)
                total = jnp.exp(gap) * mixed[:CHUNK] + vec_ref[2:3, lo:hi] * x_f
                out_ref[rows, lo:hi] = (total * jax.nn.silu(z_ref[rows, lo:hi])).astype(
                    jnp.bfloat16
                )
                h_scr[:, lo:hi] = rise * mixed[CHUNK:] + (rise * rise * keep) * h_old

    @pl.when(lowest < -RANGE)
    def _():
        for index, at in enumerate(range(0, ROWS, CHUNK)):
            rows = slice(at, at + CHUNK)
            hsave_ref[index] = h_scr[...]
            b_cols = jnp.transpose(dbl_ref[rows, 128 : 128 + STATE].astype(jnp.float32))
            c_cols = jnp.transpose(dbl_ref[rows, 128 + STATE : 128 + 2 * STATE].astype(jnp.float32))
            y_scr[...] = xa_ref[rows].astype(jnp.float32)
            rate = jnp.exp(vec_ref[1:2])

            def token(t, carry):
                step = step_scr[pl.ds(at + t, 1)]
                keep = mask_ref[pl.ds(at + t, 1)][:, 3:4]
                state = (jnp.exp(-step * rate) * keep) * h_scr[...] + token_column(b_cols, t) * (
                    step * y_scr[pl.ds(t, 1)]
                )
                h_scr[...] = state
                y_scr[pl.ds(t, 1)] = (
                    jnp.sum(state * token_column(c_cols, t), axis=0, keepdims=True)
                    + vec_ref[2:3] * y_scr[pl.ds(t, 1)]
                )
                return carry

            lax.fori_loop(0, CHUNK, token, 0)
            out_ref[rows] = (y_scr[...] * jax.nn.silu(z_ref[rows])).astype(jnp.bfloat16)


def scan_bwd_kernel(
    xa_ref, z_ref, dbl_ref, mask_ref, segr_ref, dtw_ref, vec_ref, hsave_ref, gs_ref,
    gz_ref, gx_ref, gdbl_ref, gdtw_ref, gvec_ref,
    g_scr, step_scr, cum_scr, slope_scr, gl_scr, gu_scr, gpre_scr, hall_scr, y_scr,
):
    width = xa_ref.shape[1]

    @pl.when(pl.program_id(0) == 0)
    def _():
        g_scr[...] = jnp.zeros_like(g_scr)
        gdtw_ref[...] = jnp.zeros_like(gdtw_ref)
        gvec_ref[...] = jnp.zeros_like(gvec_ref)

    lowest = scan_setup(dbl_ref, dtw_ref, vec_ref, step_scr, cum_scr, slope_scr)
    count = ROWS // CHUNK

    @pl.when(lowest >= -RANGE)
    def _():
        for index in range(count - 1, -1, -1):
            at = index * CHUNK
            rows = slice(at, at + CHUNK)
            b_map, c_map, linked, tail, keep, allowed, gram, c_link, b_tail = chunk_maps(
                dbl_ref, mask_ref, segr_ref, at
            )
            forward = mixer(gram, c_link, b_tail)
            reverse = mixer(jnp.transpose(gram), b_tail, c_link)
            cross = jnp.zeros((CHUNK + STATE, CHUNK + STATE), jnp.float32)
            for lo, hi in spans(width, LANES):
                cum = cum_scr[rows, lo:hi]
                half = 0.5 * cum[CHUNK - 1 : CHUNK]
                gap = cum - half
                fall = jnp.exp(gap)
                grow = jnp.exp(-gap)
                rise = jnp.exp(half)
                h_old = hsave_ref[index, :, lo:hi]
                g_new = g_scr[:, lo:hi]
                step = step_scr[rows, lo:hi]
                x_f = xa_ref[rows, lo:hi].astype(jnp.float32)
                skip = vec_ref[2:3, lo:hi]
                sources = jnp.concatenate([grow * (step * x_f), rise * h_old], axis=0).astype(
                    jnp.bfloat16
                )
                mixed = dot_plain(forward, sources)
                inner = mixed[:CHUNK]
                z_f = z_ref[rows, lo:hi]
                grad = gs_ref[rows, lo:hi]
                sig = jax.nn.sigmoid(z_f)
                gated = z_f * sig
                gy = grad * gated
                gz_ref[rows, lo:hi] = (
                    grad * (fall * inner + skip * x_f) * (sig + gated * (1.0 - sig))
                ).astype(jnp.bfloat16)
                sinks = jnp.concatenate([fall * gy, rise * g_new], axis=0).astype(jnp.bfloat16)
                pulled = dot_plain(reverse, sinks)
                back = pulled[:CHUNK]
                cross += dot_last(sinks, sources)
                sinks_f = sinks.astype(jnp.float32)
                sources_f = sources.astype(jnp.float32)
                ends = jnp.sum(sinks_f[CHUNK:] * mixed[CHUNK:], axis=0, keepdims=True) + (
                    rise * rise * keep
                ) * jnp.sum(g_new * h_old, axis=0, keepdims=True)
                diff = sinks_f[:CHUNK] * inner - sources_f[:CHUNK] * back
                gl_scr[rows, lo:hi] = diff
                gl_scr[at + CHUNK - 1 : at + CHUNK, lo:hi] = diff[CHUNK - 1 : CHUNK] + ends
                g_scr[:, lo:hi] = rise * pulled[CHUNK:] + (rise * rise * keep) * g_new
                gu = grow * back
                gu_scr[rows, lo:hi] = gu
                gx_ref[rows, lo:hi] = step * gu + skip * gy
                gvec_ref[2:3, lo:hi] += jnp.sum(gy * x_f, axis=0, keepdims=True)
            g_gram = jnp.where(allowed, cross[:CHUNK, :CHUNK], 0.0).astype(jnp.bfloat16)
            gdbl_ref[rows, 128 : 128 + STATE] = dot_first(g_gram, c_map) + tail * jnp.transpose(
                cross[CHUNK:, :CHUNK]
            )
            gdbl_ref[rows, 128 + STATE : 128 + 2 * STATE] = (
                dot_plain(g_gram, b_map) + linked * cross[:CHUNK, CHUNK:]
            )
        triu = tri_matrix(ROWS, True).astype(jnp.bfloat16)
        for lo, hi in spans(width, LANES):
            gl_scr[:, lo:hi] = split_sum(triu, gl_scr[:, lo:hi])

    @pl.when(lowest < -RANGE)
    def _():
        rate = jnp.exp(vec_ref[1:2])

        def chunk_step(reverse, carry):
            index = count - 1 - reverse
            at = pl.multiple_of(index * CHUNK, CHUNK)
            rows = pl.ds(at, CHUNK)
            b_cols = jnp.transpose(dbl_ref[rows, 128 : 128 + STATE].astype(jnp.float32))
            c_cols = jnp.transpose(dbl_ref[rows, 128 + STATE : 128 + 2 * STATE].astype(jnp.float32))
            hall_scr[0] = hsave_ref[index]
            y_scr[...] = xa_ref[rows].astype(jnp.float32)
            gu_scr[rows] = gs_ref[rows] * jax.nn.silu(z_ref[rows])

            def forward(t, inner_carry):
                step = step_scr[pl.ds(at + t, 1)]
                keep = mask_ref[pl.ds(at + t, 1)][:, 3:4]
                state = (jnp.exp(-step * rate) * keep) * hall_scr[t] + token_column(b_cols, t) * (
                    step * y_scr[pl.ds(t, 1)]
                )
                hall_scr[t + 1] = state
                return inner_carry

            lax.fori_loop(0, CHUNK, forward, 0)

            def backward(back, inner_carry):
                g_b, g_c = inner_carry
                t = CHUNK - 1 - back
                step = step_scr[pl.ds(at + t, 1)]
                keep = mask_ref[pl.ds(at + t, 1)][:, 3:4]
                decay = jnp.exp(-step * rate) * keep
                gy = gu_scr[pl.ds(at + t, 1)]
                x_f = y_scr[pl.ds(t, 1)]
                c_col = token_column(c_cols, t)
                b_col = token_column(b_cols, t)
                here = hall_scr[t + 1]
                grad = g_scr[...] + c_col * gy
                lanes = lax.broadcasted_iota(jnp.int32, (STATE, CHUNK), 1)
                g_b = jnp.where(
                    lanes == t, jnp.sum(grad * (step * x_f), axis=1, keepdims=True), g_b
                )
                g_c = jnp.where(lanes == t, jnp.sum(here * gy, axis=1, keepdims=True), g_c)
                gl_scr[pl.ds(at + t, 1)] = decay * jnp.sum(
                    grad * hall_scr[t], axis=0, keepdims=True
                )
                gu_scr[pl.ds(at + t, 1)] = jnp.sum(grad * b_col, axis=0, keepdims=True)
                y_scr[pl.ds(t, 1)] = (
                    jnp.sum(here * c_col, axis=0, keepdims=True) + vec_ref[2:3] * x_f
                )
                g_scr[...] = decay * grad
                return g_b, g_c

            blank = jnp.zeros((STATE, CHUNK), jnp.float32)
            g_b, g_c = lax.fori_loop(0, CHUNK, backward, (blank, blank))
            gdbl_ref[rows, 128 : 128 + STATE] = jnp.transpose(g_b)
            gdbl_ref[rows, 128 + STATE : 128 + 2 * STATE] = jnp.transpose(g_c)
            z_f = z_ref[rows]
            grad = gs_ref[rows]
            sig = jax.nn.sigmoid(z_f)
            gz_ref[rows] = (grad * y_scr[...] * (sig * (1.0 + z_f * (1.0 - sig)))).astype(
                jnp.bfloat16
            )
            gy = grad * (z_f * sig)
            x_f = xa_ref[rows].astype(jnp.float32)
            gx_ref[rows] = step_scr[rows] * gu_scr[rows] + vec_ref[2:3] * gy
            gvec_ref[2:3] += jnp.sum(gy * x_f, axis=0, keepdims=True)
            return carry

        lax.fori_loop(0, count, chunk_step, 0)

    for lo, hi in spans(width, LANES):
        rate = jnp.exp(vec_ref[1:2, lo:hi])
        x_f = xa_ref[:, lo:hi].astype(jnp.float32)
        gl = rate * gl_scr[:, lo:hi]
        gpre = (x_f * gu_scr[:, lo:hi] - gl) * slope_scr[:, lo:hi]
        gvec_ref[0:1, lo:hi] += jnp.sum(gpre, axis=0, keepdims=True)
        gvec_ref[1:2, lo:hi] -= jnp.sum(step_scr[:, lo:hi] * gl, axis=0, keepdims=True)
        gpre_scr[:, lo:hi] = gpre.astype(jnp.bfloat16)
    gdtw_ref[...] += dot_first(dbl_ref[:, :RANK], gpre_scr[...])
    gdbl_ref[:, :RANK] = dot_last(gpre_scr[...], dtw_ref[...])


def scan_specs(width, backward, blocks):
    def at(i):
        return (blocks - 1 - i) if backward else i

    rows = lambda cols: pl.BlockSpec((ROWS, cols), lambda i: (at(i), 0))
    whole = lambda *shape: pl.BlockSpec(shape, lambda i: (0, 0))
    return [
        rows(width),
        rows(width),
        rows(256),
        rows(8),
        pl.BlockSpec((1, ROWS), lambda i: (0, at(i))),
        whole(RANK, width),
        whole(8, width),
    ], pl.BlockSpec((ROWS // CHUNK, STATE, width), lambda i: (at(i), 0, 0)), rows, whole


def scan_forward(x_act, z_gate, dbl, masks, seg_row, dt_weight, vectors):
    tokens, width = x_act.shape
    blocks = tokens // ROWS
    in_specs, state_spec, rows, whole = scan_specs(width, False, blocks)
    return pl.pallas_call(
        scan_fwd_kernel,
        name="scan_fwd",
        grid=(blocks,),
        in_specs=in_specs,
        out_specs=[rows(width), state_spec],
        out_shape=[
            jax.ShapeDtypeStruct((tokens, width), jnp.bfloat16),
            jax.ShapeDtypeStruct((tokens // CHUNK, STATE, width), jnp.float32),
        ],
        scratch_shapes=[
            pltpu.VMEM((STATE, width), jnp.float32),
            pltpu.VMEM((ROWS, width), jnp.float32),
            pltpu.VMEM((ROWS, width), jnp.float32),
            pltpu.VMEM((CHUNK, width), jnp.float32),
        ],
        compiler_params=pltpu.CompilerParams(vmem_limit_bytes=40 << 20),
        cost_estimate=pl.CostEstimate(
            flops=0, bytes_accessed=93 << 20, transcendentals=0
        ),
    )(x_act, z_gate, dbl, masks, seg_row, dt_weight, vectors)


def scan_backward(x_act, z_gate, dbl, masks, seg_row, dt_weight, vectors, states, grad_rows):
    tokens, width = x_act.shape
    blocks = tokens // ROWS
    in_specs, state_spec, rows, whole = scan_specs(width, True, blocks)
    return pl.pallas_call(
        scan_bwd_kernel,
        name="scan_bwd",
        grid=(blocks,),
        in_specs=in_specs + [state_spec, rows(width)],
        out_specs=[rows(width), rows(width), rows(256), whole(RANK, width), whole(8, width)],
        out_shape=[
            jax.ShapeDtypeStruct((tokens, width), jnp.bfloat16),
            jax.ShapeDtypeStruct((tokens, width), jnp.float32),
            jax.ShapeDtypeStruct((tokens, 256), jnp.float32),
            jax.ShapeDtypeStruct((RANK, width), jnp.float32),
            jax.ShapeDtypeStruct((8, width), jnp.float32),
        ],
        scratch_shapes=[
            pltpu.VMEM((STATE, width), jnp.float32),
            pltpu.VMEM((ROWS, width), jnp.float32),
            pltpu.VMEM((ROWS, width), jnp.float32),
            pltpu.VMEM((ROWS, width), jnp.float32),
            pltpu.VMEM((ROWS, width), jnp.float32),
            pltpu.VMEM((ROWS, width), jnp.float32),
            pltpu.VMEM((ROWS, width), jnp.bfloat16),
            pltpu.VMEM((CHUNK + 1, STATE, width), jnp.float32),
            pltpu.VMEM((CHUNK, width), jnp.float32),
        ],
        compiler_params=pltpu.CompilerParams(vmem_limit_bytes=48 << 20),
        cost_estimate=pl.CostEstimate(
            flops=0, bytes_accessed=244 << 20, transcendentals=0
        ),
    )(x_act, z_gate, dbl, masks, seg_row, dt_weight, vectors, states, grad_rows)


def scan_masks(segs_flat):
    tokens = segs_flat.shape[0]
    before = jnp.concatenate([jnp.full((1,), -1, jnp.int32), segs_flat[:-1]])
    chunked = segs_flat.reshape(tokens // CHUNK, CHUNK)
    prior = before.reshape(tokens // CHUNK, CHUNK)[:, :1]
    last = chunked[:, CHUNK - 1 :]
    linked = chunked == prior
    tail = chunked == last
    keep = jnp.broadcast_to(last == prior, chunked.shape)
    same = (segs_flat == before).reshape(chunked.shape)
    blank = jnp.zeros_like(linked)
    stacked = jnp.stack([linked, tail, keep, same], axis=-1).reshape(tokens, 4).astype(jnp.float32)
    number = segs_flat.astype(jnp.float32)
    masks = jnp.concatenate(
        [stacked, number[:, None], jnp.zeros((tokens, 3), jnp.float32)], axis=1
    )
    return masks, number[None, :]


def per_device(
    inputs,
    teacher,
    segment_ids,
    valid,
    norm_in_gain,
    w_query,
    w_key,
    w_value,
    w_attn_out,
    w_mamba_in,
    conv_weight,
    conv_bias,
    x_proj,
    dt_proj,
    dt_bias,
    a_log,
    d_skip,
    w_mamba_out,
    attn_norm_gain,
    ssm_norm_gain,
    norm_mid_gain,
    w_gate,
    w_up,
    w_down,
):
    rank_index = lax.axis_index("tensor")
    first_slot, second_slot = rank_index, KV - 1
    per_slot = HEADS // KV
    group_width = per_slot * HEAD
    query_width = 2 * group_width
    qkv_width = query_width + 4 * HEAD
    width = inputs.shape[1]
    inner_width = w_mamba_out.shape[0]
    low = lambda values: values.astype(jnp.bfloat16)
    gather_dp = lambda part: lax.all_gather(part, "dp", axis=0, tiled=True)
    scatter_dp = lambda part: lax.psum_scatter(part, "dp", scatter_dimension=0, tiled=True)
    gather_t = lambda part: gather_rows(part, 1)
    tie = lax.optimization_barrier

    own_width = w_query.shape[0]
    out_local = pick_groups(w_attn_out, first_slot, second_slot, group_width, 0).T
    mamba_local = jnp.concatenate(
        [out_local, w_mamba_in.reshape(own_width, 2 * inner_width), w_mamba_out.T], axis=1
    )
    x_at, z_at = query_width, query_width + inner_width
    back_at = z_at + inner_width
    mamba_local = jnp.pad(mamba_local, ((0, 0), (0, -mamba_local.shape[1] % 128)))
    mamba_all = gather_dp(mamba_local)
    part_of = lambda at: (mamba_all, None, at // 128 * 128, -(-(at % 128 + inner_width) // 128) * 128)
    w_query, w_key, w_value, norm_in_gain, _ = tie(
        (w_query, w_key, w_value, norm_in_gain, mamba_local)
    )
    group_rows = 4 * inputs.shape[0]
    seq_count = group_rows // LEN
    segs_grid = segment_ids.reshape(seq_count, LEN)
    segs_flat = (segs_grid + 128 * jnp.arange(seq_count, dtype=jnp.int32)[:, None]).reshape(-1)
    scan_mask, seg_row = scan_masks(segs_flat)
    starts = first_blocks(segs_flat)
    blocks = jnp.arange(group_rows // BQ, dtype=jnp.int32)
    shared_here = blocks // (group_rows // BQ // 4) == rank_index
    firsts = jnp.concatenate([starts, jnp.where(shared_here, starts, blocks + 1)])
    first_local = jnp.concatenate(
        [
            pick_groups(w_query, first_slot, second_slot, group_width, 1),
            pick_groups(w_key, first_slot, second_slot, HEAD, 1),
            pick_groups(w_value, first_slot, second_slot, HEAD, 1),
        ],
        axis=1,
    )
    gain_rows = jnp.stack([norm_in_gain, attn_norm_gain, ssm_norm_gain, norm_mid_gain])
    gains, valid_total = hello(gain_rows, jnp.sum(valid).astype(jnp.float32))
    gain_in, gain_attn, gain_ssm, gain_mid = [gains[index][:, None] for index in range(4)]
    inputs_t = inputs.T
    normed_in, pull_in = jax.vjp(normalize_t, inputs_t, gain_in)
    normed_low, first_local, w_gate, w_up, w_down = tie(
        (low(normed_in), first_local, w_gate, w_up, w_down)
    )
    whole_in, qkv_w = gather_first(normed_low, first_local)
    whole_in, w_gate, w_up, w_down = tie((whole_in, w_gate, w_up, w_down))
    qkv_cols = low(dot_first(qkv_w, whole_in))
    attended_t, log_totals = attn_forward(firsts, qkv_cols, seg_row, scan_mask, 2)
    attended_t, x_proj, dt_proj, conv_weight = tie((attended_t, x_proj, dt_proj, conv_weight))
    inner_local = jnp.concatenate(
        [
            dt_bias[:, None],
            a_log[:, None],
            d_skip[:, None],
            conv_bias[:, None],
            conv_weight.T,
            x_proj,
            dt_proj.T,
        ],
        axis=1,
    )
    inner_rows = inner_spread(inner_local)
    attended_t, inner_rows = tie((attended_t, inner_rows))
    attn_sum = product_reduce(
        [(mamba_all, None, 0, query_width)],
        [(attended_t, True)],
        [(0, 0, query_width, 0)],
        10,
        "attn_reduce",
        43,
    )
    out_w = mamba_all[:, :query_width]
    weight_x = mamba_all[:, x_at:z_at]
    weight_z = mamba_all[:, z_at:back_at]
    mamba_out_w = mamba_all[:, back_at : back_at + inner_width]
    x_in = dot_first(whole_in, weight_x)
    ff_width = w_gate.shape[1]
    ff_step = -(-ff_width // 128) * 128
    blank = jnp.zeros((own_width, ff_step - ff_width), jnp.bfloat16)
    ffn_all = gather_dp(jnp.concatenate([w_gate, blank, w_up, blank, w_down.T, blank], axis=1))
    vector_rows = inner_rows[:, :8].astype(jnp.float32).T
    xproj_rows = inner_rows[:, 8 : 8 + RANK + 2 * STATE]
    dt_weight = inner_rows[:, 8 + RANK + 2 * STATE :].T
    xproj_pad = jnp.concatenate(
        [
            xproj_rows[:, :RANK],
            jnp.zeros((inner_width, 128 - RANK), jnp.bfloat16),
            xproj_rows[:, RANK:],
            jnp.zeros((inner_width, 128 - 2 * STATE), jnp.bfloat16),
        ],
        axis=1,
    )
    x_pre, pull_conv = jax.vjp(
        lambda x_part, taps, shift: conv_rows(x_part, taps, shift, segs_grid),
        x_in,
        vector_rows[4:],
        vector_rows[3],
    )
    x_act = low(x_pre)
    dbl_pad = total_rows(dot_plain(x_act, xproj_pad), 3)
    z_gate = dot_first(whole_in, weight_z)
    ssm_rows, states = scan_forward(
        x_act, z_gate, dbl_pad, scan_mask, seg_row, dt_weight, vector_rows
    )
    ssm_sum = product_reduce(
        [part_of(back_at)],
        [(ssm_rows, False)],
        [(0, back_at % 128, back_at % 128 + inner_width, 0)],
        11,
        "ssm_reduce",
        43,
    )
    mixed, pull_join = jax.vjp(join_rows_t, inputs_t, attn_sum, ssm_sum, gain_attn, gain_ssm)
    normed_mid, pull_mid = jax.vjp(normalize_t, mixed, gain_mid)
    normed_low, ffn_all = tie((low(normed_mid), ffn_all))
    whole_mid, gate_rows, up_rows, hidden = turn_rows(
        normed_low,
        ffn_all,
        [],
        [(ff_width, jnp.float32), (ff_width, jnp.float32), (ff_width, jnp.bfloat16)],
        [(0, ff_width), (ff_step, ff_step + ff_width)],
        forward_gate,
        15,
        "gate_turn",
        52,
    )
    ffn_rows = product_reduce(
        [(ffn_all, None, 2 * ff_step, ff_step)], [(hidden, False)], [(0, 0, ff_width, 0)], 6, "down_reduce", 45
    )
    result = mixed + ffn_rows
    all_rows = inputs.shape[0] * lax.axis_size("dp") * lax.axis_size("tensor")
    grad_out = all_rows / valid_total * valid.astype(jnp.float32)[None, :] * (result - teacher.T)
    grad_ffn, grad_gate, grad_up = turn_rows(
        low(grad_out),
        ffn_all,
        [gate_rows, up_rows],
        [(ff_width, jnp.bfloat16), (ff_width, jnp.bfloat16)],
        [(2 * ff_step, 2 * ff_step + ff_width)],
        backward_gate,
        16,
        "grad_turn",
        52,
    )
    ffn_grads = weight_grads(
        [
            (whole_mid, grad_gate, False),
            (whole_mid, grad_up, False),
            (grad_ffn, hidden, False),
        ],
        "ffn_weight_grads",
        44,
    )
    grad_gate, grad_up, ffn_grads = tie((grad_gate, grad_up, ffn_grads))
    ffn_shard = scatter_dp(ffn_grads)
    grad_mid_rows = product_reduce(
        [(ffn_all, None, 0, 2 * ff_step)],
        [(grad_gate, False), (grad_up, False)],
        [(0, 0, ff_width, 0), (0, ff_step, ff_step + ff_width, 1)],
        7,
        "mid_reduce",
        50,
    )
    grad_mixed_norm, grad_gain_mid = pull_mid(grad_mid_rows)
    grad_mixed = grad_out + grad_mixed_norm
    grad_resid, grad_attn_sum, grad_ssm_sum, grad_gain_attn, grad_gain_ssm = pull_join(grad_mixed)
    grad_ssm_whole = gather_t(low(grad_ssm_sum))
    grad_attn_low, grad_ssm_whole = tie((low(grad_attn_sum), grad_ssm_whole))
    grad_attn_whole = gather_t(grad_attn_low)
    grad_ssm_whole, grad_attn_whole = tie((grad_ssm_whole, grad_attn_whole))
    grad_ssm_rows = dot_first(grad_ssm_whole, mamba_out_w)
    grad_gate_part, grad_act_scan, grad_dbl_part, grad_dtproj, grad_vectors = scan_backward(
        x_act, z_gate, dbl_pad, scan_mask, seg_row, dt_weight, vector_rows, states, grad_ssm_rows
    )
    mid_grads = weight_grads(
        [
            (grad_attn_whole, attended_t, True),
            (grad_ssm_whole, ssm_rows, False),
            (whole_in, grad_gate_part, False),
        ],
        "mid_weight_grads",
        26,
        tight=True,
    )
    grad_att_t = low(
        lax.dot_general(
            out_w, grad_attn_whole, (((0,), (0,)), ((), ())), preferred_element_type=jnp.float32
        )
    )
    grad_dbl_part, mid_grads, ffn_shard = tie((grad_dbl_part, mid_grads, ffn_shard))
    mid_shard = scatter_dp(mid_grads)
    grad_qkv = attn_backward(
        firsts, qkv_cols, grad_att_t, attended_t, log_totals, seg_row, scan_mask, 2
    )
    grad_dbl = total_rows(grad_dbl_part, 3)
    grad_act = grad_act_scan + dot_last(grad_dbl, xproj_pad)
    grad_xproj_w = dot_first(x_act, grad_dbl)
    grad_x_part, grad_taps, grad_shift = pull_conv(grad_act)
    grad_x_low = low(grad_x_part)
    inner_grads = jnp.concatenate(
        [
            grad_vectors[:3].T,
            grad_shift[:, None],
            grad_taps.T,
            grad_xproj_w[:, :RANK],
            grad_xproj_w[:, 128 : 128 + 2 * STATE],
            grad_dtproj.T,
        ],
        axis=1,
    )
    last_grads = weight_grads(
        [
            (whole_in, grad_x_low, False),
            (whole_in, grad_qkv, True),
            (low(inner_grads).reshape(width, -1), None, False),
        ],
        "last_weight_grads",
        20,
    )
    grad_x_low, grad_qkv, last_grads, mid_shard = tie(
        (grad_x_low, grad_qkv, last_grads, mid_shard)
    )
    last_shard = scatter_dp(last_grads)
    grad_in_rows = product_reduce(
        [
            (qkv_w, None, None, qkv_width),
            part_of(x_at),
            part_of(z_at),
        ],
        [(grad_qkv, True), (grad_x_low, False), (grad_gate_part, False)],
        [
            (0, 0, qkv_width, 0),
            (1, x_at % 128, x_at % 128 + inner_width, 1),
            (2, z_at % 128, z_at % 128 + inner_width, 2),
        ],
        8,
        "in_reduce",
        52,
    )
    grad_in_norm, grad_gain_in = pull_in(grad_in_rows)
    grad_inputs = grad_resid + grad_in_norm
    gain_grads = jnp.concatenate(
        [grad_gain_in, grad_gain_attn, grad_gain_ssm, grad_gain_mid], axis=1
    )
    gains_own = farewell(gain_grads.T)
    wide = lambda part: jnp.pad(part, ((0, 0), (0, -part.shape[1] % 256)))
    out_stack = gather_stack(wide(mid_shard[:, :query_width]), 5)
    inner_step = -(-inner_width // 128) * 128
    mamba_at = query_width
    gate_at = query_width + inner_width
    def merge(stack, start, size):
        own = [stack[rank, :, start : start + size].astype(jnp.float32) for rank in range(4)]
        both = jnp.sum(
            stack[:, :, start + size : start + 2 * size].astype(jnp.float32), axis=0
        )
        return jnp.concatenate(own + [both], axis=1)

    early = (
        gains_own,
        grad_inputs,
        merge(out_stack, 0, group_width),
        mid_shard[:, mamba_at : mamba_at + inner_width].astype(jnp.float32),
        ffn_shard[:, :ff_width].astype(jnp.float32),
        ffn_shard[:, ff_step : ff_step + ff_width].astype(jnp.float32),
        ffn_shard[:, 2 * ff_step : 2 * ff_step + ff_width].astype(jnp.float32),
    )
    early, last_shard = tie((early, last_shard))
    gains_own, grad_inputs, grad_out_own, grad_back_own, grad_gate_own, grad_up_own, grad_down_own = early
    inner_at = inner_step + qkv_width
    shared_all, owned = gather_final(last_shard, inner_step, inner_at)
    inner_cols = inner_grads.size // width
    inner_sum = owned[:, :, :inner_cols].astype(jnp.float32).reshape(-1, inner_grads.shape[1])
    return (
        result.T,
        grad_inputs.T,
        gains_own[0],
        merge(shared_all, 0, group_width),
        merge(shared_all, query_width, HEAD),
        merge(shared_all, query_width + 2 * HEAD, HEAD),
        grad_out_own.T,
        jnp.stack(
            [last_shard[:, :inner_width], mid_shard[:, gate_at : gate_at + inner_width]], axis=1
        ).astype(jnp.float32),
        inner_sum[:, 4:8].T,
        inner_sum[:, 3],
        inner_sum[:, 8 : 8 + RANK + 2 * STATE],
        inner_sum[:, 8 + RANK + 2 * STATE :].T,
        inner_sum[:, 0],
        inner_sum[:, 1],
        inner_sum[:, 2],
        grad_back_own.T,
        gains_own[1],
        gains_own[2],
        gains_own[3],
        grad_gate_own,
        grad_up_own,
        grad_down_own.T,
    )


def solution(mesh):
    placed = (
        P(("dp", "tensor"), None),
        P(("dp", "tensor"), None),
        P("dp"),
        P(("dp", "tensor")),
        P("dp"),
        P("dp", None),
        P("dp", None),
        P("dp", None),
        P(None, "dp"),
        P("dp", None, "tensor"),
        P(None, "dp"),
        P("dp"),
        P("dp", None),
        P(None, "dp"),
        P("dp"),
        P("dp"),
        P("dp"),
        P("tensor", "dp"),
        P("dp"),
        P("dp"),
        P("dp"),
        P("dp", "tensor"),
        P("dp", "tensor"),
        P("tensor", "dp"),
    )
    return jax.shard_map(
        per_device,
        mesh=mesh,
        in_specs=placed,
        out_specs=(
            P(("dp", "tensor"), None),
            P(("dp", "tensor"), None),
            P("dp"),
            P("dp", None),
            P("dp", None),
            P("dp", None),
            P(None, "dp"),
            P("dp", None, "tensor"),
            P(None, "dp"),
            P("dp"),
            P("dp", None),
            P(None, "dp"),
            P("dp"),
            P("dp"),
            P("dp"),
            P("tensor", "dp"),
            P("dp"),
            P("dp"),
            P("dp"),
            P("dp", "tensor"),
            P("dp", "tensor"),
            P("tensor", "dp"),
        ),
        check_vma=False,
    )
```

```python
import functools

import jax
import jax.numpy as jnp
from jax import lax
from jax.experimental import pallas as pl
from jax.experimental.pallas import tpu as pltpu
from jax.sharding import PartitionSpec as P

HEADS = 25
KV = 5
HEAD = 64
STATE = 16
RANK = 100
CONV = 4
WINDOW = 1024
BLOCK = 512
STRETCH = 64
LEN = 2048


EPSILON = 1e-06
MASKED = -1e30
HIGHEST = lax.Precision.HIGHEST


def normalize_t(values, gain):
    return values * lax.rsqrt(jnp.mean(values * values, axis=0, keepdims=True) + EPSILON) * gain


def join_rows_t(resid, attn_sum, ssm_sum, gain_attn, gain_ssm):
    return resid + 0.5 * (normalize_t(attn_sum, gain_attn) + normalize_t(ssm_sum, gain_ssm))


def dot_plain(left, right):
    return jnp.dot(left, right, preferred_element_type=jnp.float32)


def dot_last(left, right):
    return lax.dot_general(
        left, right, (((1,), (1,)), ((), ())), preferred_element_type=jnp.float32
    )


def dot_first(left, right):
    return lax.dot_general(
        left, right, (((0,), (0,)), ((), ())), preferred_element_type=jnp.float32
    )


def pick_groups(weight, first_slot, second_slot, group_width, axis):
    return jnp.concatenate(
        [
            lax.dynamic_slice_in_dim(weight, first_slot * group_width, group_width, axis),
            lax.dynamic_slice_in_dim(weight, second_slot * group_width, group_width, axis),
        ],
        axis=axis,
    )


PIECES = 4
MESH = pl.DeviceIdType.MESH


def tensor_peers():
    me = lax.axis_index("tensor")
    side = me + 1 - 2 * lax.rem(me, 2)
    cross = lax.rem(me + 2, 4)
    return me, side, cross, lax.rem(side + 2, 4)


def greet(peers):
    barrier = pltpu.get_barrier_semaphore()
    for peer in peers:
        pl.semaphore_signal(barrier, inc=1, device_id={"tensor": peer}, device_id_type=MESH)
    pl.semaphore_wait(barrier, len(peers))


def push(src, dst, sems, index, peer):
    copy = pltpu.make_async_remote_copy(
        src_ref=src,
        dst_ref=dst,
        send_sem=sems[0].at[index],
        recv_sem=sems[1].at[index],
        device_id={"tensor": peer},
        device_id_type=MESH,
    )
    copy.start()
    return copy


def columns(block, size):
    return pl.ds(pl.multiple_of(block * size, size), size)


def gather_kernel(part_ref, whole_ref, own_sem, *sems):
    me, side, cross, diag = tensor_peers()
    depth, size = part_ref.shape
    step = depth // PIECES
    mine = columns(me, size)
    theirs = columns(cross, size)
    greet((side, cross))
    own = pltpu.make_async_copy(part_ref, whole_ref.at[:, mine], own_sem)
    own.start()
    over, near, relay = [], [], []
    for piece in range(PIECES):
        rows = pl.ds(piece * step, step)
        over.append(
            push(part_ref.at[rows], whole_ref.at[rows, mine], sems[0:2], piece, cross)
        )
    for piece in range(PIECES):
        rows = pl.ds(piece * step, step)
        near.append(push(part_ref.at[rows], whole_ref.at[rows, mine], sems[2:4], piece, side))
    for piece in range(PIECES):
        rows = pl.ds(piece * step, step)
        over[piece].wait_recv()
        relay.append(
            push(whole_ref.at[rows, theirs], whole_ref.at[rows, theirs], sems[4:6], piece, side)
        )
    own.wait()
    for piece in range(PIECES):
        over[piece].wait_send()
        near[piece].wait()
        relay[piece].wait()


def gather_rows(part, call_id):
    depth, size = part.shape
    return pl.pallas_call(
        gather_kernel,
        name="gather_rows",
        in_specs=[pl.BlockSpec(memory_space=pl.ANY)],
        out_specs=pl.BlockSpec(memory_space=pl.ANY),
        out_shape=jax.ShapeDtypeStruct((depth, 4 * size), part.dtype),
        scratch_shapes=[pltpu.SemaphoreType.DMA] + [pltpu.SemaphoreType.DMA((PIECES,))] * 6,
        compiler_params=pltpu.CompilerParams(
            collective_id=call_id, has_side_effects=True, vmem_limit_bytes=1 << 20
        ),
        cost_estimate=pl.CostEstimate(
            flops=0, bytes_accessed=depth * size * 2 * 90, transcendentals=0
        ),
    )(part)


def first_kernel(part_ref, shard_ref, whole_ref, all_ref, own_sem, *sems):
    me, side, cross, diag = tensor_peers()
    depth, size = part_ref.shape
    step = depth // PIECES
    mine, theirs = columns(me, size), columns(cross, size)
    place = lax.axis_index("dp")
    spot, lane = lax.div(place, 2), lax.rem(place, 2)
    length = all_ref.shape[0] // 2
    partner = 2 * spot + 1 - lane
    barrier = pltpu.get_barrier_semaphore()
    for peer in (side, cross):
        pl.semaphore_signal(barrier, inc=1, device_id={"tensor": peer}, device_id_type=MESH)
    pl.semaphore_signal(barrier, inc=1, device_id={"dp": partner}, device_id_type=MESH)
    has_left, has_right = spot > 0, spot < length - 1

    @pl.when(has_left)
    def _():
        pl.semaphore_signal(barrier, inc=1, device_id={"dp": place - 2}, device_id_type=MESH)

    @pl.when(has_right)
    def _():
        pl.semaphore_signal(barrier, inc=1, device_id={"dp": place + 2}, device_id_type=MESH)

    pl.semaphore_wait(barrier, 3 + has_left.astype(jnp.int32) + has_right.astype(jnp.int32))

    def line(origin, group, peer, source):
        slot = all_ref.at[2 * origin + lane]
        return pltpu.make_async_remote_copy(
            src_ref=slot if source is None else source,
            dst_ref=slot,
            send_sem=sems[6 + 2 * group].at[origin],
            recv_sem=sems[7 + 2 * group].at[origin],
            device_id={"dp": peer},
            device_id_type=MESH,
        )

    to_right = lambda origin, source=None: line(origin, 0, place + 2, source)
    to_left = lambda origin, source=None: line(origin, 1, place - 2, source)
    to_partner = lambda origin, source=None: line(origin, 2, partner, source)

    own = pltpu.make_async_copy(part_ref, whole_ref.at[:, mine], own_sem.at[0])
    own.start()
    kept = pltpu.make_async_copy(shard_ref, all_ref.at[place], own_sem.at[1])
    kept.start()
    pl.when(has_right)(to_right(spot, shard_ref).start)
    pl.when(has_left)(to_left(spot, shard_ref).start)
    to_partner(spot, shard_ref).start()
    over, near, relay = [], [], []
    for piece in range(PIECES):
        rows = pl.ds(piece * step, step)
        over.append(push(part_ref.at[rows], whole_ref.at[rows, mine], sems[0:2], piece, cross))
    for piece in range(PIECES):
        rows = pl.ds(piece * step, step)
        near.append(push(part_ref.at[rows], whole_ref.at[rows, mine], sems[2:4], piece, side))

    def pass_on(hop):
        left, right = spot - hop, spot + hop

        @pl.when(left >= 0)
        def _():
            to_right(left).wait_recv()
            pl.when(has_right)(to_right(left).start)
            to_partner(left).start()

        @pl.when(right < length)
        def _():
            to_left(right).wait_recv()
            pl.when(has_left)(to_left(right).start)
            to_partner(right).start()

    hops = list(range(1, length))
    for piece in range(PIECES):
        rows = pl.ds(piece * step, step)
        over[piece].wait_recv()
        relay.append(
            push(whole_ref.at[rows, theirs], whole_ref.at[rows, theirs], sems[4:6], piece, side)
        )
        if piece and hops:
            pass_on(hops.pop(0))
    for hop in hops:
        pass_on(hop)
    own.wait()
    kept.wait()
    for piece in range(PIECES):
        over[piece].wait_send()
        near[piece].wait()
        relay[piece].wait()
    for origin in range(length):
        pl.when(has_right & (origin <= spot))(to_right(origin).wait_send)
        pl.when(has_left & (origin >= spot))(to_left(origin).wait_send)
        to_partner(origin).wait_send()
        arrival = pltpu.make_async_remote_copy(
            src_ref=shard_ref,
            dst_ref=all_ref.at[2 * origin + 1 - lane],
            send_sem=sems[10].at[origin],
            recv_sem=sems[11].at[origin],
            device_id={"dp": partner},
            device_id_type=MESH,
        )
        arrival.wait_recv()


def gather_first(part, shard):
    depth, size = part.shape
    groups = lax.axis_size("dp")
    anywhere = pl.BlockSpec(memory_space=pl.ANY)
    whole, stacked = pl.pallas_call(
        first_kernel,
        name="gather_first",
        in_specs=[anywhere] * 2,
        out_specs=[anywhere] * 2,
        out_shape=[
            jax.ShapeDtypeStruct((depth, 4 * size), part.dtype),
            jax.ShapeDtypeStruct((groups,) + shard.shape, shard.dtype),
        ],
        scratch_shapes=[pltpu.SemaphoreType.DMA((2,))]
        + [pltpu.SemaphoreType.DMA((PIECES,))] * 6
        + [pltpu.SemaphoreType.DMA((groups // 2,))] * 6,
        compiler_params=pltpu.CompilerParams(
            collective_id=14, has_side_effects=True, vmem_limit_bytes=1 << 20
        ),
        cost_estimate=pl.CostEstimate(flops=0, bytes_accessed=270 << 20, transcendentals=0),
    )(part, shard)
    return whole, stacked.reshape(-1, shard.shape[1])


def turn_kernel(combine, plan, n_in, n_out, *refs):
    part_ref, weight_ref = refs[:2]
    ins = refs[2 : 2 + n_in]
    whole_ref = refs[2 + n_in]
    outs = refs[3 + n_in : 3 + n_in + n_out]
    scratch = refs[3 + n_in + n_out :]
    weight_bufs, scratch = scratch[: len(plan)], scratch[len(plan) :]
    in_bufs, out_bufs = scratch[:n_in], scratch[n_in : n_in + n_out]
    weight_sem, in_sem, out_sem, own_sem = scratch[n_in + n_out : n_in + n_out + 4]
    sems = scratch[n_in + n_out + 4 :]
    me, side, cross, diag = tensor_peers()
    depth, size = part_ref.shape
    half = size // PIECES
    tiles = [(block, at) for block in (me, side) for at in range(PIECES)]
    tiles += [(block, at) for at in range(PIECES) for block in (cross, diag)]
    place = lambda block, at: pl.ds(pl.multiple_of(block * size + at * half, half), half)
    local = lambda at: pl.ds(at * half, half)

    weight_loads = [
        pltpu.make_async_copy(
            weight_ref.at[:, pl.ds(low, buf.shape[1])], buf, weight_sem.at[index]
        )
        for index, ((low, _), buf) in enumerate(zip(plan, weight_bufs))
    ]
    own = pltpu.make_async_copy(part_ref, whole_ref.at[:, columns(me, size)], own_sem)
    own.start()
    for load in weight_loads:
        load.start()

    def in_load(index, tile):
        return pltpu.make_async_copy(
            ins[index].at[place(*tiles[tile])],
            in_bufs[index].at[tile % 2],
            in_sem.at[index, tile % 2],
        )

    def out_store(index, tile):
        return pltpu.make_async_copy(
            out_bufs[index].at[tile % 2],
            outs[index].at[place(*tiles[tile])],
            out_sem.at[index, tile % 2],
        )

    for index in range(n_in):
        in_load(index, 0).start()
    greet((side, cross))
    over = [
        push(part_ref.at[:, local(at)], whole_ref.at[:, place(me, at)], sems[0:2], at, cross)
        for at in range(PIECES)
    ]
    near = [
        push(part_ref.at[:, local(at)], whole_ref.at[:, place(me, at)], sems[2:4], at, side)
        for at in range(PIECES)
    ]
    relay = [None] * PIECES
    own.wait()
    for tile, (block, at) in enumerate(tiles):
        if tile + 1 < len(tiles):
            for index in range(n_in):
                in_load(index, tile + 1).start()
        if PIECES <= tile < 2 * PIECES:
            near[at].wait_recv()
        if tile >= 2 * PIECES and tile % 2 == 0:
            over[at].wait_recv()
            relay[at] = push(
                whole_ref.at[:, place(cross, at)],
                whole_ref.at[:, place(cross, at)],
                sems[4:6],
                at,
                side,
            )
        if tile >= 2 * PIECES and tile % 2 == 1:
            relay[at].wait_recv()
        left = whole_ref[:, place(block, at)]
        products = []
        for index, (low, high) in enumerate(plan):
            if tile == 0:
                weight_loads[index].wait()
            products.append(dot_first(left, weight_bufs[index][:, : high - low]))
        for index in range(n_in):
            in_load(index, tile).wait()
        results = combine(products, [buf[tile % 2] for buf in in_bufs])
        for index, result in enumerate(results):
            if tile >= 2:
                out_store(index, tile - 2).wait()
            out_bufs[index][tile % 2] = result
            out_store(index, tile).start()
    for tile in (len(tiles) - 2, len(tiles) - 1):
        for index in range(n_out):
            out_store(index, tile).wait()
    for at in range(PIECES):
        over[at].wait_send()
        near[at].wait_send()
        relay[at].wait_send()


def turn_rows(part, weight, ins, outs, plan, combine, call_id, name, micros):
    depth, size = part.shape
    half = size // PIECES
    anywhere = pl.BlockSpec(memory_space=pl.ANY)
    return pl.pallas_call(
        functools.partial(turn_kernel, combine, plan, len(ins), len(outs)),
        name=name,
        in_specs=[pl.BlockSpec(memory_space=pltpu.VMEM)] + [anywhere] * (1 + len(ins)),
        out_specs=[pl.BlockSpec(memory_space=pltpu.VMEM)] + [anywhere] * len(outs),
        out_shape=[jax.ShapeDtypeStruct((depth, 4 * size), part.dtype)]
        + [jax.ShapeDtypeStruct((4 * size, cols), dtype) for cols, dtype in outs],
        scratch_shapes=[
            pltpu.VMEM((depth, -(-(high - low) // 128) * 128), weight.dtype) for low, high in plan
        ]
        + [pltpu.VMEM((2, half, value.shape[1]), value.dtype) for value in ins]
        + [pltpu.VMEM((2, half, cols), dtype) for cols, dtype in outs]
        + [
            pltpu.SemaphoreType.DMA((len(plan),)),
            pltpu.SemaphoreType.DMA((max(len(ins), 1), 2)),
            pltpu.SemaphoreType.DMA((len(outs), 2)),
            pltpu.SemaphoreType.DMA,
        ]
        + [pltpu.SemaphoreType.DMA((PIECES,))] * 6,
        compiler_params=pltpu.CompilerParams(
            collective_id=call_id, has_side_effects=True, vmem_limit_bytes=52 << 20
        ),
        cost_estimate=pl.CostEstimate(
            flops=0, bytes_accessed=int(micros * 3.6) << 20, transcendentals=0
        ),
    )(part, weight, *ins)


def forward_gate(products, _):
    gate, up = products
    return gate, up, (gate * jax.nn.sigmoid(gate) * up).astype(jnp.bfloat16)


def backward_gate(products, saved):
    (grad,), (gate, up) = products, saved
    sig = jax.nn.sigmoid(gate)
    grad_gate = grad * up * sig * (1.0 + gate * (1.0 - sig))
    return grad_gate.astype(jnp.bfloat16), (grad * gate * sig).astype(jnp.bfloat16)


def total_kernel(part_ref, out_ref, near_buf, own_buf, stage_buf, far_buf, low_buf, own_sem, *sems):
    me, side, cross, diag = tensor_peers()
    size, wide = low_buf.shape
    half = size // 2
    greet((side, cross))
    rows_of = lambda block, at: pl.ds(pl.multiple_of(block * size + at, half), half)
    pieces = (0, half)
    first = [
        push(part_ref.at[rows_of(diag, at)], near_buf.at[pl.ds(at, half)], sems[0:2], i, side)
        for i, at in enumerate(pieces)
    ]
    second = [
        push(part_ref.at[rows_of(side, at)], own_buf.at[pl.ds(at, half)], sems[2:4], i, side)
        for i, at in enumerate(pieces)
    ]
    third, over, near, relay = [], [], [], []
    for i, at in enumerate(pieces):
        rows = pl.ds(at, half)
        first[i].wait_recv()
        stage_buf[rows] = (part_ref[rows_of(cross, at)] + near_buf[rows]).astype(jnp.bfloat16)
        third.append(push(stage_buf.at[rows], far_buf.at[rows], sems[4:6], i, cross))
    for i, at in enumerate(pieces):
        rows = pl.ds(at, half)
        second[i].wait_recv()
        third[i].wait_recv()
        low_buf[rows] = (
            part_ref[rows_of(me, at)] + own_buf[rows] + far_buf[rows].astype(jnp.float32)
        ).astype(jnp.bfloat16)
        over.append(push(low_buf.at[rows], out_ref.at[rows_of(me, at)], sems[6:8], i, cross))
        near.append(push(low_buf.at[rows], out_ref.at[rows_of(me, at)], sems[8:10], i, side))
    own = pltpu.make_async_copy(
        low_buf, out_ref.at[pl.ds(pl.multiple_of(me * size, size), size)], own_sem
    )
    own.start()
    for i, at in enumerate(pieces):
        over[i].wait_recv()
        relay.append(
            push(out_ref.at[rows_of(cross, at)], out_ref.at[rows_of(cross, at)], sems[10:12], i, side)
        )
    own.wait()
    for i in range(2):
        for group in (first, second, third, over):
            group[i].wait_send()
        near[i].wait()
        relay[i].wait()


def total_rows(part, call_id):
    tokens, wide = part.shape
    size = tokens // 4
    whole = pl.BlockSpec(memory_space=pltpu.VMEM)
    return pl.pallas_call(
        total_kernel,
        name="total_rows",
        in_specs=[whole],
        out_specs=whole,
        out_shape=jax.ShapeDtypeStruct((tokens, wide), jnp.bfloat16),
        scratch_shapes=[
            pltpu.VMEM((size, wide), jnp.float32),
            pltpu.VMEM((size, wide), jnp.float32),
            pltpu.VMEM((size, wide), jnp.bfloat16),
            pltpu.VMEM((size, wide), jnp.bfloat16),
            pltpu.VMEM((size, wide), jnp.bfloat16),
            pltpu.SemaphoreType.DMA,
        ]
        + [pltpu.SemaphoreType.DMA((2,))] * 12,
        compiler_params=pltpu.CompilerParams(
            collective_id=call_id, has_side_effects=True, vmem_limit_bytes=32 << 20
        ),
        cost_estimate=pl.CostEstimate(flops=0, bytes_accessed=60 << 20, transcendentals=0),
    )(part)


def hello_kernel(gain_ref, count_ref, gains_ref, counts_ref, sum_buf, local_buf, *sems):
    me = lax.axis_index("tensor")
    place = lax.axis_index("dp")
    ranks, groups = local_buf.shape[0], gains_ref.shape[0]
    barrier = pltpu.get_barrier_semaphore()
    others = [{"tensor": lax.rem(me + hop, ranks)} for hop in range(1, ranks)]
    far = [{"dp": lax.rem(place + hop, groups)} for hop in range(1, groups)]
    for peer in others + far:
        pl.semaphore_signal(barrier, inc=1, device_id=peer, device_id_type=MESH)
    pl.semaphore_wait(barrier, len(others) + len(far))

    def send(src, dst, index, peer):
        copy = pltpu.make_async_remote_copy(
            src_ref=src,
            dst_ref=dst,
            send_sem=sems[0].at[index],
            recv_sem=sems[1].at[index],
            device_id=peer,
            device_id_type=MESH,
        )
        copy.start()
        return copy

    first = [send(count_ref, local_buf.at[me], i, peer) for i, peer in enumerate(others)]
    local_buf[me] = count_ref[...]
    gains_ref[place] = gain_ref[...]
    base = len(first)
    second = [send(gain_ref, gains_ref.at[place], base + i, peer) for i, peer in enumerate(far)]
    base += len(second)
    for copy in first:
        copy.wait()
    sum_buf[...] = jnp.sum(local_buf[...], axis=0)
    counts_ref[place] = sum_buf[...]
    third = [send(sum_buf, counts_ref.at[place], base + i, peer) for i, peer in enumerate(far)]
    for copy in second + third:
        copy.wait()


def hello(gains, count):
    wide = -(-gains.shape[1] // 128) * 128
    block = jnp.zeros((8, wide), jnp.float32)
    block = lax.dynamic_update_slice(block, gains.astype(jnp.float32), (0, 0))
    counts = jnp.full((8, 128), count, jnp.float32)
    groups, ranks = lax.axis_size("dp"), lax.axis_size("tensor")
    copies = ranks - 1 + 2 * (groups - 1)
    whole = pl.BlockSpec(memory_space=pltpu.VMEM)
    gains_all, counts_all = pl.pallas_call(
        hello_kernel,
        name="hello",
        in_specs=[whole, whole],
        out_specs=[whole, whole],
        out_shape=[
            jax.ShapeDtypeStruct((groups, 8, wide), jnp.float32),
            jax.ShapeDtypeStruct((groups, 8, 128), jnp.float32),
        ],
        scratch_shapes=[
            pltpu.VMEM((8, 128), jnp.float32),
            pltpu.VMEM((ranks, 8, 128), jnp.float32),
        ]
        + [pltpu.SemaphoreType.DMA((copies,))] * 2,
        compiler_params=pltpu.CompilerParams(collective_id=0, has_side_effects=True),
        cost_estimate=pl.CostEstimate(flops=0, bytes_accessed=30 << 20, transcendentals=0),
    )(block, counts)
    gains_full = gains_all[:, :4, : gains.shape[1]].transpose(1, 0, 2).reshape(4, -1)
    return gains_full, jnp.sum(counts_all[:, 0, 0])


TILE = 320


def weights_kernel(plan, *refs):
    out_ref = refs[-1]
    index = 0
    for mode, offset, size, pad in plan:
        left = refs[index][...]
        if mode == "copy":
            product = left
            index += 1
        else:
            right = refs[index + 1][...]
            product = dot_last(left, right) if mode == "flip" else dot_plain(left, right)
            index += 2
        out_ref[:, offset : offset + size] = product.astype(jnp.bfloat16)
        if pad:
            out_ref[:, offset + size : offset + size + pad] = jnp.zeros(
                (out_ref.shape[0], pad), jnp.bfloat16
            )


def weight_grads(pairs, name, micros, tight=False):
    rows = pairs[0][0].shape[0]
    tile = TILE if rows % TILE == 0 else rows
    plan, specs, operands, offset = [], [], [], 0
    for left, right, flip in pairs:
        source = left if right is None else right
        size = source.shape[0] if flip else source.shape[1]
        pad = 0 if tight else -size % 128
        mode = "copy" if right is None else "flip" if flip else "plain"
        plan.append((mode, offset, size, pad))
        offset += size + pad
        specs.append(pl.BlockSpec((tile, left.shape[1]), lambda i: (i, 0)))
        operands.append(left)
        if right is not None:
            specs.append(
                pl.BlockSpec(right.shape, lambda i: (0, 0), pipeline_mode=pl.Buffered(1))
            )
            operands.append(right)
    return pl.pallas_call(
        functools.partial(weights_kernel, plan),
        name=name,
        grid=(rows // tile,),
        in_specs=specs,
        out_specs=pl.BlockSpec((tile, offset), lambda i: (i, 0)),
        out_shape=jax.ShapeDtypeStruct((rows, offset), jnp.bfloat16),
        compiler_params=pltpu.CompilerParams(vmem_limit_bytes=52 << 20),
        cost_estimate=pl.CostEstimate(
            flops=0, bytes_accessed=int(micros * 3.6) << 20, transcendentals=0
        ),
    )(*operands)


def farewell_kernel(part_ref, out_ref, group_buf, sum_buf, rank_buf, *sems):
    me = lax.axis_index("tensor")
    place = lax.axis_index("dp")
    ranks, groups = rank_buf.shape[0], group_buf.shape[0]
    barrier = pltpu.get_barrier_semaphore()
    others = [lax.rem(me + hop, ranks) for hop in range(1, ranks)]
    far = [lax.rem(place + hop, groups) for hop in range(1, groups)]
    for peer in others:
        pl.semaphore_signal(barrier, inc=1, device_id={"tensor": peer}, device_id_type=MESH)
    for peer in far:
        pl.semaphore_signal(barrier, inc=1, device_id={"dp": peer}, device_id_type=MESH)
    pl.semaphore_wait(barrier, len(others) + len(far))

    def send(src, dst, index, peer):
        copy = pltpu.make_async_remote_copy(
            src_ref=src,
            dst_ref=dst,
            send_sem=sems[0].at[index],
            recv_sem=sems[1].at[index],
            device_id=peer,
            device_id_type=MESH,
        )
        copy.start()
        return copy

    first = [
        send(part_ref.at[peer], group_buf.at[place], i, {"dp": peer}) for i, peer in enumerate(far)
    ]
    group_buf[place] = part_ref[place]
    for copy in first:
        copy.wait()
    sum_buf[...] = jnp.sum(group_buf[...], axis=0)
    rank_buf[me] = sum_buf[...]
    second = [
        send(sum_buf, rank_buf.at[me], len(first) + i, {"tensor": peer})
        for i, peer in enumerate(others)
    ]
    for copy in second:
        copy.wait()
    out_ref[...] = jnp.sum(rank_buf[...], axis=0)


def farewell(grads):
    groups, ranks = lax.axis_size("dp"), lax.axis_size("tensor")
    kinds, total = grads.shape
    own = total // groups
    wide = -(-own // 128) * 128
    parts = jnp.pad(
        grads.reshape(kinds, groups, own).transpose(1, 0, 2),
        ((0, 0), (0, 8 - kinds), (0, wide - own)),
    )
    whole = pl.BlockSpec(memory_space=pltpu.VMEM)
    summed = pl.pallas_call(
        farewell_kernel,
        name="farewell",
        in_specs=[whole],
        out_specs=whole,
        out_shape=jax.ShapeDtypeStruct((8, wide), jnp.float32),
        scratch_shapes=[
            pltpu.VMEM((groups, 8, wide), jnp.float32),
            pltpu.VMEM((8, wide), jnp.float32),
            pltpu.VMEM((ranks, 8, wide), jnp.float32),
        ]
        + [pltpu.SemaphoreType.DMA((groups + ranks - 2,))] * 2,
        compiler_params=pltpu.CompilerParams(
            collective_id=4, has_side_effects=True, vmem_limit_bytes=4 << 20
        ),
        cost_estimate=pl.CostEstimate(flops=0, bytes_accessed=40 << 20, transcendentals=0),
    )(parts)
    return summed[:kinds, :own]


def stack_kernel(part_ref, whole_ref, own_sem, *sems):
    me, side, cross, diag = tensor_peers()
    step = part_ref.shape[1] // 2
    greet((side, cross))
    own = pltpu.make_async_copy(part_ref, whole_ref.at[me], own_sem)
    own.start()
    cols = [pl.ds(0, step), pl.ds(step, step)]
    over = [
        push(part_ref.at[:, at], whole_ref.at[me, :, at], sems[0:2], i, cross)
        for i, at in enumerate(cols)
    ]
    near = [
        push(part_ref.at[:, at], whole_ref.at[me, :, at], sems[2:4], i, side)
        for i, at in enumerate(cols)
    ]
    relay = []
    for i, at in enumerate(cols):
        over[i].wait_recv()
        relay.append(
            push(whole_ref.at[cross, :, at], whole_ref.at[cross, :, at], sems[4:6], i, side)
        )
    own.wait()
    for i in range(2):
        over[i].wait_send()
        near[i].wait()
        relay[i].wait()


def gather_stack(part, call_id):
    return pl.pallas_call(
        stack_kernel,
        name="gather_stack",
        in_specs=[pl.BlockSpec(memory_space=pl.ANY)],
        out_specs=pl.BlockSpec(memory_space=pl.ANY),
        out_shape=jax.ShapeDtypeStruct((4,) + part.shape, part.dtype),
        scratch_shapes=[pltpu.SemaphoreType.DMA] + [pltpu.SemaphoreType.DMA((2,))] * 6,
        compiler_params=pltpu.CompilerParams(
            collective_id=call_id, has_side_effects=True, vmem_limit_bytes=1 << 20
        ),
        cost_estimate=pl.CostEstimate(flops=0, bytes_accessed=60 << 20, transcendentals=0),
    )(part)


def product_kernel(plan, leads, right_flips, *refs):
    left_count = len(leads)
    lefts = [ref if lead is None else ref.at[lead] for ref, (lead, _) in zip(refs, leads)]
    right_count = len(right_flips)
    rights = refs[left_count : left_count + right_count]
    out_ref = refs[left_count + right_count]
    scratch = refs[left_count + right_count + 1 :]
    left_bufs = scratch[:left_count]
    right_bufs = scratch[left_count : left_count + right_count]
    diag_buf, side_buf, near_buf, own_buf, stage_buf, far_buf, left_sem, right_sem = scratch[
        left_count + right_count : left_count + right_count + 8
    ]
    sems = scratch[left_count + right_count + 8 :]
    me, side, cross, diag = tensor_peers()
    depth, size = out_ref.shape
    step = depth // PIECES
    rows_of = lambda piece: pl.ds(pl.multiple_of(piece * step, 16), step)

    def left_load(index, piece):
        rows = rows_of(piece)
        start = leads[index][1]
        source = lefts[index].at[rows]
        if start is not None:
            source = lefts[index].at[rows, pl.ds(start, left_bufs[index].shape[1])]
        return pltpu.make_async_copy(source, left_bufs[index].at[rows], left_sem.at[index, piece])

    def right_load(index, order, block):
        at = columns(block, size)
        view = (slice(None), at) if right_flips[index] else (at,)
        return pltpu.make_async_copy(
            rights[index].at[view], right_bufs[index].at[view], right_sem.at[index, order]
        )

    turns = (diag, cross, side, me)
    for order, block in enumerate(turns):
        for index in range(right_count):
            right_load(index, order, block).start()
        for index in range(left_count):
            left_load(index, order).start()
    greet((side, cross))

    def product(piece, block):
        rows, at = rows_of(piece), columns(block, size)
        total = jnp.zeros((step, size), jnp.float32)
        for left, low_col, high_col, right in plan:
            weight = left_bufs[left][rows, low_col:high_col]
            if right_flips[right]:
                total += dot_plain(weight, right_bufs[right][:, at])
            else:
                total += dot_last(weight, right_bufs[right][at, :])
        return total

    def transfer(src, dst, group, piece, peer):
        rows = rows_of(piece)
        return pltpu.make_async_remote_copy(
            src_ref=src.at[rows],
            dst_ref=dst.at[rows],
            send_sem=sems[2 * group].at[piece],
            recv_sem=sems[2 * group + 1].at[piece],
            device_id={"tensor": peer},
            device_id_type=MESH,
        )

    first = lambda piece: transfer(diag_buf, near_buf, 0, piece, side)
    second = lambda piece: transfer(side_buf, own_buf, 1, piece, side)
    third = lambda piece: transfer(stage_buf, far_buf, 2, piece, cross)

    for order in (0, 1):
        for index in range(right_count):
            right_load(index, order, turns[order]).wait()

    def outward(piece, carry):
        rows = rows_of(piece)
        for index in range(left_count):
            left_load(index, piece).wait()
        diag_buf[rows] = product(piece, diag).astype(jnp.bfloat16)
        first(piece).start()
        kept = product(piece, cross)
        first(piece).wait_recv()
        stage_buf[rows] = (kept + near_buf[rows].astype(jnp.float32)).astype(jnp.bfloat16)
        third(piece).start()
        return carry

    lax.fori_loop(0, PIECES, outward, 0)
    for order in (2, 3):
        for index in range(right_count):
            right_load(index, order, turns[order]).wait()

    def inward(piece, carry):
        rows = rows_of(piece)
        side_buf[rows] = product(piece, side).astype(jnp.bfloat16)
        second(piece).start()
        out_ref[rows] = product(piece, me)
        return carry

    lax.fori_loop(0, PIECES, inward, 0)

    def finish(piece, carry):
        rows = rows_of(piece)
        second(piece).wait_recv()
        third(piece).wait_recv()
        out_ref[rows] += own_buf[rows].astype(jnp.float32) + far_buf[rows].astype(jnp.float32)
        first(piece).wait_send()
        second(piece).wait_send()
        third(piece).wait_send()
        return carry

    lax.fori_loop(0, PIECES, finish, 0)


def product_reduce(lefts, rights, plan, call_id, name, micros):
    leads = tuple((lead, start) for _, lead, start, _ in lefts)
    widths = [size for _, _, _, size in lefts]
    lefts = [left for left, _, _, _ in lefts]
    depth = lefts[0].shape[-2]
    right_flips = tuple(flip for _, flip in rights)
    tokens = rights[0][0].shape[1] if right_flips[0] else rights[0][0].shape[0]
    size = tokens // 4
    anywhere = pl.BlockSpec(memory_space=pl.ANY)
    return pl.pallas_call(
        functools.partial(product_kernel, plan, leads, right_flips),
        name=name,
        in_specs=[anywhere] * (len(lefts) + len(rights)),
        out_specs=pl.BlockSpec(memory_space=pltpu.VMEM),
        out_shape=jax.ShapeDtypeStruct((depth, size), jnp.float32),
        scratch_shapes=[pltpu.VMEM((depth, size), jnp.bfloat16) for size in widths]
        + [pltpu.VMEM(right.shape, right.dtype) for right, _ in rights]
        + [pltpu.VMEM((depth, size), jnp.bfloat16)] * 6
        + [
            pltpu.SemaphoreType.DMA((len(lefts), PIECES)),
            pltpu.SemaphoreType.DMA((len(rights), 4)),
        ]
        + [pltpu.SemaphoreType.DMA((PIECES,))] * 6,
        compiler_params=pltpu.CompilerParams(
            collective_id=call_id, has_side_effects=True, vmem_limit_bytes=48 << 20
        ),
        cost_estimate=pl.CostEstimate(
            flops=0, bytes_accessed=int(micros * 3.6) << 20, transcendentals=0
        ),
    )(*lefts, *[right for right, _ in rights])


def spread_kernel(part_ref, out_ref, own_sem, *sems):
    rank, place = lax.axis_index("tensor"), lax.axis_index("dp")
    share = out_ref.shape[0]
    target, slot = lax.div(place, share), lax.rem(place, share)
    replica = lax.rem(place, 4)
    barrier = pltpu.get_barrier_semaphore()
    for index in range(share):
        source = rank * share + index

        @pl.when((source != place) | (replica != rank))
        def _():
            pl.semaphore_signal(
                barrier,
                inc=1,
                device_id={"dp": source, "tensor": replica},
                device_id_type=MESH,
            )

    goals = [(rank + 4 * index != place) | (target != rank) for index in range(share)]
    pl.semaphore_wait(barrier, sum(goal.astype(jnp.int32) for goal in goals))

    def outgoing(index):
        goal = rank + 4 * index
        copy = pltpu.make_async_remote_copy(
            src_ref=part_ref,
            dst_ref=out_ref.at[slot],
            send_sem=sems[0].at[index],
            recv_sem=sems[1].at[slot],
            device_id={"dp": goal, "tensor": target},
            device_id_type=MESH,
        )
        return copy, (goal != place) | (target != rank)

    own = pltpu.make_async_copy(part_ref, out_ref.at[slot], own_sem)
    for index in range(share):
        copy, away = outgoing(index)
        pl.when(away)(copy.start)
        pl.when(jnp.logical_not(away))(own.start)
    for index in range(share):
        copy, away = outgoing(index)
        pl.when(away)(copy.wait_send)
        pl.when(jnp.logical_not(away))(own.wait)
        source = rank * share + index
        arrival = pltpu.make_async_remote_copy(
            src_ref=part_ref,
            dst_ref=out_ref.at[index],
            send_sem=sems[0].at[index],
            recv_sem=sems[1].at[index],
            device_id={"dp": source, "tensor": replica},
            device_id_type=MESH,
        )
        pl.when((source != place) | (replica != rank))(arrival.wait_recv)


def inner_spread(part):
    groups, ranks = lax.axis_size("dp"), lax.axis_size("tensor")
    share = groups // ranks
    rows, cols = part.shape
    padded = jnp.pad(part, ((0, -rows % 16), (0, -cols % 128)))
    whole = pl.BlockSpec(memory_space=pltpu.VMEM)
    spread = pl.pallas_call(
        spread_kernel,
        name="inner_spread",
        in_specs=[whole],
        out_specs=whole,
        out_shape=jax.ShapeDtypeStruct((share,) + padded.shape, part.dtype),
        scratch_shapes=[pltpu.SemaphoreType.DMA] + [pltpu.SemaphoreType.DMA((share,))] * 2,
        compiler_params=pltpu.CompilerParams(
            collective_id=12, has_side_effects=True, vmem_limit_bytes=8 << 20
        ),
        cost_estimate=pl.CostEstimate(flops=0, bytes_accessed=40 << 20, transcendentals=0),
    )(padded)
    return spread[:, :rows, :cols].reshape(share * rows, cols)


def final_kernel(starts, last_ref, whole_ref, owned_ref, own_sem, *sems):
    part_ref = last_ref.at[:, pl.ds(starts[0], whole_ref.shape[2])]
    inner_ref = last_ref.at[:, pl.ds(starts[1], owned_ref.shape[2])]
    me, side, cross, diag = tensor_peers()
    place = lax.axis_index("dp")
    ranks = owned_ref.shape[0]
    share = lax.axis_size("dp") // ranks
    owner, slot = me * share + lax.div(place, ranks), lax.rem(place, ranks)
    source_rank, source_base = lax.div(place, share), ranks * lax.rem(place, share)
    barrier = pltpu.get_barrier_semaphore()
    for peer in (side, cross):
        pl.semaphore_signal(barrier, inc=1, device_id={"tensor": peer}, device_id_type=MESH)
    for index in range(ranks):
        source = source_base + index

        @pl.when((source != place) | (source_rank != me))
        def _():
            pl.semaphore_signal(
                barrier,
                inc=1,
                device_id={"dp": source, "tensor": source_rank},
                device_id_type=MESH,
            )

    goals = [(owner != place) | (me != index) for index in range(ranks)]
    pl.semaphore_wait(barrier, 2 + sum(goal.astype(jnp.int32) for goal in goals))

    span = whole_ref.shape[2]
    step = -(-span // 256) * 128
    own = pltpu.make_async_copy(part_ref, whole_ref.at[me], own_sem.at[0])
    own.start()
    cols = [pl.ds(0, step), pl.ds(step, span - step)]
    shift = lambda at: pl.ds(starts[0] + at.start, at.size)
    over = [
        push(last_ref.at[:, shift(at)], whole_ref.at[me, :, at], sems[0:2], i, cross)
        for i, at in enumerate(cols)
    ]
    near = [
        push(last_ref.at[:, shift(at)], whole_ref.at[me, :, at], sems[2:4], i, side)
        for i, at in enumerate(cols)
    ]
    kept = pltpu.make_async_copy(inner_ref, owned_ref.at[slot], own_sem.at[1])

    def outgoing(index):
        copy = pltpu.make_async_remote_copy(
            src_ref=inner_ref,
            dst_ref=owned_ref.at[slot],
            send_sem=sems[6].at[index],
            recv_sem=sems[7].at[slot],
            device_id={"dp": owner, "tensor": index},
            device_id_type=MESH,
        )
        return copy, (owner != place) | (me != index)

    for index in range(ranks):
        copy, away = outgoing(index)
        pl.when(away)(copy.start)
        pl.when(jnp.logical_not(away))(kept.start)
    relay = []
    for i, at in enumerate(cols):
        over[i].wait_recv()
        relay.append(
            push(whole_ref.at[cross, :, at], whole_ref.at[cross, :, at], sems[4:6], i, side)
        )
    own.wait()
    for i in range(2):
        over[i].wait_send()
        near[i].wait()
        relay[i].wait()
    for index in range(ranks):
        copy, away = outgoing(index)
        pl.when(away)(copy.wait_send)
        pl.when(jnp.logical_not(away))(kept.wait)
        source = source_base + index
        arrival = pltpu.make_async_remote_copy(
            src_ref=inner_ref,
            dst_ref=owned_ref.at[index],
            send_sem=sems[6].at[index],
            recv_sem=sems[7].at[index],
            device_id={"dp": source, "tensor": source_rank},
            device_id_type=MESH,
        )
        pl.when((source != place) | (source_rank != me))(arrival.wait_recv)


def gather_final(last, start, middle):
    anywhere = pl.BlockSpec(memory_space=pl.ANY)
    rows, total = last.shape
    return pl.pallas_call(
        functools.partial(final_kernel, (start, middle)),
        name="gather_final",
        in_specs=[anywhere],
        out_specs=[anywhere] * 2,
        out_shape=[
            jax.ShapeDtypeStruct((4, rows, middle - start), last.dtype),
            jax.ShapeDtypeStruct((4, rows, total - middle), last.dtype),
        ],
        scratch_shapes=[pltpu.SemaphoreType.DMA((2,))]
        + [pltpu.SemaphoreType.DMA((2,))] * 6
        + [pltpu.SemaphoreType.DMA((4,))] * 2,
        compiler_params=pltpu.CompilerParams(
            collective_id=9, has_side_effects=True, vmem_limit_bytes=1 << 20
        ),
        cost_estimate=pl.CostEstimate(flops=0, bytes_accessed=60 << 20, transcendentals=0),
    )(last)


BQ = 256
BK = 256


def attn_bias(q_base, k_base, segq_row, segk_col):
    q_pos = q_base + lax.broadcasted_iota(jnp.int32, (BK, BQ), 1)
    k_pos = k_base + lax.broadcasted_iota(jnp.int32, (BK, BQ), 0)
    offset = q_pos - k_pos
    allowed = (offset >= 0) & (offset < WINDOW) & (segk_col == segq_row)
    return jnp.where(allowed, 0.0, MASKED)


def flip_rows(cols_ref, rows_scr):
    for at in range(0, rows_scr.shape[0], BK):
        block = cols_ref[:, at : at + BK].astype(jnp.float32)
        rows_scr[at : at + BK] = jnp.transpose(block).astype(jnp.bfloat16)


def attn_fwd_kernel(first_ref, qt_ref, kt_ref, vt_ref, segr_ref, mask_ref, ot_ref, lse_ref,
                    max_scr, sum_scr, acc_scr, k_scr):
    heads = qt_ref.shape[0] // HEAD
    block = pl.program_id(1)
    q_base = block * BQ

    @pl.when(block == 0)
    def _():
        flip_rows(kt_ref, k_scr)

    max_scr[...] = jnp.full_like(max_scr, MASKED)
    sum_scr[...] = jnp.zeros_like(sum_scr)
    acc_scr[...] = jnp.zeros_like(acc_scr)
    segq_row = segr_ref[0:1, :]

    def body(j, carry):
        k_base = pl.multiple_of(j * BK, BK)
        rows = pl.ds(k_base, BK)
        bias = attn_bias(q_base, k_base, segq_row, mask_ref[rows, 4:5])
        k_blk = k_scr[rows, :]
        v_blk = vt_ref[:, rows]
        for head in range(heads):
            cols = slice(head * HEAD, (head + 1) * HEAD)
            scores = dot_plain(k_blk, qt_ref[cols, :]) * 0.125 + bias
            old_max = max_scr[head : head + 1]
            new_max = jnp.maximum(old_max, jnp.max(scores, axis=0, keepdims=True))
            expo = jnp.exp(scores - new_max)
            ratio = jnp.exp(old_max - new_max)
            max_scr[head : head + 1] = new_max
            sum_scr[head : head + 1] = sum_scr[head : head + 1] * ratio + jnp.sum(
                expo, axis=0, keepdims=True
            )
            acc_scr[cols] = acc_scr[cols] * ratio + dot_plain(v_blk, expo.astype(jnp.bfloat16))
        return carry

    start = first_ref[pl.program_id(0) * pl.num_programs(1) + block]
    lax.fori_loop(start, block + 1, body, 0)
    for head in range(heads):
        cols = slice(head * HEAD, (head + 1) * HEAD)
        total = jnp.maximum(sum_scr[head : head + 1], 1e-30)
        ot_ref[cols] = (acc_scr[cols] / total).astype(jnp.bfloat16)
        lse_ref[0, head : head + 1] = max_scr[head : head + 1] + jnp.log(total)


def attn_specs(slots, group, tokens):
    queries = pl.BlockSpec((group, BQ), lambda s, i, f: (s, i))
    base = slots * group // HEAD
    keys = pl.BlockSpec((HEAD, tokens), lambda s, i, f: (base + s, 0))
    values = pl.BlockSpec((HEAD, tokens), lambda s, i, f: (base + slots + s, 0))
    stats = pl.BlockSpec((1, 8, BQ), lambda s, i, f: (s, 0, i))
    seg_row = pl.BlockSpec((1, BQ), lambda s, i, f: (0, i))
    seg_col = pl.BlockSpec((tokens, 8), lambda s, i, f: (0, 0))
    return queries, keys, values, stats, seg_row, seg_col


def attn_forward(first, qkv_t, seg_row, masks, slots):
    tokens = qkv_t.shape[1]
    group = qkv_t.shape[0] // slots - 2 * HEAD
    queries, keys, values, stats, segr, segc = attn_specs(slots, group, tokens)
    return pl.pallas_call(
        attn_fwd_kernel,
        name="attn_fwd",
        grid_spec=pltpu.PrefetchScalarGridSpec(
            num_scalar_prefetch=1,
            grid=(slots, tokens // BQ),
            in_specs=[queries, keys, values, segr, segc],
            out_specs=[queries, stats],
            scratch_shapes=[
                pltpu.VMEM((8, BQ), jnp.float32),
                pltpu.VMEM((8, BQ), jnp.float32),
                pltpu.VMEM((group, BQ), jnp.float32),
                pltpu.VMEM((tokens, HEAD), jnp.bfloat16),
            ],
        ),
        out_shape=[
            jax.ShapeDtypeStruct((slots * group, tokens), jnp.bfloat16),
            jax.ShapeDtypeStruct((slots, 8, tokens), jnp.float32),
        ],
        compiler_params=pltpu.CompilerParams(vmem_limit_bytes=32 << 20),
        cost_estimate=pl.CostEstimate(flops=0, bytes_accessed=150 << 20, transcendentals=0),
    )(first, qkv_t, qkv_t, qkv_t, seg_row, masks)


def attn_bwd_kernel(first_ref, qt_ref, dot_ref, ot_ref, lse_ref, kt_ref, vt_ref, segr_ref, mask_ref,
                    grad_ref, delta_scr, acc_scr, q_scr, do_scr, k_scr, v_scr, gk_scr, gv_scr):
    group = qt_ref.shape[0]
    heads = group // HEAD
    slot = pl.program_id(0)
    slots = pl.num_programs(0)
    block = pl.program_id(1)
    q_base = pl.multiple_of(block * BQ, BQ)

    @pl.when(block == 0)
    def _():
        flip_rows(kt_ref, k_scr)
        flip_rows(vt_ref, v_scr)
        gk_scr[...] = jnp.zeros_like(gk_scr)
        gv_scr[...] = jnp.zeros_like(gv_scr)

    acc_scr[...] = jnp.zeros_like(acc_scr)
    start = first_ref[slot * pl.num_programs(1) + block]

    @pl.when(start <= block)
    def _():
        for head in range(heads):
            cols = slice(head * HEAD, (head + 1) * HEAD)
            grad_out = dot_ref[cols].astype(jnp.float32)
            delta_scr[head : head + 1] = jnp.sum(
                grad_out * ot_ref[cols].astype(jnp.float32), axis=0, keepdims=True
            )
            q_scr[head] = jnp.transpose(qt_ref[cols].astype(jnp.float32)).astype(jnp.bfloat16)
            do_scr[head] = jnp.transpose(grad_out).astype(jnp.bfloat16)

    segq_row = segr_ref[0:1, :]

    def body(j, carry):
        k_base = pl.multiple_of(j * BK, BK)
        rows = pl.ds(k_base, BK)
        bias = attn_bias(q_base, k_base, segq_row, mask_ref[rows, 4:5])
        k_blk = k_scr[rows, :]
        kt_blk = kt_ref[:, rows]
        v_blk = v_scr[rows, :]
        gk = jnp.zeros((BK, HEAD), jnp.float32)
        gv = jnp.zeros((BK, HEAD), jnp.float32)
        for head in range(heads):
            cols = slice(head * HEAD, (head + 1) * HEAD)
            scores = dot_plain(k_blk, qt_ref[cols, :]) * 0.125 + bias
            probs = jnp.exp(scores - lse_ref[0, head : head + 1])
            grad_p = dot_plain(v_blk, dot_ref[cols, :])
            grad_s = (probs * (grad_p - delta_scr[head : head + 1])).astype(jnp.bfloat16)
            gv += dot_plain(probs.astype(jnp.bfloat16), do_scr[head])
            gk += dot_plain(grad_s, q_scr[head])
            acc_scr[cols] += dot_plain(kt_blk, grad_s)
        gk_scr[rows, :] += gk * 0.125
        gv_scr[rows, :] += gv
        return carry

    lax.fori_loop(start, block + 1, body, 0)
    grad_ref[pl.ds(pl.multiple_of(slot * group, HEAD), group), pl.ds(q_base, BQ)] = (
        acc_scr[...] * 0.125
    ).astype(jnp.bfloat16)

    @pl.when(block == pl.num_programs(1) - 1)
    def _():
        key_rows = pl.ds(pl.multiple_of(slots * group + slot * HEAD, HEAD), HEAD)
        value_rows = pl.ds(pl.multiple_of(slots * group + (slots + slot) * HEAD, HEAD), HEAD)
        for at in range(0, gk_scr.shape[0], BK):
            cols = pl.ds(at, BK)
            grad_ref[key_rows, cols] = jnp.transpose(gk_scr[at : at + BK]).astype(jnp.bfloat16)
            grad_ref[value_rows, cols] = jnp.transpose(gv_scr[at : at + BK]).astype(jnp.bfloat16)


def attn_backward(first, qkv_t, do_t, o_t, lse, seg_row, masks, slots):
    width, tokens = qkv_t.shape
    group = width // slots - 2 * HEAD
    queries, keys, values, stats, segr, segc = attn_specs(slots, group, tokens)
    return pl.pallas_call(
        attn_bwd_kernel,
        name="attn_bwd",
        grid_spec=pltpu.PrefetchScalarGridSpec(
            num_scalar_prefetch=1,
            grid=(slots, tokens // BQ),
            in_specs=[queries, queries, queries, stats, keys, values, segr, segc],
            out_specs=pl.BlockSpec((width, tokens), lambda s, i, f: (0, 0)),
            scratch_shapes=[
                pltpu.VMEM((8, BQ), jnp.float32),
                pltpu.VMEM((group, BQ), jnp.float32),
                pltpu.VMEM((group // HEAD, BQ, HEAD), jnp.bfloat16),
                pltpu.VMEM((group // HEAD, BQ, HEAD), jnp.bfloat16),
                pltpu.VMEM((tokens, HEAD), jnp.bfloat16),
                pltpu.VMEM((tokens, HEAD), jnp.bfloat16),
                pltpu.VMEM((tokens, HEAD), jnp.float32),
                pltpu.VMEM((tokens, HEAD), jnp.float32),
            ],
        ),
        out_shape=jax.ShapeDtypeStruct((width, tokens), jnp.bfloat16),
        compiler_params=pltpu.CompilerParams(vmem_limit_bytes=40 << 20),
        cost_estimate=pl.CostEstimate(flops=0, bytes_accessed=160 << 20, transcendentals=0),
    )(first, qkv_t, do_t, o_t, lse, qkv_t, qkv_t, seg_row, masks)


def first_blocks(segs_flat):
    tokens = segs_flat.shape[0]
    starts = segs_flat[::BQ]
    positions = jnp.arange(tokens // BQ, dtype=jnp.int32) * BQ
    seg_start = jnp.sum((segs_flat[None, :] < starts[:, None]).astype(jnp.int32), axis=1)
    return jnp.maximum(jnp.maximum(seg_start, positions - WINDOW + 1), 0) // BK


def conv_rows(x_in, conv_w, conv_b, segs_grid):
    seq_count, seq_len = segs_grid.shape
    width = x_in.shape[1]
    grid = x_in.reshape(seq_count, seq_len, width)
    pad_x = jnp.concatenate([jnp.zeros((seq_count, CONV - 1, width), jnp.float32), grid], axis=1)
    pad_seg = jnp.concatenate([jnp.full((seq_count, CONV - 1), -1, jnp.int32), segs_grid], axis=1)
    total = jnp.zeros((seq_count, seq_len, width), jnp.float32) + conv_b
    for tap in range(CONV):
        same = (pad_seg[:, tap : tap + seq_len] == segs_grid).astype(jnp.float32)
        total = total + conv_w[tap] * pad_x[:, tap : tap + seq_len] * same[:, :, None]
    return jax.nn.silu(total).reshape(seq_count * seq_len, width)


CHUNK = 64
ROWS = 256
RANGE = 120.0
LANES = 256


def spans(width, size):
    return [(at, min(at + size, width)) for at in range(0, width, size)]


def softplus_parts(pre):
    small = jnp.exp(-jnp.abs(pre))
    step = jnp.maximum(pre, 0.0) + jnp.log1p(small)
    slope = jnp.where(pre >= 0.0, 1.0, small) / (1.0 + small)
    return step, slope


def split_sum(tri, values):
    high = values.astype(jnp.bfloat16)
    low = (values - high.astype(jnp.float32)).astype(jnp.bfloat16)
    return dot_plain(tri, high) + dot_plain(tri, low)


def tri_matrix(size, upper):
    row = lax.broadcasted_iota(jnp.int32, (size, size), 0)
    col = lax.broadcasted_iota(jnp.int32, (size, size), 1)
    order = (col >= row) if upper else (row >= col)
    return order & (lax.div(row, CHUNK) == lax.div(col, CHUNK))


def scan_setup(dbl_ref, dtw_ref, vec_ref, step_scr, cum_scr, slope_scr):
    width = dtw_ref.shape[1]
    tri = tri_matrix(ROWS, False).astype(jnp.bfloat16)
    dt_low = dbl_ref[:, :RANK]
    lowest = jnp.zeros((), jnp.float32)
    for lo, hi in spans(width, LANES):
        pre = dot_plain(dt_low, dtw_ref[:, lo:hi]) + vec_ref[0:1, lo:hi]
        step, slope = softplus_parts(pre)
        cum = split_sum(tri, -step * jnp.exp(vec_ref[1:2, lo:hi]))
        step_scr[:, lo:hi] = step
        cum_scr[:, lo:hi] = cum
        if slope_scr is not None:
            slope_scr[:, lo:hi] = slope
        least = jnp.zeros((1, hi - lo), jnp.float32)
        for at in range(0, ROWS, CHUNK):
            least = jnp.minimum(least, cum[at + CHUNK - 1 : at + CHUNK])
        lowest = jnp.minimum(lowest, jnp.min(least))
    return lowest


def chunk_maps(dbl_ref, mask_ref, segr_ref, at):
    rows = slice(at, at + CHUNK)
    b_map = dbl_ref[rows, 128 : 128 + STATE]
    c_map = dbl_ref[rows, 128 + STATE : 128 + 2 * STATE]
    linked = mask_ref[rows, 0:1]
    tail = mask_ref[rows, 1:2]
    keep = mask_ref[at + CHUNK - 1 : at + CHUNK, 2:3]
    allowed = tri_matrix(CHUNK, False) & (mask_ref[rows, 4:5] == segr_ref[0:1, rows])
    gram = jnp.where(allowed, dot_last(c_map, b_map), 0.0)
    c_link = c_map.astype(jnp.float32) * linked
    b_tail = b_map.astype(jnp.float32) * tail
    return b_map, c_map, linked, tail, keep, allowed, gram, c_link, b_tail


def mixer(square, side, bottom):
    corner = jnp.zeros((STATE, STATE), jnp.float32)
    top = jnp.concatenate([square, side], axis=1)
    low = jnp.concatenate([jnp.transpose(bottom), corner], axis=1)
    return jnp.concatenate([top, low], axis=0).astype(jnp.bfloat16)


def token_column(block, lane_index):
    lanes = lax.broadcasted_iota(jnp.int32, block.shape, 1)
    return jnp.sum(jnp.where(lanes == lane_index, block, 0.0), axis=1, keepdims=True)


def scan_fwd_kernel(
    xa_ref, z_ref, dbl_ref, mask_ref, segr_ref, dtw_ref, vec_ref,
    out_ref, hsave_ref, h_scr, step_scr, cum_scr, y_scr,
):
    width = xa_ref.shape[1]

    @pl.when(pl.program_id(0) == 0)
    def _():
        h_scr[...] = jnp.zeros_like(h_scr)

    lowest = scan_setup(dbl_ref, dtw_ref, vec_ref, step_scr, cum_scr, None)

    @pl.when(lowest >= -RANGE)
    def _():
        for index, at in enumerate(range(0, ROWS, CHUNK)):
            rows = slice(at, at + CHUNK)
            _, _, _, _, keep, _, gram, c_link, b_tail = chunk_maps(dbl_ref, mask_ref, segr_ref, at)
            forward = mixer(gram, c_link, b_tail)
            for lo, hi in spans(width, LANES):
                cum = cum_scr[rows, lo:hi]
                half = 0.5 * cum[CHUNK - 1 : CHUNK]
                gap = cum - half
                rise = jnp.exp(half)
                h_old = h_scr[:, lo:hi]
                hsave_ref[index, :, lo:hi] = h_old
                x_f = xa_ref[rows, lo:hi].astype(jnp.float32)
                sources = jnp.concatenate(
                    [jnp.exp(-gap) * (step_scr[rows, lo:hi] * x_f), rise * h_old], axis=0
                ).astype(jnp.bfloat16)
                mixed = dot_plain(forward, sources)
                total = jnp.exp(gap) * mixed[:CHUNK] + vec_ref[2:3, lo:hi] * x_f
                out_ref[rows, lo:hi] = (total * jax.nn.silu(z_ref[rows, lo:hi])).astype(
                    jnp.bfloat16
                )
                h_scr[:, lo:hi] = rise * mixed[CHUNK:] + (rise * rise * keep) * h_old

    @pl.when(lowest < -RANGE)
    def _():
        for index, at in enumerate(range(0, ROWS, CHUNK)):
            rows = slice(at, at + CHUNK)
            hsave_ref[index] = h_scr[...]
            b_cols = jnp.transpose(dbl_ref[rows, 128 : 128 + STATE].astype(jnp.float32))
            c_cols = jnp.transpose(dbl_ref[rows, 128 + STATE : 128 + 2 * STATE].astype(jnp.float32))
            y_scr[...] = xa_ref[rows].astype(jnp.float32)
            rate = jnp.exp(vec_ref[1:2])

            def token(t, carry):
                step = step_scr[pl.ds(at + t, 1)]
                keep = mask_ref[pl.ds(at + t, 1)][:, 3:4]
                state = (jnp.exp(-step * rate) * keep) * h_scr[...] + token_column(b_cols, t) * (
                    step * y_scr[pl.ds(t, 1)]
                )
                h_scr[...] = state
                y_scr[pl.ds(t, 1)] = (
                    jnp.sum(state * token_column(c_cols, t), axis=0, keepdims=True)
                    + vec_ref[2:3] * y_scr[pl.ds(t, 1)]
                )
                return carry

            lax.fori_loop(0, CHUNK, token, 0)
            out_ref[rows] = (y_scr[...] * jax.nn.silu(z_ref[rows])).astype(jnp.bfloat16)


def scan_bwd_kernel(
    xa_ref, z_ref, dbl_ref, mask_ref, segr_ref, dtw_ref, vec_ref, hsave_ref, gs_ref,
    gz_ref, gx_ref, gdbl_ref, gdtw_ref, gvec_ref,
    g_scr, step_scr, cum_scr, slope_scr, gl_scr, gu_scr, gpre_scr, hall_scr, y_scr,
):
    width = xa_ref.shape[1]

    @pl.when(pl.program_id(0) == 0)
    def _():
        g_scr[...] = jnp.zeros_like(g_scr)
        gdtw_ref[...] = jnp.zeros_like(gdtw_ref)
        gvec_ref[...] = jnp.zeros_like(gvec_ref)

    lowest = scan_setup(dbl_ref, dtw_ref, vec_ref, step_scr, cum_scr, slope_scr)
    count = ROWS // CHUNK

    @pl.when(lowest >= -RANGE)
    def _():
        for index in range(count - 1, -1, -1):
            at = index * CHUNK
            rows = slice(at, at + CHUNK)
            b_map, c_map, linked, tail, keep, allowed, gram, c_link, b_tail = chunk_maps(
                dbl_ref, mask_ref, segr_ref, at
            )
            forward = mixer(gram, c_link, b_tail)
            reverse = mixer(jnp.transpose(gram), b_tail, c_link)
            cross = jnp.zeros((CHUNK + STATE, CHUNK + STATE), jnp.float32)
            for lo, hi in spans(width, LANES):
                cum = cum_scr[rows, lo:hi]
                half = 0.5 * cum[CHUNK - 1 : CHUNK]
                gap = cum - half
                fall = jnp.exp(gap)
                grow = jnp.exp(-gap)
                rise = jnp.exp(half)
                h_old = hsave_ref[index, :, lo:hi]
                g_new = g_scr[:, lo:hi]
                step = step_scr[rows, lo:hi]
                x_f = xa_ref[rows, lo:hi].astype(jnp.float32)
                skip = vec_ref[2:3, lo:hi]
                sources = jnp.concatenate([grow * (step * x_f), rise * h_old], axis=0).astype(
                    jnp.bfloat16
                )
                mixed = dot_plain(forward, sources)
                inner = mixed[:CHUNK]
                z_f = z_ref[rows, lo:hi]
                grad = gs_ref[rows, lo:hi]
                sig = jax.nn.sigmoid(z_f)
                gated = z_f * sig
                gy = grad * gated
                gz_ref[rows, lo:hi] = (
                    grad * (fall * inner + skip * x_f) * (sig + gated * (1.0 - sig))
                ).astype(jnp.bfloat16)
                sinks = jnp.concatenate([fall * gy, rise * g_new], axis=0).astype(jnp.bfloat16)
                pulled = dot_plain(reverse, sinks)
                back = pulled[:CHUNK]
                cross += dot_last(sinks, sources)
                sinks_f = sinks.astype(jnp.float32)
                sources_f = sources.astype(jnp.float32)
                ends = jnp.sum(sinks_f[CHUNK:] * mixed[CHUNK:], axis=0, keepdims=True) + (
                    rise * rise * keep
                ) * jnp.sum(g_new * h_old, axis=0, keepdims=True)
                diff = sinks_f[:CHUNK] * inner - sources_f[:CHUNK] * back
                gl_scr[rows, lo:hi] = diff
                gl_scr[at + CHUNK - 1 : at + CHUNK, lo:hi] = diff[CHUNK - 1 : CHUNK] + ends
                g_scr[:, lo:hi] = rise * pulled[CHUNK:] + (rise * rise * keep) * g_new
                gu = grow * back
                gu_scr[rows, lo:hi] = gu
                gx_ref[rows, lo:hi] = step * gu + skip * gy
                gvec_ref[2:3, lo:hi] += jnp.sum(gy * x_f, axis=0, keepdims=True)
            g_gram = jnp.where(allowed, cross[:CHUNK, :CHUNK], 0.0).astype(jnp.bfloat16)
            gdbl_ref[rows, 128 : 128 + STATE] = dot_first(g_gram, c_map) + tail * jnp.transpose(
                cross[CHUNK:, :CHUNK]
            )
            gdbl_ref[rows, 128 + STATE : 128 + 2 * STATE] = (
                dot_plain(g_gram, b_map) + linked * cross[:CHUNK, CHUNK:]
            )
        triu = tri_matrix(ROWS, True).astype(jnp.bfloat16)
        for lo, hi in spans(width, LANES):
            gl_scr[:, lo:hi] = split_sum(triu, gl_scr[:, lo:hi])

    @pl.when(lowest < -RANGE)
    def _():
        rate = jnp.exp(vec_ref[1:2])

        def chunk_step(reverse, carry):
            index = count - 1 - reverse
            at = pl.multiple_of(index * CHUNK, CHUNK)
            rows = pl.ds(at, CHUNK)
            b_cols = jnp.transpose(dbl_ref[rows, 128 : 128 + STATE].astype(jnp.float32))
            c_cols = jnp.transpose(dbl_ref[rows, 128 + STATE : 128 + 2 * STATE].astype(jnp.float32))
            hall_scr[0] = hsave_ref[index]
            y_scr[...] = xa_ref[rows].astype(jnp.float32)
            gu_scr[rows] = gs_ref[rows] * jax.nn.silu(z_ref[rows])

            def forward(t, inner_carry):
                step = step_scr[pl.ds(at + t, 1)]
                keep = mask_ref[pl.ds(at + t, 1)][:, 3:4]
                state = (jnp.exp(-step * rate) * keep) * hall_scr[t] + token_column(b_cols, t) * (
                    step * y_scr[pl.ds(t, 1)]
                )
                hall_scr[t + 1] = state
                return inner_carry

            lax.fori_loop(0, CHUNK, forward, 0)

            def backward(back, inner_carry):
                g_b, g_c = inner_carry
                t = CHUNK - 1 - back
                step = step_scr[pl.ds(at + t, 1)]
                keep = mask_ref[pl.ds(at + t, 1)][:, 3:4]
                decay = jnp.exp(-step * rate) * keep
                gy = gu_scr[pl.ds(at + t, 1)]
                x_f = y_scr[pl.ds(t, 1)]
                c_col = token_column(c_cols, t)
                b_col = token_column(b_cols, t)
                here = hall_scr[t + 1]
                grad = g_scr[...] + c_col * gy
                lanes = lax.broadcasted_iota(jnp.int32, (STATE, CHUNK), 1)
                g_b = jnp.where(
                    lanes == t, jnp.sum(grad * (step * x_f), axis=1, keepdims=True), g_b
                )
                g_c = jnp.where(lanes == t, jnp.sum(here * gy, axis=1, keepdims=True), g_c)
                gl_scr[pl.ds(at + t, 1)] = decay * jnp.sum(
                    grad * hall_scr[t], axis=0, keepdims=True
                )
                gu_scr[pl.ds(at + t, 1)] = jnp.sum(grad * b_col, axis=0, keepdims=True)
                y_scr[pl.ds(t, 1)] = (
                    jnp.sum(here * c_col, axis=0, keepdims=True) + vec_ref[2:3] * x_f
                )
                g_scr[...] = decay * grad
                return g_b, g_c

            blank = jnp.zeros((STATE, CHUNK), jnp.float32)
            g_b, g_c = lax.fori_loop(0, CHUNK, backward, (blank, blank))
            gdbl_ref[rows, 128 : 128 + STATE] = jnp.transpose(g_b)
            gdbl_ref[rows, 128 + STATE : 128 + 2 * STATE] = jnp.transpose(g_c)
            z_f = z_ref[rows]
            grad = gs_ref[rows]
            sig = jax.nn.sigmoid(z_f)
            gz_ref[rows] = (grad * y_scr[...] * (sig * (1.0 + z_f * (1.0 - sig)))).astype(
                jnp.bfloat16
            )
            gy = grad * (z_f * sig)
            x_f = xa_ref[rows].astype(jnp.float32)
            gx_ref[rows] = step_scr[rows] * gu_scr[rows] + vec_ref[2:3] * gy
            gvec_ref[2:3] += jnp.sum(gy * x_f, axis=0, keepdims=True)
            return carry

        lax.fori_loop(0, count, chunk_step, 0)

    for lo, hi in spans(width, LANES):
        rate = jnp.exp(vec_ref[1:2, lo:hi])
        x_f = xa_ref[:, lo:hi].astype(jnp.float32)
        gl = rate * gl_scr[:, lo:hi]
        gpre = (x_f * gu_scr[:, lo:hi] - gl) * slope_scr[:, lo:hi]
        gvec_ref[0:1, lo:hi] += jnp.sum(gpre, axis=0, keepdims=True)
        gvec_ref[1:2, lo:hi] -= jnp.sum(step_scr[:, lo:hi] * gl, axis=0, keepdims=True)
        gpre_scr[:, lo:hi] = gpre.astype(jnp.bfloat16)
    gdtw_ref[...] += dot_first(dbl_ref[:, :RANK], gpre_scr[...])
    gdbl_ref[:, :RANK] = dot_last(gpre_scr[...], dtw_ref[...])


def scan_specs(width, backward, blocks):
    def at(i):
        return (blocks - 1 - i) if backward else i

    rows = lambda cols: pl.BlockSpec((ROWS, cols), lambda i: (at(i), 0))
    whole = lambda *shape: pl.BlockSpec(shape, lambda i: (0, 0))
    return [
        rows(width),
        rows(width),
        rows(256),
        rows(8),
        pl.BlockSpec((1, ROWS), lambda i: (0, at(i))),
        whole(RANK, width),
        whole(8, width),
    ], pl.BlockSpec((ROWS // CHUNK, STATE, width), lambda i: (at(i), 0, 0)), rows, whole


def scan_forward(x_act, z_gate, dbl, masks, seg_row, dt_weight, vectors):
    tokens, width = x_act.shape
    blocks = tokens // ROWS
    in_specs, state_spec, rows, whole = scan_specs(width, False, blocks)
    return pl.pallas_call(
        scan_fwd_kernel,
        name="scan_fwd",
        grid=(blocks,),
        in_specs=in_specs,
        out_specs=[rows(width), state_spec],
        out_shape=[
            jax.ShapeDtypeStruct((tokens, width), jnp.bfloat16),
            jax.ShapeDtypeStruct((tokens // CHUNK, STATE, width), jnp.float32),
        ],
        scratch_shapes=[
            pltpu.VMEM((STATE, width), jnp.float32),
            pltpu.VMEM((ROWS, width), jnp.float32),
            pltpu.VMEM((ROWS, width), jnp.float32),
            pltpu.VMEM((CHUNK, width), jnp.float32),
        ],
        compiler_params=pltpu.CompilerParams(vmem_limit_bytes=40 << 20),
        cost_estimate=pl.CostEstimate(
            flops=0, bytes_accessed=93 << 20, transcendentals=0
        ),
    )(x_act, z_gate, dbl, masks, seg_row, dt_weight, vectors)


def scan_backward(x_act, z_gate, dbl, masks, seg_row, dt_weight, vectors, states, grad_rows):
    tokens, width = x_act.shape
    blocks = tokens // ROWS
    in_specs, state_spec, rows, whole = scan_specs(width, True, blocks)
    return pl.pallas_call(
        scan_bwd_kernel,
        name="scan_bwd",
        grid=(blocks,),
        in_specs=in_specs + [state_spec, rows(width)],
        out_specs=[rows(width), rows(width), rows(256), whole(RANK, width), whole(8, width)],
        out_shape=[
            jax.ShapeDtypeStruct((tokens, width), jnp.bfloat16),
            jax.ShapeDtypeStruct((tokens, width), jnp.float32),
            jax.ShapeDtypeStruct((tokens, 256), jnp.float32),
            jax.ShapeDtypeStruct((RANK, width), jnp.float32),
            jax.ShapeDtypeStruct((8, width), jnp.float32),
        ],
        scratch_shapes=[
            pltpu.VMEM((STATE, width), jnp.float32),
            pltpu.VMEM((ROWS, width), jnp.float32),
            pltpu.VMEM((ROWS, width), jnp.float32),
            pltpu.VMEM((ROWS, width), jnp.float32),
            pltpu.VMEM((ROWS, width), jnp.float32),
            pltpu.VMEM((ROWS, width), jnp.float32),
            pltpu.VMEM((ROWS, width), jnp.bfloat16),
            pltpu.VMEM((CHUNK + 1, STATE, width), jnp.float32),
            pltpu.VMEM((CHUNK, width), jnp.float32),
        ],
        compiler_params=pltpu.CompilerParams(vmem_limit_bytes=48 << 20),
        cost_estimate=pl.CostEstimate(
            flops=0, bytes_accessed=244 << 20, transcendentals=0
        ),
    )(x_act, z_gate, dbl, masks, seg_row, dt_weight, vectors, states, grad_rows)


def scan_masks(segs_flat):
    tokens = segs_flat.shape[0]
    before = jnp.concatenate([jnp.full((1,), -1, jnp.int32), segs_flat[:-1]])
    chunked = segs_flat.reshape(tokens // CHUNK, CHUNK)
    prior = before.reshape(tokens // CHUNK, CHUNK)[:, :1]
    last = chunked[:, CHUNK - 1 :]
    linked = chunked == prior
    tail = chunked == last
    keep = jnp.broadcast_to(last == prior, chunked.shape)
    same = (segs_flat == before).reshape(chunked.shape)
    blank = jnp.zeros_like(linked)
    stacked = jnp.stack([linked, tail, keep, same], axis=-1).reshape(tokens, 4).astype(jnp.float32)
    number = segs_flat.astype(jnp.float32)
    masks = jnp.concatenate(
        [stacked, number[:, None], jnp.zeros((tokens, 3), jnp.float32)], axis=1
    )
    return masks, number[None, :]


def per_device(
    inputs,
    teacher,
    segment_ids,
    valid,
    norm_in_gain,
    w_query,
    w_key,
    w_value,
    w_attn_out,
    w_mamba_in,
    conv_weight,
    conv_bias,
    x_proj,
    dt_proj,
    dt_bias,
    a_log,
    d_skip,
    w_mamba_out,
    attn_norm_gain,
    ssm_norm_gain,
    norm_mid_gain,
    w_gate,
    w_up,
    w_down,
):
    rank_index = lax.axis_index("tensor")
    first_slot, second_slot = rank_index, KV - 1
    per_slot = HEADS // KV
    group_width = per_slot * HEAD
    query_width = 2 * group_width
    qkv_width = query_width + 4 * HEAD
    width = inputs.shape[1]
    inner_width = w_mamba_out.shape[0]
    low = lambda values: values.astype(jnp.bfloat16)
    gather_dp = lambda part: lax.all_gather(part, "dp", axis=0, tiled=True)
    scatter_dp = lambda part: lax.psum_scatter(part, "dp", scatter_dimension=0, tiled=True)
    gather_t = lambda part: gather_rows(part, 1)
    tie = lax.optimization_barrier

    own_width = w_query.shape[0]
    out_local = pick_groups(w_attn_out, first_slot, second_slot, group_width, 0).T
    mamba_local = jnp.concatenate(
        [out_local, w_mamba_in.reshape(own_width, 2 * inner_width), w_mamba_out.T], axis=1
    )
    x_at, z_at = query_width, query_width + inner_width
    back_at = z_at + inner_width
    mamba_local = jnp.pad(mamba_local, ((0, 0), (0, -mamba_local.shape[1] % 128)))
    mamba_all = gather_dp(mamba_local)
    part_of = lambda at: (mamba_all, None, at // 128 * 128, -(-(at % 128 + inner_width) // 128) * 128)
    w_query, w_key, w_value, norm_in_gain, _ = tie(
        (w_query, w_key, w_value, norm_in_gain, mamba_local)
    )
    group_rows = 4 * inputs.shape[0]
    seq_count = group_rows // LEN
    segs_grid = segment_ids.reshape(seq_count, LEN)
    segs_flat = (segs_grid + 128 * jnp.arange(seq_count, dtype=jnp.int32)[:, None]).reshape(-1)
    scan_mask, seg_row = scan_masks(segs_flat)
    starts = first_blocks(segs_flat)
    blocks = jnp.arange(group_rows // BQ, dtype=jnp.int32)
    shared_here = blocks // (group_rows // BQ // 4) == rank_index
    firsts = jnp.concatenate([starts, jnp.where(shared_here, starts, blocks + 1)])
    first_local = jnp.concatenate(
        [
            pick_groups(w_query, first_slot, second_slot, group_width, 1),
            pick_groups(w_key, first_slot, second_slot, HEAD, 1),
            pick_groups(w_value, first_slot, second_slot, HEAD, 1),
        ],
        axis=1,
    )
    gain_rows = jnp.stack([norm_in_gain, attn_norm_gain, ssm_norm_gain, norm_mid_gain])
    gains, valid_total = hello(gain_rows, jnp.sum(valid).astype(jnp.float32))
    gain_in, gain_attn, gain_ssm, gain_mid = [gains[index][:, None] for index in range(4)]
    inputs_t = inputs.T
    normed_in, pull_in = jax.vjp(normalize_t, inputs_t, gain_in)
    normed_low, first_local, w_gate, w_up, w_down = tie(
        (low(normed_in), first_local, w_gate, w_up, w_down)
    )
    whole_in, qkv_w = gather_first(normed_low, first_local)
    whole_in, w_gate, w_up, w_down = tie((whole_in, w_gate, w_up, w_down))
    qkv_cols = low(dot_first(qkv_w, whole_in))
    attended_t, log_totals = attn_forward(firsts, qkv_cols, seg_row, scan_mask, 2)
    attended_t, x_proj, dt_proj, conv_weight = tie((attended_t, x_proj, dt_proj, conv_weight))
    inner_local = jnp.concatenate(
        [
            dt_bias[:, None],
            a_log[:, None],
            d_skip[:, None],
            conv_bias[:, None],
            conv_weight.T,
            x_proj,
            dt_proj.T,
        ],
        axis=1,
    )
    inner_rows = inner_spread(inner_local)
    attended_t, inner_rows = tie((attended_t, inner_rows))
    attn_sum = product_reduce(
        [(mamba_all, None, 0, query_width)],
        [(attended_t, True)],
        [(0, 0, query_width, 0)],
        10,
        "attn_reduce",
        43,
    )
    out_w = mamba_all[:, :query_width]
    weight_x = mamba_all[:, x_at:z_at]
    weight_z = mamba_all[:, z_at:back_at]
    mamba_out_w = mamba_all[:, back_at : back_at + inner_width]
    x_in = dot_first(whole_in, weight_x)
    ff_width = w_gate.shape[1]
    ff_step = -(-ff_width // 128) * 128
    blank = jnp.zeros((own_width, ff_step - ff_width), jnp.bfloat16)
    gate_up_local = jnp.concatenate([w_gate, blank, w_up, blank], axis=1)
    down_local = jnp.concatenate([w_down.T, blank], axis=1)
    gate_up_local, down_local = tie((gate_up_local, down_local))
    gate_up_all = gather_dp(gate_up_local)
    down_all = gather_dp(down_local)
    vector_rows = inner_rows[:, :8].astype(jnp.float32).T
    xproj_rows = inner_rows[:, 8 : 8 + RANK + 2 * STATE]
    dt_weight = inner_rows[:, 8 + RANK + 2 * STATE :].T
    xproj_pad = jnp.concatenate(
        [
            xproj_rows[:, :RANK],
            jnp.zeros((inner_width, 128 - RANK), jnp.bfloat16),
            xproj_rows[:, RANK:],
            jnp.zeros((inner_width, 128 - 2 * STATE), jnp.bfloat16),
        ],
        axis=1,
    )
    x_pre, pull_conv = jax.vjp(
        lambda x_part, taps, shift: conv_rows(x_part, taps, shift, segs_grid),
        x_in,
        vector_rows[4:],
        vector_rows[3],
    )
    x_act = low(x_pre)
    dbl_pad = total_rows(dot_plain(x_act, xproj_pad), 3)
    z_gate = dot_first(whole_in, weight_z)
    ssm_rows, states = scan_forward(
        x_act, z_gate, dbl_pad, scan_mask, seg_row, dt_weight, vector_rows
    )
    ssm_sum = product_reduce(
        [part_of(back_at)],
        [(ssm_rows, False)],
        [(0, back_at % 128, back_at % 128 + inner_width, 0)],
        11,
        "ssm_reduce",
        43,
    )
    mixed, pull_join = jax.vjp(join_rows_t, inputs_t, attn_sum, ssm_sum, gain_attn, gain_ssm)
    normed_mid, pull_mid = jax.vjp(normalize_t, mixed, gain_mid)
    normed_low, gate_up_all = tie((low(normed_mid), gate_up_all))
    whole_mid, gate_rows, up_rows, hidden = turn_rows(
        normed_low,
        gate_up_all,
        [],
        [(ff_width, jnp.float32), (ff_width, jnp.float32), (ff_width, jnp.bfloat16)],
        [(0, ff_width), (ff_step, ff_step + ff_width)],
        forward_gate,
        15,
        "gate_turn",
        52,
    )
    ffn_rows = product_reduce(
        [(down_all, None, 0, ff_step)], [(hidden, False)], [(0, 0, ff_width, 0)], 6, "down_reduce", 45
    )
    result = mixed + ffn_rows
    all_rows = inputs.shape[0] * lax.axis_size("dp") * lax.axis_size("tensor")
    grad_out = all_rows / valid_total * valid.astype(jnp.float32)[None, :] * (result - teacher.T)
    grad_ffn, grad_gate, grad_up = turn_rows(
        low(grad_out),
        down_all,
        [gate_rows, up_rows],
        [(ff_width, jnp.bfloat16), (ff_width, jnp.bfloat16)],
        [(0, ff_width)],
        backward_gate,
        16,
        "grad_turn",
        52,
    )
    ffn_grads = weight_grads(
        [
            (whole_mid, grad_gate, False),
            (whole_mid, grad_up, False),
            (grad_ffn, hidden, False),
        ],
        "ffn_weight_grads",
        44,
    )
    grad_gate, grad_up, ffn_grads = tie((grad_gate, grad_up, ffn_grads))
    ffn_shard = scatter_dp(ffn_grads)
    grad_mid_rows = product_reduce(
        [(gate_up_all, None, 0, 2 * ff_step)],
        [(grad_gate, False), (grad_up, False)],
        [(0, 0, ff_width, 0), (0, ff_step, ff_step + ff_width, 1)],
        7,
        "mid_reduce",
        50,
    )
    grad_mixed_norm, grad_gain_mid = pull_mid(grad_mid_rows)
    grad_mixed = grad_out + grad_mixed_norm
    grad_resid, grad_attn_sum, grad_ssm_sum, grad_gain_attn, grad_gain_ssm = pull_join(grad_mixed)
    grad_ssm_whole = gather_t(low(grad_ssm_sum))
    grad_attn_low, grad_ssm_whole = tie((low(grad_attn_sum), grad_ssm_whole))
    grad_attn_whole = gather_t(grad_attn_low)
    grad_ssm_whole, grad_attn_whole = tie((grad_ssm_whole, grad_attn_whole))
    grad_ssm_rows = dot_first(grad_ssm_whole, mamba_out_w)
    grad_gate_part, grad_act_scan, grad_dbl_part, grad_dtproj, grad_vectors = scan_backward(
        x_act, z_gate, dbl_pad, scan_mask, seg_row, dt_weight, vector_rows, states, grad_ssm_rows
    )
    mid_grads = weight_grads(
        [
            (grad_attn_whole, attended_t, True),
            (grad_ssm_whole, ssm_rows, False),
            (whole_in, grad_gate_part, False),
        ],
        "mid_weight_grads",
        26,
        tight=True,
    )
    grad_att_t = low(
        lax.dot_general(
            out_w, grad_attn_whole, (((0,), (0,)), ((), ())), preferred_element_type=jnp.float32
        )
    )
    grad_dbl_part, mid_grads, ffn_shard = tie((grad_dbl_part, mid_grads, ffn_shard))
    mid_shard = scatter_dp(mid_grads)
    grad_qkv = attn_backward(
        firsts, qkv_cols, grad_att_t, attended_t, log_totals, seg_row, scan_mask, 2
    )
    grad_dbl = total_rows(grad_dbl_part, 3)
    grad_act = grad_act_scan + dot_last(grad_dbl, xproj_pad)
    grad_xproj_w = dot_first(x_act, grad_dbl)
    grad_x_part, grad_taps, grad_shift = pull_conv(grad_act)
    grad_x_low = low(grad_x_part)
    inner_grads = jnp.concatenate(
        [
            grad_vectors[:3].T,
            grad_shift[:, None],
            grad_taps.T,
            grad_xproj_w[:, :RANK],
            grad_xproj_w[:, 128 : 128 + 2 * STATE],
            grad_dtproj.T,
        ],
        axis=1,
    )
    last_grads = weight_grads(
        [
            (whole_in, grad_x_low, False),
            (whole_in, grad_qkv, True),
            (low(inner_grads).reshape(width, -1), None, False),
        ],
        "last_weight_grads",
        20,
    )
    grad_x_low, grad_qkv, last_grads, mid_shard = tie(
        (grad_x_low, grad_qkv, last_grads, mid_shard)
    )
    last_shard = scatter_dp(last_grads)
    grad_in_rows = product_reduce(
        [
            (qkv_w, None, None, qkv_width),
            part_of(x_at),
            part_of(z_at),
        ],
        [(grad_qkv, True), (grad_x_low, False), (grad_gate_part, False)],
        [
            (0, 0, qkv_width, 0),
            (1, x_at % 128, x_at % 128 + inner_width, 1),
            (2, z_at % 128, z_at % 128 + inner_width, 2),
        ],
        8,
        "in_reduce",
        52,
    )
    grad_in_norm, grad_gain_in = pull_in(grad_in_rows)
    grad_inputs = grad_resid + grad_in_norm
    gain_grads = jnp.concatenate(
        [grad_gain_in, grad_gain_attn, grad_gain_ssm, grad_gain_mid], axis=1
    )
    gains_own = farewell(gain_grads.T)
    wide = lambda part: jnp.pad(part, ((0, 0), (0, -part.shape[1] % 256)))
    out_stack = gather_stack(wide(mid_shard[:, :query_width]), 5)
    inner_step = -(-inner_width // 128) * 128
    mamba_at = query_width
    gate_at = query_width + inner_width
    def merge(stack, start, size):
        own = [stack[rank, :, start : start + size].astype(jnp.float32) for rank in range(4)]
        both = jnp.sum(
            stack[:, :, start + size : start + 2 * size].astype(jnp.float32), axis=0
        )
        return jnp.concatenate(own + [both], axis=1)

    early = (
        gains_own,
        grad_inputs,
        merge(out_stack, 0, group_width),
        mid_shard[:, mamba_at : mamba_at + inner_width].astype(jnp.float32),
        ffn_shard[:, :ff_width].astype(jnp.float32),
        ffn_shard[:, ff_step : ff_step + ff_width].astype(jnp.float32),
        ffn_shard[:, 2 * ff_step : 2 * ff_step + ff_width].astype(jnp.float32),
    )
    early, last_shard = tie((early, last_shard))
    gains_own, grad_inputs, grad_out_own, grad_back_own, grad_gate_own, grad_up_own, grad_down_own = early
    inner_at = inner_step + qkv_width
    shared_all, owned = gather_final(last_shard, inner_step, inner_at)
    inner_cols = inner_grads.size // width
    inner_sum = owned[:, :, :inner_cols].astype(jnp.float32).reshape(-1, inner_grads.shape[1])
    return (
        result.T,
        grad_inputs.T,
        gains_own[0],
        merge(shared_all, 0, group_width),
        merge(shared_all, query_width, HEAD),
        merge(shared_all, query_width + 2 * HEAD, HEAD),
        grad_out_own.T,
        jnp.stack(
            [last_shard[:, :inner_width], mid_shard[:, gate_at : gate_at + inner_width]], axis=1
        ).astype(jnp.float32),
        inner_sum[:, 4:8].T,
        inner_sum[:, 3],
        inner_sum[:, 8 : 8 + RANK + 2 * STATE],
        inner_sum[:, 8 + RANK + 2 * STATE :].T,
        inner_sum[:, 0],
        inner_sum[:, 1],
        inner_sum[:, 2],
        grad_back_own.T,
        gains_own[1],
        gains_own[2],
        gains_own[3],
        grad_gate_own,
        grad_up_own,
        grad_down_own.T,
    )


def solution(mesh):
    placed = (
        P(("dp", "tensor"), None),
        P(("dp", "tensor"), None),
        P("dp"),
        P(("dp", "tensor")),
        P("dp"),
        P("dp", None),
        P("dp", None),
        P("dp", None),
        P(None, "dp"),
        P("dp", None, "tensor"),
        P(None, "dp"),
        P("dp"),
        P("dp", None),
        P(None, "dp"),
        P("dp"),
        P("dp"),
        P("dp"),
        P("tensor", "dp"),
        P("dp"),
        P("dp"),
        P("dp"),
        P("dp", "tensor"),
        P("dp", "tensor"),
        P("tensor", "dp"),
    )
    return jax.shard_map(
        per_device,
        mesh=mesh,
        in_specs=placed,
        out_specs=(
            P(("dp", "tensor"), None),
            P(("dp", "tensor"), None),
            P("dp"),
            P("dp", None),
            P("dp", None),
            P("dp", None),
            P(None, "dp"),
            P("dp", None, "tensor"),
            P(None, "dp"),
            P("dp"),
            P("dp", None),
            P(None, "dp"),
            P("dp"),
            P("dp"),
            P("dp"),
            P("tensor", "dp"),
            P("dp"),
            P("dp"),
            P("dp"),
            P("dp", "tensor"),
            P("dp", "tensor"),
            P("tensor", "dp"),
        ),
        check_vma=False,
    )
```
